32 devices in a mesh: dp: 8 (over z, y), group: 4 (over x, core).
Axes of the slice: x: 2, y: 2, z: 4, core: 2. Of those that a mesh axis runs over, the one named last changes fastest.
Arguments:
- features: bfloat16 [2, 32, 128, 512], P(None, ('dp', 'group')), may hold values from -6 to 6
- span_starts: int32 [2, 32, 10], P(None, ('dp', 'group')), may hold values from 0 to 128, as said below
- labels: int32 [2, 32, 128], P(None, ('dp', 'group')), may hold values from 0 to 503
- feature_norm: float32 [2, 512], replicated
- feature_first: float32 [2, 512], replicated, may hold values from -1.9073486e-05 to 1.9073486e-05
- feature_second: float32 [2, 512], replicated, may hold values from 2.6034745e-12 to 1.0381954e-11
- projection: float32 [512, 768], P('dp', 'group'), may hold values from -0.25 to 0.25
- projection_first: float32 [512, 768], P('dp', 'group'), may hold values from -4.7683716e-06 to 4.7683716e-06
- projection_second: float32 [512, 768], P('dp', 'group'), may hold values from 1.6291681e-13 to 6.5166725e-13
- vectors: float32 [7, 768], replicated
- vector_first: float32 [7, 768], replicated, may hold values from -1.9073486e-05 to 1.9073486e-05
- vector_second: float32 [7, 768], replicated, may hold values from 2.6034745e-12 to 1.0381954e-11
- conv_weight: float32 [128, 48, 768], P('group', None, 'dp'), may hold values from -0.078125 to 0.078125
- conv_first: float32 [128, 48, 768], P('group', None, 'dp'), may hold values from -4.7683716e-06 to 4.7683716e-06
- conv_second: float32 [128, 48, 768], P('group', None, 'dp'), may hold values from 1.6291681e-13 to 6.5166725e-13
- head: float32 [768, 256], P('dp', 'group'), may hold values from -0.21875 to 0.21875
- head_first: float32 [768, 256], P('dp', 'group'), may hold values from -4.7683716e-06 to 4.7683716e-06
- head_second: float32 [768, 256], P('dp', 'group'), may hold values from 1.6291681e-13 to 6.5166725e-13
- clusters: float32 [504, 256], P('group', 'dp'), may hold values from -0.3 to 0.3
- cluster_first: float32 [504, 256], P('group', 'dp'), may hold values from -4.7683716e-06 to 4.7683716e-06
- cluster_second: float32 [504, 256], P('group', 'dp'), may hold values from 1.6291681e-13 to 6.5166725e-13
- blocks: float32 [12, 768, 768], P('group', 'dp'), may hold values from -0.21875 to 0.21875
- statistics: float32 [12, 2, 768, 768], P('group', None, 'dp'), as said below
Outputs:
- loss_sum: float32 [], replicated
- masked_count: float32 [], replicated
- grad_norm: float32 [], replicated
- feature_first_new: float32 [2, 512], replicated
- feature_second_new: float32 [2, 512], replicated
- feature_norm_new: float32 [2, 512], replicated
- projection_first_new: float32 [512, 768], P('dp', 'group')
- projection_second_new: float32 [512, 768], P('dp', 'group')
- projection_new: float32 [512, 768], P('dp', 'group')
- vector_first_new: float32 [7, 768], replicated
- vector_second_new: float32 [7, 768], replicated
- vectors_new: float32 [7, 768], replicated
- conv_first_new: float32 [128, 48, 768], P('group', None, 'dp')
- conv_second_new: float32 [128, 48, 768], P('group', None, 'dp')
- conv_weight_new: float32 [128, 48, 768], P('group', None, 'dp')
- head_first_new: float32 [768, 256], P('dp', 'group')
- head_second_new: float32 [768, 256], P('dp', 'group')
- head_new: float32 [768, 256], P('dp', 'group')
- cluster_first_new: float32 [504, 256], P('group', 'dp')
- cluster_second_new: float32 [504, 256], P('group', 'dp')
- clusters_new: float32 [504, 256], P('group', 'dp')
- block_grad: float32 [12, 768, 768], P('group', 'dp')
- statistics_new: float32 [12, 2, 768, 768], P('group', None, 'dp')
- blocks_new: float32 [12, 768, 768], P('group', 'dp')
The draws below stay inside these ranges and needn't reach their ends.
Inputs may be any that keep to these rules, and one draw needn't show every extreme that they name: `span_starts`: an entry equal to 128 names no span; every other entry is at most 118; every clip has at least 3 spans. `statistics`: each left and right matrix is symmetric and positive definite.
All inputs are finite; a program needn't handle non-finite values.
Results may differ from the reference program's by a relative error of at most 0.008.
The reference program's roundings to bfloat16 on the way count: a program that leaves them out, or rounds other values in their place, can miss the bound.
Values may be sent and summed in bfloat16 or wider, within the bound.
A program may use at most 448 MiB of HBM per device.

```python
import math
import jax
import jax.numpy as jnp
from jax import lax

FEAT = 512
D = 768
HEADS = 12
HEAD = 64
FF = 3072
PROJ = 256
CLUSTERS = 504
TAPS = 128
CGROUPS = 16
CLIP = 128
SPAN = 10
SPANS = 10
LAYERS = 1
MICRO = 2
NEWTON = 3
STEP = 10
CLIPS = 32
NB = 12
VEC = 7
PARAMS = 12521728


def draw_span_starts(key, part):
    key = jax.random.fold_in(key, 1)
    start_key, extra_key = jax.random.split(key)
    clip_index = jnp.arange(CLIPS, dtype=jnp.int32)[None, :, None]
    least = SPANS // 3
    live = least + (SPANS - least) * clip_index // CLIPS + jax.random.randint(extra_key, (MICRO, CLIPS, 1), 0, 2)
    slot = jnp.arange(SPANS, dtype=jnp.int32)[None, None, :]
    starts = jax.random.randint(start_key, (MICRO, CLIPS, SPANS), 0, CLIP - SPAN + 1)
    return jnp.where(slot < live, starts, CLIP).astype(jnp.int32)


def draw_feature_norm(key, part):
    key = jax.random.fold_in(key, 2)
    gain_key, bias_key = jax.random.split(key)
    ramp = 0.5 + jnp.arange(FEAT, dtype=jnp.float32) / FEAT
    gains = ramp * jax.random.uniform(gain_key, (FEAT,), jnp.float32, 0.7, 1.3)
    biases = 0.3 * jax.random.normal(bias_key, (FEAT,), jnp.float32)
    return jnp.stack([gains, biases])


def draw_vectors(key, part):
    key = jax.random.fold_in(key, 3)
    gain_key, other_key = jax.random.split(key)
    row = jnp.arange(VEC, dtype=jnp.int32)[:, None]
    ramp = 0.5 + jnp.arange(D, dtype=jnp.float32)[None, :] / D
    gains = ramp * jax.random.uniform(gain_key, (VEC, D), jnp.float32, 0.7, 1.3)
    others = jnp.where(row == 0, 1.0, 0.3) * jax.random.normal(other_key, (VEC, D), jnp.float32)
    is_gain = (row == 1) | (row >= 3) & (row % 2 == 1)
    return jnp.where(is_gain, gains, others)


def draw_statistics(key, part):
    key = jax.random.fold_in(key, 4)
    diagonal_key, spread_key = jax.random.split(key)
    scale = 5.26e-06 * D / PARAMS
    diagonal = scale * jnp.exp(jax.random.uniform(diagonal_key, (NB, 2, D, 1), jnp.float32, 0.0, 1.3863))
    noise = jax.random.uniform(spread_key, (NB, 2, D, D), jnp.float32, -1.0, 1.0)
    mixed = 0.5 * (noise + jnp.swapaxes(noise, 2, 3))
    rows = jnp.arange(D, dtype=jnp.int32)
    same = rows[:, None] == rows[None, :]
    return jnp.where(same, diagonal, 0.95 * scale / D * mixed)


def touch_ends(array, rng, low, top_value):
    longest = array.shape.index(max(array.shape))
    spots = []
    for shift in (0, 1):
        where = [jax.random.randint(jax.random.fold_in(rng, axis), (), 0, length) for axis, length in enumerate(array.shape)]
        where[longest] = (where[longest] + shift) % array.shape[longest]
        spots.append(tuple(where))
    return array.at[spots[0]].set(low).at[spots[1]].set(top_value)


def block_scale(stream_key, dims, shards, low, top_value):
    loudness, own = 1.0, jax.random.fold_in(stream_key, 6)
    for axis_at, blocks in shards:
        draws = jnp.exp(jax.random.uniform(jax.random.fold_in(own, axis_at), (blocks,), jnp.float32, low / len(shards), top_value / len(shards)))
        loudness = loudness * jnp.repeat(draws, dims[axis_at] // blocks).reshape([-1 if axis == axis_at else 1 for axis in range(len(dims))])
    return loudness


def bell_draw(rng, shape, deviation, reach, shards=(), kind=jnp.bfloat16):
    loudness = block_scale(rng, shape, shards, -0.22, 0.18) if shards else 1.0
    drawn = jax.random.normal(rng, shape, jnp.float32) * deviation * loudness
    return jnp.minimum(jnp.maximum(drawn, -reach), reach).astype(kind)


def setup_inputs(seed: int = 0) -> dict:
    key_of = jax.random.split(jax.random.key(seed), 24)
    features = bell_draw(key_of[0], (MICRO, CLIPS, CLIP, FEAT), 1.0, 6.0, ((1, 32),))
    span_starts = draw_span_starts(jax.random.fold_in(key_of[23], 71), 0)
    labels = touch_ends(jax.random.randint(key_of[2], (MICRO, CLIPS, CLIP), 0, CLUSTERS), jax.random.fold_in(key_of[2], 1), 0, CLUSTERS - 1).astype(jnp.int32)
    feature_norm = draw_feature_norm(jax.random.fold_in(key_of[23], 71), 0)
    feature_first = bell_draw(key_of[4], (2, FEAT), (0.00444 * PARAMS ** -0.5), 1.9073486328125e-05, (), jnp.float32)
    feature_second = jnp.clip(jnp.exp(jax.random.uniform(key_of[5], (2, FEAT), jnp.float32, math.log(2.6034745106290336e-12), math.log(1.038195397706776e-11))), 2.6034745106290336e-12, 1.038195397706776e-11)
    projection = bell_draw(key_of[6], (FEAT, D), FEAT ** -0.5, 0.25, ((0, 8), (1, 4)), jnp.float32)
    projection_first = bell_draw(key_of[7], (FEAT, D), (0.00111 * PARAMS ** -0.5), 4.76837158203125e-06, ((0, 8), (1, 4)), jnp.float32)
    projection_second = jnp.clip(jnp.exp(math.log(6.516672509775112e-13) - 1.3862944 * jax.random.uniform(key_of[8], (FEAT, D), jnp.float32) ** block_scale(key_of[8], (FEAT, D), ((0, 8), (1, 4)), -0.2, 0.2)), 1.629168127443778e-13, 6.516672509775112e-13)
    vectors = draw_vectors(jax.random.fold_in(key_of[23], 71), 0)
    vector_first = bell_draw(key_of[10], (VEC, D), (0.00444 * PARAMS ** -0.5), 1.9073486328125e-05, (), jnp.float32)
    vector_second = jnp.clip(jnp.exp(jax.random.uniform(key_of[11], (VEC, D), jnp.float32, math.log(2.6034745106290336e-12), math.log(1.038195397706776e-11))), 2.6034745106290336e-12, 1.038195397706776e-11)
    conv_weight = bell_draw(key_of[12], (TAPS, D // CGROUPS, D), (TAPS * D // CGROUPS) ** -0.5, 0.078125, ((0, 4), (2, 8)), jnp.float32)
    conv_first = bell_draw(key_of[13], (TAPS, D // CGROUPS, D), (0.00111 * PARAMS ** -0.5), 4.76837158203125e-06, ((0, 4), (2, 8)), jnp.float32)
    conv_second = jnp.clip(jnp.exp(math.log(6.516672509775112e-13) - 1.3862944 * jax.random.uniform(key_of[14], (TAPS, D // CGROUPS, D), jnp.float32) ** block_scale(key_of[14], (TAPS, D // CGROUPS, D), ((0, 4), (2, 8)), -0.2, 0.2)), 1.629168127443778e-13, 6.516672509775112e-13)
    head = bell_draw(key_of[15], (D, PROJ), D ** -0.5, 0.21875, ((0, 8), (1, 4)), jnp.float32)
    head_first = bell_draw(key_of[16], (D, PROJ), (0.00111 * PARAMS ** -0.5), 4.76837158203125e-06, ((0, 8), (1, 4)), jnp.float32)
    head_second = jnp.clip(jnp.exp(math.log(6.516672509775112e-13) - 1.3862944 * jax.random.uniform(key_of[17], (D, PROJ), jnp.float32) ** block_scale(key_of[17], (D, PROJ), ((0, 8), (1, 4)), -0.2, 0.2)), 1.629168127443778e-13, 6.516672509775112e-13)
    clusters = bell_draw(key_of[18], (CLUSTERS, PROJ), 0.05, 0.3, ((0, 4), (1, 8)), jnp.float32)
    cluster_first = bell_draw(key_of[19], (CLUSTERS, PROJ), (0.00111 * PARAMS ** -0.5), 4.76837158203125e-06, ((0, 4), (1, 8)), jnp.float32)
    cluster_second = jnp.clip(jnp.exp(math.log(6.516672509775112e-13) - 1.3862944 * jax.random.uniform(key_of[20], (CLUSTERS, PROJ), jnp.float32) ** block_scale(key_of[20], (CLUSTERS, PROJ), ((0, 4), (1, 8)), -0.2, 0.2)), 1.629168127443778e-13, 6.516672509775112e-13)
    blocks = bell_draw(key_of[21], (NB, D, D), D ** -0.5, 0.21875, ((0, 4), (1, 8)), jnp.float32)
    statistics = draw_statistics(jax.random.fold_in(key_of[23], 71), 0)
    return {"features": features, "span_starts": span_starts, "labels": labels, "feature_norm": feature_norm, "feature_first": feature_first, "feature_second": feature_second, "projection": projection, "projection_first": projection_first, "projection_second": projection_second, "vectors": vectors, "vector_first": vector_first, "vector_second": vector_second, "conv_weight": conv_weight, "conv_first": conv_first, "conv_second": conv_second, "head": head, "head_first": head_first, "head_second": head_second, "clusters": clusters, "cluster_first": cluster_first, "cluster_second": cluster_second, "blocks": blocks, "statistics": statistics}


HIGH = lax.Precision.HIGHEST
beta_one = 0.9
beta_two = 0.98
adam_eps = 1e-08
rate_matrix = 0.02
rate_vector = 0.5
rate_shampoo = 0.2
decay_weight = 0.01
stat_decay = 0.95
max_norm = 0.01
inv_temp = 10.0

@jax.custom_vjp
def low(v):
    return lax.optimization_barrier(v.astype(jnp.bfloat16)).astype(jnp.float32)

@jax.custom_vjp
def low_back(v):
    return v

def low_keep(v):
    return (low(v), None)

def low_pass(kept, grad):
    return (grad,)

def back_keep(v):
    return (v, None)

def back_low(kept, grad):
    return (low(grad),)
low.defvjp(low_keep, low_pass)
low_back.defvjp(back_keep, back_low)

def rounded(values):
    return low(low_back(values))

def norm_rows(values, gain, bias):
    average = lax.optimization_barrier(jnp.mean(values, -1, keepdims=True))
    centred = values - average
    spread = lax.optimization_barrier(jnp.mean(centred * centred, -1, keepdims=True))
    return centred * lax.rsqrt(spread + 1e-05) * gain + bias

def unit_rows(values):
    return values * lax.rsqrt(lax.optimization_barrier(jnp.sum(values * values, -1, keepdims=True)) + 1e-06)

def gelu_exact(values):
    return jax.nn.gelu(values, approximate=False)

def frame_mask(starts):
    frames = jnp.arange(CLIP, dtype=jnp.int32)[:, None]
    inside = (frames >= starts[None, :]) & (frames < starts[None, :] + SPAN)
    return jnp.any(inside, axis=1).astype(jnp.float32)

def layer(hidden, weights, gains):
    frames = hidden.shape[0]
    blocks_ff = FF // D
    triple = rounded(jnp.einsum('nd,jde->nje', low(hidden), weights[:3], precision=HIGH))
    heads = triple.reshape(frames, 3, HEADS, HEAD)
    query, keys, values = (heads[:, 0], heads[:, 1], heads[:, 2])
    scores = low_back(jnp.einsum('qhd,khd->hqk', query, keys, precision=HIGH) * HEAD ** (-0.5))
    attention = low(jax.nn.softmax(scores, axis=-1))
    mixed = rounded(jnp.einsum('hqk,khd->qhd', attention, values, precision=HIGH).reshape(frames, D))
    attended = low_back(jnp.dot(mixed, weights[3], precision=HIGH))
    middle = norm_rows(hidden + attended, gains[0], gains[1])
    expanded = low_back(jnp.einsum('nd,jde->nje', low(middle), weights[4:4 + blocks_ff], precision=HIGH))
    active = low(gelu_exact(expanded))
    reduced = low_back(jnp.einsum('nje,jed->nd', active, weights[4 + blocks_ff:], precision=HIGH))
    return norm_rows(middle + reduced, gains[2], gains[3])

def clip_loss(params, frames_in, starts, targets, centers):
    feature_norm, projection, vectors, kernel, blocks, head = params
    mask = frame_mask(starts)
    normed = norm_rows(frames_in, feature_norm[0], feature_norm[1])
    projected = low_back(jnp.dot(low(normed), projection, precision=HIGH))
    hidden = jnp.where(mask[:, None] > 0, vectors[0][None, :], projected)
    kernel_out = low_back(lax.conv_general_dilated(low(hidden)[None], kernel, (1,), [(TAPS // 2, TAPS // 2 - 1)], dimension_numbers=('NWC', 'WIO', 'NWC'), feature_group_count=CGROUPS, precision=HIGH)[0])
    hidden = norm_rows(hidden + gelu_exact(kernel_out), vectors[1], vectors[2])
    per_layer = NB // LAYERS
    for level in range(LAYERS):
        hidden = layer(hidden, blocks[level * per_layer:(level + 1) * per_layer], vectors[3 + 4 * level:7 + 4 * level])
    embedded = low_back(jnp.dot(low(hidden), head, precision=HIGH))
    logits = low_back(inv_temp * jnp.dot(low(unit_rows(embedded)), centers.T, precision=HIGH))
    choose = targets[:, None] == jnp.arange(CLUSTERS, dtype=jnp.int32)[None, :]
    target = lax.optimization_barrier(jnp.sum(jnp.where(choose, logits, 0.0), axis=-1))
    return jnp.sum(mask * (jax.nn.logsumexp(logits, axis=-1) - target))

def adamw(weight, grad, first, second, rate, decay):
    first = beta_one * first + (1 - beta_one) * grad
    second = beta_two * second + (1 - beta_two) * grad * grad
    corrected = first / (1 - beta_one ** STEP)
    scaled = jnp.sqrt(second / (1 - beta_two ** STEP)) + adam_eps
    return (first, second, weight - rate * (corrected / scaled + decay * weight))

def inverse_root(matrix):
    size = matrix.shape[0]
    identity = jnp.eye(size, dtype=jnp.float32)
    damped = matrix + 0.0001 * (jnp.trace(matrix) / size) * identity
    magnitude = jnp.sqrt(jnp.sum(damped * damped))
    current = damped / magnitude
    result = identity * magnitude ** (-0.25)
    for sweep in range(NEWTON):
        factor = (5.0 * identity - current) * 0.25
        result = jnp.dot(result, factor, precision=HIGH)
        square = jnp.dot(factor, factor, precision=HIGH)
        current = jnp.dot(jnp.dot(square, square, precision=HIGH), current, precision=HIGH)
    return result

def shampoo_block(operands):
    weight, grad, stats = operands
    left = stat_decay * stats[0] + (1 - stat_decay) * jnp.dot(grad, grad.T, precision=HIGH)
    right = stat_decay * stats[1] + (1 - stat_decay) * jnp.dot(grad.T, grad, precision=HIGH)
    update = jnp.dot(jnp.dot(inverse_root(left), grad, precision=HIGH), inverse_root(right), precision=HIGH)
    return (jnp.stack([left, right]), weight - rate_shampoo * (update + decay_weight * weight))

def reference(features, span_starts, labels, feature_norm, feature_first, feature_second, projection, projection_first, projection_second, vectors, vector_first, vector_second, conv_weight, conv_first, conv_second, head, head_first, head_second, clusters, cluster_first, cluster_second, blocks, statistics):
    frames_all = features.astype(jnp.float32).reshape(MICRO * CLIPS, CLIP, FEAT)
    starts_all = span_starts.reshape(MICRO * CLIPS, SPANS)
    targets_all = labels.reshape(MICRO * CLIPS, CLIP)
    masked_count = jnp.sum(jax.vmap(frame_mask)(starts_all))

    def objective(norm_params, proj_params, vector_params, kernel_params, head_params, cluster_params, block_params):
        centers = low(unit_rows(low(cluster_params)))
        params = (norm_params, low(proj_params), vector_params, low(kernel_params), low(block_params), low(head_params))

        def one_clip(total, inputs):
            return (total + clip_loss(params, inputs[0], inputs[1], inputs[2], centers), None)
        total, _ = lax.scan(jax.checkpoint(one_clip), jnp.zeros((), jnp.float32), (frames_all, starts_all, targets_all))
        return total
    loss_sum, back = jax.vjp(objective, feature_norm, projection, vectors, conv_weight, head, clusters, blocks)
    gradients = back(1.0 / masked_count)
    grad_norm = jnp.sqrt(sum((jnp.sum(grad * grad) for grad in gradients)))
    factor = jnp.minimum(1.0, max_norm / (grad_norm + 1e-06))
    clipped = [grad * factor for grad in gradients]
    feature_out = adamw(feature_norm, clipped[0], feature_first, feature_second, rate_vector, 0.0)
    projection_out = adamw(projection, clipped[1], projection_first, projection_second, rate_matrix, decay_weight)
    vector_out = adamw(vectors, clipped[2], vector_first, vector_second, rate_vector, 0.0)
    conv_out = adamw(conv_weight, clipped[3], conv_first, conv_second, rate_matrix, decay_weight)
    head_out = adamw(head, clipped[4], head_first, head_second, rate_matrix, decay_weight)
    cluster_out = adamw(clusters, clipped[5], cluster_first, cluster_second, rate_matrix, decay_weight)
    statistics_new, blocks_new = lax.map(shampoo_block, (blocks, clipped[6], statistics))
    return (loss_sum, masked_count, grad_norm, feature_out[0], feature_out[1], feature_out[2], projection_out[0], projection_out[1], projection_out[2], vector_out[0], vector_out[1], vector_out[2], conv_out[0], conv_out[1], conv_out[2], head_out[0], head_out[1], head_out[2], cluster_out[0], cluster_out[1], cluster_out[2], clipped[6], statistics_new, blocks_new)
```

```python
import functools

import jax
import jax.numpy as jnp
from jax import lax
from jax.experimental import pallas as pl
from jax.experimental.pallas import tpu as pltpu
from jax.sharding import PartitionSpec as P

D = 768
HEADS = 12
HEAD = 64
TAPS = 128
CLIP = 128
SPAN = 10
NEWTON = 3
STEP = 10


HIGH = lax.Precision.HIGHEST
beta_one = 0.9
beta_two = 0.98
adam_eps = 1e-08
rate_matrix = 0.02
rate_vector = 0.5
rate_shampoo = 0.2
decay_weight = 0.01
stat_decay = 0.95
max_norm = 0.01
inv_temp = 10.0
STRIDE = 4


def for_sending(array):

    def short(part):
        return part.astype(jnp.bfloat16) if part.dtype == jnp.float32 else part

    return jax.tree.map(short, array)


def spread_2(array, axis, root):
    mine = lax.axis_index(axis) == root
    return lax.psum(jnp.where(mine, array, jnp.zeros_like(array)), axis)


def to_low(values):
    return values.astype(jnp.bfloat16)


def product(spec, left, right):
    return jnp.einsum(spec, left, right, preferred_element_type=jnp.float32)


def unit_rows(values):
    return values * lax.rsqrt(jnp.sum(values * values, -1, keepdims=True) + 1e-06)


def frame_mask(starts):
    frames = jnp.arange(CLIP, dtype=jnp.int32)[:, None]
    inside = (frames >= starts[None, :]) & (frames < starts[None, :] + SPAN)
    return jnp.any(inside, axis=1).astype(jnp.float32)


def inverse_root(matrix):
    size = matrix.shape[0]
    identity = jnp.eye(size, dtype=jnp.float32)
    damped = matrix + 0.0001 * (jnp.trace(matrix) / size) * identity
    magnitude = jnp.sqrt(jnp.sum(damped * damped))
    current = damped / magnitude
    result = identity * magnitude ** (-0.25)
    for sweep in range(NEWTON):
        factor = (5.0 * identity - current) * 0.25
        result = jnp.dot(result, factor, precision=HIGH)
        square = jnp.dot(factor, factor, precision=HIGH)
        current = jnp.dot(jnp.dot(square, square, precision=HIGH), current, precision=HIGH)
    return result


def adamw(weight, grad, first, second, rate, decay):
    first = beta_one * first + (1 - beta_one) * grad
    second = beta_two * second + (1 - beta_two) * grad * grad
    corrected = first / (1 - beta_one**STEP)
    scaled = jnp.sqrt(second / (1 - beta_two**STEP)) + adam_eps
    return (first, second, weight - rate * (corrected / scaled + decay * weight))


def reduce_grads(parts):
    proj_part, kernel_part, head_part, center_part, block_part = parts
    grouped = (
        lax.psum_scatter(proj_part, "group", scatter_dimension=1, tiled=True),
        lax.psum_scatter(kernel_part, "group", scatter_dimension=0, tiled=True),
        lax.psum_scatter(head_part, "group", scatter_dimension=1, tiled=True),
        lax.psum_scatter(center_part, "group", scatter_dimension=0, tiled=True),
        lax.psum_scatter(block_part, "group", scatter_dimension=0, tiled=True),
    )
    proj_part, kernel_part, head_part, center_part, block_part = grouped
    return (
        lax.psum_scatter(proj_part, "dp", scatter_dimension=0, tiled=True),
        lax.psum_scatter(kernel_part, "dp", scatter_dimension=2, tiled=True),
        lax.psum_scatter(head_part, "dp", scatter_dimension=0, tiled=True),
        lax.psum_scatter(center_part, "dp", scatter_dimension=1, tiled=True),
        lax.psum_scatter(block_part, "dp", scatter_dimension=1, tiled=True),
    )


def gather_plain(projection, conv_weight, head, clusters, blocks):
    gathered = (
        lax.all_gather(to_low(projection), "dp", axis=0, tiled=True),
        lax.all_gather(to_low(conv_weight), "dp", axis=2, tiled=True),
        lax.all_gather(to_low(head), "dp", axis=0, tiled=True),
        lax.all_gather(to_low(clusters), "dp", axis=1, tiled=True),
        lax.all_gather(to_low(blocks), "dp", axis=1, tiled=True),
    )
    proj_part, kernel_part, head_part, center_part, block_part = gathered
    return (
        lax.all_gather(proj_part, "group", axis=1, tiled=True),
        lax.all_gather(kernel_part, "group", axis=0, tiled=True),
        lax.all_gather(head_part, "group", axis=1, tiled=True),
        lax.all_gather(center_part, "group", axis=0, tiled=True),
        lax.all_gather(block_part, "group", axis=0, tiled=True),
    )


def shampoo_plain(block_rows, statistics):
    full_blocks = lax.all_gather(block_rows.astype(jnp.bfloat16), "dp", axis=1, tiled=True).astype(
        block_rows.dtype
    )
    rows = block_rows.shape[1]
    here = lax.axis_index("dp")
    first_row = here * rows
    column_slice = lax.dynamic_slice_in_dim(full_blocks, first_row, rows, 2)
    left_rows = stat_decay * statistics[:, 0] + (1 - stat_decay) * jnp.einsum(
        "brk,bck->brc", block_rows, full_blocks, precision=HIGH
    )
    right_rows = stat_decay * statistics[:, 1] + (1 - stat_decay) * jnp.einsum(
        "bkr,bkc->brc", column_slice, full_blocks, precision=HIGH
    )
    group_blocks = block_rows.shape[0]
    dp_size = lax.axis_size("dp")
    owners = [
        (2 * member + side) * dp_size // (2 * group_blocks)
        for member in range(group_blocks)
        for side in range(2)
    ]
    left_full, right_full = (
        lax.all_gather(left_rows.astype(jnp.bfloat16), "dp", axis=1, tiled=True).astype(
            left_rows.dtype
        ),
        lax.all_gather(right_rows.astype(jnp.bfloat16), "dp", axis=1, tiled=True).astype(
            right_rows.dtype
        ),
    )
    sources = [
        left_full[member] if side == 0 else right_full[member]
        for member in range(group_blocks)
        for side in range(2)
    ]
    roots = []
    for index in range(2 * group_blocks):
        owner = owners[index]
        root = lax.cond(here == owner, inverse_root, jnp.zeros_like, sources[index])
        root = spread_2(for_sending(root), "dp", owner).astype(root.dtype)
        roots.append(root)
    stacked = jnp.stack(roots).reshape(group_blocks, 2, D, D)
    left_root_rows = lax.dynamic_slice_in_dim(stacked[:, 0], first_row, rows, 1)
    update_rows = jnp.einsum(
        "brk,bkc->brc",
        jnp.einsum("brk,bkc->brc", left_root_rows, full_blocks, precision=HIGH),
        stacked[:, 1],
        precision=HIGH,
    )
    return jnp.stack([left_rows, right_rows], 1), update_rows


MESH = pl.DeviceIdType.MESH
HBM = pl.BlockSpec(memory_space=pltpu.HBM)
VMEM = pl.BlockSpec(memory_space=pltpu.VMEM)
VMEM_LIMIT = 60 * 1024 * 1024


class Place:
    def __init__(self, dp_size, group_size):
        self.dp_size, self.group_size = dp_size, group_size
        self.lines = dp_size // 2
        self.dp, self.group = lax.axis_index("dp"), lax.axis_index("group")
        self.z, self.y = self.dp // 2, self.dp % 2
        self.x, self.core = self.group // 2, self.group % 2

    def at(self, z, flip_y=0, flip_x=0, flip_core=0):
        y = self.y + flip_y * (1 - 2 * self.y)
        x = self.x + flip_x * (1 - 2 * self.x)
        core = self.core + flip_core * (1 - 2 * self.core)
        return (z * 2 + y, x * 2 + core)

    def near(self, z, p, q):
        return self.at(z, p * (1 - self.core) + q * self.core, q * (1 - self.core) + p * self.core)

    def across(self, z, p, q):
        return self.at(z, p * self.core + q * (1 - self.core), q * self.core + p * (1 - self.core), 1)


def greet(place):
    barrier = pltpu.get_barrier_semaphore()
    first = place.x * 2
    for other in range(place.dp_size):
        for core in range(2):

            @pl.when((place.dp != other) | (place.core != core))
            def _():
                pl.semaphore_signal(
                    barrier, inc=1, device_id=(other, first + core), device_id_type=MESH
                )

    for core in range(2):
        pl.semaphore_signal(
            barrier,
            inc=1,
            device_id=(place.dp, (1 - place.x) * 2 + core),
            device_id_type=MESH,
        )
    pl.semaphore_wait(barrier, 2 * place.dp_size - 1 + 2)


def guarded(condition, action):
    if condition is None:
        action()
    else:
        pl.when(condition)(action)


def both(one, two):
    if one is None:
        return two
    if two is None:
        return one
    return one & two


def piece_at(kind, ref, dp, group, shape):
    if kind == "blocks":
        start = pl.multiple_of(dp * shape[1], shape[1])
        return ref.at[pl.ds(group * shape[0], shape[0]), pl.ds(start, shape[1])]
    if kind == "conv":
        return ref.at[group, pl.ds(dp * shape[0], shape[0])]
    return ref.at[dp, group]


KINDS = ("conv", "small", "blocks")


def gather_kernel(sizes, shapes, *refs):
    place = Place(*sizes)
    count = len(KINDS)
    ins, stats_in = refs[:count], refs[count]
    outs, stats_out = refs[count + 1 : 2 * count + 1], refs[2 * count + 1]
    send_sem, recv_sem, own_sem, stat_send, stat_recv, stat_own = refs[2 * count + 2 :]
    z, last = place.z, place.lines - 1
    me = (place.dp, place.group)
    greet(place)
    sent = []
    slots = [0] * count

    def view(k, source):
        return piece_at(KINDS[k], outs[k], source[0], source[1], shapes[k])

    def identity(source):
        return source[0] * place.group_size + source[1]

    def copy_of(k, source, target, slot, own=False):
        spot = view(k, source)
        return pltpu.make_async_remote_copy(
            src_ref=ins[k] if own else spot,
            dst_ref=spot,
            send_sem=send_sem.at[k, slot],
            recv_sem=recv_sem.at[k, identity(source)],
            device_id=target,
            device_id_type=MESH,
        )

    def send(k, source, target, condition=None, own=False):
        slot = slots[k]
        slots[k] += 1
        guarded(condition, lambda: copy_of(k, source, target, slot, own).start())
        sent.append((k, source, target, slot, condition, own))

    def arrive(k, source, condition=None):
        guarded(condition, lambda: copy_of(k, source, me, 0).wait_recv())

    links = {
        "left": (place.at(z - 1), z > 0),
        "right": (place.at(z + 1), z < last),
        "p": (place.near(z, 1, 0), None),
        "q": (place.near(z, 0, 1), None),
        "core": (place.at(z, 0, 0, 1), None),
    }

    def forward(k, source, ways, condition=None, own=False):
        for way in ways:
            target, open_way = links[way]
            send(k, source, target, both(condition, open_way), own)

    def spots(offset):
        if offset == 0:
            return [(z, None, ("left", "right"))]
        return [
            (z - offset, z >= offset, ("right",)),
            (z + offset, z + offset <= last, ("left",)),
        ]

    def take(k, source, condition, ways):
        arrive(k, source, condition)
        forward(k, source, ways, condition)

    steps = place.lines + 3

    def step_z_first(k, step):
        if step == 0:
            forward(k, me, ("left", "right", "q", "p", "core"), own=True)
            return
        if step < place.lines:
            for spot, there, ways in spots(step):
                take(k, place.near(spot, 0, 0), there, ways + ("q", "p", "core"))
        if 0 <= step - 1 < place.lines:
            for spot, there, _ in spots(step - 1):
                take(k, place.near(spot, 1, 0), there, ("q", "core"))
                take(k, place.near(spot, 0, 1), there, ("core",))
        if 0 <= step - 2 < place.lines:
            for spot, there, _ in spots(step - 2):
                take(k, place.near(spot, 1, 1), there, ("core",))

    def step_z_second(k, step):
        if step == 0:
            forward(k, me, ("q", "left", "right", "p", "core"), own=True)
            return
        if step == 1:
            take(k, place.near(z, 0, 1), None, ("left", "right", "p", "core"))
        if step < place.lines:
            for spot, there, ways in spots(step):
                take(k, place.near(spot, 0, 0), there, ways + ("p", "core"))
        if 1 <= step - 1 < place.lines:
            for spot, there, ways in spots(step - 1):
                take(k, place.near(spot, 0, 1), there, ways + ("p", "core"))
        if 0 <= step - 1 < place.lines:
            for spot, there, _ in spots(step - 1):
                take(k, place.near(spot, 1, 0), there, ("core",))
        if 0 <= step - 2 < place.lines:
            for spot, there, _ in spots(step - 2):
                take(k, place.near(spot, 1, 1), there, ("core",))

    members = shapes[KINDS.index("blocks")][0]
    rows = shapes[KINDS.index("blocks")][1]

    def stat_copy(member, side):
        owner = place.core * members + member
        start = pl.multiple_of(place.dp * rows, rows)
        return owner, pltpu.make_async_remote_copy(
            src_ref=stats_in.at[member, side],
            dst_ref=stats_out.at[pl.ds(start, rows)],
            send_sem=stat_send.at[member, side],
            recv_sem=stat_recv.at[place.dp],
            device_id=(owner, place.x * 2 + side),
            device_id_type=MESH,
        )

    def stat_local(member, side):
        start = pl.multiple_of(place.dp * rows, rows)
        return pltpu.make_async_copy(
            stats_in.at[member, side], stats_out.at[pl.ds(start, rows)], stat_own
        )

    def each_stat(remote, local):
        for member in range(members):
            for side in range(2):
                owner = place.core * members + member
                mine = (place.dp == owner) & (place.core == side)
                pl.when(jnp.logical_not(mine))(lambda m=member, s=side: remote(m, s))
                pl.when(mine)(lambda m=member, s=side: local(m, s))

    own_copies = [
        pltpu.make_async_copy(ins[k], view(k, me), own_sem.at[k]) for k in range(count)
    ]
    for step in range(steps):
        for k, kind in enumerate(KINDS):
            if kind == "blocks":
                step_z_second(k, step)
            else:
                step_z_first(k, step)
        if step == 0:
            for own in own_copies:
                own.start()
        if step == 1:
            each_stat(
                lambda m, s: stat_copy(m, s)[1].start(), lambda m, s: stat_local(m, s).start()
            )
    for k in range(count):
        for spot in range(place.lines):
            for p in range(2):
                for q in range(2):
                    arrive(k, place.across(spot, p, q))
    for own in own_copies:
        own.wait()
    each_stat(lambda m, s: stat_copy(m, s)[1].wait_send(), lambda m, s: stat_local(m, s).wait())
    owned_group = place.x * 2 + place.dp // members

    @pl.when(place.dp < 2 * members)
    def _():
        for other in range(place.dp_size):

            @pl.when((place.dp != other) | (place.group != owned_group))
            def _():
                pltpu.make_async_remote_copy(
                    src_ref=stats_in.at[0, 0],
                    dst_ref=stats_out.at[pl.ds(other * rows, rows)],
                    send_sem=stat_send.at[0, 0],
                    recv_sem=stat_recv.at[other],
                    device_id=me,
                    device_id_type=MESH,
                ).wait_recv()

    for k, source, target, slot, condition, own in sent:
        guarded(
            condition,
            lambda k=k, source=source, target=target, slot=slot, own=own: copy_of(
                k, source, target, slot, own
            ).wait_send(),
        )


def full_shapes(sizes, shapes):
    dp_size, group_size = sizes
    conv, small, blocks = shapes
    return [
        (group_size, dp_size * conv[0]) + conv[1:],
        (dp_size, group_size) + small,
        (group_size * blocks[0], dp_size * blocks[1], blocks[2]),
    ]


def gather_weights(sizes, pieces, stats_low):
    shapes = [piece.shape for piece in pieces]
    outs = [
        jax.ShapeDtypeStruct(shape, jnp.bfloat16) for shape in full_shapes(sizes, shapes)
    ] + [jax.ShapeDtypeStruct((D, D), jnp.bfloat16)]
    count, devices = len(pieces), sizes[0] * sizes[1]
    members = shapes[-1][0]
    return pl.pallas_call(
        functools.partial(gather_kernel, sizes, shapes),
        out_shape=outs,
        in_specs=[HBM] * (count + 1),
        out_specs=[HBM] * (count + 1),
        scratch_shapes=[
            pltpu.SemaphoreType.DMA((count, 3 * devices)),
            pltpu.SemaphoreType.DMA((count, devices)),
            pltpu.SemaphoreType.DMA((count,)),
            pltpu.SemaphoreType.DMA((members, 2)),
            pltpu.SemaphoreType.DMA((sizes[0],)),
            pltpu.SemaphoreType.DMA,
        ],
        name="gather_weights",
        compiler_params=pltpu.CompilerParams(
            collective_id=0, has_side_effects=True, vmem_limit_bytes=16 * 1024 * 1024
        ),
    )(*pieces, stats_low)


def reduce_kernel(sizes, shapes, *refs):
    place = Place(*sizes)
    count = len(KINDS)
    refs = list(refs)

    def pull(number):
        taken = refs[:number]
        del refs[:number]
        return taken

    ins, (small_in,) = pull(count), pull(1)
    outs, (small_out, square_out, whole_out) = pull(count), pull(3)
    held, crossed, first_in, second_in, from_left, from_right = (pull(count) for _ in range(6))
    (group_box, dp_box, rows_low, whole_box) = pull(4)
    (load_sem, cross_send, cross_recv, first_send, first_recv) = pull(5)
    (second_send, second_recv, left_send, left_recv, right_send, right_recv) = pull(6)
    (group_send, group_recv, dp_send, dp_recv, row_send, row_recv, pair_send, pair_recv) = pull(8)
    z, lines, last = place.z, place.lines, place.lines - 1
    me = (place.dp, place.group)
    p_mate, q_mate, c_mate = place.near(z, 1, 0), place.near(z, 0, 1), place.at(z, 0, 0, 1)
    left, right = place.at(z - 1), place.at(z + 1)
    greet(place)

    def remote(source, target, send, recv, device):
        return pltpu.make_async_remote_copy(
            src_ref=source,
            dst_ref=target,
            send_sem=send,
            recv_sem=recv,
            device_id=device,
            device_id_type=MESH,
        )

    def f32(ref, at):
        return ref[at].astype(jnp.float32)

    z_first = [kind != "blocks" for kind in KINDS]

    def order(k):
        if z_first[k]:
            return [(p, q) for q in (1, 0) for p in (1, 0)]
        return [(p, q) for p in (1, 0) for q in (1, 0)]

    def load_of(k, p, q, spot):
        dp, group = place.near(spot, p, q)
        return pltpu.make_async_copy(
            piece_at(KINDS[k], ins[k], dp, group, shapes[k]),
            held[k].at[p, q, spot],
            load_sem.at[k, p, q, spot],
        )

    def cross_of(k, p, q, spot):
        dp, group = place.across(spot, p, q)
        return remote(
            piece_at(KINDS[k], ins[k], dp, group, shapes[k]),
            crossed[k].at[p, q, spot],
            cross_send.at[k, p, q, spot],
            cross_recv.at[k, p, q, spot],
            c_mate,
        )

    sequence = (KINDS.index("blocks"), KINDS.index("small"), KINDS.index("conv"))
    for turn in range(4):
        for k in sequence:
            p, q = order(k)[turn]

            def start_one(spot, _, k=k, p=p, q=q):
                cross_of(k, p, q, spot).start()
                load_of(k, p, q, spot).start()
                return 0

            lax.fori_loop(0, lines, start_one, 0)

    def group_copy(other):
        return remote(
            small_in, group_box.at[place.group], group_send.at[other], group_recv.at[place.group], (place.dp, other)
        )

    def each_other(size, mine, action):
        for other in range(size):
            pl.when(mine != other)(functools.partial(action, other))

    each_other(place.group_size, place.group, lambda other: group_copy(other).start())
    group_box[place.group] = small_in[...]

    def first_ready(k, p, q, spot):
        load_of(k, p, q, spot).wait()
        cross_of(k, p, q, spot).wait_recv()

    def first_out(k, a, spot):
        source = held[k].at[a, 1, spot] if z_first[k] else held[k].at[1, a, spot]
        return remote(
            source,
            first_in[k].at[a, spot],
            first_send.at[k, a, spot],
            first_recv.at[k, a, spot],
            q_mate if z_first[k] else p_mate,
        )

    def stage_one(k):
        for a in (1, 0):

            def one(spot, _, a=a):
                p, q = (a, 1) if z_first[k] else (1, a)
                first_ready(k, p, q, spot)
                total = f32(held[k], (p, q, spot)) + f32(crossed[k], (p, q, spot))
                held[k][p, q, spot] = total.astype(jnp.bfloat16)
                first_out(k, a, spot).start()
                return 0

            lax.fori_loop(0, lines, one, 0)

    for k in sequence:
        stage_one(k)

    def dp_copy(other):
        return remote(
            dp_box.at[place.dp], dp_box.at[place.dp], dp_send.at[other], dp_recv.at[place.dp], (other, place.group)
        )

    def group_wait(other):
        group_copy(other).wait_send()
        remote(small_in, group_box.at[other], group_send.at[other], group_recv.at[other], me).wait_recv()

    each_other(place.group_size, place.group, group_wait)
    total = group_box[0]
    for other in range(1, place.group_size):
        total = total + group_box[other]
    dp_box[place.dp] = total
    each_other(place.dp_size, place.dp, lambda other: dp_copy(other).start())

    def second_out(k, spot):
        return remote(
            held[k].at[1, 0, spot],
            second_in[k].at[spot],
            second_send.at[k, spot],
            second_recv.at[k, spot],
            p_mate,
        )

    def gathered_sum(k, p, q, spot):
        first_ready(k, p, q, spot)
        a = p if z_first[k] else q
        first_out(k, a, spot).wait_recv()
        return (
            f32(held[k], (p, q, spot))
            + f32(crossed[k], (p, q, spot))
            + f32(first_in[k], (a, spot))
        )

    def stage_two(k):
        def one(spot, _):
            held[k][1, 0, spot] = gathered_sum(k, 1, 0, spot).astype(jnp.bfloat16)
            second_out(k, spot).start()
            return 0

        lax.fori_loop(0, lines, one, 0)

    def line_out(k, a, spot, way):
        boxes, send, recv, device = (
            (from_left, right_send, left_recv, right)
            if way == "right"
            else (from_right, left_send, right_recv, left)
        )
        source = held[k].at[0, a, spot]
        box = boxes[k].at[spot] if z_first[k] else boxes[k].at[a, spot]
        return remote(source, box, send.at[k, a, spot], recv.at[k, a, spot], device)

    def line_total(k, a, spot):
        total = gathered_sum(k, 0, a, spot)
        if z_first[k]:
            second_out(k, spot).wait_recv()
            total = total + f32(second_in[k], (spot,))
        return total

    def box_at(k, a, spot):
        return (spot,) if z_first[k] else (a, spot)

    def stage_line(k, a):
        def pass_on(spot, way):
            passing = (z < spot) if way == "right" else (z > spot)
            inner = (z > 0) if way == "right" else (z < last)

            @pl.when(passing)
            def _():
                held[k][0, a, spot] = line_total(k, a, spot).astype(jnp.bfloat16)

                @pl.when(inner)
                def _():
                    line_out(k, a, spot, way).wait_recv()
                    box = from_left if way == "right" else from_right
                    held[k][0, a, spot] = (
                        f32(held[k], (0, a, spot)) + f32(box[k], box_at(k, a, spot))
                    ).astype(jnp.bfloat16)

                line_out(k, a, spot, way).start()

        def one(step, _):
            pass_on(last - step, "right")
            pass_on(step, "left")
            return 0

        lax.fori_loop(0, lines, one, 0)

    def line_end(k, a):
        outs[k][...] = line_total(k, a, z)

        @pl.when(z > 0)
        def _():
            line_out(k, a, z, "right").wait_recv()
            outs[k][...] += f32(from_left[k], box_at(k, a, z))

        @pl.when(z < last)
        def _():
            line_out(k, a, z, "left").wait_recv()
            outs[k][...] += f32(from_right[k], box_at(k, a, z))

    b = KINDS.index("blocks")
    rest = [k for k in sequence if k != b]

    def last_out(k):
        return remote(
            held[k].at[0, 1, z],
            second_in[k].at[0],
            second_send.at[k, 0],
            second_recv.at[k, 0],
            q_mate,
        )

    for k in rest:
        stage_two(k)
    stage_line(b, 1)
    stage_line(b, 0)
    for k in rest:
        stage_line(k, 0)
    line_end(b, 1)
    held[b][0, 1, z] = outs[b][...].astype(jnp.bfloat16)
    last_out(b).start()
    line_end(b, 0)
    last_out(b).wait_recv()
    outs[b][...] += f32(second_in[b], (0,))
    rows_low[...] = outs[b][...].astype(jnp.bfloat16)

    members, rows = shapes[b][0], shapes[b][1]
    my_rows = pl.ds(pl.multiple_of(place.dp * rows, rows), rows)
    owned = place.dp - place.core * members
    owner_here = (place.dp >= place.core * members) & (place.dp < (place.core + 1) * members)
    owner_there = (place.dp < 2 * members) & jnp.logical_not(owner_here)

    def row_copy(member):
        return remote(
            rows_low.at[member],
            whole_box.at[my_rows],
            row_send.at[member],
            row_recv.at[place.dp],
            (place.core * members + member, place.group),
        )

    def pair_copy(other):
        spot = pl.ds(pl.multiple_of(other * rows, rows), rows)
        return remote(
            whole_box.at[spot], whole_box.at[spot], pair_send.at[other], pair_recv.at[other], c_mate
        )

    for member in range(members):

        @pl.when(place.dp != place.core * members + member)
        def _(member=member):
            row_copy(member).start()

        @pl.when(place.dp == place.core * members + member)
        def _(member=member):
            whole_box[my_rows] = rows_low[member]
            pair_copy(place.dp).start()

    for k in rest:
        line_end(k, 0)
    square = jnp.sum(outs[b][...] * outs[b][...])
    for k in rest:
        square = square + jnp.sum(outs[k][...] * outs[k][...])
    square_out[...] = jnp.full(square_out.shape, square, jnp.float32)

    def dp_wait(other):
        dp_copy(other).wait_send()
        remote(dp_box.at[other], dp_box.at[other], dp_send.at[other], dp_recv.at[other], me).wait_recv()

    each_other(place.dp_size, place.dp, dp_wait)
    total = dp_box[0]
    for other in range(1, place.dp_size):
        total = total + dp_box[other]
    small_out[...] = total

    @pl.when(owner_here)
    def _():
        for other in range(place.dp_size):

            @pl.when(place.dp != other)
            def _(other=other):
                spot = pl.ds(other * rows, rows)
                remote(
                    rows_low.at[0], whole_box.at[spot], row_send.at[0], row_recv.at[other], me
                ).wait_recv()
                pair_copy(other).start()

        for other in range(place.dp_size):
            pair_copy(other).wait_send()

    @pl.when(owner_there)
    def _():
        for other in range(place.dp_size):
            pair_copy(other).wait_recv()

    @pl.when(place.dp < 2 * members)
    def _():
        whole_out[...] = whole_box[...]

    for member in range(members):

        @pl.when(place.dp != place.core * members + member)
        def _(member=member):
            row_copy(member).wait_send()

    last_out(b).wait_send()
    for k in range(count):

        def drain(spot, _, k=k):
            for p in range(2):
                for q in range(2):
                    cross_of(k, p, q, spot).wait_send()
            for a in range(2):
                first_out(k, a, spot).wait_send()
            if z_first[k]:
                second_out(k, spot).wait_send()
            for a in (0,) if z_first[k] else (0, 1):

                @pl.when(z < spot)
                def _():
                    line_out(k, a, spot, "right").wait_send()

                @pl.when(z > spot)
                def _():
                    line_out(k, a, spot, "left").wait_send()

            return 0

        lax.fori_loop(0, lines, drain, 0)


def reduce_gradients(sizes, pieces, shapes, small):
    dp_size, group_size = sizes
    lines, count = dp_size // 2, len(pieces)
    low = jnp.bfloat16

    def boxes(lead):
        return [
            pltpu.VMEM(tuple(lead(kind)) + tuple(shape), low) for kind, shape in zip(KINDS, shapes)
        ]

    dma = pltpu.SemaphoreType.DMA
    scratch = (
        boxes(lambda kind: (2, 2, lines))
        + boxes(lambda kind: (2, 2, lines))
        + boxes(lambda kind: (2, lines))
        + boxes(lambda kind: (1,) if kind == "blocks" else (lines,))
        + boxes(lambda kind: (2, lines) if kind == "blocks" else (lines,))
        + boxes(lambda kind: (2, lines) if kind == "blocks" else (lines,))
        + [
            pltpu.VMEM((group_size,) + small.shape, jnp.float32),
            pltpu.VMEM((dp_size,) + small.shape, jnp.float32),
            pltpu.VMEM(shapes[-1], low),
            pltpu.VMEM((D, D), low),
        ]
        + [dma((count, 2, 2, lines))] * 3
        + [dma((count, 2, lines))] * 2
        + [dma((count, lines))] * 2
        + [dma((count, 2, lines))] * 4
        + [dma((group_size,))] * 2
        + [dma((dp_size,))] * 2
        + [dma((shapes[-1][0],)), dma((dp_size,))]
        + [dma((dp_size,))] * 2
    )
    return pl.pallas_call(
        functools.partial(reduce_kernel, sizes, shapes),
        out_shape=[jax.ShapeDtypeStruct(shape, jnp.float32) for shape in shapes]
        + [
            jax.ShapeDtypeStruct(small.shape, jnp.float32),
            jax.ShapeDtypeStruct((8, 128), jnp.float32),
            jax.ShapeDtypeStruct((D, D), low),
        ],
        in_specs=[HBM] * count + [VMEM],
        out_specs=[VMEM] * (count + 3),
        scratch_shapes=scratch,
        name="reduce_gradients",
        compiler_params=pltpu.CompilerParams(
            collective_id=1, has_side_effects=True, vmem_limit_bytes=VMEM_LIMIT
        ),
    )(*pieces, small)


def shift_right(values, by):
    if by == 0:
        return values
    parts = []
    for first in range(0, values.shape[1], CLIP):
        part = values[:, first : first + CLIP]
        lane = lax.broadcasted_iota(jnp.int32, part.shape, 1)
        turned = pltpu.roll(part, by % CLIP, 1)
        inside = lane >= by if by > 0 else lane < CLIP + by
        parts.append(jnp.where(inside, turned, 0.0))
    return jnp.concatenate(parts, 1)


def place_windows(hidden, windows, taps):
    channels = hidden.shape[0]
    runs, half = taps // STRIDE, taps // STRIDE // 2
    for run in range(runs):
        by = STRIDE * (half - 1 - run) if run < half else -STRIDE * (run - half)
        windows[run * channels : (run + 1) * channels, :] = shift_right(hidden, by).astype(
            jnp.bfloat16
        )


def conv_group(hidden, weight_at, windows, taps, shape):
    channels = hidden.shape[0]
    chunks, _, _, chunk = shape
    place_windows(hidden, windows, taps)
    total = None
    for side in range(2):
        part = None
        for index in range(side * chunks // 2, (side + 1) * chunks // 2):
            term = dot(weight_at(index), windows[index * chunk : (index + 1) * chunk, :])
            part = term if part is None else part + term
        for offset in range(STRIDE):
            by = STRIDE - offset if side == 0 else -offset
            moved = shift_right(part[offset * channels : (offset + 1) * channels], by)
            total = moved if total is None else total + moved
    return total


def conv_group_back(hidden, grad, weight_at, put, windows, moved, taps, shape):
    channels = hidden.shape[0]
    chunks, _, _, chunk = shape
    half, runs = taps // STRIDE // 2, chunk // channels
    place_windows(hidden, windows, taps)
    total = None
    for side in range(2):
        for offset in range(STRIDE):
            by = offset - STRIDE if side == 0 else offset
            moved[offset * channels : (offset + 1) * channels, :] = shift_right(grad, by).astype(
                jnp.bfloat16
            )
        for index in range(side * chunks // 2, (side + 1) * chunks // 2):
            put(
                index,
                dot_nt(moved[...], windows[index * chunk : (index + 1) * chunk, :]).astype(
                    jnp.bfloat16
                ),
            )
            turned = dot_tn(weight_at(index), moved[...])
            for step in range(runs):
                run = index * runs + step
                by = -STRIDE * (half - 1 - run) if run < half else STRIDE * (run - half)
                part = shift_right(turned[step * channels : (step + 1) * channels], by)
                total = part if total is None else total + part
    return total


def over_rows(total, tile, action):
    def step(index, _):
        action(pl.ds(pl.multiple_of(index * tile, tile), tile))
        return 0

    lax.fori_loop(0, total // tile, step, 0)


def dot(one, two):
    return jnp.dot(one, two, preferred_element_type=jnp.float32)


def dot_nt(one, two):
    return lax.dot_general(one, two, (((1,), (1,)), ((), ())), preferred_element_type=jnp.float32)


def dot_tn(one, two):
    return lax.dot_general(one, two, (((0,), (0,)), ((), ())), preferred_element_type=jnp.float32)


def norm_parts(values):
    average = jnp.mean(values, -1, keepdims=True)
    centred = values - average
    inverse = lax.rsqrt(jnp.mean(centred * centred, -1, keepdims=True) + 1e-05)
    return centred * inverse, inverse


def norm_back(upstream, unit, inverse, gain):
    scaled = upstream * gain
    along = jnp.mean(scaled * unit, -1, keepdims=True)
    return inverse * (scaled - jnp.mean(scaled, -1, keepdims=True) - unit * along)


def gelu_pair(values):
    below = 0.5 + 0.5 * lax.erf(values * 0.7071067811865476)
    density = jnp.exp(values * values * -0.5) * 0.3989422804014327
    return values * below, below + values * density


def add_row(ref, row, values):
    ref[row : row + 1, :] += jnp.sum(values, 0, keepdims=True)


def front_kernel(taps, *refs):
    (
        features, mask, feature_norm, vectors, projection, kernel,
        feature_unit, normed, hidden_t, encoded, encoder_unit, encoder_inverse, slope,
        held, windows, hidden, out_t, load_sem,
    ) = refs
    frames = features.shape[0]
    groups = kernel.shape[1]
    channels = hidden_t.shape[0] // groups

    def load(group):
        return pltpu.make_async_copy(kernel.at[:, group], held.at[:, group], load_sem.at[group])

    for group in range(groups):
        load(group).start()

    def enter(at):
        unit, _ = norm_parts(features[at, :].astype(jnp.float32))
        feature_unit[at, :] = unit
        normed[at, :] = (unit * feature_norm[0:1, :] + feature_norm[1:2, :]).astype(jnp.bfloat16)

    over_rows(frames, 32, enter)
    projected = dot(normed[...], projection[...])
    hidden[...] = jnp.where(mask[...] > 0, vectors[0:1, :], projected)
    hidden_t[...] = hidden[...].T.astype(jnp.bfloat16)

    def one_group(group, _):
        load(group).wait()
        at = pl.ds(pl.multiple_of(group * channels, channels), channels)
        out_t[at, :] = conv_group(
            hidden_t[at, :].astype(jnp.float32), lambda index: held[index, group], windows, taps, kernel.shape
        )
        return 0

    lax.fori_loop(0, groups, one_group, 0)
    slope[...] = out_t[...].T

    def leave(at):
        active, derivative = gelu_pair(slope[at, :])
        slope[at, :] = derivative
        unit, inverse = norm_parts(hidden[at, :] + active)
        encoder_unit[at, :] = unit
        encoder_inverse[at, :] = inverse
        encoded[at, :] = unit * vectors[1:2, :] + vectors[2:3, :]

    over_rows(frames, 32, leave)


def front(features, mask, feature_norm, vectors, projection, kernel, taps):
    frames, width = features.shape
    chunks, groups, rows, chunk = kernel.shape
    full, low = jnp.float32, jnp.bfloat16
    out = jax.ShapeDtypeStruct
    return pl.pallas_call(
        functools.partial(front_kernel, taps),
        out_shape=[
            out((frames, width), full),
            out((frames, width), low),
            out((D, frames), low),
            out((frames, D), full),
            out((frames, D), full),
            out((frames, 1), full),
            out((frames, D), full),
        ],
        in_specs=[VMEM] * 5 + [HBM],
        out_specs=[VMEM] * 7,
        scratch_shapes=[
            pltpu.VMEM(kernel.shape, low),
            pltpu.VMEM((chunks * chunk, frames), low),
            pltpu.VMEM((frames, D), full),
            pltpu.VMEM((D, frames), full),
            pltpu.SemaphoreType.DMA((groups,)),
        ],
        name="front",
        compiler_params=pltpu.CompilerParams(vmem_limit_bytes=32 * 1024 * 1024),
    )(features, mask, feature_norm, vectors, projection, kernel)


def trunk_kernel(*refs):
    (
        encoded, mask, labels, scale, vectors, head, centers, blocks,
        encoded_grad, block_grad, head_grad, center_grad, rows_out,
        held, made, low, triple, attention, mixed, unit_one, inverse_one, middle, middle_low,
        active, slope, unit_two, inverse_two, work, work_low, flow_low, triple_grad, turned,
        load_sem, save_sem,
    ) = refs
    frames = encoded.shape[0]
    count = blocks.shape[0]
    ups = (count - 4) // 2
    tile = 32
    pairs = D // 128

    def load(block):
        return pltpu.make_async_copy(blocks.at[block], held.at[block], load_sem.at[block])

    def save(block):
        return pltpu.make_async_copy(made.at[block], block_grad.at[block], save_sem.at[block])

    for block in range(count):
        load(block).start()
    rows_out[...] = jnp.zeros_like(rows_out)

    def to_inputs(at):
        low[at, :] = encoded[at, :].astype(jnp.bfloat16)

    over_rows(frames, tile, to_inputs)

    def first_three(block, _):
        load(block).wait()
        triple[block] = dot(low[...], held[block]).astype(jnp.bfloat16)
        return 0

    lax.fori_loop(0, 3, first_three, 0)
    lane = lax.broadcasted_iota(jnp.int32, (CLIP, 128), 1)
    even = lane < HEAD

    def apart(values):
        zero = jnp.zeros_like(values)
        return jnp.concatenate([jnp.where(even, values, zero), jnp.where(even, zero, values)], 0)

    def beside(values):
        return jnp.concatenate([values[:CLIP], values[CLIP:]], 1)

    def spot(index):
        at = pl.ds(pl.multiple_of(index // pairs * CLIP, CLIP), CLIP)
        return at, pl.ds(pl.multiple_of(index % pairs * 128, 128), 128)

    def attend(index, _):
        at, lanes = spot(index)
        query, keys, values = triple[0, at, lanes], triple[1, at, lanes], triple[2, at, lanes]
        scores = dot_nt(apart(query), keys) * HEAD ** (-0.5)
        raised = jnp.exp(scores - jnp.max(scores, -1, keepdims=True))
        full = raised / jnp.sum(raised, -1, keepdims=True)
        attention[index] = full
        mixed[at, lanes] = dot(beside(full.astype(jnp.bfloat16)), apart(values)).astype(jnp.bfloat16)
        return 0

    lax.fori_loop(0, frames // CLIP * pairs, attend, 0)
    load(3).wait()
    work[...] = dot(mixed[...], held[3])

    def first_norm(at):
        unit, inverse = norm_parts(encoded[at, :] + work[at, :])
        unit_one[at, :] = unit
        inverse_one[at, :] = inverse
        value = unit * vectors[3:4, :] + vectors[4:5, :]
        middle[at, :] = value
        middle_low[at, :] = value.astype(jnp.bfloat16)

    over_rows(frames, tile, first_norm)

    def expand(step, _):
        load(4 + step).wait()
        slope[step] = dot(middle_low[...], held[4 + step])

        def bend(at):
            value, derivative = gelu_pair(slope[step, at, :])
            active[step, at, :] = value.astype(jnp.bfloat16)
            slope[step, at, :] = derivative

        over_rows(frames, tile, bend)
        return 0

    lax.fori_loop(0, ups, expand, 0)

    def contract(step, _):
        load(4 + ups + step).wait()
        middle[...] += dot(active[step], held[4 + ups + step])
        return 0

    lax.fori_loop(0, ups, contract, 0)

    def second_norm(at):
        unit, inverse = norm_parts(middle[at, :])
        unit_two[at, :] = unit
        inverse_two[at, :] = inverse
        flow_low[at, :] = (unit * vectors[5:6, :] + vectors[6:7, :]).astype(jnp.bfloat16)

    over_rows(frames, tile, second_norm)
    embedded = dot(flow_low[...], head[...])
    length = lax.rsqrt(jnp.sum(embedded * embedded, -1, keepdims=True) + 1e-06)
    unit_low = (embedded * length).astype(jnp.bfloat16)
    logits = dot_nt(unit_low, centers[...]) * inv_temp
    top = jnp.max(logits, -1, keepdims=True)
    raised = jnp.exp(logits - top)
    amount = jnp.sum(raised, -1, keepdims=True)
    choose = labels[...] == lax.broadcasted_iota(jnp.int32, logits.shape, 1)
    target = jnp.sum(jnp.where(choose, logits, 0.0), -1, keepdims=True)
    losses = mask[...] * (jnp.log(amount) + top - target)
    rows_out[7:8, :] = jnp.broadcast_to(jnp.sum(losses, 0, keepdims=True), (1, D))
    logit_grad = (
        (raised / amount - choose.astype(jnp.float32)) * (mask[...] * scale[0:1, 0:1])
    ).astype(jnp.bfloat16)
    unit_grad = dot(logit_grad, centers[...]) * inv_temp
    center_grad[...] = dot_tn(logit_grad, unit_low) * inv_temp
    along = jnp.sum(unit_grad * embedded, -1, keepdims=True)
    embedded_grad = (
        length * unit_grad - embedded * (length * length * length * along)
    ).astype(jnp.bfloat16)
    work[...] = dot_nt(embedded_grad, head[...])
    head_grad[...] = dot_tn(flow_low[...], embedded_grad).astype(jnp.bfloat16)

    def second_back(at):
        upstream = work[at, :]
        add_row(rows_out, 5, upstream * unit_two[at, :])
        add_row(rows_out, 6, upstream)
        value = norm_back(upstream, unit_two[at, :], inverse_two[at, :], vectors[5:6, :])
        middle[at, :] = value
        flow_low[at, :] = value.astype(jnp.bfloat16)

    over_rows(frames, tile, second_back)
    turned[...] = middle_low[...].T

    def feed_back(step, _):
        work[...] = dot_nt(flow_low[...], held[4 + ups + step])
        made[4 + ups + step] = dot_tn(active[step], flow_low[...]).astype(jnp.bfloat16)
        save(4 + ups + step).start()

        def bend(at):
            work_low[at, :] = (work[at, :] * slope[step, at, :]).astype(jnp.bfloat16)

        over_rows(frames, tile, bend)
        made[4 + step] = dot(turned[...], work_low[...]).astype(jnp.bfloat16)
        save(4 + step).start()
        middle[...] += dot_nt(work_low[...], held[4 + step])
        return 0

    lax.fori_loop(0, ups, feed_back, 0)

    def first_back(at):
        upstream = middle[at, :]
        add_row(rows_out, 3, upstream * unit_one[at, :])
        add_row(rows_out, 4, upstream)
        value = norm_back(upstream, unit_one[at, :], inverse_one[at, :], vectors[3:4, :])
        middle[at, :] = value
        flow_low[at, :] = value.astype(jnp.bfloat16)

    over_rows(frames, tile, first_back)
    made[3] = dot_tn(mixed[...], flow_low[...]).astype(jnp.bfloat16)
    save(3).start()
    work_low[...] = dot_nt(flow_low[...], held[3]).astype(jnp.bfloat16)

    def attend_back(index, _):
        at, lanes = spot(index)
        query, keys, values = triple[0, at, lanes], triple[1, at, lanes], triple[2, at, lanes]
        upstream = apart(work_low[at, lanes])
        full = attention[index]
        full_grad = dot_nt(upstream, values)
        triple_grad[2, at, lanes] = dot_tn(full.astype(jnp.bfloat16), upstream).astype(jnp.bfloat16)
        along = jnp.sum(full * full_grad, -1, keepdims=True)
        score_grad = (full * (full_grad - along)).astype(jnp.bfloat16)
        triple_grad[0, at, lanes] = (
            dot(beside(score_grad), apart(keys)) * HEAD ** (-0.5)
        ).astype(jnp.bfloat16)
        triple_grad[1, at, lanes] = (
            dot_tn(score_grad, apart(query)) * HEAD ** (-0.5)
        ).astype(jnp.bfloat16)
        return 0

    lax.fori_loop(0, frames // CLIP * pairs, attend_back, 0)
    turned[...] = low[...].T

    def last_three(block, _):
        made[block] = dot(turned[...], triple_grad[block]).astype(jnp.bfloat16)
        save(block).start()
        middle[...] += dot_nt(triple_grad[block], held[block])
        return 0

    lax.fori_loop(0, 3, last_three, 0)
    encoded_grad[...] = middle[...]
    for block in range(count):
        save(block).wait()


def trunk(encoded, mask, labels, scale, vectors, head, centers, blocks):
    frames, count = encoded.shape[0], blocks.shape[0]
    ups = (count - 4) // 2
    full, low = jnp.float32, jnp.bfloat16
    out = jax.ShapeDtypeStruct
    wide, wide_low = pltpu.VMEM((frames, D), full), pltpu.VMEM((frames, D), low)
    column = pltpu.VMEM((frames, 1), full)
    return pl.pallas_call(
        trunk_kernel,
        out_shape=[
            out((frames, D), full),
            out(blocks.shape, low),
            out(head.shape, low),
            out(centers.shape, full),
            out((8, D), full),
        ],
        in_specs=[VMEM] * 7 + [HBM],
        out_specs=[VMEM, HBM, VMEM, VMEM, VMEM],
        scratch_shapes=[
            pltpu.VMEM(blocks.shape, low),
            pltpu.VMEM(blocks.shape, low),
            wide_low,
            pltpu.VMEM((3, frames, D), low),
            pltpu.VMEM((frames // CLIP * D // 128, 2 * CLIP, CLIP), full),
            wide_low,
            wide,
            column,
            wide,
            wide_low,
            pltpu.VMEM((ups, frames, D), low),
            pltpu.VMEM((ups, frames, D), full),
            wide,
            column,
            wide,
            wide_low,
            wide_low,
            pltpu.VMEM((3, frames, D), low),
            pltpu.VMEM((D, frames), low),
            pltpu.SemaphoreType.DMA((count,)),
            pltpu.SemaphoreType.DMA((count,)),
        ],
        name="trunk",
        compiler_params=pltpu.CompilerParams(vmem_limit_bytes=VMEM_LIMIT),
    )(encoded, mask, labels, scale, vectors, head, centers, blocks)


def back_kernel(taps, *refs):
    (
        encoded_grad, mask, feature_norm, vectors, projection, feature_unit, normed, hidden_t,
        encoder_unit, encoder_inverse, slope, trunk_rows, kernel,
        kernel_grad, projection_grad, rows_out,
        held, made, windows, moved, grad, grad_t, through, through_t, load_sem, save_sem,
    ) = refs
    frames, width = feature_unit.shape
    groups = kernel.shape[1]
    channels = hidden_t.shape[0] // groups

    def load(group):
        return pltpu.make_async_copy(kernel.at[:, group], held.at[:, group], load_sem.at[group])

    def save(group):
        return pltpu.make_async_copy(made.at[:, group], kernel_grad.at[:, group], save_sem.at[group])

    for group in range(groups):
        load(group).start()
    rows_out[...] = jnp.zeros_like(rows_out)
    rows_out[0:8, :] = trunk_rows[...]

    def enter(at):
        upstream = encoded_grad[at, :]
        add_row(rows_out, 1, upstream * encoder_unit[at, :])
        add_row(rows_out, 2, upstream)
        value = norm_back(upstream, encoder_unit[at, :], encoder_inverse[at, :], vectors[1:2, :])
        grad[at, :] = value
        through[at, :] = value * slope[at, :]

    over_rows(frames, 32, enter)
    grad_t[...] = through[...].T.astype(jnp.bfloat16)

    def one_group(group, _):
        load(group).wait()
        at = pl.ds(pl.multiple_of(group * channels, channels), channels)

        def put(index, value):
            made[index, group] = value

        through_t[at, :] = conv_group_back(
            hidden_t[at, :].astype(jnp.float32),
            grad_t[at, :].astype(jnp.float32),
            lambda index: held[index, group],
            put,
            windows,
            moved,
            taps,
            kernel.shape,
        )
        save(group).start()
        return 0

    lax.fori_loop(0, groups, one_group, 0)
    through[...] = through_t[...].T

    def leave(at):
        total = grad[at, :] + through[at, :]
        inside = mask[at, :] > 0
        add_row(rows_out, 0, jnp.where(inside, total, 0.0))
        grad[at, :] = jnp.where(inside, 0.0, total)

    over_rows(frames, 32, leave)
    projected_grad = grad[...].astype(jnp.bfloat16)
    projection_grad[...] = dot_tn(normed[...], projected_grad).astype(jnp.bfloat16)
    normed_grad = dot_nt(projected_grad, projection[...])
    rows_out[8:9, 0:width] = jnp.sum(normed_grad * feature_unit[...], 0, keepdims=True)
    rows_out[9:10, 0:width] = jnp.sum(normed_grad, 0, keepdims=True)
    for group in range(groups):
        save(group).wait()


def back(encoded_grad, mask, feature_norm, vectors, projection, saved, trunk_rows, kernel, taps):
    chunks, groups, rows, chunk = kernel.shape
    feature_unit, normed, hidden_t, encoder_unit, encoder_inverse, slope = saved
    frames = encoded_grad.shape[0]
    full, low = jnp.float32, jnp.bfloat16
    out = jax.ShapeDtypeStruct
    return pl.pallas_call(
        functools.partial(back_kernel, taps),
        out_shape=[
            out(kernel.shape, low),
            out(projection.shape, low),
            out((16, D), full),
        ],
        in_specs=[VMEM] * 12 + [HBM],
        out_specs=[HBM, VMEM, VMEM],
        scratch_shapes=[
            pltpu.VMEM(kernel.shape, low),
            pltpu.VMEM(kernel.shape, low),
            pltpu.VMEM((chunks * chunk, frames), low),
            pltpu.VMEM((rows, frames), low),
            pltpu.VMEM((frames, D), full),
            pltpu.VMEM((D, frames), low),
            pltpu.VMEM((frames, D), full),
            pltpu.VMEM((D, frames), full),
            pltpu.SemaphoreType.DMA((groups,)),
            pltpu.SemaphoreType.DMA((groups,)),
        ],
        name="back",
        compiler_params=pltpu.CompilerParams(vmem_limit_bytes=48 * 1024 * 1024),
    )(
        encoded_grad, mask, feature_norm, vectors, projection, feature_unit, normed, hidden_t,
        encoder_unit, encoder_inverse, slope, trunk_rows, kernel,
    )


def local_step(weights, features, masks, labels, inverse_count):
    feature_norm, projection, vectors, kernel, head, centers_low, blocks = weights
    frames = features.shape[0] * features.shape[1] * CLIP
    taps = kernel.shape[0] * kernel.shape[3] // (D // kernel.shape[1]) * STRIDE
    mask = masks.reshape(frames, 1)
    feature_unit, normed, hidden_t, encoded, encoder_unit, encoder_inverse, slope = front(
        features.reshape(frames, -1), mask, feature_norm, vectors, projection, kernel, taps
    )
    encoded_grad, block_grad, head_grad, center_grad, trunk_rows = trunk(
        encoded,
        mask,
        labels.reshape(frames, 1),
        jnp.full((8, 128), inverse_count),
        vectors,
        head,
        centers_low,
        blocks,
    )
    kernel_grad, projection_grad, rows = back(
        encoded_grad,
        mask,
        feature_norm,
        vectors,
        projection,
        (feature_unit, normed, hidden_t, encoder_unit, encoder_inverse, slope),
        trunk_rows,
        kernel,
        taps,
    )
    return rows, projection_grad, kernel_grad, head_grad, center_grad, block_grad


def roots_kernel(sizes, members, *refs):
    (
        whole, stat, square_in, extra_in, sides_out, update_out, square_out,
        big, low, m0, m0b, m1, m1b, s1, s1b, s2b, s3, s3b, root, mixed,
        group_box, dp_box, group_send, group_recv, dp_send, dp_recv,
        side_send, side_recv, side_own, mixed_send, mixed_recv, update_send, update_recv, update_own,
    ) = refs
    place = Place(*sizes)
    dp_size, rows = place.dp_size, D // place.dp_size
    me, c_mate = (place.dp, place.group), place.at(place.z, 0, 0, 1)
    owner = place.dp < 2 * members
    owned_group = place.x * 2 + place.dp // members
    owned_member = place.dp % members
    tile = 256
    greet(place)

    def remote(source, target, send, recv, device):
        return pltpu.make_async_remote_copy(
            src_ref=source,
            dst_ref=target,
            send_sem=send,
            recv_sem=recv,
            device_id=device,
            device_id_type=MESH,
        )

    def each_other(size, mine, action):
        for other in range(size):
            pl.when(mine != other)(functools.partial(action, other))

    def group_copy(other, slot):
        return remote(
            group_box.at[slot], group_box.at[slot], group_send.at[other], group_recv.at[slot], (place.dp, other)
        )

    def dp_copy(other, slot):
        return remote(dp_box.at[slot], dp_box.at[slot], dp_send.at[other], dp_recv.at[slot], (other, place.group))

    group_box[place.group] = square_in[...]
    each_other(place.group_size, place.group, lambda other: group_copy(other, place.group).start())

    def product_rows(one, two, then):
        def step(index, _):
            at = pl.ds(pl.multiple_of(index * tile, tile), tile)
            then(at, jnp.dot(one[at, :], two[...], preferred_element_type=jnp.float32))
            return 0

        lax.fori_loop(0, D // tile, step, 0)

    def side_copy(other):
        spot = pl.ds(pl.multiple_of(other * rows, rows), rows)
        return remote(
            low.at[spot],
            sides_out.at[owned_member, place.core],
            side_send.at[other],
            side_recv.at[owned_member, place.core],
            (other, owned_group),
        )

    def side_local():
        spot = pl.ds(pl.multiple_of(place.dp * rows, rows), rows)
        return pltpu.make_async_copy(low.at[spot], sides_out.at[owned_member, place.core], side_own)

    mine = place.group == owned_group

    def to_rows(other, remote_action, local_action):
        away = (place.dp != other) | jnp.logical_not(mine)
        pl.when(away)(functools.partial(remote_action, other))
        pl.when(jnp.logical_not(away))(local_action)

    @pl.when(owner)
    def _():
        @pl.when(place.core == 0)
        def _():
            def step(index, _):
                at = pl.ds(pl.multiple_of(index * tile, tile), tile)
                value = lax.dot_general(
                    whole[at, :],
                    whole[...],
                    (((1,), (1,)), ((), ())),
                    preferred_element_type=jnp.float32,
                )
                big[at, :] = value
                low[at, :] = value.astype(jnp.bfloat16)
                return 0

            lax.fori_loop(0, D // tile, step, 0)

        @pl.when(place.core == 1)
        def _():
            s1b[...] = whole[...].T

            def keep(at, value):
                big[at, :] = value
                low[at, :] = value.astype(jnp.bfloat16)

            product_rows(s1b, whole, keep)

        for other in range(dp_size):
            to_rows(other, lambda other: side_copy(other).start(), lambda: side_local().start())

    def group_wait(other):
        group_copy(other, place.group).wait_send()
        group_copy(other, other).wait_recv()

    each_other(place.group_size, place.group, group_wait)
    total = group_box[0]
    for other in range(1, place.group_size):
        total = total + group_box[other]
    dp_box[place.dp] = total
    each_other(dp_size, place.dp, lambda other: dp_copy(other, place.dp).start())

    def dp_wait(other):
        dp_copy(other, place.dp).wait_send()
        dp_copy(other, other).wait_recv()

    each_other(dp_size, place.dp, dp_wait)
    total = dp_box[0]
    for other in range(1, dp_size):
        total = total + dp_box[other]
    total = total + extra_in[...]
    square_out[...] = total

    @pl.when(owner)
    def _():
        factor = jnp.minimum(1.0, max_norm / (jnp.sqrt(total[0:1, 0:1]) + 1e-06))
        square_factor = factor * factor
        spread_f = (1 - stat_decay) * square_factor

        def diagonal(at_start, shape):
            row = lax.broadcasted_iota(jnp.int32, shape, 0) + at_start
            return row == lax.broadcasted_iota(jnp.int32, shape, 1)

        def each_tile(action, carry):
            def step(index, carry):
                start = pl.multiple_of(index * tile, tile)
                return action(pl.ds(start, tile), start, carry)

            return lax.fori_loop(0, D // tile, step, carry)

        def renew(at, start, trace):
            value = stat_decay * stat[at, :].astype(jnp.float32) + spread_f * big[at, :]
            big[at, :] = value
            on = jnp.where(diagonal(start, value.shape), value, 0.0)
            return trace + jnp.sum(jnp.sum(on, 1, keepdims=True), 0, keepdims=True)

        trace = each_tile(renew, jnp.zeros((1, 1), jnp.float32))
        damping = 0.0001 * (trace / D)

        def damp(at, start, total):
            value = big[at, :]
            value = value + jnp.where(diagonal(start, value.shape), damping, 0.0)
            big[at, :] = value
            return total + jnp.sum(jnp.sum(value * value, 1, keepdims=True), 0, keepdims=True)

        magnitude = jnp.sqrt(each_tile(damp, jnp.zeros((1, 1), jnp.float32)))

        def scale(at, start, carry):
            value = big[at, :] / magnitude
            m0[at, :] = value
            m0b[at, :] = value.astype(jnp.bfloat16)
            return carry

        each_tile(scale, 0)
        a = 1.5625

        def square_of(source):
            def then(at, value):
                value = value * 0.0625 - 0.625 * source[at, :]
                s1[at, :] = value
                s1b[at, :] = value.astype(jnp.bfloat16)

            return then

        def fourth(at, value):
            s2b[at, :] = (value + (2 * a) * s1[at, :]).astype(jnp.bfloat16)

        product_rows(m0b, m0b, square_of(m0))
        product_rows(s1b, s1b, fourth)

        def next_one(at, value):
            value = value + (a * a) * m0[at, :]
            m1[at, :] = value
            m1b[at, :] = value.astype(jnp.bfloat16)

        product_rows(s2b, m0b, next_one)

        def joined(at, value):
            value = value * 0.0625 - 0.3125 * (m0[at, :] + m1[at, :])
            s3[at, :] = value
            s3b[at, :] = value.astype(jnp.bfloat16)

        product_rows(m0b, m1b, joined)
        product_rows(m1b, m1b, square_of(m1))
        product_rows(s1b, s1b, fourth)

        def next_two(at, value):
            value = value + (a * a) * m1[at, :]
            m0[at, :] = value
            m0b[at, :] = value.astype(jnp.bfloat16)

        product_rows(s2b, m1b, next_two)
        outer = lax.rsqrt(jnp.sqrt(magnitude))

        def final(at, value):
            value = 1.25 * s3[at, :] - (0.25 * a) * m0[at, :] - 0.25 * value
            start = at.start
            value = value + jnp.where(diagonal(start, value.shape), 1.25 * a, 0.0)
            root[at, :] = (value * outer).astype(jnp.bfloat16)

        product_rows(s3b, m0b, final)

    def mixed_copy():
        return remote(mixed, mixed, mixed_send, mixed_recv, c_mate)

    def update_copy(other):
        spot = pl.ds(pl.multiple_of(other * rows, rows), rows)
        return remote(
            m1b.at[spot],
            update_out.at[owned_member],
            update_send.at[other],
            update_recv.at[owned_member],
            (other, owned_group),
        )

    def update_local():
        spot = pl.ds(pl.multiple_of(place.dp * rows, rows), rows)
        return pltpu.make_async_copy(m1b.at[spot], update_out.at[owned_member], update_own)

    @pl.when(owner & (place.core == 0))
    def _():
        def keep(at, value):
            mixed[at, :] = value.astype(jnp.bfloat16)

        product_rows(root, whole, keep)
        mixed_copy().start()
        mixed_copy().wait_send()

    @pl.when(owner & (place.core == 1))
    def _():
        mixed_copy().wait_recv()

        def keep(at, value):
            m1b[at, :] = value.astype(jnp.bfloat16)

        product_rows(mixed, root, keep)
        for other in range(dp_size):
            to_rows(other, lambda other: update_copy(other).start(), lambda: update_local().start())
        for other in range(dp_size):
            to_rows(other, lambda other: update_copy(other).wait_send(), lambda: update_local().wait())

    @pl.when(owner)
    def _():
        for other in range(dp_size):
            to_rows(other, lambda other: side_copy(other).wait_send(), lambda: side_local().wait())

    for member in range(members):
        holder = place.core * members + member
        for side in range(2):

            @pl.when((place.dp != holder) | (place.core != side))
            def _(member=member, side=side):
                remote(
                    low.at[pl.ds(0, rows)],
                    sides_out.at[member, side],
                    side_send.at[0],
                    side_recv.at[member, side],
                    me,
                ).wait_recv()

        @pl.when((place.dp != holder) | (place.core != 1))
        def _(member=member):
            remote(
                m1b.at[pl.ds(0, rows)],
                update_out.at[member],
                update_send.at[0],
                update_recv.at[member],
                me,
            ).wait_recv()


def shampoo_roots(sizes, members, whole, stat, square, extra):
    dp_size, group_size = sizes
    rows = D // dp_size
    low, full = jnp.bfloat16, jnp.float32
    dma = pltpu.SemaphoreType.DMA
    half, word = pltpu.VMEM((D, D), low), pltpu.VMEM((D, D), full)
    return pl.pallas_call(
        functools.partial(roots_kernel, sizes, members),
        out_shape=[
            jax.ShapeDtypeStruct((members, 2, rows, D), low),
            jax.ShapeDtypeStruct((members, rows, D), low),
            jax.ShapeDtypeStruct((8, 128), full),
        ],
        in_specs=[VMEM] * 4,
        out_specs=[VMEM] * 3,
        scratch_shapes=[word, half, word, half, word, half, word, half, half, word, half, half, half]
        + [pltpu.VMEM((group_size, 8, 128), full), pltpu.VMEM((dp_size, 8, 128), full)]
        + [dma((group_size,))] * 2
        + [dma((dp_size,))] * 2
        + [dma((dp_size,)), dma((members, 2)), dma]
        + [dma, dma]
        + [dma((dp_size,)), dma((members,)), dma],
        name="shampoo_roots",
        compiler_params=pltpu.CompilerParams(
            collective_id=2, has_side_effects=True, vmem_limit_bytes=VMEM_LIMIT
        ),
    )(whole, stat, square, extra)


def conv_to_shard(weight):
    taps, c, channels = weight.shape
    split = weight.reshape(taps // STRIDE, STRIDE, c, channels // c, c)
    return split.transpose(3, 1, 4, 0, 2).reshape(channels // c, STRIDE * c, taps // STRIDE * c)


def conv_from_shard(shard):
    groups, rows, columns = shard.shape
    c = rows // STRIDE
    split = shard.reshape(groups, STRIDE, c, columns // c, c)
    return split.transpose(3, 1, 4, 0, 2).reshape(columns // c * STRIDE, c, groups * c)


def pack_small(projection, head, clusters, note):
    lead, kind = projection.shape[:-2], projection.dtype
    spare = jnp.broadcast_to(note, lead + (96, 64)).astype(kind)
    padded = jnp.concatenate([clusters, jnp.zeros(lead + (2, 32), kind)], -2)
    return jnp.concatenate(
        [
            projection[..., :128],
            jnp.concatenate([projection[..., 128:], jnp.zeros(lead + (64, 64), kind)], -1),
            jnp.concatenate([head, spare], -1),
            jnp.concatenate([padded[..., 32 * j : 32 * j + 32, :] for j in range(4)], -1),
        ],
        -2,
    )


def unpack_small(packed):
    projection = jnp.concatenate([packed[..., :64, :], packed[..., 64:128, :64]], -1)
    head = packed[..., 128:224, :64]
    clusters = jnp.concatenate(
        [packed[..., 224:, 32 * j : 32 * j + 32] for j in range(4)], -2
    )[..., :126, :]
    return projection, head, clusters, packed[..., 128, 64]


def parts_of_rows(rows, vector_rows, width):
    return rows[:vector_rows], rows[vector_rows + 1 : vector_rows + 3, :width], rows[vector_rows, 0]


SMALL = ((64, 192), (96, 64), (126, 32))


def body(
    sizes,
    features,
    span_starts,
    labels,
    feature_norm,
    feature_first,
    feature_second,
    projection,
    projection_first,
    projection_second,
    vectors,
    vector_first,
    vector_second,
    conv_weight,
    conv_first,
    conv_second,
    head,
    head_first,
    head_second,
    clusters,
    cluster_first,
    cluster_second,
    blocks,
    statistics,
):
    dp_size, group_size = sizes
    members, rows = blocks.shape[0], blocks.shape[1]
    fast = (
        rows % 16 == 0
        and dp_size % 2 == 0
        and group_size == 4
        and dp_size >= 2 * members
        and (projection.shape, head.shape, clusters.shape) == SMALL
        and conv_weight.shape[2] % conv_weight.shape[1] == 0
    )
    masks = jax.vmap(jax.vmap(frame_mask))(span_starts)
    local_count = jnp.sum(masks)
    if fast:
        pieces = (
            conv_to_shard(to_low(conv_weight)),
            pack_small(to_low(projection), to_low(head), to_low(clusters), to_low(local_count)),
            to_low(blocks),
        )
        shapes = [piece.shape for piece in pieces]
        kernel_w, small_w, blocks_w, stat_whole = gather_weights(sizes, pieces, to_low(statistics))
        proj_s, head_s, clusters_s, counts = unpack_small(small_w)
        proj_w = proj_s.transpose(0, 2, 1, 3).reshape(dp_size * SMALL[0][0], -1)
        head_w = head_s.transpose(0, 2, 1, 3).reshape(dp_size * SMALL[1][0], -1)
        clusters_w = clusters_s.transpose(1, 2, 0, 3).reshape(group_size * SMALL[2][0], -1)
        masked_count = jnp.sum(counts.astype(jnp.float32))
    else:
        proj_w, kernel_full, head_w, clusters_w, blocks_w = gather_plain(
            projection, conv_weight, head, clusters, blocks
        )
        whole = conv_to_shard(kernel_full)
        kernel_w = whole.reshape(whole.shape[:2] + (4, -1)).transpose(2, 0, 1, 3)
        masked_count = lax.psum(local_count, ("dp", "group"))
    center_table = clusters_w.astype(jnp.float32)
    _, center_back = jax.vjp(unit_rows, center_table)
    weights = (
        feature_norm,
        proj_w,
        vectors,
        kernel_w,
        head_w,
        to_low(unit_rows(center_table)),
        blocks_w,
    )
    row_part, proj_part, kernel_part, head_part, center_part, block_part = local_step(
        weights, features, masks, labels, 1.0 / masked_count
    )
    vector_rows, width = vectors.shape[0], feature_norm.shape[1]
    center_part = center_back(center_part)[0]
    if fast:
        small_part = pack_small(
            proj_part.reshape(dp_size, SMALL[0][0], group_size, -1).transpose(0, 2, 1, 3),
            head_part.reshape(dp_size, SMALL[1][0], group_size, -1).transpose(0, 2, 1, 3),
            to_low(center_part).reshape(group_size, SMALL[2][0], dp_size, -1).transpose(2, 0, 1, 3),
            jnp.zeros((), jnp.bfloat16),
        )
        kernel_sum, small_sum, block_sum, extra, square, whole = reduce_gradients(
            sizes, (kernel_part, small_part, block_part), shapes, row_part
        )
        vector_grad, feature_grad, loss_sum = parts_of_rows(extra, vector_rows, width)
        proj_sum, head_sum, cluster_sum, _ = unpack_small(small_sum)
        large_total = (proj_sum, conv_from_shard(kernel_sum), head_sum, cluster_sum, block_sum)
        replicated = jnp.sum(feature_grad * feature_grad) + jnp.sum(vector_grad * vector_grad)
        sides, update_rows, square = shampoo_roots(
            sizes, members, whole, stat_whole, square, jnp.full((8, 128), replicated)
        )
        norm_square = square[0, 0]
    else:
        kernel_plain = conv_from_shard(
            kernel_part.transpose(1, 2, 0, 3).reshape(kernel_part.shape[1:3] + (-1,))
        )
        large_total = reduce_grads(
            tuple(
                part.astype(jnp.float32)
                for part in (proj_part, kernel_plain, head_part, center_part, block_part)
            )
        )
        vector_grad, feature_grad, loss_sum = parts_of_rows(
            lax.psum(row_part, ("dp", "group")), vector_rows, width
        )
        local_squares = sum((jnp.sum(part * part) for part in large_total))
        norm_square = (
            lax.psum(local_squares, ("dp", "group"))
            + jnp.sum(feature_grad * feature_grad)
            + jnp.sum(vector_grad * vector_grad)
        )
    grad_norm = jnp.sqrt(norm_square)
    factor = jnp.minimum(1.0, max_norm / (grad_norm + 1e-06))
    proj_grad, kernel_grad, head_grad, cluster_grad, block_rows = [
        part * factor for part in large_total
    ]
    feature_out = adamw(
        feature_norm, feature_grad * factor, feature_first, feature_second, rate_vector, 0.0
    )
    projection_out = adamw(
        projection, proj_grad, projection_first, projection_second, rate_matrix, decay_weight
    )
    vector_out = adamw(vectors, vector_grad * factor, vector_first, vector_second, rate_vector, 0.0)
    conv_out = adamw(conv_weight, kernel_grad, conv_first, conv_second, rate_matrix, decay_weight)
    head_out = adamw(head, head_grad, head_first, head_second, rate_matrix, decay_weight)
    cluster_out = adamw(
        clusters, cluster_grad, cluster_first, cluster_second, rate_matrix, decay_weight
    )
    if fast:
        statistics_new = stat_decay * statistics + (1 - stat_decay) * factor * factor * sides.astype(
            jnp.float32
        )
        update_rows = update_rows.astype(jnp.float32) * factor
    else:
        statistics_new, update_rows = shampoo_plain(block_rows, statistics)
    blocks_new = blocks - rate_shampoo * (update_rows + decay_weight * blocks)
    return (
        loss_sum,
        masked_count,
        grad_norm,
        *feature_out,
        *projection_out,
        *vector_out,
        *conv_out,
        *head_out,
        *cluster_out,
        block_rows,
        statistics_new,
        blocks_new,
    )


def solution(mesh):
    in_specs = (
        P(None, ("dp", "group"), None, None),
        P(None, ("dp", "group"), None),
        P(None, ("dp", "group"), None),
        P(),
        P(),
        P(),
        P("dp", "group"),
        P("dp", "group"),
        P("dp", "group"),
        P(),
        P(),
        P(),
        P("group", None, "dp"),
        P("group", None, "dp"),
        P("group", None, "dp"),
        P("dp", "group"),
        P("dp", "group"),
        P("dp", "group"),
        P("group", "dp"),
        P("group", "dp"),
        P("group", "dp"),
        P("group", "dp", None),
        P("group", None, "dp", None),
    )
    out_specs = (
        P(),
        P(),
        P(),
        P(),
        P(),
        P(),
        P("dp", "group"),
        P("dp", "group"),
        P("dp", "group"),
        P(),
        P(),
        P(),
        P("group", None, "dp"),
        P("group", None, "dp"),
        P("group", None, "dp"),
        P("dp", "group"),
        P("dp", "group"),
        P("dp", "group"),
        P("group", "dp"),
        P("group", "dp"),
        P("group", "dp"),
        P("group", "dp", None),
        P("group", None, "dp", None),
        P("group", "dp", None),
    )
    return jax.shard_map(
        functools.partial(body, (mesh.shape["dp"], mesh.shape["group"])), mesh=mesh, in_specs=in_specs, out_specs=out_specs, check_vma=False)
```

```python
import functools

import jax
import jax.numpy as jnp
from jax import lax
from jax.experimental import pallas as pl
from jax.experimental.pallas import tpu as pltpu
from jax.sharding import PartitionSpec as P

D = 768
HEADS = 12
HEAD = 64
TAPS = 128
CLIP = 128
SPAN = 10
NEWTON = 3
STEP = 10


HIGH = lax.Precision.HIGHEST
beta_one = 0.9
beta_two = 0.98
adam_eps = 1e-08
rate_matrix = 0.02
rate_vector = 0.5
rate_shampoo = 0.2
decay_weight = 0.01
stat_decay = 0.95
max_norm = 0.01
inv_temp = 10.0
STRIDE = 4


def for_sending(array):

    def short(part):
        return part.astype(jnp.bfloat16) if part.dtype == jnp.float32 else part

    return jax.tree.map(short, array)


def spread_2(array, axis, root):
    mine = lax.axis_index(axis) == root
    return lax.psum(jnp.where(mine, array, jnp.zeros_like(array)), axis)


def to_low(values):
    return values.astype(jnp.bfloat16)


def frame_mask(starts):
    frames = jnp.arange(CLIP, dtype=jnp.int32)[:, None]
    inside = (frames >= starts[None, :]) & (frames < starts[None, :] + SPAN)
    return jnp.any(inside, axis=1).astype(jnp.float32)


def inverse_root(matrix):
    size = matrix.shape[0]
    identity = jnp.eye(size, dtype=jnp.float32)
    damped = matrix + 0.0001 * (jnp.trace(matrix) / size) * identity
    magnitude = jnp.sqrt(jnp.sum(damped * damped))
    current = damped / magnitude
    result = identity * magnitude ** (-0.25)
    for sweep in range(NEWTON):
        factor = (5.0 * identity - current) * 0.25
        result = jnp.dot(result, factor, precision=HIGH)
        square = jnp.dot(factor, factor, precision=HIGH)
        current = jnp.dot(jnp.dot(square, square, precision=HIGH), current, precision=HIGH)
    return result


def adamw(weight, grad, first, second, rate, decay):
    first = beta_one * first + (1 - beta_one) * grad
    second = beta_two * second + (1 - beta_two) * grad * grad
    corrected = first / (1 - beta_one**STEP)
    scaled = jnp.sqrt(second / (1 - beta_two**STEP)) + adam_eps
    return (first, second, weight - rate * (corrected / scaled + decay * weight))


def reduce_grads(parts):
    proj_part, kernel_part, head_part, center_part, block_part = parts
    grouped = (
        lax.psum_scatter(proj_part, "group", scatter_dimension=1, tiled=True),
        lax.psum_scatter(kernel_part, "group", scatter_dimension=0, tiled=True),
        lax.psum_scatter(head_part, "group", scatter_dimension=1, tiled=True),
        lax.psum_scatter(center_part, "group", scatter_dimension=0, tiled=True),
        lax.psum_scatter(block_part, "group", scatter_dimension=0, tiled=True),
    )
    proj_part, kernel_part, head_part, center_part, block_part = grouped
    return (
        lax.psum_scatter(proj_part, "dp", scatter_dimension=0, tiled=True),
        lax.psum_scatter(kernel_part, "dp", scatter_dimension=2, tiled=True),
        lax.psum_scatter(head_part, "dp", scatter_dimension=0, tiled=True),
        lax.psum_scatter(center_part, "dp", scatter_dimension=1, tiled=True),
        lax.psum_scatter(block_part, "dp", scatter_dimension=1, tiled=True),
    )


def gather_plain(projection, conv_weight, head, clusters, blocks):
    gathered = (
        lax.all_gather(to_low(projection), "dp", axis=0, tiled=True),
        lax.all_gather(to_low(conv_weight), "dp", axis=2, tiled=True),
        lax.all_gather(to_low(head), "dp", axis=0, tiled=True),
        lax.all_gather(to_low(clusters), "dp", axis=1, tiled=True),
        lax.all_gather(to_low(blocks), "dp", axis=1, tiled=True),
    )
    proj_part, kernel_part, head_part, center_part, block_part = gathered
    return (
        lax.all_gather(proj_part, "group", axis=1, tiled=True),
        lax.all_gather(kernel_part, "group", axis=0, tiled=True),
        lax.all_gather(head_part, "group", axis=1, tiled=True),
        lax.all_gather(center_part, "group", axis=0, tiled=True),
        lax.all_gather(block_part, "group", axis=0, tiled=True),
    )


def shampoo_plain(block_rows, statistics):
    full_blocks = lax.all_gather(block_rows.astype(jnp.bfloat16), "dp", axis=1, tiled=True).astype(
        block_rows.dtype
    )
    rows = block_rows.shape[1]
    here = lax.axis_index("dp")
    first_row = here * rows
    column_slice = lax.dynamic_slice_in_dim(full_blocks, first_row, rows, 2)
    left_rows = stat_decay * statistics[:, 0] + (1 - stat_decay) * jnp.einsum(
        "brk,bck->brc", block_rows, full_blocks, precision=HIGH
    )
    right_rows = stat_decay * statistics[:, 1] + (1 - stat_decay) * jnp.einsum(
        "bkr,bkc->brc", column_slice, full_blocks, precision=HIGH
    )
    group_blocks = block_rows.shape[0]
    dp_size = lax.axis_size("dp")
    owners = [
        (2 * member + side) * dp_size // (2 * group_blocks)
        for member in range(group_blocks)
        for side in range(2)
    ]
    left_full, right_full = (
        lax.all_gather(left_rows.astype(jnp.bfloat16), "dp", axis=1, tiled=True).astype(
            left_rows.dtype
        ),
        lax.all_gather(right_rows.astype(jnp.bfloat16), "dp", axis=1, tiled=True).astype(
            right_rows.dtype
        ),
    )
    sources = [
        left_full[member] if side == 0 else right_full[member]
        for member in range(group_blocks)
        for side in range(2)
    ]
    roots = []
    for index in range(2 * group_blocks):
        owner = owners[index]
        root = lax.cond(here == owner, inverse_root, jnp.zeros_like, sources[index])
        root = spread_2(for_sending(root), "dp", owner).astype(root.dtype)
        roots.append(root)
    stacked = jnp.stack(roots).reshape(group_blocks, 2, D, D)
    left_root_rows = lax.dynamic_slice_in_dim(stacked[:, 0], first_row, rows, 1)
    update_rows = jnp.einsum(
        "brk,bkc->brc",
        jnp.einsum("brk,bkc->brc", left_root_rows, full_blocks, precision=HIGH),
        stacked[:, 1],
        precision=HIGH,
    )
    return jnp.stack([left_rows, right_rows], 1), update_rows


MESH = pl.DeviceIdType.MESH
HBM = pl.BlockSpec(memory_space=pltpu.HBM)
VMEM = pl.BlockSpec(memory_space=pltpu.VMEM)
VMEM_LIMIT = 60 * 1024 * 1024


class Place:
    def __init__(self, dp_size, group_size):
        self.dp_size, self.group_size = dp_size, group_size
        self.lines = dp_size // 2
        self.dp, self.group = lax.axis_index("dp"), lax.axis_index("group")
        self.z, self.y = self.dp // 2, self.dp % 2
        self.x, self.core = self.group // 2, self.group % 2

    def at(self, z, flip_y=0, flip_x=0, flip_core=0):
        y = self.y + flip_y * (1 - 2 * self.y)
        x = self.x + flip_x * (1 - 2 * self.x)
        core = self.core + flip_core * (1 - 2 * self.core)
        return (z * 2 + y, x * 2 + core)

    def near(self, z, p, q):
        return self.at(z, p * (1 - self.core) + q * self.core, q * (1 - self.core) + p * self.core)

    def across(self, z, p, q):
        return self.at(z, p * self.core + q * (1 - self.core), q * self.core + p * (1 - self.core), 1)


def greet(place):
    barrier = pltpu.get_barrier_semaphore()
    first = place.x * 2
    for other in range(place.dp_size):
        for core in range(2):

            @pl.when((place.dp != other) | (place.core != core))
            def _():
                pl.semaphore_signal(
                    barrier, inc=1, device_id=(other, first + core), device_id_type=MESH
                )

    for core in range(2):
        pl.semaphore_signal(
            barrier,
            inc=1,
            device_id=(place.dp, (1 - place.x) * 2 + core),
            device_id_type=MESH,
        )
    pl.semaphore_wait(barrier, 2 * place.dp_size - 1 + 2)


def guarded(condition, action):
    if condition is None:
        action()
    else:
        pl.when(condition)(action)


def both(one, two):
    if one is None:
        return two
    if two is None:
        return one
    return one & two


def piece_at(kind, ref, dp, group, shape):
    if kind == "blocks":
        start = pl.multiple_of(dp * shape[1], shape[1])
        return ref.at[pl.ds(group * shape[0], shape[0]), pl.ds(start, shape[1])]
    if kind == "conv":
        return ref.at[group, pl.ds(dp * shape[0], shape[0])]
    return ref.at[dp, group]


KINDS = ("conv", "small", "blocks")


def gather_kernel(sizes, shapes, *refs):
    place = Place(*sizes)
    count = len(KINDS)
    ins, stats_in = refs[:count], refs[count]
    outs, stats_out = refs[count + 1 : 2 * count + 1], refs[2 * count + 1]
    send_sem, recv_sem, own_sem, stat_send, stat_recv, stat_own = refs[2 * count + 2 :]
    z, last = place.z, place.lines - 1
    me = (place.dp, place.group)
    greet(place)
    sent = []
    slots = [0] * count

    def view(k, source):
        return piece_at(KINDS[k], outs[k], source[0], source[1], shapes[k])

    def identity(source):
        return source[0] * place.group_size + source[1]

    def copy_of(k, source, target, slot, own=False):
        spot = view(k, source)
        return pltpu.make_async_remote_copy(
            src_ref=ins[k] if own else spot,
            dst_ref=spot,
            send_sem=send_sem.at[k, slot],
            recv_sem=recv_sem.at[k, identity(source)],
            device_id=target,
            device_id_type=MESH,
        )

    def send(k, source, target, condition=None, own=False):
        slot = slots[k]
        slots[k] += 1
        guarded(condition, lambda: copy_of(k, source, target, slot, own).start())
        sent.append((k, source, target, slot, condition, own))

    def arrive(k, source, condition=None):
        guarded(condition, lambda: copy_of(k, source, me, 0).wait_recv())

    links = {
        "left": (place.at(z - 1), z > 0),
        "right": (place.at(z + 1), z < last),
        "p": (place.near(z, 1, 0), None),
        "q": (place.near(z, 0, 1), None),
        "core": (place.at(z, 0, 0, 1), None),
    }

    def forward(k, source, ways, condition=None, own=False):
        for way in ways:
            target, open_way = links[way]
            send(k, source, target, both(condition, open_way), own)

    def spots(offset):
        if offset == 0:
            return [(z, None, ("left", "right"))]
        return [
            (z - offset, z >= offset, ("right",)),
            (z + offset, z + offset <= last, ("left",)),
        ]

    def take(k, source, condition, ways):
        arrive(k, source, condition)
        forward(k, source, ways, condition)

    steps = place.lines + 3

    def step_z_first(k, step):
        if step == 0:
            forward(k, me, ("left", "right", "q", "p", "core"), own=True)
            return
        if step < place.lines:
            for spot, there, ways in spots(step):
                take(k, place.near(spot, 0, 0), there, ways + ("q", "p", "core"))
        if 0 <= step - 1 < place.lines:
            for spot, there, _ in spots(step - 1):
                take(k, place.near(spot, 1, 0), there, ("q", "core"))
                take(k, place.near(spot, 0, 1), there, ("core",))
        if 0 <= step - 2 < place.lines:
            for spot, there, _ in spots(step - 2):
                take(k, place.near(spot, 1, 1), there, ("core",))

    def step_z_second(k, step):
        if step == 0:
            forward(k, me, ("q", "left", "right", "p", "core"), own=True)
            return
        if step == 1:
            take(k, place.near(z, 0, 1), None, ("left", "right", "p", "core"))
        if step < place.lines:
            for spot, there, ways in spots(step):
                take(k, place.near(spot, 0, 0), there, ways + ("p", "core"))
        if 1 <= step - 1 < place.lines:
            for spot, there, ways in spots(step - 1):
                take(k, place.near(spot, 0, 1), there, ways + ("p", "core"))
        if 0 <= step - 1 < place.lines:
            for spot, there, _ in spots(step - 1):
                take(k, place.near(spot, 1, 0), there, ("core",))
        if 0 <= step - 2 < place.lines:
            for spot, there, _ in spots(step - 2):
                take(k, place.near(spot, 1, 1), there, ("core",))

    members = shapes[KINDS.index("blocks")][0]
    rows = shapes[KINDS.index("blocks")][1]

    def stat_copy(member, side):
        owner = place.core * members + member
        start = pl.multiple_of(place.dp * rows, rows)
        return owner, pltpu.make_async_remote_copy(
            src_ref=stats_in.at[member, side],
            dst_ref=stats_out.at[pl.ds(start, rows)],
            send_sem=stat_send.at[member, side],
            recv_sem=stat_recv.at[place.dp],
            device_id=(owner, place.x * 2 + side),
            device_id_type=MESH,
        )

    def stat_local(member, side):
        start = pl.multiple_of(place.dp * rows, rows)
        return pltpu.make_async_copy(
            stats_in.at[member, side], stats_out.at[pl.ds(start, rows)], stat_own
        )

    def each_stat(remote, local):
        for member in range(members):
            for side in range(2):
                owner = place.core * members + member
                mine = (place.dp == owner) & (place.core == side)
                pl.when(jnp.logical_not(mine))(lambda m=member, s=side: remote(m, s))
                pl.when(mine)(lambda m=member, s=side: local(m, s))

    own_copies = [
        pltpu.make_async_copy(ins[k], view(k, me), own_sem.at[k]) for k in range(count)
    ]
    for step in range(steps):
        for k, kind in enumerate(KINDS):
            if kind == "blocks":
                step_z_second(k, step)
            else:
                step_z_first(k, step)
        if step == 0:
            for own in own_copies:
                own.start()
        if step == 1:
            each_stat(
                lambda m, s: stat_copy(m, s)[1].start(), lambda m, s: stat_local(m, s).start()
            )
    for k in range(count):
        for spot in range(place.lines):
            for p in range(2):
                for q in range(2):
                    arrive(k, place.across(spot, p, q))
    for own in own_copies:
        own.wait()
    each_stat(lambda m, s: stat_copy(m, s)[1].wait_send(), lambda m, s: stat_local(m, s).wait())
    owned_group = place.x * 2 + place.dp // members

    @pl.when(place.dp < 2 * members)
    def _():
        for other in range(place.dp_size):

            @pl.when((place.dp != other) | (place.group != owned_group))
            def _():
                pltpu.make_async_remote_copy(
                    src_ref=stats_in.at[0, 0],
                    dst_ref=stats_out.at[pl.ds(other * rows, rows)],
                    send_sem=stat_send.at[0, 0],
                    recv_sem=stat_recv.at[other],
                    device_id=me,
                    device_id_type=MESH,
                ).wait_recv()

    for k, source, target, slot, condition, own in sent:
        guarded(
            condition,
            lambda k=k, source=source, target=target, slot=slot, own=own: copy_of(
                k, source, target, slot, own
            ).wait_send(),
        )


def full_shapes(sizes, shapes):
    dp_size, group_size = sizes
    conv, small, blocks = shapes
    return [
        (group_size, dp_size * conv[0]) + conv[1:],
        (dp_size, group_size) + small,
        (group_size * blocks[0], dp_size * blocks[1], blocks[2]),
    ]


def gather_weights(sizes, pieces, stats_low):
    shapes = [piece.shape for piece in pieces]
    outs = [
        jax.ShapeDtypeStruct(shape, jnp.bfloat16) for shape in full_shapes(sizes, shapes)
    ] + [jax.ShapeDtypeStruct((D, D), jnp.bfloat16)]
    count, devices = len(pieces), sizes[0] * sizes[1]
    members = shapes[-1][0]
    return pl.pallas_call(
        functools.partial(gather_kernel, sizes, shapes),
        out_shape=outs,
        in_specs=[HBM] * (count + 1),
        out_specs=[HBM] * (count + 1),
        scratch_shapes=[
            pltpu.SemaphoreType.DMA((count, 3 * devices)),
            pltpu.SemaphoreType.DMA((count, devices)),
            pltpu.SemaphoreType.DMA((count,)),
            pltpu.SemaphoreType.DMA((members, 2)),
            pltpu.SemaphoreType.DMA((sizes[0],)),
            pltpu.SemaphoreType.DMA,
        ],
        name="gather_weights",
        compiler_params=pltpu.CompilerParams(
            collective_id=0, has_side_effects=True, vmem_limit_bytes=VMEM_LIMIT
        ),
    )(*pieces, stats_low)


def shift_right(values, by):
    if by == 0:
        return values
    parts = []
    for first in range(0, values.shape[1], CLIP):
        part = values[:, first : first + CLIP]
        lane = lax.broadcasted_iota(jnp.int32, part.shape, 1)
        turned = pltpu.roll(part, by % CLIP, 1)
        inside = lane >= by if by > 0 else lane < CLIP + by
        parts.append(jnp.where(inside, turned, 0.0))
    return jnp.concatenate(parts, 1)


def place_windows(hidden, windows, taps):
    channels = hidden.shape[0]
    runs, half = taps // STRIDE, taps // STRIDE // 2
    for run in range(runs):
        by = STRIDE * (half - 1 - run) if run < half else -STRIDE * (run - half)
        windows[run * channels : (run + 1) * channels, :] = shift_right(hidden, by).astype(
            jnp.bfloat16
        )


def conv_group(hidden, weight_at, windows, taps, shape):
    channels = hidden.shape[0]
    chunks, _, _, chunk = shape
    place_windows(hidden, windows, taps)
    total = None
    for side in range(2):
        part = None
        for index in range(side * chunks // 2, (side + 1) * chunks // 2):
            term = dot(weight_at(index), windows[index * chunk : (index + 1) * chunk, :])
            part = term if part is None else part + term
        for offset in range(STRIDE):
            by = STRIDE - offset if side == 0 else -offset
            moved = shift_right(part[offset * channels : (offset + 1) * channels], by)
            total = moved if total is None else total + moved
    return total


def conv_group_back(hidden, grad, weight_at, put, windows, moved, taps, shape):
    channels = hidden.shape[0]
    chunks, _, _, chunk = shape
    half, runs = taps // STRIDE // 2, chunk // channels
    place_windows(hidden, windows, taps)
    total = None
    for side in range(2):
        for offset in range(STRIDE):
            by = offset - STRIDE if side == 0 else offset
            moved[offset * channels : (offset + 1) * channels, :] = shift_right(grad, by).astype(
                jnp.bfloat16
            )
        for index in range(side * chunks // 2, (side + 1) * chunks // 2):
            put(
                index,
                dot_nt(moved[...], windows[index * chunk : (index + 1) * chunk, :]).astype(
                    jnp.bfloat16
                ),
            )
            turned = dot_tn(weight_at(index), moved[...])
            for step in range(runs):
                run = index * runs + step
                by = -STRIDE * (half - 1 - run) if run < half else STRIDE * (run - half)
                part = shift_right(turned[step * channels : (step + 1) * channels], by)
                total = part if total is None else total + part
    return total


def over_rows(total, tile, action):
    def step(index, _):
        action(pl.ds(pl.multiple_of(index * tile, tile), tile))
        return 0

    lax.fori_loop(0, total // tile, step, 0)


def dot(one, two):
    return jnp.dot(one, two, preferred_element_type=jnp.float32)


def dot_nt(one, two):
    return lax.dot_general(one, two, (((1,), (1,)), ((), ())), preferred_element_type=jnp.float32)


def dot_tn(one, two):
    return lax.dot_general(one, two, (((0,), (0,)), ((), ())), preferred_element_type=jnp.float32)


def norm_parts(values):
    average = jnp.mean(values, -1, keepdims=True)
    centred = values - average
    inverse = lax.rsqrt(jnp.mean(centred * centred, -1, keepdims=True) + 1e-05)
    return centred * inverse, inverse


def norm_back(upstream, unit, inverse, gain):
    scaled = upstream * gain
    along = jnp.mean(scaled * unit, -1, keepdims=True)
    return inverse * (scaled - jnp.mean(scaled, -1, keepdims=True) - unit * along)


def gelu_pair(values):
    below = 0.5 + 0.5 * lax.erf(values * 0.7071067811865476)
    density = jnp.exp(values * values * -0.5) * 0.3989422804014327
    return values * below, below + values * density


def add_row(ref, row, values):
    ref[row : row + 1, :] += jnp.sum(values, 0, keepdims=True)


def front_kernel(taps, *refs):
    (
        features, mask, feature_norm, vectors, small, kernel,
        feature_unit, normed, hidden_t, encoded, encoder_unit, encoder_inverse, slope,
        held, windows, hidden, out_t, load_sem,
    ) = refs
    frames = features.shape[0]
    groups = kernel.shape[1]
    channels = hidden_t.shape[0] // groups

    def load(group):
        return pltpu.make_async_copy(kernel.at[:, group], held.at[:, group], load_sem.at[group])

    for group in range(groups):
        load(group).start()

    def enter(at):
        unit, _ = norm_parts(features[at, :].astype(jnp.float32))
        feature_unit[at, :] = unit
        normed[at, :] = (unit * feature_norm[0:1, :] + feature_norm[1:2, :]).astype(jnp.bfloat16)

    over_rows(frames, 32, enter)
    normed_t = normed[...].T
    parts, columns = small.shape[0], small.shape[1]
    third = D // columns
    for group in range(columns):
        for first, size in ((0, 128), (128, third - 128)):
            row = first // 2
            part = small[:, group, row : row + 64, :].reshape(parts * 64, 128)
            at = group * third + first
            out_t[at : at + size, :] = dot_tn(part, normed_t)[:size]
    hidden[...] = jnp.where(mask[...] > 0, vectors[0:1, :], out_t[...].T)
    hidden_t[...] = hidden[...].T.astype(jnp.bfloat16)

    def one_group(group, _):
        load(group).wait()
        at = pl.ds(pl.multiple_of(group * channels, channels), channels)
        out_t[at, :] = conv_group(
            hidden_t[at, :].astype(jnp.float32), lambda index: held[index, group], windows, taps, kernel.shape
        )
        return 0

    lax.fori_loop(0, groups, one_group, 0)
    slope[...] = out_t[...].T

    def leave(at):
        active, derivative = gelu_pair(slope[at, :])
        slope[at, :] = derivative
        unit, inverse = norm_parts(hidden[at, :] + active)
        encoder_unit[at, :] = unit
        encoder_inverse[at, :] = inverse
        encoded[at, :] = unit * vectors[1:2, :] + vectors[2:3, :]

    over_rows(frames, 32, leave)


def front(features, mask, feature_norm, vectors, small, kernel, taps):
    frames, width = features.shape
    chunks, groups, rows, chunk = kernel.shape
    full, low = jnp.float32, jnp.bfloat16
    out = jax.ShapeDtypeStruct
    return pl.pallas_call(
        functools.partial(front_kernel, taps),
        out_shape=[
            out((frames, width), full),
            out((frames, width), low),
            out((D, frames), low),
            out((frames, D), full),
            out((frames, D), full),
            out((frames, 1), full),
            out((frames, D), full),
        ],
        in_specs=[VMEM] * 5 + [HBM],
        out_specs=[VMEM] * 7,
        scratch_shapes=[
            pltpu.VMEM(kernel.shape, low),
            pltpu.VMEM((chunks * chunk, frames), low),
            pltpu.VMEM((frames, D), full),
            pltpu.VMEM((D, frames), full),
            pltpu.SemaphoreType.DMA((groups,)),
        ],
        name="front",
        compiler_params=pltpu.CompilerParams(vmem_limit_bytes=32 * 1024 * 1024),
    )(features, mask, feature_norm, vectors, small, kernel)


def trunk_kernel(*refs):
    (
        encoded, mask, labels, vectors, small, blocks,
        encoded_grad, block_grad, head_grad, center_grad_t, rows_out, counted,
        head, table, centers, held, made, low, triple, attention, mixed, unit_one, inverse_one, middle, middle_low,
        active, slope, unit_two, inverse_two, work, work_low, flow_low, triple_grad, turned,
        load_sem, save_sem,
    ) = refs
    frames = encoded.shape[0]
    count = blocks.shape[0]
    ups = (count - 4) // 2
    tile = 32
    pairs = D // 128

    def load(block):
        return pltpu.make_async_copy(blocks.at[block], held.at[block], load_sem.at[block])

    def save(block):
        return pltpu.make_async_copy(made.at[block], block_grad.at[block], save_sem.at[block])

    for block in range(count):
        load(block).start()
    rows_out[...] = jnp.zeros_like(rows_out)
    parts, columns = small.shape[0], small.shape[1]
    notes = small[:, :, 224:240, :].astype(jnp.float32)
    first = lax.broadcasted_iota(jnp.int32, notes.shape, 2) == 0
    first &= lax.broadcasted_iota(jnp.int32, notes.shape, 3) == CLUSTER_ROWS
    notes = jnp.sum(jnp.where(first, notes, 0.0), (0, 1))
    masked = jnp.sum(jnp.sum(notes, 1, keepdims=True), 0, keepdims=True)
    counted[...] = jnp.broadcast_to(masked, counted.shape)

    def to_inputs(at):
        low[at, :] = encoded[at, :].astype(jnp.bfloat16)

    over_rows(frames, tile, to_inputs)

    def first_three(block, _):
        load(block).wait()
        triple[block] = dot(low[...], held[block]).astype(jnp.bfloat16)
        return 0

    lax.fori_loop(0, 3, first_three, 0)
    lane = lax.broadcasted_iota(jnp.int32, (CLIP, 128), 1)
    even = lane < HEAD

    def apart(values):
        zero = jnp.zeros_like(values)
        return jnp.concatenate([jnp.where(even, values, zero), jnp.where(even, zero, values)], 0)

    def beside(values):
        return jnp.concatenate([values[:CLIP], values[CLIP:]], 1)

    def spot(index):
        at = pl.ds(pl.multiple_of(index // pairs * CLIP, CLIP), CLIP)
        return at, pl.ds(pl.multiple_of(index % pairs * 128, 128), 128)

    def attend(index, _):
        at, lanes = spot(index)
        query, keys, values = triple[0, at, lanes], triple[1, at, lanes], triple[2, at, lanes]
        scores = dot_nt(apart(query), keys) * HEAD ** (-0.5)
        raised = jnp.exp(scores - jnp.max(scores, -1, keepdims=True))
        full = raised / jnp.sum(raised, -1, keepdims=True)
        attention[index] = full
        mixed[at, lanes] = dot(beside(full.astype(jnp.bfloat16)), apart(values)).astype(jnp.bfloat16)
        return 0

    lax.fori_loop(0, frames // CLIP * pairs, attend, 0)
    load(3).wait()
    work[...] = dot(mixed[...], held[3])

    def first_norm(at):
        unit, inverse = norm_parts(encoded[at, :] + work[at, :])
        unit_one[at, :] = unit
        inverse_one[at, :] = inverse
        value = unit * vectors[3:4, :] + vectors[4:5, :]
        middle[at, :] = value
        middle_low[at, :] = value.astype(jnp.bfloat16)

    over_rows(frames, tile, first_norm)

    def expand(step, _):
        load(4 + step).wait()
        slope[step] = dot(middle_low[...], held[4 + step])

        def bend(at):
            value, derivative = gelu_pair(slope[step, at, :])
            active[step, at, :] = value.astype(jnp.bfloat16)
            slope[step, at, :] = derivative

        over_rows(frames, tile, bend)
        return 0

    lax.fori_loop(0, ups, expand, 0)

    def contract(step, _):
        load(4 + ups + step).wait()
        middle[...] += dot(active[step], held[4 + ups + step])
        return 0

    lax.fori_loop(0, ups, contract, 0)

    def second_norm(at):
        unit, inverse = norm_parts(middle[at, :])
        unit_two[at, :] = unit
        inverse_two[at, :] = inverse
        flow_low[at, :] = (unit * vectors[5:6, :] + vectors[6:7, :]).astype(jnp.bfloat16)

    over_rows(frames, tile, second_norm)
    table[...] = jnp.zeros_like(table)
    for group in range(columns):
        across = slice(group * 128, group * 128 + 128)
        head[:, across] = small[:, group, 128:224, :].reshape(parts * 96, 128)
        for part in range(parts):
            row = part // 2 * 128 + part % 2 * 32
            table[row : row + 32, across] = small[part, group, 224:256, :].astype(jnp.float32)
    real = lax.broadcasted_iota(jnp.int32, (1, table.shape[1]), 1) % 128 < CLUSTER_ROWS
    table[...] = jnp.where(real, table[...], 0.0)
    size = lax.rsqrt(jnp.sum(table[...] * table[...], 0, keepdims=True) + 1e-06)
    centers[...] = (table[...] * size).astype(jnp.bfloat16)
    embedded = dot(flow_low[...], head[...])
    length = lax.rsqrt(jnp.sum(embedded * embedded, -1, keepdims=True) + 1e-06)
    unit_low = (embedded * length).astype(jnp.bfloat16)
    logits = jnp.where(real, dot(unit_low, centers[...]) * inv_temp, -1e30)
    top = jnp.max(logits, -1, keepdims=True)
    raised = jnp.exp(logits - top)
    amount = jnp.sum(raised, -1, keepdims=True)
    choose = labels[...] == lax.broadcasted_iota(jnp.int32, logits.shape, 1)
    target = jnp.sum(jnp.where(choose, logits, 0.0), -1, keepdims=True)
    losses = mask[...] * (jnp.log(amount) + top - target)
    rows_out[7:8, :] = jnp.broadcast_to(jnp.sum(losses, 0, keepdims=True), (1, D))
    logit_grad = (
        (raised / amount - choose.astype(jnp.float32)) * (mask[...] * (1.0 / masked))
    ).astype(jnp.bfloat16)
    unit_grad = dot_nt(logit_grad, centers[...]) * inv_temp
    spread = dot_tn(unit_low, logit_grad) * inv_temp
    shared = jnp.sum(spread * table[...], 0, keepdims=True)
    spread = size * spread - table[...] * (size * size * size * shared)
    for group in range(columns):
        center_grad_t[group * 64 : group * 64 + 64, :] = spread[group * 128 : group * 128 + 64, :]
    along = jnp.sum(unit_grad * embedded, -1, keepdims=True)
    embedded_grad = (
        length * unit_grad - embedded * (length * length * length * along)
    ).astype(jnp.bfloat16)
    work[...] = dot_nt(embedded_grad, head[...])
    head_grad[...] = dot_tn(flow_low[...], embedded_grad).astype(jnp.bfloat16)

    def second_back(at):
        upstream = work[at, :]
        add_row(rows_out, 5, upstream * unit_two[at, :])
        add_row(rows_out, 6, upstream)
        value = norm_back(upstream, unit_two[at, :], inverse_two[at, :], vectors[5:6, :])
        middle[at, :] = value
        flow_low[at, :] = value.astype(jnp.bfloat16)

    over_rows(frames, tile, second_back)
    turned[...] = middle_low[...].T

    def feed_back(step, _):
        work[...] = dot_nt(flow_low[...], held[4 + ups + step])
        made[4 + ups + step] = dot_tn(active[step], flow_low[...]).astype(jnp.bfloat16)
        save(4 + ups + step).start()

        def bend(at):
            work_low[at, :] = (work[at, :] * slope[step, at, :]).astype(jnp.bfloat16)

        over_rows(frames, tile, bend)
        made[4 + step] = dot(turned[...], work_low[...]).astype(jnp.bfloat16)
        save(4 + step).start()
        middle[...] += dot_nt(work_low[...], held[4 + step])
        return 0

    lax.fori_loop(0, ups, feed_back, 0)

    def first_back(at):
        upstream = middle[at, :]
        add_row(rows_out, 3, upstream * unit_one[at, :])
        add_row(rows_out, 4, upstream)
        value = norm_back(upstream, unit_one[at, :], inverse_one[at, :], vectors[3:4, :])
        middle[at, :] = value
        flow_low[at, :] = value.astype(jnp.bfloat16)

    over_rows(frames, tile, first_back)
    made[3] = dot_tn(mixed[...], flow_low[...]).astype(jnp.bfloat16)
    save(3).start()
    work_low[...] = dot_nt(flow_low[...], held[3]).astype(jnp.bfloat16)

    def attend_back(index, _):
        at, lanes = spot(index)
        query, keys, values = triple[0, at, lanes], triple[1, at, lanes], triple[2, at, lanes]
        upstream = apart(work_low[at, lanes])
        full = attention[index]
        full_grad = dot_nt(upstream, values)
        triple_grad[2, at, lanes] = dot_tn(full.astype(jnp.bfloat16), upstream).astype(jnp.bfloat16)
        along = jnp.sum(full * full_grad, -1, keepdims=True)
        score_grad = (full * (full_grad - along)).astype(jnp.bfloat16)
        triple_grad[0, at, lanes] = (
            dot(beside(score_grad), apart(keys)) * HEAD ** (-0.5)
        ).astype(jnp.bfloat16)
        triple_grad[1, at, lanes] = (
            dot_tn(score_grad, apart(query)) * HEAD ** (-0.5)
        ).astype(jnp.bfloat16)
        return 0

    lax.fori_loop(0, frames // CLIP * pairs, attend_back, 0)
    turned[...] = low[...].T

    def last_three(block, _):
        made[block] = dot(turned[...], triple_grad[block]).astype(jnp.bfloat16)
        save(block).start()
        middle[...] += dot_nt(triple_grad[block], held[block])
        return 0

    lax.fori_loop(0, 3, last_three, 0)
    encoded_grad[...] = middle[...]
    for block in range(count):
        save(block).wait()


def trunk(encoded, mask, labels, vectors, small, blocks):
    frames, count = encoded.shape[0], blocks.shape[0]
    ups, columns = (count - 4) // 2, small.shape[1] * 128
    full, low = jnp.float32, jnp.bfloat16
    out = jax.ShapeDtypeStruct
    wide, wide_low = pltpu.VMEM((frames, D), full), pltpu.VMEM((frames, D), low)
    column = pltpu.VMEM((frames, 1), full)
    return pl.pallas_call(
        trunk_kernel,
        out_shape=[
            out((frames, D), full),
            out(blocks.shape, low),
            out((D, columns), low),
            out((columns // 2, columns), full),
            out((8, D), full),
            out((8, 128), full),
        ],
        in_specs=[VMEM] * 5 + [HBM],
        out_specs=[VMEM, HBM] + [VMEM] * 4,
        scratch_shapes=[
            pltpu.VMEM((D, columns), low),
            pltpu.VMEM((columns, columns), full),
            pltpu.VMEM((columns, columns), low),
            pltpu.VMEM(blocks.shape, low),
            pltpu.VMEM(blocks.shape, low),
            wide_low,
            pltpu.VMEM((3, frames, D), low),
            pltpu.VMEM((frames // CLIP * D // 128, 2 * CLIP, CLIP), full),
            wide_low,
            wide,
            column,
            wide,
            wide_low,
            pltpu.VMEM((ups, frames, D), low),
            pltpu.VMEM((ups, frames, D), full),
            wide,
            column,
            wide,
            wide_low,
            wide_low,
            pltpu.VMEM((3, frames, D), low),
            pltpu.VMEM((D, frames), low),
            pltpu.SemaphoreType.DMA((count,)),
            pltpu.SemaphoreType.DMA((count,)),
        ],
        name="trunk",
        compiler_params=pltpu.CompilerParams(vmem_limit_bytes=VMEM_LIMIT),
    )(encoded, mask, labels, vectors, small, blocks)


class Reducer:
    def __init__(self, place, shapes, local, refs, sems):
        self.place, self.shapes, self.local = place, shapes, local
        self.z, self.lines, self.last = place.z, place.lines, place.lines - 1
        self.blocks = KINDS.index("blocks")
        self.rest = [k for k in range(len(KINDS)) if k != self.blocks]
        self.crossed, self.first_in, self.second_in, self.line_in = refs[:4]
        self.held, self.source = refs[4:]
        (
            self.load_sem, self.cross_send, self.cross_recv, self.first_send, self.first_recv,
            self.second_send, self.second_recv, self.left_send, self.left_recv, self.right_send,
            self.right_recv,
        ) = sems
        self.p_mate, self.q_mate = place.near(self.z, 1, 0), place.near(self.z, 0, 1)
        self.c_mate = place.at(self.z, 0, 0, 1)
        self.left, self.right = place.at(self.z - 1), place.at(self.z + 1)

    def z_first(self, k):
        return k != self.blocks

    def remote(self, source, target, send, recv, device):
        return pltpu.make_async_remote_copy(
            src_ref=source,
            dst_ref=target,
            send_sem=send,
            recv_sem=recv,
            device_id=device,
            device_id_type=MESH,
        )

    def load_of(self, p, q, spot):
        k = self.blocks
        dp, group = self.place.near(spot, p, q)
        return pltpu.make_async_copy(
            piece_at("blocks", self.source[k], dp, group, self.shapes[k]),
            self.held.at[q, spot],
            self.load_sem.at[p, q, spot],
        )

    def cross_of(self, k, p, q, spot):
        dp, group = self.place.across(spot, p, q)
        return self.remote(
            piece_at(KINDS[k], self.source[k], dp, group, self.shapes[k]),
            self.crossed[k].at[p, q, spot],
            self.cross_send.at[k, p, q, spot],
            self.cross_recv.at[k, p, q, spot],
            self.c_mate,
        )

    def own(self, k, p, q, spot):
        if k == self.blocks:
            self.load_of(p, q, spot).wait()
            return f32(self.held, (q, spot))
        dp, group = self.place.near(spot, p, q)
        return piece_at(KINDS[k], self.source[k], dp, group, self.shapes[k])[...].astype(jnp.float32)

    def met(self, k, p, q, spot):
        own = self.own(k, p, q, spot)
        self.cross_of(k, p, q, spot).wait_recv()
        return own + f32(self.crossed[k], (p, q, spot))

    def first_out(self, k, a, spot):
        p, q = (a, 1) if self.z_first(k) else (1, a)
        return self.remote(
            self.crossed[k].at[p, q, spot],
            self.first_in[k].at[a, spot],
            self.first_send.at[k, a, spot],
            self.first_recv.at[k, a, spot],
            self.q_mate if self.z_first(k) else self.p_mate,
        )

    def stage_one(self, k, index):
        lines = self.lines
        a, turn = 1 - index // lines, index % lines
        odd = turn % 2
        spot = (1 - odd) * (self.last - turn // 2) + odd * (turn // 2)
        p, q = (a, 1) if self.z_first(k) else (1, a)
        total = self.met(k, p, q, spot)
        self.crossed[k][p, q, spot] = total.astype(jnp.bfloat16)
        self.first_out(k, a, spot).start()
        if k == self.blocks:
            self.load_of(0, a, spot).start()

    def joined(self, k, p, q, spot):
        total = self.met(k, p, q, spot)
        a = p if self.z_first(k) else q
        self.first_out(k, a, spot).wait_recv()
        return total + f32(self.first_in[k], (a, spot))

    def second_out(self, k, spot):
        return self.remote(
            self.crossed[k].at[1, 0, spot],
            self.second_in[k].at[spot],
            self.second_send.at[k, spot],
            self.second_recv.at[k, spot],
            self.p_mate,
        )

    def stage_two(self, k, spot):
        self.crossed[k][1, 0, spot] = self.joined(k, 1, 0, spot).astype(jnp.bfloat16)
        self.second_out(k, spot).start()

    def line_total(self, k, a, spot):
        total = self.joined(k, 0, a, spot)
        if self.z_first(k):
            self.second_out(k, spot).wait_recv()
            total = total + f32(self.second_in[k], (spot,))
        return total

    def line_out(self, k, a, spot, way):
        if way == "right":
            send, recv, device, slot = self.right_send, self.left_recv, self.right, spot
        else:
            send, recv, device = self.left_send, self.right_recv, self.left
            ends = (self.last - (self.z - 1 - spot)) // self.last
            slot = spot + ends * (self.lines - spot)
        return self.remote(
            self.crossed[k].at[0, a, spot],
            self.line_in[k].at[a, slot],
            send.at[k, a, spot],
            recv.at[k, a, spot],
            device,
        )

    def came_in(self, k, a, spot, way):
        recv = self.left_recv if way == "right" else self.right_recv
        send = self.right_send if way == "right" else self.left_send
        return self.remote(
            self.crossed[k].at[0, a, spot],
            self.line_in[k].at[a, spot],
            send.at[k, a, spot],
            recv.at[k, a, spot],
            self.c_mate,
        )

    def pass_on(self, k, a, spot, way, inner):
        z = self.z
        if way == "right":
            here = (z < spot) & ((z > 0) if inner else (z == 0))
        else:
            here = (z > spot) & ((z < self.last) if inner else (z == self.last))

        @pl.when(here)
        def _():
            total = self.line_total(k, a, spot)
            if inner:
                self.came_in(k, a, spot, way).wait_recv()
                total = total + f32(self.line_in[k], (a, spot))
            self.crossed[k][0, a, spot] = total.astype(jnp.bfloat16)
            self.line_out(k, a, spot, way).start()

    def line_step(self, k, a, step, inner):
        self.pass_on(k, a, self.last - step, "right", inner)
        self.pass_on(k, a, step, "left", inner)

    def line_end(self, k, a, out):
        z = self.z
        out[...] = self.line_total(k, a, z)

        @pl.when(z > 0)
        def _():
            self.came_in(k, a, z, "right").wait_recv()
            out[...] += f32(self.line_in[k], (a, z))

        @pl.when(z < self.last)
        def _():
            self.came_in(k, a, z, "left").wait_recv()
            out[...] += f32(self.line_in[k], (a, self.lines))

    def last_out(self):
        k = self.blocks
        return self.remote(
            self.crossed[k].at[0, 1, self.z],
            self.second_in[k].at[0],
            self.second_send.at[k, 0],
            self.second_recv.at[k, 0],
            self.q_mate,
        )

    def drain(self):
        self.last_out().wait_send()
        for k in range(len(KINDS)):

            def one(spot, _, k=k):
                for p in range(2):
                    for q in range(2):
                        self.cross_of(k, p, q, spot).wait_send()
                for a in range(2):
                    self.first_out(k, a, spot).wait_send()
                if self.z_first(k):
                    self.second_out(k, spot).wait_send()
                for a in (0,) if self.z_first(k) else (0, 1):

                    @pl.when(self.z < spot)
                    def _(a=a):
                        self.line_out(k, a, spot, "right").wait_send()

                    @pl.when(self.z > spot)
                    def _(a=a):
                        self.line_out(k, a, spot, "left").wait_send()

                return 0

            lax.fori_loop(0, self.lines, one, 0)


def f32(ref, at):
    return ref[at].astype(jnp.float32)


def back_compute(taps, refs, made, small_made, rows, scratch, hook):
    (
        encoded_grad, mask, vectors, small, feature_unit, normed, hidden_t,
        encoder_unit, encoder_inverse, slope, trunk_rows, head_grad, center_grad_t, kernel,
    ) = refs
    slots, windows, moved, grad, grad_t, through, through_t, load_sem = scratch
    frames, width = feature_unit.shape
    groups = kernel.shape[1]
    channels = hidden_t.shape[0] // groups

    def load(group):
        slot = group % 2
        return pltpu.make_async_copy(kernel.at[:, group], slots.at[slot], load_sem.at[slot])

    load(0).start()
    rows[...] = jnp.zeros_like(rows)
    rows[0:8, :] = trunk_rows[...]

    def enter(at):
        upstream = encoded_grad[at, :]
        add_row(rows, 1, upstream * encoder_unit[at, :])
        add_row(rows, 2, upstream)
        value = norm_back(upstream, encoder_unit[at, :], encoder_inverse[at, :], vectors[1:2, :])
        grad[at, :] = value
        through[at, :] = value * slope[at, :]

    over_rows(frames, 32, enter)
    grad_t[...] = through[...].T.astype(jnp.bfloat16)

    def one_group(group, _):
        pl.when(group + 1 < groups)(lambda: load(group + 1).start())
        load(group).wait()
        at = pl.ds(pl.multiple_of(group * channels, channels), channels)

        def put(index, value):
            made[index, group] = value

        through_t[at, :] = conv_group_back(
            hidden_t[at, :].astype(jnp.float32),
            grad_t[at, :].astype(jnp.float32),
            lambda index: slots[group % 2, index],
            put,
            windows,
            moved,
            taps,
            kernel.shape,
        )
        hook(group)
        return 0

    lax.fori_loop(0, groups, one_group, 0)
    through[...] = through_t[...].T

    def leave(at):
        total = grad[at, :] + through[at, :]
        inside = mask[at, :] > 0
        add_row(rows, 0, jnp.where(inside, total, 0.0))
        grad[at, :] = jnp.where(inside, 0.0, total)

    over_rows(frames, 32, leave)
    grad_t[...] = grad[...].T.astype(jnp.bfloat16)
    normed_t = normed[...].T
    parts, columns = small.shape[0], small.shape[1]
    third = D // columns
    total = None
    for group in range(columns):
        one = grad_t[group * third : group * third + 128, :]
        two = grad_t[group * third + 128 : (group + 1) * third, :]
        lane = third - 128
        wide = dot_nt(normed_t, one).astype(jnp.bfloat16)
        thin = dot_nt(normed_t, two).astype(jnp.bfloat16)
        small_made[:, group, 0:64, :] = wide.reshape(parts, 64, 128)
        small_made[:, group, 64:128, :] = jnp.concatenate(
            [thin, jnp.zeros((thin.shape[0], 128 - lane), jnp.bfloat16)], 1
        ).reshape(parts, 64, 128)
        small_made[:, group, 128:224, :] = head_grad[:, group * 128 : group * 128 + 128].reshape(
            parts, 96, 128
        )
        small_made[:, group, 224:256, :] = (
            center_grad_t[:, group * 128 : group * 128 + 128]
            .astype(jnp.bfloat16)
            .reshape(parts, 32, 128)
        )
        first = small[:, group, 0:64, :].reshape(parts * 64, 128)
        second = small[:, group, 64:128, :].reshape(parts * 64, 128)[:, :lane]
        term = dot(first, one) + dot(second, two)
        total = term if total is None else total + term
    normed_grad = total.T
    rows[8:9, 0:width] = jnp.sum(normed_grad * feature_unit[...], 0, keepdims=True)
    rows[9:10, 0:width] = jnp.sum(normed_grad, 0, keepdims=True)


def back_scratch(kernel_shape, frames):
    chunks, groups, rows, chunk = kernel_shape
    full, low = jnp.float32, jnp.bfloat16
    return [
        pltpu.VMEM((2, chunks, rows, chunk), low),
        pltpu.VMEM((chunks * chunk, frames), low),
        pltpu.VMEM((rows, frames), low),
        pltpu.VMEM((frames, D), full),
        pltpu.VMEM((D, frames), low),
        pltpu.VMEM((frames, D), full),
        pltpu.VMEM((D, frames), full),
        pltpu.SemaphoreType.DMA((2,)),
    ]


BACK_INPUTS = 14


def back_kernel(taps, *refs):
    made, small_made, rows = refs[BACK_INPUTS : BACK_INPUTS + 3]
    back_compute(
        taps, refs[:BACK_INPUTS], made, small_made, rows, refs[BACK_INPUTS + 3 :], lambda group: None
    )


def back(taps, operands):
    kernel, small, frames = operands[-1], operands[3], operands[0].shape[0]
    return pl.pallas_call(
        functools.partial(back_kernel, taps),
        out_shape=[
            jax.ShapeDtypeStruct(kernel.shape, jnp.bfloat16),
            jax.ShapeDtypeStruct(small.shape, jnp.bfloat16),
            jax.ShapeDtypeStruct((16, D), jnp.float32),
        ],
        in_specs=[VMEM] * (BACK_INPUTS - 1) + [HBM],
        out_specs=[VMEM] * 3,
        scratch_shapes=back_scratch(kernel.shape, frames),
        name="back",
        compiler_params=pltpu.CompilerParams(vmem_limit_bytes=48 * 1024 * 1024),
    )(*operands)


def back_reduce_kernel(sizes, shapes, taps, *refs):
    place = Place(*sizes)
    refs = list(refs)

    def pull(number):
        taken = refs[:number]
        del refs[:number]
        return taken

    count = len(KINDS)
    inputs, (block_grad,) = pull(BACK_INPUTS), pull(1)
    outs, (small_out, square_out, whole_out) = pull(count), pull(3)
    made, small_made, rows, scratch = *pull(3), pull(8)
    crossed, first_in, second_in, line_in = (pull(count) for _ in range(4))
    (held, group_box, dp_box, rows_low, whole_box) = pull(5)
    sems = pull(11)
    (group_send, group_recv, dp_send, dp_recv, row_send, row_recv, pair_send, pair_recv) = pull(8)
    me = (place.dp, place.group)
    source = {"conv": made, "small": small_made, "blocks": block_grad}
    run = Reducer(
        place,
        shapes,
        None,
        (crossed, first_in, second_in, line_in, held, [source[kind] for kind in KINDS]),
        sems,
    )
    lines, b = run.lines, run.blocks
    conv, tiny = KINDS.index("conv"), KINDS.index("small")
    greet(place)
    for p in (1, 0):
        for q in (1, 0):

            def begin(turn, _, p=p, q=q):
                odd = turn % 2
                spot = (1 - odd) * (run.last - turn // 2) + odd * (turn // 2)
                run.cross_of(b, p, q, spot).start()
                if p == 1:
                    run.load_of(p, q, spot).start()
                return 0

            lax.fori_loop(0, lines, begin, 0)

    def hook(group):
        pairs = shapes[conv][0]

        @pl.when(group % pairs == pairs - 1)
        def _():
            dp = group // pairs
            spot, flip_y = dp // 2, (dp % 2 + place.y) % 2
            for x in range(2):
                flip_x = (x + place.x) % 2
                p = flip_y * place.core + flip_x * (1 - place.core)
                q = flip_x * place.core + flip_y * (1 - place.core)
                run.cross_of(conv, p, q, spot).start()

        pl.when(group < 2 * lines)(lambda: run.stage_one(b, group))
        for step in range(lines - 1):
            pl.when(group == 2 * lines + 1 + 2 * step)(lambda step=step: run.line_step(b, 1, step, False))

    back_compute(taps, inputs, made, small_made, rows, scratch, hook)

    def remote(source, target, send, recv, device):
        return run.remote(source, target, send, recv, device)

    def each_other(size, mine, action):
        for other in range(size):
            pl.when(mine != other)(functools.partial(action, other))

    def group_copy(other):
        return remote(
            rows,
            group_box.at[place.group],
            group_send.at[other],
            group_recv.at[place.group],
            (place.dp, other),
        )

    def dp_copy(other):
        return remote(
            dp_box.at[place.dp], dp_box.at[place.dp], dp_send.at[other], dp_recv.at[place.dp], (other, place.group)
        )

    def group_wait(other):
        group_copy(other).wait_send()
        remote(rows, group_box.at[other], group_send.at[other], group_recv.at[other], me).wait_recv()

    def dp_wait(other):
        dp_copy(other).wait_send()
        remote(dp_box.at[other], dp_box.at[other], dp_send.at[other], dp_recv.at[other], me).wait_recv()

    for p in range(2):
        for q in (1, 0):

            def begin_small(spot, _, p=p, q=q):
                run.cross_of(tiny, p, q, spot).start()
                return 0

            lax.fori_loop(0, lines, begin_small, 0)
    group_box[place.group] = rows[...]
    each_other(place.group_size, place.group, lambda other: group_copy(other).start())

    def some(first, last, action):
        def one(index, _):
            action(index)
            return 0

        lax.fori_loop(first, last, one, 0)

    run.line_step(b, 1, 0, True)
    some(0, lines, lambda index: run.stage_one(conv, index))
    run.line_step(b, 1, 1, True)
    some(lines, 2 * lines, lambda index: run.stage_one(conv, index))
    some(2, lines - 1, lambda step: run.line_step(b, 1, step, True))
    some(0, 2 * lines, lambda index: run.stage_one(tiny, index))
    each_other(place.group_size, place.group, group_wait)
    total = group_box[0]
    for other in range(1, place.group_size):
        total = total + group_box[other]
    dp_box[place.dp] = total
    each_other(place.dp_size, place.dp, lambda other: dp_copy(other).start())

    def both_ways(k, a, step):
        run.line_step(k, a, step, False)
        run.line_step(k, a, step, True)

    some(0, 1, lambda step: both_ways(b, 0, step))
    some(0, lines, lambda spot: run.stage_two(conv, spot))
    some(1, lines - 1, lambda step: both_ways(b, 0, step))
    some(0, lines, lambda spot: run.stage_two(tiny, spot))
    run.line_end(b, 1, outs[b])
    crossed[b][0, 1, place.z] = outs[b][...].astype(jnp.bfloat16)
    run.last_out().start()
    some(0, lines - 1, lambda step: both_ways(conv, 0, step))
    some(0, lines - 1, lambda step: both_ways(tiny, 0, step))
    run.line_end(b, 0, outs[b])
    run.last_out().wait_recv()
    outs[b][...] += f32(second_in[b], (0,))
    rows_low[...] = outs[b][...].astype(jnp.bfloat16)

    members, depth = shapes[b][0], shapes[b][1]
    my_rows = pl.ds(pl.multiple_of(place.dp * depth, depth), depth)
    owner_here = (place.dp >= place.core * members) & (place.dp < (place.core + 1) * members)
    owner_there = (place.dp < 2 * members) & jnp.logical_not(owner_here)

    def row_copy(member):
        return remote(
            rows_low.at[member],
            whole_box.at[my_rows],
            row_send.at[member],
            row_recv.at[place.dp],
            (place.core * members + member, place.group),
        )

    def pair_copy(other):
        spot = pl.ds(pl.multiple_of(other * depth, depth), depth)
        return remote(
            whole_box.at[spot], whole_box.at[spot], pair_send.at[other], pair_recv.at[other], run.c_mate
        )

    for member in range(members):

        @pl.when(place.dp != place.core * members + member)
        def _(member=member):
            row_copy(member).start()

        @pl.when(place.dp == place.core * members + member)
        def _(member=member):
            whole_box[my_rows] = rows_low[member]
            pair_copy(place.dp).start()

    for k in run.rest:
        run.line_end(k, 0, outs[k])
    square = jnp.sum(outs[b][...] * outs[b][...])
    for k in run.rest:
        square = square + jnp.sum(outs[k][...] * outs[k][...])
    square_out[...] = jnp.full(square_out.shape, square, jnp.float32)
    each_other(place.dp_size, place.dp, dp_wait)
    total = dp_box[0]
    for other in range(1, place.dp_size):
        total = total + dp_box[other]
    small_out[...] = total

    @pl.when(owner_here)
    def _():
        for other in range(place.dp_size):

            @pl.when(place.dp != other)
            def _(other=other):
                spot = pl.ds(other * depth, depth)
                remote(
                    rows_low.at[0], whole_box.at[spot], row_send.at[0], row_recv.at[other], me
                ).wait_recv()
                pair_copy(other).start()

        for other in range(place.dp_size):
            pair_copy(other).wait_send()

    @pl.when(owner_there)
    def _():
        for other in range(place.dp_size):
            pair_copy(other).wait_recv()

    @pl.when(place.dp < 2 * members)
    def _():
        whole_out[...] = whole_box[...]

    for member in range(members):

        @pl.when(place.dp != place.core * members + member)
        def _(member=member):
            row_copy(member).wait_send()

    run.drain()


def back_reduce(sizes, shapes, taps, operands, block_grad):
    dp_size, group_size = sizes
    lines, count = dp_size // 2, len(KINDS)
    kernel, small, frames = operands[-1], operands[3], operands[0].shape[0]
    low, full = jnp.bfloat16, jnp.float32

    def boxes(lead):
        return [
            pltpu.VMEM(tuple(lead(kind)) + tuple(shape), low) for kind, shape in zip(KINDS, shapes)
        ]

    dma = pltpu.SemaphoreType.DMA
    scratch = (
        [pltpu.VMEM(kernel.shape, low), pltpu.VMEM(small.shape, low), pltpu.VMEM((16, D), full)]
        + back_scratch(kernel.shape, frames)
        + boxes(lambda kind: (2, 2, lines))
        + boxes(lambda kind: (2, lines))
        + boxes(lambda kind: (1,) if kind == "blocks" else (lines,))
        + boxes(lambda kind: (2 if kind == "blocks" else 1, lines + 1))
        + [
            pltpu.VMEM((2, lines) + tuple(shapes[-1]), low),
            pltpu.VMEM((group_size, 16, D), full),
            pltpu.VMEM((dp_size, 16, D), full),
            pltpu.VMEM(shapes[-1], low),
            pltpu.VMEM((D, D), low),
        ]
        + [dma((2, 2, lines))]
        + [dma((count, 2, 2, lines))] * 2
        + [dma((count, 2, lines))] * 2
        + [dma((count, lines))] * 2
        + [dma((count, 2, lines))] * 4
        + [dma((group_size,))] * 2
        + [dma((dp_size,))] * 2
        + [dma((shapes[-1][0],)), dma((dp_size,))]
        + [dma((dp_size,))] * 2
    )
    return pl.pallas_call(
        functools.partial(back_reduce_kernel, sizes, shapes, taps),
        out_shape=[jax.ShapeDtypeStruct(shape, full) for shape in shapes]
        + [
            jax.ShapeDtypeStruct((16, D), full),
            jax.ShapeDtypeStruct((8, 128), full),
            jax.ShapeDtypeStruct((D, D), low),
        ],
        in_specs=[VMEM] * (BACK_INPUTS - 1) + [HBM, HBM],
        out_specs=[VMEM] * (count + 3),
        scratch_shapes=scratch,
        name="back_reduce",
        compiler_params=pltpu.CompilerParams(
            collective_id=1, has_side_effects=True, vmem_limit_bytes=VMEM_LIMIT
        ),
    )(*operands, block_grad)


def roots_kernel(sizes, members, *refs):
    (
        whole, stat, square_in, extra_in, sides_out, update_out, square_out,
        big, low, m0, m0b, m1, m1b, s1, s1b, s2b, s3, s3b, root, mixed,
        group_box, dp_box, group_send, group_recv, dp_send, dp_recv,
        side_send, side_recv, side_own, mixed_send, mixed_recv, update_send, update_recv, update_own,
    ) = refs
    place = Place(*sizes)
    dp_size, rows = place.dp_size, D // place.dp_size
    me, c_mate = (place.dp, place.group), place.at(place.z, 0, 0, 1)
    owner = place.dp < 2 * members
    owned_group = place.x * 2 + place.dp // members
    owned_member = place.dp % members
    tile = 256
    greet(place)

    def remote(source, target, send, recv, device):
        return pltpu.make_async_remote_copy(
            src_ref=source,
            dst_ref=target,
            send_sem=send,
            recv_sem=recv,
            device_id=device,
            device_id_type=MESH,
        )

    def each_other(size, mine, action):
        for other in range(size):
            pl.when(mine != other)(functools.partial(action, other))

    def group_copy(other, slot):
        return remote(
            group_box.at[slot], group_box.at[slot], group_send.at[other], group_recv.at[slot], (place.dp, other)
        )

    def dp_copy(other, slot):
        return remote(dp_box.at[slot], dp_box.at[slot], dp_send.at[other], dp_recv.at[slot], (other, place.group))

    group_box[place.group] = square_in[...]
    each_other(place.group_size, place.group, lambda other: group_copy(other, place.group).start())

    def product_rows(one, two, then):
        def step(index, _):
            at = pl.ds(pl.multiple_of(index * tile, tile), tile)
            then(at, jnp.dot(one[at, :], two[...], preferred_element_type=jnp.float32))
            return 0

        lax.fori_loop(0, D // tile, step, 0)

    def side_copy(other):
        spot = pl.ds(pl.multiple_of(other * rows, rows), rows)
        return remote(
            low.at[spot],
            sides_out.at[owned_member, place.core],
            side_send.at[other],
            side_recv.at[owned_member, place.core],
            (other, owned_group),
        )

    def side_local():
        spot = pl.ds(pl.multiple_of(place.dp * rows, rows), rows)
        return pltpu.make_async_copy(low.at[spot], sides_out.at[owned_member, place.core], side_own)

    mine = place.group == owned_group

    def to_rows(other, remote_action, local_action):
        away = (place.dp != other) | jnp.logical_not(mine)
        pl.when(away)(functools.partial(remote_action, other))
        pl.when(jnp.logical_not(away))(local_action)

    @pl.when(owner)
    def _():
        @pl.when(place.core == 0)
        def _():
            def step(index, _):
                at = pl.ds(pl.multiple_of(index * tile, tile), tile)
                value = lax.dot_general(
                    whole[at, :],
                    whole[...],
                    (((1,), (1,)), ((), ())),
                    preferred_element_type=jnp.float32,
                )
                big[at, :] = value
                low[at, :] = value.astype(jnp.bfloat16)
                return 0

            lax.fori_loop(0, D // tile, step, 0)

        @pl.when(place.core == 1)
        def _():
            s1b[...] = whole[...].T

            def keep(at, value):
                big[at, :] = value
                low[at, :] = value.astype(jnp.bfloat16)

            product_rows(s1b, whole, keep)

        for other in range(dp_size):
            to_rows(other, lambda other: side_copy(other).start(), lambda: side_local().start())

    def group_wait(other):
        group_copy(other, place.group).wait_send()
        group_copy(other, other).wait_recv()

    each_other(place.group_size, place.group, group_wait)
    total = group_box[0]
    for other in range(1, place.group_size):
        total = total + group_box[other]
    dp_box[place.dp] = total
    each_other(dp_size, place.dp, lambda other: dp_copy(other, place.dp).start())

    def dp_wait(other):
        dp_copy(other, place.dp).wait_send()
        dp_copy(other, other).wait_recv()

    each_other(dp_size, place.dp, dp_wait)
    total = dp_box[0]
    for other in range(1, dp_size):
        total = total + dp_box[other]
    total = total + extra_in[...]
    square_out[...] = total

    @pl.when(owner)
    def _():
        factor = jnp.minimum(1.0, max_norm / (jnp.sqrt(total[0:1, 0:1]) + 1e-06))
        square_factor = factor * factor
        spread_f = (1 - stat_decay) * square_factor

        def diagonal(at_start, shape):
            row = lax.broadcasted_iota(jnp.int32, shape, 0) + at_start
            return row == lax.broadcasted_iota(jnp.int32, shape, 1)

        def each_tile(action, carry):
            def step(index, carry):
                start = pl.multiple_of(index * tile, tile)
                return action(pl.ds(start, tile), start, carry)

            return lax.fori_loop(0, D // tile, step, carry)

        def renew(at, start, trace):
            value = stat_decay * stat[at, :].astype(jnp.float32) + spread_f * big[at, :]
            big[at, :] = value
            on = jnp.where(diagonal(start, value.shape), value, 0.0)
            return trace + jnp.sum(jnp.sum(on, 1, keepdims=True), 0, keepdims=True)

        trace = each_tile(renew, jnp.zeros((1, 1), jnp.float32))
        damping = 0.0001 * (trace / D)

        def damp(at, start, total):
            value = big[at, :]
            value = value + jnp.where(diagonal(start, value.shape), damping, 0.0)
            big[at, :] = value
            return total + jnp.sum(jnp.sum(value * value, 1, keepdims=True), 0, keepdims=True)

        magnitude = jnp.sqrt(each_tile(damp, jnp.zeros((1, 1), jnp.float32)))

        def scale(at, start, carry):
            value = big[at, :] / magnitude
            m0[at, :] = value
            m0b[at, :] = value.astype(jnp.bfloat16)
            return carry

        each_tile(scale, 0)
        a = 1.5625

        def square_of(source):
            def then(at, value):
                value = value * 0.0625 - 0.625 * source[at, :]
                s1[at, :] = value
                s1b[at, :] = value.astype(jnp.bfloat16)

            return then

        def fourth(at, value):
            s2b[at, :] = (value + (2 * a) * s1[at, :]).astype(jnp.bfloat16)

        product_rows(m0b, m0b, square_of(m0))
        product_rows(s1b, s1b, fourth)

        def next_one(at, value):
            value = value + (a * a) * m0[at, :]
            m1[at, :] = value
            m1b[at, :] = value.astype(jnp.bfloat16)

        product_rows(s2b, m0b, next_one)

        def joined(at, value):
            value = value * 0.0625 - 0.3125 * (m0[at, :] + m1[at, :])
            s3[at, :] = value
            s3b[at, :] = value.astype(jnp.bfloat16)

        product_rows(m0b, m1b, joined)
        product_rows(m1b, m1b, square_of(m1))
        product_rows(s1b, s1b, fourth)

        def next_two(at, value):
            value = value + (a * a) * m1[at, :]
            m0[at, :] = value
            m0b[at, :] = value.astype(jnp.bfloat16)

        product_rows(s2b, m1b, next_two)
        outer = lax.rsqrt(jnp.sqrt(magnitude))

        def final(at, value):
            value = 1.25 * s3[at, :] - (0.25 * a) * m0[at, :] - 0.25 * value
            start = at.start
            value = value + jnp.where(diagonal(start, value.shape), 1.25 * a, 0.0)
            root[at, :] = (value * outer).astype(jnp.bfloat16)

        product_rows(s3b, m0b, final)

    def mixed_copy():
        return remote(mixed, mixed, mixed_send, mixed_recv, c_mate)

    def update_copy(other):
        spot = pl.ds(pl.multiple_of(other * rows, rows), rows)
        return remote(
            m1b.at[spot],
            update_out.at[owned_member],
            update_send.at[other],
            update_recv.at[owned_member],
            (other, owned_group),
        )

    def update_local():
        spot = pl.ds(pl.multiple_of(place.dp * rows, rows), rows)
        return pltpu.make_async_copy(m1b.at[spot], update_out.at[owned_member], update_own)

    @pl.when(owner & (place.core == 0))
    def _():
        def keep(at, value):
            mixed[at, :] = value.astype(jnp.bfloat16)

        product_rows(root, whole, keep)
        mixed_copy().start()
        mixed_copy().wait_send()

    @pl.when(owner & (place.core == 1))
    def _():
        mixed_copy().wait_recv()

        def keep(at, value):
            m1b[at, :] = value.astype(jnp.bfloat16)

        product_rows(mixed, root, keep)
        for other in range(dp_size):
            to_rows(other, lambda other: update_copy(other).start(), lambda: update_local().start())
        for other in range(dp_size):
            to_rows(other, lambda other: update_copy(other).wait_send(), lambda: update_local().wait())

    @pl.when(owner)
    def _():
        for other in range(dp_size):
            to_rows(other, lambda other: side_copy(other).wait_send(), lambda: side_local().wait())

    for member in range(members):
        holder = place.core * members + member
        for side in range(2):

            @pl.when((place.dp != holder) | (place.core != side))
            def _(member=member, side=side):
                remote(
                    low.at[pl.ds(0, rows)],
                    sides_out.at[member, side],
                    side_send.at[0],
                    side_recv.at[member, side],
                    me,
                ).wait_recv()

        @pl.when((place.dp != holder) | (place.core != 1))
        def _(member=member):
            remote(
                m1b.at[pl.ds(0, rows)],
                update_out.at[member],
                update_send.at[0],
                update_recv.at[member],
                me,
            ).wait_recv()


def shampoo_roots(sizes, members, whole, stat, square, extra):
    dp_size, group_size = sizes
    rows = D // dp_size
    low, full = jnp.bfloat16, jnp.float32
    dma = pltpu.SemaphoreType.DMA
    half, word = pltpu.VMEM((D, D), low), pltpu.VMEM((D, D), full)
    return pl.pallas_call(
        functools.partial(roots_kernel, sizes, members),
        out_shape=[
            jax.ShapeDtypeStruct((members, 2, rows, D), low),
            jax.ShapeDtypeStruct((members, rows, D), low),
            jax.ShapeDtypeStruct((8, 128), full),
        ],
        in_specs=[VMEM] * 4,
        out_specs=[VMEM] * 3,
        scratch_shapes=[word, half, word, half, word, half, word, half, half, word, half, half, half]
        + [pltpu.VMEM((group_size, 8, 128), full), pltpu.VMEM((dp_size, 8, 128), full)]
        + [dma((group_size,))] * 2
        + [dma((dp_size,))] * 2
        + [dma((dp_size,)), dma((members, 2)), dma]
        + [dma, dma]
        + [dma((dp_size,)), dma((members,)), dma],
        name="shampoo_roots",
        compiler_params=pltpu.CompilerParams(
            collective_id=2, has_side_effects=True, vmem_limit_bytes=VMEM_LIMIT
        ),
    )(whole, stat, square, extra)


def conv_to_shard(weight):
    taps, c, channels = weight.shape
    split = weight.reshape(taps // STRIDE, STRIDE, c, channels // c, c)
    return split.transpose(3, 1, 4, 0, 2).reshape(channels // c, STRIDE * c, taps // STRIDE * c)


def conv_from_shard(shard):
    groups, rows, columns = shard.shape
    c = rows // STRIDE
    split = shard.reshape(groups, STRIDE, c, columns // c, c)
    return split.transpose(3, 1, 4, 0, 2).reshape(columns // c * STRIDE, c, groups * c)


def pack_small(projection, head, clusters, note):
    lead, kind = projection.shape[:-2], projection.dtype
    notes = jnp.broadcast_to(note, lead + (32, 2)).astype(kind)
    return jnp.concatenate(
        [
            projection[..., :128],
            jnp.concatenate([projection[..., 128:], jnp.zeros(lead + (64, 64), kind)], -1),
            jnp.concatenate([head, jnp.zeros(lead + (96, 64), kind)], -1),
            jnp.concatenate([jnp.swapaxes(clusters, -1, -2), notes], -1),
        ],
        -2,
    )


def unpack_small(packed):
    projection = jnp.concatenate([packed[..., :64, :], packed[..., 64:128, :64]], -1)
    head = packed[..., 128:224, :64]
    clusters = jnp.swapaxes(packed[..., 224:, :CLUSTER_ROWS], -1, -2)
    return projection, head, clusters


def pack_whole(projection, head, clusters, note):
    def cut(values, down, across):
        rows, columns = values.shape
        return values.reshape(down, rows // down, across, columns // across).transpose(0, 2, 1, 3)

    return pack_small(
        cut(projection, 8, 4), cut(head, 8, 4), cut(clusters, 4, 8).transpose(1, 0, 2, 3), note
    )


def unpack_whole(packed):
    def join(values):
        down, across, rows, columns = values.shape
        return values.transpose(0, 2, 1, 3).reshape(down * rows, across * columns)

    projection, head, clusters = unpack_small(packed)
    return join(projection), join(head), join(clusters.transpose(1, 0, 2, 3))


def parts_of_rows(rows, vector_rows, width):
    return rows[:vector_rows], rows[vector_rows + 1 : vector_rows + 3, :width], rows[vector_rows, 0]


CLUSTER_ROWS = 126
SMALL = ((64, 192), (96, 64), (CLUSTER_ROWS, 32))


def body(
    sizes,
    features,
    span_starts,
    labels,
    feature_norm,
    feature_first,
    feature_second,
    projection,
    projection_first,
    projection_second,
    vectors,
    vector_first,
    vector_second,
    conv_weight,
    conv_first,
    conv_second,
    head,
    head_first,
    head_second,
    clusters,
    cluster_first,
    cluster_second,
    blocks,
    statistics,
):
    dp_size, group_size = sizes
    members, rows = blocks.shape[0], blocks.shape[1]
    masks = jax.vmap(jax.vmap(frame_mask))(span_starts)
    local_count = jnp.sum(masks)
    fast = (
        rows % 16 == 0
        and dp_size % 2 == 0
        and group_size == 4
        and dp_size >= 2 * members
        and (projection.shape, head.shape, clusters.shape) == SMALL
        and conv_weight.shape[2] % conv_weight.shape[1] == 0
        and masks.size <= 256
    )
    if fast:
        pieces = (
            conv_to_shard(to_low(conv_weight)),
            pack_small(to_low(projection), to_low(head), to_low(clusters), to_low(local_count)),
            to_low(blocks),
        )
        shapes = [piece.shape for piece in pieces]
        kernel_w, small_w, blocks_w, stat_whole = gather_weights(sizes, pieces, to_low(statistics))
    else:
        proj_w, kernel_full, head_w, clusters_w, blocks_w = gather_plain(
            projection, conv_weight, head, clusters, blocks
        )
        whole = conv_to_shard(kernel_full)
        kernel_w = whole.reshape(whole.shape[:2] + (4, -1)).transpose(2, 0, 1, 3)
        count = lax.psum(local_count, ("dp", "group"))
        high = jnp.floor(count / 256.0) * 256.0
        notes = jnp.concatenate([jnp.stack([high, count - high]), jnp.zeros(30, jnp.float32)])
        small_w = pack_whole(proj_w, head_w, clusters_w, notes.reshape(8, 4, 1, 1))
    frames = features.shape[0] * features.shape[1] * CLIP
    taps = kernel_w.shape[0] * kernel_w.shape[3] // (D // kernel_w.shape[1]) * STRIDE
    mask = masks.reshape(frames, 1)
    saved = front(
        features.reshape(frames, -1), mask, feature_norm, vectors, small_w, kernel_w, taps
    )
    feature_unit, normed, hidden_t, encoded, encoder_unit, encoder_inverse, slope = saved
    targets = labels.reshape(frames, 1)
    encoded_grad, block_part, head_part, center_part, trunk_rows, counted = trunk(
        encoded, mask, targets + targets // CLUSTER_ROWS * 2, vectors, small_w, blocks_w
    )
    masked_count = counted[0, 0]
    operands = (
        encoded_grad, mask, vectors, small_w, feature_unit, normed, hidden_t,
        encoder_unit, encoder_inverse, slope, trunk_rows, head_part, center_part, kernel_w,
    )
    vector_rows, width = vectors.shape[0], feature_norm.shape[1]
    if fast:
        kernel_sum, small_sum, block_sum, extra, square, whole = back_reduce(
            sizes, shapes, taps, operands, block_part
        )
        vector_grad, feature_grad, loss_sum = parts_of_rows(extra, vector_rows, width)
        proj_sum, head_sum, cluster_sum = unpack_small(small_sum)
        large_total = (proj_sum, conv_from_shard(kernel_sum), head_sum, cluster_sum, block_sum)
        replicated = jnp.sum(feature_grad * feature_grad) + jnp.sum(vector_grad * vector_grad)
        sides, update_rows, square = shampoo_roots(
            sizes, members, whole, stat_whole, square, jnp.full((8, 128), replicated)
        )
        norm_square = square[0, 0]
    else:
        kernel_part, small_part, row_part = back(taps, operands)
        proj_part, head_part, center_part = unpack_whole(small_part)
        kernel_plain = conv_from_shard(
            kernel_part.transpose(1, 2, 0, 3).reshape(kernel_part.shape[1:3] + (-1,))
        )
        large_total = reduce_grads(
            tuple(
                part.astype(jnp.float32)
                for part in (proj_part, kernel_plain, head_part, center_part, block_part)
            )
        )
        vector_grad, feature_grad, loss_sum = parts_of_rows(
            lax.psum(row_part, ("dp", "group")), vector_rows, width
        )
        local_squares = sum((jnp.sum(part * part) for part in large_total))
        norm_square = (
            lax.psum(local_squares, ("dp", "group"))
            + jnp.sum(feature_grad * feature_grad)
            + jnp.sum(vector_grad * vector_grad)
        )
    grad_norm = jnp.sqrt(norm_square)
    factor = jnp.minimum(1.0, max_norm / (grad_norm + 1e-06))
    proj_grad, kernel_grad, head_grad, cluster_grad, block_rows = [
        part * factor for part in large_total
    ]
    feature_out = adamw(
        feature_norm, feature_grad * factor, feature_first, feature_second, rate_vector, 0.0
    )
    projection_out = adamw(
        projection, proj_grad, projection_first, projection_second, rate_matrix, decay_weight
    )
    vector_out = adamw(vectors, vector_grad * factor, vector_first, vector_second, rate_vector, 0.0)
    conv_out = adamw(conv_weight, kernel_grad, conv_first, conv_second, rate_matrix, decay_weight)
    head_out = adamw(head, head_grad, head_first, head_second, rate_matrix, decay_weight)
    cluster_out = adamw(
        clusters, cluster_grad, cluster_first, cluster_second, rate_matrix, decay_weight
    )
    if fast:
        statistics_new = stat_decay * statistics + (1 - stat_decay) * factor * factor * sides.astype(
            jnp.float32
        )
        update_rows = update_rows.astype(jnp.float32) * factor
    else:
        statistics_new, update_rows = shampoo_plain(block_rows, statistics)
    blocks_new = blocks - rate_shampoo * (update_rows + decay_weight * blocks)
    return (
        loss_sum,
        masked_count,
        grad_norm,
        *feature_out,
        *projection_out,
        *vector_out,
        *conv_out,
        *head_out,
        *cluster_out,
        block_rows,
        statistics_new,
        blocks_new,
    )


def solution(mesh):
    in_specs = (
        P(None, ("dp", "group"), None, None),
        P(None, ("dp", "group"), None),
        P(None, ("dp", "group"), None),
        P(),
        P(),
        P(),
        P("dp", "group"),
        P("dp", "group"),
        P("dp", "group"),
        P(),
        P(),
        P(),
        P("group", None, "dp"),
        P("group", None, "dp"),
        P("group", None, "dp"),
        P("dp", "group"),
        P("dp", "group"),
        P("dp", "group"),
        P("group", "dp"),
        P("group", "dp"),
        P("group", "dp"),
        P("group", "dp", None),
        P("group", None, "dp", None),
    )
    out_specs = (
        P(),
        P(),
        P(),
        P(),
        P(),
        P(),
        P("dp", "group"),
        P("dp", "group"),
        P("dp", "group"),
        P(),
        P(),
        P(),
        P("group", None, "dp"),
        P("group", None, "dp"),
        P("group", None, "dp"),
        P("dp", "group"),
        P("dp", "group"),
        P("dp", "group"),
        P("group", "dp"),
        P("group", "dp"),
        P("group", "dp"),
        P("group", "dp", None),
        P("group", None, "dp", None),
        P("group", "dp", None),
    )
    return jax.shard_map(
        functools.partial(body, (mesh.shape["dp"], mesh.shape["group"])), mesh=mesh, in_specs=in_specs, out_specs=out_specs, check_vma=False)
```

```python
import functools

import jax
import jax.numpy as jnp
from jax import lax
from jax.experimental import pallas as pl
from jax.experimental.pallas import tpu as pltpu
from jax.sharding import PartitionSpec as P

D = 768
HEADS = 12
HEAD = 64
TAPS = 128
CLIP = 128
SPAN = 10
NEWTON = 3
STEP = 10


HIGH = lax.Precision.HIGHEST
beta_one = 0.9
beta_two = 0.98
adam_eps = 1e-08
rate_matrix = 0.02
rate_vector = 0.5
rate_shampoo = 0.2
decay_weight = 0.01
stat_decay = 0.95
max_norm = 0.01
inv_temp = 10.0
STRIDE = 4


def for_sending(array):

    def short(part):
        return part.astype(jnp.bfloat16) if part.dtype == jnp.float32 else part

    return jax.tree.map(short, array)


def spread_2(array, axis, root):
    mine = lax.axis_index(axis) == root
    return lax.psum(jnp.where(mine, array, jnp.zeros_like(array)), axis)


def to_low(values):
    return values.astype(jnp.bfloat16)


def frame_mask(starts):
    frames = jnp.arange(CLIP, dtype=jnp.int32)[:, None]
    inside = (frames >= starts[None, :]) & (frames < starts[None, :] + SPAN)
    return jnp.any(inside, axis=1).astype(jnp.float32)


def inverse_root(matrix):
    size = matrix.shape[0]
    identity = jnp.eye(size, dtype=jnp.float32)
    damped = matrix + 0.0001 * (jnp.trace(matrix) / size) * identity
    magnitude = jnp.sqrt(jnp.sum(damped * damped))
    current = damped / magnitude
    result = identity * magnitude ** (-0.25)
    for sweep in range(NEWTON):
        factor = (5.0 * identity - current) * 0.25
        result = jnp.dot(result, factor, precision=HIGH)
        square = jnp.dot(factor, factor, precision=HIGH)
        current = jnp.dot(jnp.dot(square, square, precision=HIGH), current, precision=HIGH)
    return result


def adamw(weight, grad, first, second, rate, decay):
    first = beta_one * first + (1 - beta_one) * grad
    second = beta_two * second + (1 - beta_two) * grad * grad
    corrected = first / (1 - beta_one**STEP)
    scaled = jnp.sqrt(second / (1 - beta_two**STEP)) + adam_eps
    return (first, second, weight - rate * (corrected / scaled + decay * weight))


def reduce_grads(parts):
    proj_part, kernel_part, head_part, center_part, block_part = parts
    grouped = (
        lax.psum_scatter(proj_part, "group", scatter_dimension=1, tiled=True),
        lax.psum_scatter(kernel_part, "group", scatter_dimension=0, tiled=True),
        lax.psum_scatter(head_part, "group", scatter_dimension=1, tiled=True),
        lax.psum_scatter(center_part, "group", scatter_dimension=0, tiled=True),
        lax.psum_scatter(block_part, "group", scatter_dimension=0, tiled=True),
    )
    proj_part, kernel_part, head_part, center_part, block_part = grouped
    return (
        lax.psum_scatter(proj_part, "dp", scatter_dimension=0, tiled=True),
        lax.psum_scatter(kernel_part, "dp", scatter_dimension=2, tiled=True),
        lax.psum_scatter(head_part, "dp", scatter_dimension=0, tiled=True),
        lax.psum_scatter(center_part, "dp", scatter_dimension=1, tiled=True),
        lax.psum_scatter(block_part, "dp", scatter_dimension=1, tiled=True),
    )


def gather_plain(projection, conv_weight, head, clusters, blocks):
    gathered = (
        lax.all_gather(to_low(projection), "dp", axis=0, tiled=True),
        lax.all_gather(to_low(conv_weight), "dp", axis=2, tiled=True),
        lax.all_gather(to_low(head), "dp", axis=0, tiled=True),
        lax.all_gather(to_low(clusters), "dp", axis=1, tiled=True),
        lax.all_gather(to_low(blocks), "dp", axis=1, tiled=True),
    )
    proj_part, kernel_part, head_part, center_part, block_part = gathered
    return (
        lax.all_gather(proj_part, "group", axis=1, tiled=True),
        lax.all_gather(kernel_part, "group", axis=0, tiled=True),
        lax.all_gather(head_part, "group", axis=1, tiled=True),
        lax.all_gather(center_part, "group", axis=0, tiled=True),
        lax.all_gather(block_part, "group", axis=0, tiled=True),
    )


def shampoo_plain(block_rows, statistics):
    full_blocks = lax.all_gather(block_rows.astype(jnp.bfloat16), "dp", axis=1, tiled=True).astype(
        block_rows.dtype
    )
    rows = block_rows.shape[1]
    here = lax.axis_index("dp")
    first_row = here * rows
    column_slice = lax.dynamic_slice_in_dim(full_blocks, first_row, rows, 2)
    left_rows = stat_decay * statistics[:, 0] + (1 - stat_decay) * jnp.einsum(
        "brk,bck->brc", block_rows, full_blocks, precision=HIGH
    )
    right_rows = stat_decay * statistics[:, 1] + (1 - stat_decay) * jnp.einsum(
        "bkr,bkc->brc", column_slice, full_blocks, precision=HIGH
    )
    group_blocks = block_rows.shape[0]
    dp_size = lax.axis_size("dp")
    owners = [
        (2 * member + side) * dp_size // (2 * group_blocks)
        for member in range(group_blocks)
        for side in range(2)
    ]
    left_full, right_full = (
        lax.all_gather(left_rows.astype(jnp.bfloat16), "dp", axis=1, tiled=True).astype(
            left_rows.dtype
        ),
        lax.all_gather(right_rows.astype(jnp.bfloat16), "dp", axis=1, tiled=True).astype(
            right_rows.dtype
        ),
    )
    sources = [
        left_full[member] if side == 0 else right_full[member]
        for member in range(group_blocks)
        for side in range(2)
    ]
    roots = []
    for index in range(2 * group_blocks):
        owner = owners[index]
        root = lax.cond(here == owner, inverse_root, jnp.zeros_like, sources[index])
        root = spread_2(for_sending(root), "dp", owner).astype(root.dtype)
        roots.append(root)
    stacked = jnp.stack(roots).reshape(group_blocks, 2, D, D)
    left_root_rows = lax.dynamic_slice_in_dim(stacked[:, 0], first_row, rows, 1)
    update_rows = jnp.einsum(
        "brk,bkc->brc",
        jnp.einsum("brk,bkc->brc", left_root_rows, full_blocks, precision=HIGH),
        stacked[:, 1],
        precision=HIGH,
    )
    return jnp.stack([left_rows, right_rows], 1), update_rows


MESH = pl.DeviceIdType.MESH
HBM = pl.BlockSpec(memory_space=pltpu.HBM)
VMEM = pl.BlockSpec(memory_space=pltpu.VMEM)
VMEM_LIMIT = 60 * 1024 * 1024


class Place:
    def __init__(self, dp_size, group_size):
        self.dp_size, self.group_size = dp_size, group_size
        self.lines = dp_size // 2
        self.dp, self.group = lax.axis_index("dp"), lax.axis_index("group")
        self.z, self.y = self.dp // 2, self.dp % 2
        self.x, self.core = self.group // 2, self.group % 2

    def at(self, z, flip_y=0, flip_x=0, flip_core=0):
        y = self.y + flip_y * (1 - 2 * self.y)
        x = self.x + flip_x * (1 - 2 * self.x)
        core = self.core + flip_core * (1 - 2 * self.core)
        return (z * 2 + y, x * 2 + core)

    def near(self, z, p, q):
        return self.at(z, p * (1 - self.core) + q * self.core, q * (1 - self.core) + p * self.core)

    def across(self, z, p, q):
        return self.at(z, p * self.core + q * (1 - self.core), q * self.core + p * (1 - self.core), 1)


def greet(place):
    barrier = pltpu.get_barrier_semaphore()
    first = place.x * 2
    for other in range(place.dp_size):
        for core in range(2):

            @pl.when((place.dp != other) | (place.core != core))
            def _():
                pl.semaphore_signal(
                    barrier, inc=1, device_id=(other, first + core), device_id_type=MESH
                )

    for core in range(2):
        pl.semaphore_signal(
            barrier,
            inc=1,
            device_id=(place.dp, (1 - place.x) * 2 + core),
            device_id_type=MESH,
        )
    pl.semaphore_wait(barrier, 2 * place.dp_size - 1 + 2)


def guarded(condition, action):
    if condition is None:
        action()
    else:
        pl.when(condition)(action)


def both(one, two):
    if one is None:
        return two
    if two is None:
        return one
    return one & two


def piece_at(kind, ref, dp, group, shape):
    if kind == "blocks":
        start = pl.multiple_of(dp * shape[1], shape[1])
        return ref.at[pl.ds(group * shape[0], shape[0]), pl.ds(start, shape[1])]
    if kind == "conv":
        return ref.at[group, pl.ds(dp * shape[0], shape[0])]
    return ref.at[dp, group]


KINDS = ("conv", "small", "blocks")


def make_shards(refs, mask, conv, small, blocks_low, stats_low):
    starts, projection, weight, head_t, clusters_t, blocks, statistics = refs
    for clip in range(starts.shape[0]):
        frame = lax.broadcasted_iota(jnp.int32, (CLIP, starts.shape[1]), 0)
        begins = starts[clip : clip + 1, :]
        inside = ((frame >= begins) & (frame < begins + SPAN)).astype(jnp.float32)
        mask[clip * CLIP : (clip + 1) * CLIP, :] = jnp.max(inside, 1, keepdims=True)
    note = jnp.sum(mask[...], 0, keepdims=True)
    runs, steps, c, channels = weight.shape
    for offset in range(steps):
        turned = weight[:, offset].reshape(runs * c, channels).T.astype(jnp.bfloat16)
        for group in range(channels // c):
            conv[group, offset * c : (offset + 1) * c, :] = turned[group * c : (group + 1) * c]
    low = jnp.bfloat16

    def padded(values):
        spare = jnp.zeros((values.shape[0], 128 - values.shape[1]), jnp.float32)
        return jnp.concatenate([values, spare], 1)

    small[0:64, :] = projection[:, 0:128].astype(low)
    small[64:128, :] = padded(projection[:, 128:]).astype(low)
    small[128:224, :] = padded(head_t[...].T).astype(low)
    lane = lax.broadcasted_iota(jnp.int32, (32, 128), 1)
    small[224:256, :] = jnp.where(lane < CLUSTER_ROWS, padded(clusters_t[...]), note).astype(low)
    blocks_low[...] = blocks[...].astype(low)
    stats_low[...] = statistics[...].astype(low)


def gather_kernel(sizes, shapes, taps, *refs):
    place = Place(*sizes)
    count = len(KINDS)
    refs = list(refs)

    def pull(number):
        taken = refs[:number]
        del refs[:number]
        return taken

    raw, (features, feature_norm, vectors) = pull(7), pull(3)
    outs, (stats_out,), results, (mask,) = pull(count), pull(1), pull(7), pull(1)
    ins, (stats_in, small_here), scratch = pull(count), pull(2), pull(5)
    (send_sem, recv_sem, own_sem, stat_send, stat_recv, stat_own, small_sem) = pull(7)
    z, last = place.z, place.lines - 1
    me = (place.dp, place.group)
    make_shards(raw, mask, *ins, stats_in)
    greet(place)
    sent = []
    slots = [0] * count
    conv, tiny = KINDS.index("conv"), KINDS.index("small")
    enter, project, convolve, leave = front_compute(
        taps,
        (features, mask, feature_norm, vectors, small_here, outs[conv]),
        results,
        scratch,
    )

    def view(k, source):
        return piece_at(KINDS[k], outs[k], source[0], source[1], shapes[k])

    def identity(source):
        return source[0] * place.group_size + source[1]

    def copy_of(k, source, target, slot, own=False):
        spot = view(k, source)
        return pltpu.make_async_remote_copy(
            src_ref=ins[k] if own else spot,
            dst_ref=spot,
            send_sem=send_sem.at[k, slot],
            recv_sem=recv_sem.at[k, identity(source)],
            device_id=target,
            device_id_type=MESH,
        )

    def send(k, source, target, condition=None, own=False):
        slot = slots[k]
        slots[k] += 1
        guarded(condition, lambda: copy_of(k, source, target, slot, own).start())
        sent.append((k, source, target, slot, condition, own))

    def arrive(k, source, condition=None):
        guarded(condition, lambda: copy_of(k, source, me, 0).wait_recv())

    links = {
        "left": (place.at(z - 1), z > 0),
        "right": (place.at(z + 1), z < last),
        "p": (place.near(z, 1, 0), None),
        "q": (place.near(z, 0, 1), None),
        "core": (place.at(z, 0, 0, 1), None),
    }

    def forward(k, source, ways, condition=None, own=False):
        for way in ways:
            target, open_way = links[way]
            send(k, source, target, both(condition, open_way), own)

    def spots(offset):
        if offset == 0:
            return [(z, None, ("left", "right"))]
        return [
            (z - offset, z >= offset, ("right",)),
            (z + offset, z + offset <= last, ("left",)),
        ]

    def take(k, source, condition, ways):
        arrive(k, source, condition)
        forward(k, source, ways, condition)

    def step_z_first(k, step):
        if step == 0:
            forward(k, me, ("left", "right", "q", "p", "core"), own=True)
            return
        if step < place.lines:
            for spot, there, ways in spots(step):
                take(k, place.near(spot, 0, 0), there, ways + ("q", "p", "core"))
        if 0 <= step - 1 < place.lines:
            for spot, there, _ in spots(step - 1):
                take(k, place.near(spot, 1, 0), there, ("q", "core"))
                take(k, place.near(spot, 0, 1), there, ("core",))
        if 0 <= step - 2 < place.lines:
            for spot, there, _ in spots(step - 2):
                take(k, place.near(spot, 1, 1), there, ("core",))

    def step_z_second(k, step):
        if step == 0:
            forward(k, me, ("q", "left", "right", "p", "core"), own=True)
            return
        if step == 1:
            take(k, place.near(z, 0, 1), None, ("left", "right", "p", "core"))
        if step < place.lines:
            for spot, there, ways in spots(step):
                take(k, place.near(spot, 0, 0), there, ways + ("p", "core"))
        if 1 <= step - 1 < place.lines:
            for spot, there, ways in spots(step - 1):
                take(k, place.near(spot, 0, 1), there, ways + ("p", "core"))
        if 0 <= step - 1 < place.lines:
            for spot, there, _ in spots(step - 1):
                take(k, place.near(spot, 1, 0), there, ("core",))
        if 0 <= step - 2 < place.lines:
            for spot, there, _ in spots(step - 2):
                take(k, place.near(spot, 1, 1), there, ("core",))

    members = shapes[KINDS.index("blocks")][0]
    rows = shapes[KINDS.index("blocks")][1]

    owners = Owners(place, members)

    def stat_copy(member, side):
        owner = owners.of(member)
        start = pl.multiple_of(place.dp * rows, rows)
        return owner, pltpu.make_async_remote_copy(
            src_ref=stats_in.at[member, side],
            dst_ref=stats_out.at[pl.ds(start, rows)],
            send_sem=stat_send.at[member, side],
            recv_sem=stat_recv.at[place.dp],
            device_id=(owner, place.x * 2 + side),
            device_id_type=MESH,
        )

    def stat_local(member, side):
        start = pl.multiple_of(place.dp * rows, rows)
        return pltpu.make_async_copy(
            stats_in.at[member, side], stats_out.at[pl.ds(start, rows)], stat_own
        )

    def each_stat(remote, local):
        for member in range(members):
            for side in range(2):
                owner = owners.of(member)
                mine = (place.dp == owner) & (place.core == side)
                pl.when(jnp.logical_not(mine))(lambda m=member, s=side: remote(m, s))
                pl.when(mine)(lambda m=member, s=side: local(m, s))

    own_copies = [
        pltpu.make_async_copy(ins[k], view(k, me), own_sem.at[k]) for k in range(count)
    ]
    def from_core(k):
        for spot in range(place.lines):
            for p in range(2):
                for q in range(2):
                    arrive(k, place.across(spot, p, q))

    def read_small():
        copy = pltpu.make_async_copy(outs[tiny], small_here, small_sem)
        copy.start()
        copy.wait()

    def compute(part):
        groups = outs[conv].shape[1]
        if part == 0:
            read_small()
            project()
        elif part < 4:
            convolve(groups * (part - 1) // 3, groups * part // 3)
        else:
            leave()

    for name, kind, step in GATHER_PLAN:
        if name == "step":
            k = KINDS.index(kind)
            (step_z_second if kind == "blocks" else step_z_first)(k, step)
            if step == 0:
                own_copies[k].start()
        elif name == "stats":
            each_stat(
                lambda m, s: stat_copy(m, s)[1].start(), lambda m, s: stat_local(m, s).start()
            )
        elif name == "core":
            from_core(KINDS.index(kind))
            own_copies[KINDS.index(kind)].wait()
        elif name == "enter":
            enter()
        else:
            compute(step)
    from_core(KINDS.index("blocks"))
    own_copies[KINDS.index("blocks")].wait()
    each_stat(lambda m, s: stat_copy(m, s)[1].wait_send(), lambda m, s: stat_local(m, s).wait())

    @pl.when(owners.here)
    def _():
        for other in range(place.dp_size):

            @pl.when((place.dp != other) | (place.group != owners.group))
            def _():
                pltpu.make_async_remote_copy(
                    src_ref=stats_in.at[0, 0],
                    dst_ref=stats_out.at[pl.ds(other * rows, rows)],
                    send_sem=stat_send.at[0, 0],
                    recv_sem=stat_recv.at[other],
                    device_id=me,
                    device_id_type=MESH,
                ).wait_recv()

    for k, source, target, slot, condition, own in sent:
        guarded(
            condition,
            lambda k=k, source=source, target=target, slot=slot, own=own: copy_of(
                k, source, target, slot, own
            ).wait_send(),
        )


def full_shapes(sizes, shapes):
    dp_size, group_size = sizes
    conv, small, blocks = shapes
    return [
        (group_size, dp_size * conv[0]) + conv[1:],
        (dp_size, group_size) + small,
        (group_size * blocks[0], dp_size * blocks[1], blocks[2]),
    ]


def gather_weights(sizes, shapes, taps, raw, features, feature_norm, vectors):
    low, out = jnp.bfloat16, jax.ShapeDtypeStruct
    full = full_shapes(sizes, shapes)
    frames, width = features.shape
    count, devices = len(shapes), sizes[0] * sizes[1]
    members = shapes[-1][0]
    dma = pltpu.SemaphoreType.DMA
    return pl.pallas_call(
        functools.partial(gather_kernel, sizes, shapes, taps),
        out_shape=[out(shape, low) for shape in full]
        + [out((D, D), low)]
        + front_shapes(frames, width)
        + [out((frames, 1), jnp.float32)],
        in_specs=[VMEM] * (len(raw) + 3),
        out_specs=[HBM] * (count + 1) + [VMEM] * 8,
        scratch_shapes=[pltpu.VMEM(shape, low) for shape in shapes]
        + [pltpu.VMEM(raw[-1].shape, low), pltpu.VMEM(full[1], low)]
        + front_scratch(full[0], frames)
        + [
            dma((count, 3 * devices)),
            dma((count, devices)),
            dma((count,)),
            dma((members, 2)),
            dma((sizes[0],)),
            dma,
            dma,
        ],
        name="gather_front",
        compiler_params=pltpu.CompilerParams(
            collective_id=0, has_side_effects=True, vmem_limit_bytes=VMEM_LIMIT
        ),
    )(*raw, features, feature_norm, vectors)


def shift_right(values, by):
    if by == 0:
        return values
    parts = []
    for first in range(0, values.shape[1], CLIP):
        part = values[:, first : first + CLIP]
        lane = lax.broadcasted_iota(jnp.int32, part.shape, 1)
        turned = pltpu.roll(part, by % CLIP, 1)
        inside = lane >= by if by > 0 else lane < CLIP + by
        parts.append(jnp.where(inside, turned, 0.0))
    return jnp.concatenate(parts, 1)


def place_windows(hidden, windows, taps):
    channels = hidden.shape[0]
    runs, half = taps // STRIDE, taps // STRIDE // 2
    for run in range(runs):
        by = STRIDE * (half - 1 - run) if run < half else -STRIDE * (run - half)
        windows[run * channels : (run + 1) * channels, :] = shift_right(hidden, by).astype(
            jnp.bfloat16
        )


def conv_group(hidden, weight_at, windows, taps, shape):
    channels = hidden.shape[0]
    chunks, _, _, chunk = shape
    place_windows(hidden, windows, taps)
    total = None
    for side in range(2):
        part = None
        for index in range(side * chunks // 2, (side + 1) * chunks // 2):
            term = dot(weight_at(index), windows[index * chunk : (index + 1) * chunk, :])
            part = term if part is None else part + term
        for offset in range(STRIDE):
            by = STRIDE - offset if side == 0 else -offset
            moved = shift_right(part[offset * channels : (offset + 1) * channels], by)
            total = moved if total is None else total + moved
    return total


def conv_group_back(hidden, grad, weight_at, put, windows, moved, taps, shape):
    channels = hidden.shape[0]
    chunks, _, _, chunk = shape
    half, runs = taps // STRIDE // 2, chunk // channels
    place_windows(hidden, windows, taps)
    total = None
    for side in range(2):
        for offset in range(STRIDE):
            by = offset - STRIDE if side == 0 else offset
            moved[offset * channels : (offset + 1) * channels, :] = shift_right(grad, by).astype(
                jnp.bfloat16
            )
        for index in range(side * chunks // 2, (side + 1) * chunks // 2):
            put(
                index,
                dot_nt(moved[...], windows[index * chunk : (index + 1) * chunk, :]).astype(
                    jnp.bfloat16
                ),
            )
            turned = dot_tn(weight_at(index), moved[...])
            for step in range(runs):
                run = index * runs + step
                by = -STRIDE * (half - 1 - run) if run < half else STRIDE * (run - half)
                part = shift_right(turned[step * channels : (step + 1) * channels], by)
                total = part if total is None else total + part
    return total


def over_rows(total, tile, action):
    def step(index, _):
        action(pl.ds(pl.multiple_of(index * tile, tile), tile))
        return 0

    lax.fori_loop(0, total // tile, step, 0)


def dot(one, two):
    return jnp.dot(one, two, preferred_element_type=jnp.float32)


def dot_nt(one, two):
    return lax.dot_general(one, two, (((1,), (1,)), ((), ())), preferred_element_type=jnp.float32)


def dot_tn(one, two):
    return lax.dot_general(one, two, (((0,), (0,)), ((), ())), preferred_element_type=jnp.float32)


def norm_parts(values):
    average = jnp.mean(values, -1, keepdims=True)
    centred = values - average
    inverse = lax.rsqrt(jnp.mean(centred * centred, -1, keepdims=True) + 1e-05)
    return centred * inverse, inverse


def norm_back(upstream, unit, inverse, gain):
    scaled = upstream * gain
    along = jnp.mean(scaled * unit, -1, keepdims=True)
    return inverse * (scaled - jnp.mean(scaled, -1, keepdims=True) - unit * along)


def gelu_pair(values):
    below = 0.5 + 0.5 * lax.erf(values * 0.7071067811865476)
    density = jnp.exp(values * values * -0.5) * 0.3989422804014327
    return values * below, below + values * density


def add_row(ref, row, values):
    ref[row : row + 1, :] += jnp.sum(values, 0, keepdims=True)


def front_compute(taps, refs, outs, scratch):
    features, mask, feature_norm, vectors, small, kernel = refs
    feature_unit, normed, hidden_t, encoded, encoder_unit, encoder_inverse, slope = outs
    held, windows, hidden, out_t, load_sem = scratch
    frames = features.shape[0]
    groups = kernel.shape[1]
    channels = hidden_t.shape[0] // groups

    def load(group):
        return pltpu.make_async_copy(kernel.at[:, group], held.at[:, group], load_sem.at[group])

    def enter():
        def one(at):
            unit, _ = norm_parts(features[at, :].astype(jnp.float32))
            feature_unit[at, :] = unit
            scaled = unit * feature_norm[0:1, :] + feature_norm[1:2, :]
            normed[at, :] = scaled.astype(jnp.bfloat16)

        over_rows(frames, 32, one)

    def project():
        for group in range(groups):
            load(group).start()
        normed_t = normed[...].T
        parts, columns = small.shape[0], small.shape[1]
        third = D // columns
        for group in range(columns):
            for first, size in ((0, 128), (128, third - 128)):
                row = first // 2
                part = small[:, group, row : row + 64, :].reshape(parts * 64, 128)
                at = group * third + first
                out_t[at : at + size, :] = dot_tn(part, normed_t)[:size]
        hidden[...] = jnp.where(mask[...] > 0, vectors[0:1, :], out_t[...].T)
        hidden_t[...] = hidden[...].T.astype(jnp.bfloat16)

    def one_group(group, _):
        load(group).wait()
        at = pl.ds(pl.multiple_of(group * channels, channels), channels)
        out_t[at, :] = conv_group(
            hidden_t[at, :].astype(jnp.float32),
            lambda index: held[index, group],
            windows,
            taps,
            kernel.shape,
        )
        return 0

    def convolve(first, last):
        lax.fori_loop(first, last, one_group, 0)

    def leave():
        slope[...] = out_t[...].T

        def one(at):
            active, derivative = gelu_pair(slope[at, :])
            slope[at, :] = derivative
            unit, inverse = norm_parts(hidden[at, :] + active)
            encoder_unit[at, :] = unit
            encoder_inverse[at, :] = inverse
            encoded[at, :] = unit * vectors[1:2, :] + vectors[2:3, :]

        over_rows(frames, 32, one)

    return enter, project, convolve, leave


def front_kernel(taps, *refs):
    enter, project, convolve, leave = front_compute(taps, refs[:6], refs[6:13], refs[13:])
    enter()
    project()
    convolve(0, refs[5].shape[1])
    leave()


def front_shapes(frames, width):
    out, full, low = jax.ShapeDtypeStruct, jnp.float32, jnp.bfloat16
    return [
        out((frames, width), full),
        out((frames, width), low),
        out((D, frames), low),
        out((frames, D), full),
        out((frames, D), full),
        out((frames, 1), full),
        out((frames, D), full),
    ]


def front_scratch(kernel_shape, frames):
    chunks, groups, rows, chunk = kernel_shape
    return [
        pltpu.VMEM(kernel_shape, jnp.bfloat16),
        pltpu.VMEM((chunks * chunk, frames), jnp.bfloat16),
        pltpu.VMEM((frames, D), jnp.float32),
        pltpu.VMEM((D, frames), jnp.float32),
        pltpu.SemaphoreType.DMA((groups,)),
    ]


def front(features, mask, feature_norm, vectors, small, kernel, taps):
    frames, width = features.shape
    return pl.pallas_call(
        functools.partial(front_kernel, taps),
        out_shape=front_shapes(frames, width),
        in_specs=[VMEM] * 5 + [HBM],
        out_specs=[VMEM] * 7,
        scratch_shapes=front_scratch(kernel.shape, frames),
        name="front",
        compiler_params=pltpu.CompilerParams(vmem_limit_bytes=VMEM_LIMIT),
    )(features, mask, feature_norm, vectors, small, kernel)


def trunk_kernel(*refs):
    (
        encoded, mask, labels, vectors, small, blocks,
        encoded_grad, block_grad, head_grad, center_grad_t, rows_out, counted,
        head, table, centers, held, made, low, triple, attention, mixed, unit_one, inverse_one, middle, middle_low,
        active, slope, unit_two, inverse_two, work, work_low, flow_low, triple_grad, turned,
        load_sem, save_sem,
    ) = refs
    frames = encoded.shape[0]
    count = blocks.shape[0]
    ups = (count - 4) // 2
    tile = 32
    pairs = D // 128

    def load(block):
        return pltpu.make_async_copy(blocks.at[block], held.at[block], load_sem.at[block])

    def save(block):
        return pltpu.make_async_copy(made.at[block], block_grad.at[block], save_sem.at[block])

    for block in range(count):
        load(block).start()
    rows_out[...] = jnp.zeros_like(rows_out)
    parts, columns = small.shape[0], small.shape[1]
    notes = small[:, :, 224:240, :].astype(jnp.float32)
    first = lax.broadcasted_iota(jnp.int32, notes.shape, 2) == 0
    first &= lax.broadcasted_iota(jnp.int32, notes.shape, 3) == CLUSTER_ROWS
    notes = jnp.sum(jnp.where(first, notes, 0.0), (0, 1))
    masked = jnp.sum(jnp.sum(notes, 1, keepdims=True), 0, keepdims=True)
    counted[...] = jnp.broadcast_to(masked, counted.shape)

    def to_inputs(at):
        low[at, :] = encoded[at, :].astype(jnp.bfloat16)

    over_rows(frames, tile, to_inputs)

    def first_three(block, _):
        load(block).wait()
        triple[block] = dot(low[...], held[block]).astype(jnp.bfloat16)
        return 0

    lax.fori_loop(0, 3, first_three, 0)
    lane = lax.broadcasted_iota(jnp.int32, (CLIP, 128), 1)
    even = lane < HEAD

    def apart(values):
        zero = jnp.zeros_like(values)
        return jnp.concatenate([jnp.where(even, values, zero), jnp.where(even, zero, values)], 0)

    def beside(values):
        return jnp.concatenate([values[:CLIP], values[CLIP:]], 1)

    def spot(index):
        at = pl.ds(pl.multiple_of(index // pairs * CLIP, CLIP), CLIP)
        return at, pl.ds(pl.multiple_of(index % pairs * 128, 128), 128)

    def attend(index, _):
        at, lanes = spot(index)
        query, keys, values = triple[0, at, lanes], triple[1, at, lanes], triple[2, at, lanes]
        scores = dot_nt(apart(query), keys) * HEAD ** (-0.5)
        raised = jnp.exp(scores - jnp.max(scores, -1, keepdims=True))
        full = raised / jnp.sum(raised, -1, keepdims=True)
        attention[index] = full
        mixed[at, lanes] = dot(beside(full.astype(jnp.bfloat16)), apart(values)).astype(jnp.bfloat16)
        return 0

    lax.fori_loop(0, frames // CLIP * pairs, attend, 0)
    load(3).wait()
    work[...] = dot(mixed[...], held[3])

    def first_norm(at):
        unit, inverse = norm_parts(encoded[at, :] + work[at, :])
        unit_one[at, :] = unit
        inverse_one[at, :] = inverse
        value = unit * vectors[3:4, :] + vectors[4:5, :]
        middle[at, :] = value
        middle_low[at, :] = value.astype(jnp.bfloat16)

    over_rows(frames, tile, first_norm)

    def expand(step, _):
        load(4 + step).wait()
        slope[step] = dot(middle_low[...], held[4 + step])

        def bend(at):
            value, derivative = gelu_pair(slope[step, at, :])
            active[step, at, :] = value.astype(jnp.bfloat16)
            slope[step, at, :] = derivative

        over_rows(frames, tile, bend)
        return 0

    lax.fori_loop(0, ups, expand, 0)

    def contract(step, _):
        load(4 + ups + step).wait()
        middle[...] += dot(active[step], held[4 + ups + step])
        return 0

    lax.fori_loop(0, ups, contract, 0)

    def second_norm(at):
        unit, inverse = norm_parts(middle[at, :])
        unit_two[at, :] = unit
        inverse_two[at, :] = inverse
        flow_low[at, :] = (unit * vectors[5:6, :] + vectors[6:7, :]).astype(jnp.bfloat16)

    over_rows(frames, tile, second_norm)
    table[...] = jnp.zeros_like(table)
    for group in range(columns):
        across = slice(group * 128, group * 128 + 128)
        head[:, across] = small[:, group, 128:224, :].reshape(parts * 96, 128)
        for part in range(parts):
            row = part // 2 * 128 + part % 2 * 32
            table[row : row + 32, across] = small[part, group, 224:256, :].astype(jnp.float32)
    real = lax.broadcasted_iota(jnp.int32, (1, table.shape[1]), 1) % 128 < CLUSTER_ROWS
    table[...] = jnp.where(real, table[...], 0.0)
    size = lax.rsqrt(jnp.sum(table[...] * table[...], 0, keepdims=True) + 1e-06)
    centers[...] = (table[...] * size).astype(jnp.bfloat16)
    embedded = dot(flow_low[...], head[...])
    length = lax.rsqrt(jnp.sum(embedded * embedded, -1, keepdims=True) + 1e-06)
    unit_low = (embedded * length).astype(jnp.bfloat16)
    logits = jnp.where(real, dot(unit_low, centers[...]) * inv_temp, -1e30)
    top = jnp.max(logits, -1, keepdims=True)
    raised = jnp.exp(logits - top)
    amount = jnp.sum(raised, -1, keepdims=True)
    choose = labels[...] == lax.broadcasted_iota(jnp.int32, logits.shape, 1)
    target = jnp.sum(jnp.where(choose, logits, 0.0), -1, keepdims=True)
    losses = mask[...] * (jnp.log(amount) + top - target)
    rows_out[7:8, :] = jnp.broadcast_to(jnp.sum(losses, 0, keepdims=True), (1, D))
    logit_grad = (
        (raised / amount - choose.astype(jnp.float32)) * (mask[...] * (1.0 / masked))
    ).astype(jnp.bfloat16)
    unit_grad = dot_nt(logit_grad, centers[...]) * inv_temp
    spread = dot_tn(unit_low, logit_grad) * inv_temp
    shared = jnp.sum(spread * table[...], 0, keepdims=True)
    spread = size * spread - table[...] * (size * size * size * shared)
    for group in range(columns):
        center_grad_t[group * 64 : group * 64 + 64, :] = spread[group * 128 : group * 128 + 64, :]
    along = jnp.sum(unit_grad * embedded, -1, keepdims=True)
    embedded_grad = (
        length * unit_grad - embedded * (length * length * length * along)
    ).astype(jnp.bfloat16)
    work[...] = dot_nt(embedded_grad, head[...])
    head_grad[...] = dot_tn(flow_low[...], embedded_grad).astype(jnp.bfloat16)

    def second_back(at):
        upstream = work[at, :]
        add_row(rows_out, 5, upstream * unit_two[at, :])
        add_row(rows_out, 6, upstream)
        value = norm_back(upstream, unit_two[at, :], inverse_two[at, :], vectors[5:6, :])
        middle[at, :] = value
        flow_low[at, :] = value.astype(jnp.bfloat16)

    over_rows(frames, tile, second_back)
    turned[...] = middle_low[...].T

    def feed_back(step, _):
        work[...] = dot_nt(flow_low[...], held[4 + ups + step])
        made[4 + ups + step] = dot_tn(active[step], flow_low[...]).astype(jnp.bfloat16)
        save(4 + ups + step).start()

        def bend(at):
            work_low[at, :] = (work[at, :] * slope[step, at, :]).astype(jnp.bfloat16)

        over_rows(frames, tile, bend)
        made[4 + step] = dot(turned[...], work_low[...]).astype(jnp.bfloat16)
        save(4 + step).start()
        middle[...] += dot_nt(work_low[...], held[4 + step])
        return 0

    lax.fori_loop(0, ups, feed_back, 0)

    def first_back(at):
        upstream = middle[at, :]
        add_row(rows_out, 3, upstream * unit_one[at, :])
        add_row(rows_out, 4, upstream)
        value = norm_back(upstream, unit_one[at, :], inverse_one[at, :], vectors[3:4, :])
        middle[at, :] = value
        flow_low[at, :] = value.astype(jnp.bfloat16)

    over_rows(frames, tile, first_back)
    made[3] = dot_tn(mixed[...], flow_low[...]).astype(jnp.bfloat16)
    save(3).start()
    work_low[...] = dot_nt(flow_low[...], held[3]).astype(jnp.bfloat16)

    def attend_back(index, _):
        at, lanes = spot(index)
        query, keys, values = triple[0, at, lanes], triple[1, at, lanes], triple[2, at, lanes]
        upstream = apart(work_low[at, lanes])
        full = attention[index]
        full_grad = dot_nt(upstream, values)
        triple_grad[2, at, lanes] = dot_tn(full.astype(jnp.bfloat16), upstream).astype(jnp.bfloat16)
        along = jnp.sum(full * full_grad, -1, keepdims=True)
        score_grad = (full * (full_grad - along)).astype(jnp.bfloat16)
        triple_grad[0, at, lanes] = (
            dot(beside(score_grad), apart(keys)) * HEAD ** (-0.5)
        ).astype(jnp.bfloat16)
        triple_grad[1, at, lanes] = (
            dot_tn(score_grad, apart(query)) * HEAD ** (-0.5)
        ).astype(jnp.bfloat16)
        return 0

    lax.fori_loop(0, frames // CLIP * pairs, attend_back, 0)
    turned[...] = low[...].T

    def last_three(block, _):
        made[block] = dot(turned[...], triple_grad[block]).astype(jnp.bfloat16)
        save(block).start()
        middle[...] += dot_nt(triple_grad[block], held[block])
        return 0

    lax.fori_loop(0, 3, last_three, 0)
    encoded_grad[...] = middle[...]
    for block in range(count):
        save(block).wait()


def trunk(encoded, mask, labels, vectors, small, blocks):
    frames, count = encoded.shape[0], blocks.shape[0]
    ups, columns = (count - 4) // 2, small.shape[1] * 128
    full, low = jnp.float32, jnp.bfloat16
    out = jax.ShapeDtypeStruct
    wide, wide_low = pltpu.VMEM((frames, D), full), pltpu.VMEM((frames, D), low)
    column = pltpu.VMEM((frames, 1), full)
    return pl.pallas_call(
        trunk_kernel,
        out_shape=[
            out((frames, D), full),
            out(blocks.shape, low),
            out((D, columns), low),
            out((columns // 2, columns), full),
            out((8, D), full),
            out((8, 128), full),
        ],
        in_specs=[VMEM] * 5 + [HBM],
        out_specs=[VMEM, HBM] + [VMEM] * 4,
        scratch_shapes=[
            pltpu.VMEM((D, columns), low),
            pltpu.VMEM((columns, columns), full),
            pltpu.VMEM((columns, columns), low),
            pltpu.VMEM(blocks.shape, low),
            pltpu.VMEM(blocks.shape, low),
            wide_low,
            pltpu.VMEM((3, frames, D), low),
            pltpu.VMEM((frames // CLIP * D // 128, 2 * CLIP, CLIP), full),
            wide_low,
            wide,
            column,
            wide,
            wide_low,
            pltpu.VMEM((ups, frames, D), low),
            pltpu.VMEM((ups, frames, D), full),
            wide,
            column,
            wide,
            wide_low,
            wide_low,
            pltpu.VMEM((3, frames, D), low),
            pltpu.VMEM((D, frames), low),
            pltpu.SemaphoreType.DMA((count,)),
            pltpu.SemaphoreType.DMA((count,)),
        ],
        name="trunk",
        compiler_params=pltpu.CompilerParams(vmem_limit_bytes=VMEM_LIMIT),
    )(encoded, mask, labels, vectors, small, blocks)


LOSS_ROW = 7


class Owners:
    def __init__(self, place, members):
        self.place, self.members = place, members
        self.first = (place.dp_size - 2 * members) // 2
        index = place.dp - self.first
        self.here = (index >= 0) & (index < 2 * members)
        self.group = place.x * 2 + index // members
        self.member = index % members

    def of(self, member):
        return self.first + self.place.core * self.members + member

    def to_rows(self, other, remote_action, local_action):
        place = self.place
        away = (place.dp != other) | (place.group != self.group)
        pl.when(away)(functools.partial(remote_action, other))
        pl.when(jnp.logical_not(away))(local_action)


class Reducer:
    def __init__(self, place, shapes, local, refs, sems):
        self.place, self.shapes, self.local = place, shapes, local
        self.z, self.lines, self.last = place.z, place.lines, place.lines - 1
        self.blocks = KINDS.index("blocks")
        self.rest = [k for k in range(len(KINDS)) if k != self.blocks]
        self.crossed, self.first_in, self.second_in, self.line_in = refs[:4]
        self.held, self.source = refs[4:]
        (
            self.load_sem, self.cross_send, self.cross_recv, self.first_send, self.first_recv,
            self.second_send, self.second_recv, self.left_send, self.left_recv, self.right_send,
            self.right_recv,
        ) = sems
        self.p_mate, self.q_mate = place.near(self.z, 1, 0), place.near(self.z, 0, 1)
        self.c_mate = place.at(self.z, 0, 0, 1)
        self.left, self.right = place.at(self.z - 1), place.at(self.z + 1)

    def remote(self, source, target, send, recv, device):
        return pltpu.make_async_remote_copy(
            src_ref=source,
            dst_ref=target,
            send_sem=send,
            recv_sem=recv,
            device_id=device,
            device_id_type=MESH,
        )

    def load_of(self, p, q, spot):
        k = self.blocks
        dp, group = self.place.near(spot, p, q)
        return pltpu.make_async_copy(
            piece_at("blocks", self.source[k], dp, group, self.shapes[k]),
            self.held.at[p, spot],
            self.load_sem.at[p, q, spot],
        )

    def cross_of(self, k, p, q, spot):
        dp, group = self.place.across(spot, p, q)
        return self.remote(
            piece_at(KINDS[k], self.source[k], dp, group, self.shapes[k]),
            self.crossed[k].at[p, q, spot],
            self.cross_send.at[k, p, q, spot],
            self.cross_recv.at[k, p, q, spot],
            self.c_mate,
        )

    def own(self, k, p, q, spot):
        if k == self.blocks:
            self.load_of(p, q, spot).wait()
            return f32(self.held, (p, spot))
        dp, group = self.place.near(spot, p, q)
        return piece_at(KINDS[k], self.source[k], dp, group, self.shapes[k])[...].astype(jnp.float32)

    def met(self, k, p, q, spot):
        own = self.own(k, p, q, spot)
        self.cross_of(k, p, q, spot).wait_recv()
        return own + f32(self.crossed[k], (p, q, spot))

    def turn(self, index):
        odd = index % 2
        return (1 - odd) * (self.last - index // 2) + odd * (index // 2)

    def first_out(self, k, p, spot):
        return self.remote(
            self.crossed[k].at[p, 1, spot],
            self.first_in[k].at[p, spot],
            self.first_send.at[k, p, spot],
            self.first_recv.at[k, p, spot],
            self.q_mate,
        )

    def stage_one(self, k, index):
        p, spot = 1 - index // self.lines, self.turn(index % self.lines)
        self.crossed[k][p, 1, spot] = self.met(k, p, 1, spot).astype(jnp.bfloat16)
        self.first_out(k, p, spot).start()
        if k == self.blocks:
            self.load_of(p, 0, spot).start()

    def joined(self, k, p, spot):
        total = self.met(k, p, 0, spot)
        self.first_out(k, p, spot).wait_recv()
        return total + f32(self.first_in[k], (p, spot))

    def second_out(self, k, spot):
        return self.remote(
            self.crossed[k].at[1, 0, spot],
            self.second_in[k].at[spot],
            self.second_send.at[k, spot],
            self.second_recv.at[k, spot],
            self.p_mate,
        )

    def stage_two(self, k, index):
        spot = self.turn(index)
        self.crossed[k][1, 0, spot] = self.joined(k, 1, spot).astype(jnp.bfloat16)
        self.second_out(k, spot).start()

    def line_total(self, k, spot):
        total = self.joined(k, 0, spot)
        self.second_out(k, spot).wait_recv()
        return total + f32(self.second_in[k], (spot,))

    def line_out(self, k, spot, way):
        if way == "right":
            send, recv, device, slot = self.right_send, self.left_recv, self.right, spot
        else:
            send, recv, device = self.left_send, self.right_recv, self.left
            ends = (self.last - (self.z - 1 - spot)) // self.last
            slot = spot + ends * (self.lines - spot)
        return self.remote(
            self.crossed[k].at[0, 0, spot],
            self.line_in[k].at[slot],
            send.at[k, spot],
            recv.at[k, spot],
            device,
        )

    def came_in(self, k, spot, way):
        recv = self.left_recv if way == "right" else self.right_recv
        send = self.right_send if way == "right" else self.left_send
        return self.remote(
            self.crossed[k].at[0, 0, spot],
            self.line_in[k].at[spot],
            send.at[k, spot],
            recv.at[k, spot],
            self.c_mate,
        )

    def pass_on(self, k, spot, way, inner):
        z = self.z
        if way == "right":
            here = (z < spot) & ((z > 0) if inner else (z == 0))
        else:
            here = (z > spot) & ((z < self.last) if inner else (z == self.last))

        @pl.when(here)
        def _():
            total = self.line_total(k, spot)
            if inner:
                self.came_in(k, spot, way).wait_recv()
                total = total + f32(self.line_in[k], (spot,))
            self.crossed[k][0, 0, spot] = total.astype(jnp.bfloat16)
            self.line_out(k, spot, way).start()

    def line_step(self, k, step, inner):
        self.pass_on(k, self.last - step, "right", inner)
        self.pass_on(k, step, "left", inner)

    def line_end(self, k, out):
        z = self.z
        out[...] = self.line_total(k, z)

        @pl.when(z > 0)
        def _():
            self.came_in(k, z, "right").wait_recv()
            out[...] += f32(self.line_in[k], (z,))

        @pl.when(z < self.last)
        def _():
            self.came_in(k, z, "left").wait_recv()
            out[...] += f32(self.line_in[k], (self.lines,))

    def drain(self):
        for k in range(len(KINDS)):

            def one(spot, _, k=k):
                for p in range(2):
                    for q in range(2):
                        self.cross_of(k, p, q, spot).wait_send()
                    self.first_out(k, p, spot).wait_send()
                self.second_out(k, spot).wait_send()

                @pl.when(self.z < spot)
                def _():
                    self.line_out(k, spot, "right").wait_send()

                @pl.when(self.z > spot)
                def _():
                    self.line_out(k, spot, "left").wait_send()

                return 0

            lax.fori_loop(0, self.lines, one, 0)


def f32(ref, at):
    return ref[at].astype(jnp.float32)


def back_compute(taps, refs, made, small_made, rows, scratch, hook):
    (
        encoded_grad, mask, vectors, small, feature_unit, normed, hidden_t,
        encoder_unit, encoder_inverse, slope, trunk_rows, head_grad, center_grad_t, kernel,
    ) = refs
    slots, windows, moved, grad, grad_t, through, through_t, load_sem = scratch
    frames, width = feature_unit.shape
    groups = kernel.shape[1]
    channels = hidden_t.shape[0] // groups

    def load(group):
        slot = group % 2
        return pltpu.make_async_copy(kernel.at[:, group], slots.at[slot], load_sem.at[slot])

    def begin():
        load(0).start()
        rows[...] = jnp.zeros_like(rows)
        rows[0:8, :] = trunk_rows[...]
        over_rows(frames, 32, enter)
        grad_t[...] = through[...].T.astype(jnp.bfloat16)

    def enter(at):
        upstream = encoded_grad[at, :]
        add_row(rows, 1, upstream * encoder_unit[at, :])
        add_row(rows, 2, upstream)
        value = norm_back(upstream, encoder_unit[at, :], encoder_inverse[at, :], vectors[1:2, :])
        grad[at, :] = value
        through[at, :] = value * slope[at, :]

    def one_group(group, _):
        pl.when(group + 1 < groups)(lambda: load(group + 1).start())
        load(group).wait()
        at = pl.ds(pl.multiple_of(group * channels, channels), channels)

        def put(index, value):
            made[index, group] = value

        through_t[at, :] = conv_group_back(
            hidden_t[at, :].astype(jnp.float32),
            grad_t[at, :].astype(jnp.float32),
            lambda index: slots[group % 2, index],
            put,
            windows,
            moved,
            taps,
            kernel.shape,
        )
        hook(group)
        return 0

    def convolve(first, last):
        lax.fori_loop(first, last, one_group, 0)

    def leave(at):
        total = grad[at, :] + through[at, :]
        inside = mask[at, :] > 0
        add_row(rows, 0, jnp.where(inside, total, 0.0))
        grad[at, :] = jnp.where(inside, 0.0, total)

    def finish():
        through[...] = through_t[...].T
        over_rows(frames, 32, leave)
        grad_t[...] = grad[...].T.astype(jnp.bfloat16)
        normed_t = normed[...].T
        parts, columns = small.shape[0], small.shape[1]
        third = D // columns
        total = None
        for group in range(columns):
            one = grad_t[group * third : group * third + 128, :]
            two = grad_t[group * third + 128 : (group + 1) * third, :]
            lane = third - 128
            wide = dot_nt(normed_t, one).astype(jnp.bfloat16)
            thin = dot_nt(normed_t, two).astype(jnp.bfloat16)
            small_made[:, group, 0:64, :] = wide.reshape(parts, 64, 128)
            small_made[:, group, 64:128, :] = jnp.concatenate(
                [thin, jnp.zeros((thin.shape[0], 128 - lane), jnp.bfloat16)], 1
            ).reshape(parts, 64, 128)
            small_made[:, group, 128:224, :] = head_grad[:, group * 128 : group * 128 + 128].reshape(
                parts, 96, 128
            )
            small_made[:, group, 224:256, :] = (
                center_grad_t[:, group * 128 : group * 128 + 128]
                .astype(jnp.bfloat16)
                .reshape(parts, 32, 128)
            )
            first = small[:, group, 0:64, :].reshape(parts * 64, 128)
            second = small[:, group, 64:128, :].reshape(parts * 64, 128)[:, :lane]
            term = dot(first, one) + dot(second, two)
            total = term if total is None else total + term
        normed_grad = total.T
        rows[8:9, 0:width] = jnp.sum(normed_grad * feature_unit[...], 0, keepdims=True)
        rows[9:10, 0:width] = jnp.sum(normed_grad, 0, keepdims=True)

    return begin, convolve, finish


def back_scratch(kernel_shape, frames):
    chunks, groups, rows, chunk = kernel_shape
    full, low = jnp.float32, jnp.bfloat16
    return [
        pltpu.VMEM((2, chunks, rows, chunk), low),
        pltpu.VMEM((chunks * chunk, frames), low),
        pltpu.VMEM((rows, frames), low),
        pltpu.VMEM((frames, D), full),
        pltpu.VMEM((D, frames), low),
        pltpu.VMEM((frames, D), full),
        pltpu.VMEM((D, frames), full),
        pltpu.SemaphoreType.DMA((2,)),
    ]


BACK_INPUTS = 14


def back_kernel(taps, *refs):
    made, small_made, rows = refs[BACK_INPUTS : BACK_INPUTS + 3]
    begin, convolve, finish = back_compute(
        taps, refs[:BACK_INPUTS], made, small_made, rows, refs[BACK_INPUTS + 3 :], lambda group: None
    )
    begin()
    convolve(0, made.shape[1])
    finish()


def back(taps, operands):
    kernel, small, frames = operands[-1], operands[3], operands[0].shape[0]
    return pl.pallas_call(
        functools.partial(back_kernel, taps),
        out_shape=[
            jax.ShapeDtypeStruct(kernel.shape, jnp.bfloat16),
            jax.ShapeDtypeStruct(small.shape, jnp.bfloat16),
            jax.ShapeDtypeStruct((16, D), jnp.float32),
        ],
        in_specs=[VMEM] * (BACK_INPUTS - 1) + [HBM],
        out_specs=[VMEM] * 3,
        scratch_shapes=back_scratch(kernel.shape, frames),
        name="back",
        compiler_params=pltpu.CompilerParams(vmem_limit_bytes=48 * 1024 * 1024),
    )(*operands)


def back_reduce_kernel(sizes, shapes, taps, *refs):
    place = Place(*sizes)
    refs = list(refs)

    def pull(number):
        taken = refs[:number]
        del refs[:number]
        return taken

    count = len(KINDS)
    inputs, (block_grad,) = pull(BACK_INPUTS), pull(1)
    outs, (small_out, square_out, whole_box, gram_low, sides_out) = pull(count), pull(5)
    made, small_made, rows, scratch = *pull(3), pull(8)
    crossed, first_in, second_in, line_in = (pull(count) for _ in range(4))
    (held, group_box, dp_box, rows_low) = pull(4)
    sems = pull(11)
    (group_send, group_recv, dp_send, dp_recv, row_send, row_recv, pair_send, pair_recv) = pull(8)
    (side_send, side_recv, side_own) = pull(3)
    me = (place.dp, place.group)
    source = {"conv": made, "small": small_made, "blocks": block_grad}
    run = Reducer(
        place,
        shapes,
        None,
        (crossed, first_in, second_in, line_in, held, [source[kind] for kind in KINDS]),
        sems,
    )
    lines, b = run.lines, run.blocks
    conv, tiny = KINDS.index("conv"), KINDS.index("small")
    greet(place)

    def cross_all(k):
        for q in (1, 0):
            for p in (1, 0):

                def begin_one(index, _, p=p, q=q):
                    run.cross_of(k, p, q, run.turn(index)).start()
                    if k == b and q == 1:
                        run.load_of(p, q, run.turn(index)).start()
                    return 0

                lax.fori_loop(0, lines, begin_one, 0)

    def hook(group):
        pairs = shapes[conv][0]

        @pl.when(group % pairs == pairs - 1)
        def _():
            dp = group // pairs
            spot, flip_y = dp // 2, (dp % 2 + place.y) % 2
            for x in range(2):
                flip_x = (x + place.x) % 2
                p = flip_y * place.core + flip_x * (1 - place.core)
                q = flip_x * place.core + flip_y * (1 - place.core)
                run.cross_of(conv, p, q, spot).start()

    begin, convolve, finish = back_compute(taps, inputs, made, small_made, rows, scratch, hook)

    def remote(source, target, send, recv, device):
        return run.remote(source, target, send, recv, device)

    def each_other(size, mine, action):
        for other in range(size):
            pl.when(mine != other)(functools.partial(action, other))

    def group_copy(other):
        return remote(
            rows,
            group_box.at[place.group],
            group_send.at[other],
            group_recv.at[place.group],
            (place.dp, other),
        )

    def dp_copy(other):
        return remote(
            dp_box.at[place.dp], dp_box.at[place.dp], dp_send.at[other], dp_recv.at[place.dp], (other, place.group)
        )

    def group_wait(other):
        group_copy(other).wait_send()
        remote(rows, group_box.at[other], group_send.at[other], group_recv.at[other], me).wait_recv()

    def dp_wait(other):
        dp_copy(other).wait_send()
        remote(dp_box.at[other], dp_box.at[other], dp_send.at[other], dp_recv.at[other], me).wait_recv()

    def rows_to_group():
        group_box[place.group] = rows[...]
        each_other(place.group_size, place.group, lambda other: group_copy(other).start())

    def rows_to_all():
        each_other(place.group_size, place.group, group_wait)
        total = group_box[0]
        for other in range(1, place.group_size):
            total = total + group_box[other]
        dp_box[place.dp] = total
        each_other(place.dp_size, place.dp, lambda other: dp_copy(other).start())

    def some(first, last, action):
        def one(index, _):
            action(index)
            return 0

        lax.fori_loop(first, last, one, 0)

    members, depth = shapes[b][0], shapes[b][1]
    owners = Owners(place, members)
    my_rows = pl.ds(pl.multiple_of(place.dp * depth, depth), depth)
    owner_here = owners.here & (owners.group == place.group)
    owner_there = owners.here & (owners.group != place.group)

    def row_copy(member):
        return remote(
            rows_low.at[member],
            whole_box.at[my_rows],
            row_send.at[member],
            row_recv.at[place.dp],
            (owners.of(member), place.group),
        )

    def pair_copy(other):
        spot = pl.ds(pl.multiple_of(other * depth, depth), depth)
        return remote(
            whole_box.at[spot], whole_box.at[spot], pair_send.at[other], pair_recv.at[other], run.c_mate
        )

    def send_rows():
        rows_low[...] = outs[b][...].astype(jnp.bfloat16)
        for member in range(members):

            @pl.when(place.dp != owners.of(member))
            def _(member=member):
                row_copy(member).start()

            @pl.when(place.dp == owners.of(member))
            def _(member=member):
                whole_box[my_rows] = rows_low[member]
                pair_copy(place.dp).start()

    def take_rows():
        @pl.when(owner_here)
        def _():
            for other in range(place.dp_size):

                @pl.when(place.dp != other)
                def _(other=other):
                    spot = pl.ds(other * depth, depth)
                    remote(
                        rows_low.at[0], whole_box.at[spot], row_send.at[0], row_recv.at[other], me
                    ).wait_recv()
                    pair_copy(other).start()

        @pl.when(owner_there)
        def _():
            for other in range(place.dp_size):
                pair_copy(other).wait_recv()

    def side_copy(other):
        spot = pl.ds(pl.multiple_of(other * depth, depth), depth)
        return remote(
            gram_low.at[spot],
            sides_out.at[owners.member, place.core],
            side_send.at[other],
            side_recv.at[owners.member, place.core],
            (other, owners.group),
        )

    def side_local():
        return pltpu.make_async_copy(
            gram_low.at[my_rows], sides_out.at[owners.member, place.core], side_own
        )

    per_tile = place.dp_size // 2
    tile = per_tile * depth

    def sides():
        @pl.when(owners.here)
        def _():
            def keep(index, value):
                at = pl.ds(pl.multiple_of(index * tile, tile), tile)
                gram_low[at, :] = value.astype(jnp.bfloat16)
                for offset in range(per_tile):
                    owners.to_rows(
                        index * per_tile + offset,
                        lambda other: side_copy(other).start(),
                        lambda: side_local().start(),
                    )

            for index in range(2):
                first = slice(index * tile, (index + 1) * tile)
                pl.when(place.core == 0)(
                    lambda index=index, first=first: keep(
                        index, dot_nt(whole_box[first, :], whole_box[...])
                    )
                )
                pl.when(place.core == 1)(
                    lambda index=index, first=first: keep(
                        index, dot_tn(whole_box[:, first], whole_box[...])
                    )
                )

    cross_all(b)
    begin()
    actions = {
        "one": lambda index, k: run.stage_one(k, index),
        "two": lambda index, k: run.stage_two(k, index),
        "edge": lambda index, k: run.line_step(k, index, False),
        "inner": lambda index, k: run.line_step(k, index, True),
        "end": lambda index, k: run.line_end(k, outs[k]),
    }

    def leave():
        finish()
        cross_all(tiny)
        rows_to_group()

    plain = {"leave": leave, "rows": send_rows, "take": take_rows, "sides": sides}
    for name, kind, first, last in PLAN:
        if name == "groups":
            convolve(first, last)
        elif name in plain:
            plain[name]()
        else:
            action = functools.partial(lambda index, k, name: actions[name](index, k), k=KINDS.index(kind), name=name)
            if last - first == 1:
                action(first)
            else:
                some(first, last, action)
        if name == "rows":
            rows_to_all()
    square = jnp.sum(outs[b][...] * outs[b][...])
    for k in run.rest:
        square = square + jnp.sum(outs[k][...] * outs[k][...])
    each_other(place.dp_size, place.dp, dp_wait)
    total = dp_box[0]
    for other in range(1, place.dp_size):
        total = total + dp_box[other]
    small_out[...] = total
    skipped = lax.broadcasted_iota(jnp.int32, total.shape, 0) != LOSS_ROW
    square = square + jnp.sum(jnp.where(skipped, total * total, 0.0)) * (
        1.0 / (place.dp_size * place.group_size)
    )
    square_out[...] = jnp.full(square_out.shape, square, jnp.float32)
    for member in range(members):
        for side in range(2):

            @pl.when((place.dp != owners.of(member)) | (place.core != side))
            def _(member=member, side=side):
                remote(
                    gram_low.at[pl.ds(0, depth)],
                    sides_out.at[member, side],
                    side_send.at[0],
                    side_recv.at[member, side],
                    me,
                ).wait_recv()

        @pl.when(place.dp != owners.of(member))
        def _(member=member):
            row_copy(member).wait_send()

    @pl.when(owner_here)
    def _():
        for other in range(place.dp_size):
            pair_copy(other).wait_send()

    @pl.when(owners.here)
    def _():
        for other in range(place.dp_size):
            owners.to_rows(
                other, lambda other: side_copy(other).wait_send(), lambda: side_local().wait()
            )

    run.drain()


def back_reduce(sizes, shapes, taps, operands, block_grad):
    dp_size, group_size = sizes
    lines, count = dp_size // 2, len(KINDS)
    kernel, small, frames = operands[-1], operands[3], operands[0].shape[0]
    low, full = jnp.bfloat16, jnp.float32

    def boxes(lead):
        return [
            pltpu.VMEM(tuple(lead(kind)) + tuple(shape), low) for kind, shape in zip(KINDS, shapes)
        ]

    dma = pltpu.SemaphoreType.DMA
    scratch = (
        [pltpu.VMEM(kernel.shape, low), pltpu.VMEM(small.shape, low), pltpu.VMEM((16, D), full)]
        + back_scratch(kernel.shape, frames)
        + boxes(lambda kind: (2, 2, lines))
        + boxes(lambda kind: (2, lines))
        + boxes(lambda kind: (lines,))
        + boxes(lambda kind: (lines + 1,))
        + [
            pltpu.VMEM((2, lines) + tuple(shapes[-1]), low),
            pltpu.VMEM((group_size, 16, D), full),
            pltpu.VMEM((dp_size, 16, D), full),
            pltpu.VMEM(shapes[-1], low),
        ]
        + [dma((2, 2, lines))]
        + [dma((count, 2, 2, lines))] * 2
        + [dma((count, 2, lines))] * 2
        + [dma((count, lines))] * 6
        + [dma((group_size,))] * 2
        + [dma((dp_size,))] * 2
        + [dma((shapes[-1][0],)), dma((dp_size,))]
        + [dma((dp_size,))] * 2
        + [dma((dp_size,)), dma((shapes[-1][0], 2)), dma]
    )
    return pl.pallas_call(
        functools.partial(back_reduce_kernel, sizes, shapes, taps),
        out_shape=[jax.ShapeDtypeStruct(shape, full) for shape in shapes]
        + [
            jax.ShapeDtypeStruct((16, D), full),
            jax.ShapeDtypeStruct((8, 128), full),
            jax.ShapeDtypeStruct((D, D), low),
            jax.ShapeDtypeStruct((D, D), low),
            jax.ShapeDtypeStruct((shapes[-1][0], 2) + tuple(shapes[-1][1:]), low),
        ],
        in_specs=[VMEM] * (BACK_INPUTS - 1) + [HBM, HBM],
        out_specs=[VMEM] * (count + 5),
        scratch_shapes=scratch,
        name="back_reduce",
        compiler_params=pltpu.CompilerParams(
            collective_id=1, has_side_effects=True, vmem_limit_bytes=VMEM_LIMIT
        ),
    )(*operands, block_grad)


PLAN = (
    ("one", "blocks", 0, 1),
    ("groups", "", 0, 3),
    ("one", "blocks", 2, 3),
    ("two", "blocks", 0, 1),
    ("one", "blocks", 4, 5),
    ("groups", "", 3, 9),
    ("one", "blocks", 7, 8),
    ("one", "blocks", 1, 2),
    ("one", "blocks", 5, 6),
    ("one", "blocks", 3, 4),
    ("groups", "", 9, 12),
    ("inner", "blocks", 2, 3),
    ("groups", "", 12, 16),
    ("one", "conv", 4, 5),
    ("one", "conv", 0, 1),
    ("two", "blocks", 2, 3),
    ("one", "blocks", 6, 7),
    ("leave", "", 0, 1),
    ("one", "conv", 5, 6),
    ("one", "small", 3, 4),
    ("two", "blocks", 1, 2),
    ("one", "conv", 2, 3),
    ("one", "small", 2, 3),
    ("one", "small", 1, 2),
    ("inner", "small", 2, 3),
    ("edge", "blocks", 0, 1),
    ("one", "small", 6, 7),
    ("one", "conv", 1, 2),
    ("two", "blocks", 3, 4),
    ("edge", "blocks", 1, 2),
    ("inner", "blocks", 0, 1),
    ("one", "conv", 3, 4),
    ("one", "small", 0, 1),
    ("inner", "blocks", 1, 2),
    ("one", "small", 5, 6),
    ("one", "conv", 7, 8),
    ("edge", "blocks", 2, 3),
    ("end", "blocks", 0, 1),
    ("one", "small", 4, 5),
    ("one", "conv", 6, 7),
    ("two", "small", 3, 4),
    ("two", "small", 0, 1),
    ("rows", "", 0, 1),
    ("two", "conv", 0, 4),
    ("edge", "conv", 0, 1),
    ("inner", "conv", 0, 1),
    ("two", "small", 1, 2),
    ("inner", "conv", 2, 3),
    ("edge", "small", 0, 1),
    ("two", "small", 2, 3),
    ("edge", "conv", 1, 2),
    ("one", "small", 7, 8),
    ("inner", "small", 0, 1),
    ("edge", "small", 1, 2),
    ("inner", "small", 1, 2),
    ("edge", "conv", 2, 3),
    ("inner", "conv", 1, 2),
    ("edge", "small", 2, 3),
    ("end", "small", 0, 1),
    ("take", "", 0, 1),
    ("end", "conv", 0, 1),
    ("sides", "", 0, 1),
)


GATHER_PLAN = (
    ("step", "small", 0),
    ("step", "blocks", 0),
    ("step", "conv", 0),
    ("enter", "", 0),
    ("step", "small", 1),
    ("step", "conv", 1),
    ("step", "blocks", 1),
    ("step", "small", 2),
    ("step", "conv", 2),
    ("step", "blocks", 2),
    ("step", "small", 3),
    ("step", "conv", 3),
    ("stats", "", 0),
    ("step", "small", 4),
    ("step", "conv", 4),
    ("step", "conv", 5),
    ("step", "small", 5),
    ("step", "blocks", 3),
    ("core", "conv", 0),
    ("core", "small", 0),
    ("compute", "", 0),
    ("compute", "", 1),
    ("compute", "", 2),
    ("compute", "", 3),
    ("step", "blocks", 4),
    ("compute", "", 4),
    ("step", "blocks", 5),
    ("step", "blocks", 6),
    ("step", "conv", 6),
    ("step", "small", 6),
)


def roots_kernel(sizes, members, *refs):
    (
        whole, gram, stat, square_in, update_out, square_out,
        big, m0, m0b, m1, m1b, s1, s1b, s2b, s3, s3b, root, mixed,
        group_box, dp_box, group_send, group_recv, dp_send, dp_recv,
        mixed_send, mixed_recv, update_send, update_recv, update_own,
    ) = refs
    place = Place(*sizes)
    owners = Owners(place, members)
    dp_size, rows = place.dp_size, D // place.dp_size
    me, c_mate = (place.dp, place.group), place.at(place.z, 0, 0, 1)
    owner = owners.here
    tile = 256
    greet(place)

    def remote(source, target, send, recv, device):
        return pltpu.make_async_remote_copy(
            src_ref=source,
            dst_ref=target,
            send_sem=send,
            recv_sem=recv,
            device_id=device,
            device_id_type=MESH,
        )

    def each_other(size, mine, action):
        for other in range(size):
            pl.when(mine != other)(functools.partial(action, other))

    def group_copy(other, slot):
        return remote(
            group_box.at[slot], group_box.at[slot], group_send.at[other], group_recv.at[slot], (place.dp, other)
        )

    def dp_copy(other, slot):
        return remote(dp_box.at[slot], dp_box.at[slot], dp_send.at[other], dp_recv.at[slot], (other, place.group))

    group_box[place.group] = square_in[...]
    each_other(place.group_size, place.group, lambda other: group_copy(other, place.group).start())

    def product_rows(one, two, then):
        def step(index, _):
            at = pl.ds(pl.multiple_of(index * tile, tile), tile)
            then(at, jnp.dot(one[at, :], two[...], preferred_element_type=jnp.float32))
            return 0

        lax.fori_loop(0, D // tile, step, 0)

    def group_wait(other):
        group_copy(other, place.group).wait_send()
        group_copy(other, other).wait_recv()

    each_other(place.group_size, place.group, group_wait)
    total = group_box[0]
    for other in range(1, place.group_size):
        total = total + group_box[other]
    dp_box[place.dp] = total
    each_other(dp_size, place.dp, lambda other: dp_copy(other, place.dp).start())

    def dp_wait(other):
        dp_copy(other, place.dp).wait_send()
        dp_copy(other, other).wait_recv()

    each_other(dp_size, place.dp, dp_wait)
    total = dp_box[0]
    for other in range(1, dp_size):
        total = total + dp_box[other]
    square_out[...] = total

    @pl.when(owner)
    def _():
        factor = jnp.minimum(1.0, max_norm / (jnp.sqrt(total[0:1, 0:1]) + 1e-06))
        square_factor = factor * factor
        spread_f = (1 - stat_decay) * square_factor

        def diagonal(at_start, shape):
            row = lax.broadcasted_iota(jnp.int32, shape, 0) + at_start
            return row == lax.broadcasted_iota(jnp.int32, shape, 1)

        def each_tile(action, carry):
            def step(index, carry):
                start = pl.multiple_of(index * tile, tile)
                return action(pl.ds(start, tile), start, carry)

            return lax.fori_loop(0, D // tile, step, carry)

        def renew(at, start, trace):
            value = stat_decay * stat[at, :].astype(jnp.float32) + spread_f * gram[at, :].astype(
                jnp.float32
            )
            big[at, :] = value
            on = jnp.where(diagonal(start, value.shape), value, 0.0)
            return trace + jnp.sum(jnp.sum(on, 1, keepdims=True), 0, keepdims=True)

        trace = each_tile(renew, jnp.zeros((1, 1), jnp.float32))
        damping = 0.0001 * (trace / D)

        def damp(at, start, total):
            value = big[at, :]
            value = value + jnp.where(diagonal(start, value.shape), damping, 0.0)
            big[at, :] = value
            return total + jnp.sum(jnp.sum(value * value, 1, keepdims=True), 0, keepdims=True)

        magnitude = jnp.sqrt(each_tile(damp, jnp.zeros((1, 1), jnp.float32)))

        def scale(at, start, carry):
            value = big[at, :] / magnitude
            m0[at, :] = value
            m0b[at, :] = value.astype(jnp.bfloat16)
            return carry

        each_tile(scale, 0)
        a = 1.5625

        def square_of(source):
            def then(at, value):
                value = value * 0.0625 - 0.625 * source[at, :]
                s1[at, :] = value
                s1b[at, :] = value.astype(jnp.bfloat16)

            return then

        def fourth(at, value):
            s2b[at, :] = (value + (2 * a) * s1[at, :]).astype(jnp.bfloat16)

        product_rows(m0b, m0b, square_of(m0))
        product_rows(s1b, s1b, fourth)

        def next_one(at, value):
            value = value + (a * a) * m0[at, :]
            m1[at, :] = value
            m1b[at, :] = value.astype(jnp.bfloat16)

        product_rows(s2b, m0b, next_one)

        def joined(at, value):
            value = value * 0.0625 - 0.3125 * (m0[at, :] + m1[at, :])
            s3[at, :] = value
            s3b[at, :] = value.astype(jnp.bfloat16)

        product_rows(m0b, m1b, joined)
        product_rows(m1b, m1b, square_of(m1))
        product_rows(s1b, s1b, fourth)

        def next_two(at, value):
            value = value + (a * a) * m1[at, :]
            m0[at, :] = value
            m0b[at, :] = value.astype(jnp.bfloat16)

        product_rows(s2b, m1b, next_two)
        outer = lax.rsqrt(jnp.sqrt(magnitude))

        def final(at, value):
            value = 1.25 * s3[at, :] - (0.25 * a) * m0[at, :] - 0.25 * value
            start = at.start
            value = value + jnp.where(diagonal(start, value.shape), 1.25 * a, 0.0)
            root[at, :] = (value * outer).astype(jnp.bfloat16)

        product_rows(s3b, m0b, final)

    def mixed_copy():
        return remote(mixed, mixed, mixed_send, mixed_recv, c_mate)

    def update_copy(other):
        spot = pl.ds(pl.multiple_of(other * rows, rows), rows)
        return remote(
            m1b.at[spot],
            update_out.at[owners.member],
            update_send.at[other],
            update_recv.at[owners.member],
            (other, owners.group),
        )

    def update_local():
        spot = pl.ds(pl.multiple_of(place.dp * rows, rows), rows)
        return pltpu.make_async_copy(m1b.at[spot], update_out.at[owners.member], update_own)

    @pl.when(owner & (place.core == 0))
    def _():
        def keep(at, value):
            mixed[at, :] = value.astype(jnp.bfloat16)

        product_rows(root, whole, keep)
        mixed_copy().start()
        mixed_copy().wait_send()

    @pl.when(owner & (place.core == 1))
    def _():
        mixed_copy().wait_recv()

        def keep(at, value):
            m1b[at, :] = value.astype(jnp.bfloat16)

        product_rows(mixed, root, keep)
        for other in range(dp_size):
            owners.to_rows(other, lambda other: update_copy(other).start(), lambda: update_local().start())
        for other in range(dp_size):
            owners.to_rows(other, lambda other: update_copy(other).wait_send(), lambda: update_local().wait())

    for member in range(members):

        @pl.when((place.dp != owners.of(member)) | (place.core != 1))
        def _(member=member):
            remote(
                m1b.at[pl.ds(0, rows)],
                update_out.at[member],
                update_send.at[0],
                update_recv.at[member],
                me,
            ).wait_recv()


def shampoo_roots(sizes, members, whole, gram, stat, square):
    dp_size, group_size = sizes
    rows = D // dp_size
    low, full = jnp.bfloat16, jnp.float32
    dma = pltpu.SemaphoreType.DMA
    half, word = pltpu.VMEM((D, D), low), pltpu.VMEM((D, D), full)
    return pl.pallas_call(
        functools.partial(roots_kernel, sizes, members),
        out_shape=[
            jax.ShapeDtypeStruct((members, rows, D), low),
            jax.ShapeDtypeStruct((8, 128), full),
        ],
        in_specs=[VMEM] * 4,
        out_specs=[VMEM] * 2,
        scratch_shapes=[word, word, half, word, half, word, half, half, word, half, half, half]
        + [pltpu.VMEM((group_size, 8, 128), full), pltpu.VMEM((dp_size, 8, 128), full)]
        + [dma((group_size,))] * 2
        + [dma((dp_size,))] * 2
        + [dma, dma]
        + [dma((dp_size,)), dma((members,)), dma],
        name="shampoo_roots",
        compiler_params=pltpu.CompilerParams(
            collective_id=2, has_side_effects=True, vmem_limit_bytes=VMEM_LIMIT
        ),
    )(whole, gram, stat, square)


def finish_kernel(rates, *refs):
    square, rows, block_sum, small, kernel, sides, update = refs[:7]
    weights, blocks, statistics = refs[7:25], refs[25], refs[26]
    norm_out, outs = refs[27], refs[28:46]
    block_out, stat_out, blocks_out = refs[46:]
    norm = jnp.sqrt(square[0:1, 0:1])
    norm_out[...] = norm
    factor = jnp.minimum(1.0, max_norm / (norm + 1e-06))

    def renew(index, at, grad):
        rate, decay = rates[index]
        ins, out = weights[3 * index : 3 * index + 3], outs[3 * index : 3 * index + 3]
        result = adamw(ins[0][at], grad * factor, ins[1][at], ins[2][at], rate, decay)
        for ref, value in zip(out, result):
            ref[at] = value

    width = weights[0].shape[1]
    vector_rows = weights[6].shape[0]
    renew(0, ..., rows[LOSS_ROW + 1 : LOSS_ROW + 3, :width])
    renew(1, (slice(None), slice(0, 128)), small[0:64, :])
    renew(1, (slice(None), slice(128, 192)), small[64:128, 0:64])
    renew(2, ..., rows[0:vector_rows, :])
    runs, steps, c, channels = weights[9].shape
    for offset in range(steps):
        parts = [kernel[group, offset * c : (offset + 1) * c, :] for group in range(channels // c)]
        renew(
            3,
            (slice(None), offset),
            jnp.concatenate(parts, 0).T.reshape(runs, c, channels),
        )
    renew(4, ..., small[128:224, :].T[0:64])
    renew(5, ..., small[224:256, 0:CLUSTER_ROWS])
    for member in range(blocks.shape[0]):
        block_out[member] = block_sum[member] * factor
        step = update[member].astype(jnp.float32) * factor + decay_weight * blocks[member]
        blocks_out[member] = blocks[member] - rate_shampoo * step
        for side in range(2):
            spread = (1 - stat_decay) * factor * factor
            stat_out[member, side] = stat_decay * statistics[member, side] + spread * sides[
                member, side
            ].astype(jnp.float32)


def finish(sums, weights, blocks, statistics):
    full = jnp.float32
    rates = [(rate_vector, 0.0), (rate_matrix, decay_weight), (rate_vector, 0.0)]
    rates += [(rate_matrix, decay_weight)] * 3
    operands = [*sums, *weights, blocks, statistics]
    shapes = [(1, 1)] + [weight.shape for weight in weights]
    shapes += [blocks.shape, statistics.shape, blocks.shape]
    return pl.pallas_call(
        functools.partial(finish_kernel, rates),
        out_shape=[jax.ShapeDtypeStruct(shape, full) for shape in shapes],
        in_specs=[VMEM] * len(operands),
        out_specs=[VMEM] * len(shapes),
        name="finish",
        compiler_params=pltpu.CompilerParams(vmem_limit_bytes=VMEM_LIMIT),
    )(*operands)


def conv_to_shard(weight):
    taps, c, channels = weight.shape
    split = weight.reshape(taps // STRIDE, STRIDE, c, channels // c, c)
    return split.transpose(3, 1, 4, 0, 2).reshape(channels // c, STRIDE * c, taps // STRIDE * c)


def conv_from_shard(shard):
    groups, rows, columns = shard.shape
    c = rows // STRIDE
    split = shard.reshape(groups, STRIDE, c, columns // c, c)
    return split.transpose(3, 1, 4, 0, 2).reshape(columns // c * STRIDE, c, groups * c)


def pack_small(projection, head, clusters, note):
    lead, kind = projection.shape[:-2], projection.dtype
    notes = jnp.broadcast_to(note, lead + (32, 2)).astype(kind)
    return jnp.concatenate(
        [
            projection[..., :128],
            jnp.concatenate([projection[..., 128:], jnp.zeros(lead + (64, 64), kind)], -1),
            jnp.concatenate([head, jnp.zeros(lead + (96, 64), kind)], -1),
            jnp.concatenate([jnp.swapaxes(clusters, -1, -2), notes], -1),
        ],
        -2,
    )


def unpack_small(packed):
    projection = jnp.concatenate([packed[..., :64, :], packed[..., 64:128, :64]], -1)
    head = packed[..., 128:224, :64]
    clusters = jnp.swapaxes(packed[..., 224:, :CLUSTER_ROWS], -1, -2)
    return projection, head, clusters


def pack_whole(projection, head, clusters, note):
    def cut(values, down, across):
        rows, columns = values.shape
        return values.reshape(down, rows // down, across, columns // across).transpose(0, 2, 1, 3)

    return pack_small(
        cut(projection, 8, 4), cut(head, 8, 4), cut(clusters, 4, 8).transpose(1, 0, 2, 3), note
    )


def unpack_whole(packed):
    def join(values):
        down, across, rows, columns = values.shape
        return values.transpose(0, 2, 1, 3).reshape(down * rows, across * columns)

    projection, head, clusters = unpack_small(packed)
    return join(projection), join(head), join(clusters.transpose(1, 0, 2, 3))


def parts_of_rows(rows, vector_rows, width):
    return rows[:vector_rows], rows[vector_rows + 1 : vector_rows + 3, :width], rows[vector_rows, 0]


CLUSTER_ROWS = 126
SMALL = ((64, 192), (96, 64), (CLUSTER_ROWS, 32))


def body(
    sizes,
    features,
    span_starts,
    labels,
    feature_norm,
    feature_first,
    feature_second,
    projection,
    projection_first,
    projection_second,
    vectors,
    vector_first,
    vector_second,
    conv_weight,
    conv_first,
    conv_second,
    head,
    head_first,
    head_second,
    clusters,
    cluster_first,
    cluster_second,
    blocks,
    statistics,
):
    dp_size, group_size = sizes
    members, rows = blocks.shape[0], blocks.shape[1]
    masks = jax.vmap(jax.vmap(frame_mask))(span_starts)
    local_count = jnp.sum(masks)
    fast = (
        rows % 16 == 0
        and dp_size % 2 == 0
        and group_size == 4
        and dp_size >= 2 * members
        and (projection.shape, head.shape, clusters.shape) == SMALL
        and conv_weight.shape[2] % conv_weight.shape[1] == 0
        and masks.size <= 256
    )
    frames, vector_rows, width = masks.size, vectors.shape[0], feature_norm.shape[1]
    flat = features.reshape(frames, -1)

    def runs(values):
        return values.reshape((-1, STRIDE) + values.shape[1:])

    if fast:
        taps, c, channels = conv_weight.shape
        taps *= group_size
        shapes = [
            (channels // c, STRIDE * c, taps // group_size // STRIDE * c),
            (256, 128),
            blocks.shape,
        ]
        raw = (
            span_starts.reshape(-1, span_starts.shape[-1]),
            projection, runs(conv_weight), head.T, clusters.T, blocks, statistics,
        )
        kernel_w, small_w, blocks_w, stat_whole, *saved, mask = gather_weights(
            sizes, shapes, taps, raw, flat, feature_norm, vectors
        )
    else:
        proj_w, kernel_full, head_w, clusters_w, blocks_w = gather_plain(
            projection, conv_weight, head, clusters, blocks
        )
        whole = conv_to_shard(kernel_full)
        kernel_w = whole.reshape(whole.shape[:2] + (4, -1)).transpose(2, 0, 1, 3)
        count = lax.psum(local_count, ("dp", "group"))
        high = jnp.floor(count / 256.0) * 256.0
        notes = jnp.concatenate([jnp.stack([high, count - high]), jnp.zeros(30, jnp.float32)])
        small_w = pack_whole(proj_w, head_w, clusters_w, notes.reshape(8, 4, 1, 1))
        taps = kernel_w.shape[0] * kernel_w.shape[3] // (D // kernel_w.shape[1]) * STRIDE
        mask = masks.reshape(frames, 1)
        saved = front(flat, mask, feature_norm, vectors, small_w, kernel_w, taps)
    feature_unit, normed, hidden_t, encoded, encoder_unit, encoder_inverse, slope = saved
    targets = labels.reshape(frames, 1)
    encoded_grad, block_part, head_part, center_part, trunk_rows, counted = trunk(
        encoded, mask, targets + targets // CLUSTER_ROWS * 2, vectors, small_w, blocks_w
    )
    masked_count = counted[0, 0]
    operands = (
        encoded_grad, mask, vectors, small_w, feature_unit, normed, hidden_t,
        encoder_unit, encoder_inverse, slope, trunk_rows, head_part, center_part, kernel_w,
    )
    if fast:
        kernel_sum, small_sum, block_sum, extra, square, whole, gram, sides = back_reduce(
            sizes, shapes, taps, operands, block_part
        )
        update_rows, square = shampoo_roots(sizes, members, whole, gram, stat_whole, square)

        done = finish(
            (square, extra, block_sum, small_sum, kernel_sum, sides, update_rows),
            (
                feature_norm, feature_first, feature_second,
                projection, projection_first, projection_second,
                vectors, vector_first, vector_second,
                runs(conv_weight), runs(conv_first), runs(conv_second),
                head.T, head_first.T, head_second.T,
                clusters.T, cluster_first.T, cluster_second.T,
            ),
            blocks,
            statistics,
        )
        outs = []
        for index in range(0, 18, 3):
            parts = done[1 + index : 4 + index]
            if index == 9:
                parts = [part.reshape(conv_weight.shape) for part in parts]
            if index >= 12:
                parts = [part.T for part in parts]
            outs += parts
        return (extra[LOSS_ROW, 0], masked_count, done[0][0, 0], *outs, *done[19:])
    kernel_part, small_part, row_part = back(taps, operands)
    proj_part, head_part, center_part = unpack_whole(small_part)
    kernel_plain = conv_from_shard(
        kernel_part.transpose(1, 2, 0, 3).reshape(kernel_part.shape[1:3] + (-1,))
    )
    large_total = reduce_grads(
        tuple(
            part.astype(jnp.float32)
            for part in (proj_part, kernel_plain, head_part, center_part, block_part)
        )
    )
    vector_grad, feature_grad, loss_sum = parts_of_rows(
        lax.psum(row_part, ("dp", "group")), vector_rows, width
    )
    local_squares = sum((jnp.sum(part * part) for part in large_total))
    norm_square = (
        lax.psum(local_squares, ("dp", "group"))
        + jnp.sum(feature_grad * feature_grad)
        + jnp.sum(vector_grad * vector_grad)
    )
    grad_norm = jnp.sqrt(norm_square)
    factor = jnp.minimum(1.0, max_norm / (grad_norm + 1e-06))
    proj_grad, kernel_grad, head_grad, cluster_grad, block_rows = [
        part * factor for part in large_total
    ]
    feature_out = adamw(
        feature_norm, feature_grad * factor, feature_first, feature_second, rate_vector, 0.0
    )
    projection_out = adamw(
        projection, proj_grad, projection_first, projection_second, rate_matrix, decay_weight
    )
    vector_out = adamw(vectors, vector_grad * factor, vector_first, vector_second, rate_vector, 0.0)
    conv_out = adamw(conv_weight, kernel_grad, conv_first, conv_second, rate_matrix, decay_weight)
    head_out = adamw(head, head_grad, head_first, head_second, rate_matrix, decay_weight)
    cluster_out = adamw(
        clusters, cluster_grad, cluster_first, cluster_second, rate_matrix, decay_weight
    )
    statistics_new, update_rows = shampoo_plain(block_rows, statistics)
    blocks_new = blocks - rate_shampoo * (update_rows + decay_weight * blocks)
    return (
        loss_sum,
        masked_count,
        grad_norm,
        *feature_out,
        *projection_out,
        *vector_out,
        *conv_out,
        *head_out,
        *cluster_out,
        block_rows,
        statistics_new,
        blocks_new,
    )


def solution(mesh):
    in_specs = (
        P(None, ("dp", "group"), None, None),
        P(None, ("dp", "group"), None),
        P(None, ("dp", "group"), None),
        P(),
        P(),
        P(),
        P("dp", "group"),
        P("dp", "group"),
        P("dp", "group"),
        P(),
        P(),
        P(),
        P("group", None, "dp"),
        P("group", None, "dp"),
        P("group", None, "dp"),
        P("dp", "group"),
        P("dp", "group"),
        P("dp", "group"),
        P("group", "dp"),
        P("group", "dp"),
        P("group", "dp"),
        P("group", "dp", None),
        P("group", None, "dp", None),
    )
    out_specs = (
        P(),
        P(),
        P(),
        P(),
        P(),
        P(),
        P("dp", "group"),
        P("dp", "group"),
        P("dp", "group"),
        P(),
        P(),
        P(),
        P("group", None, "dp"),
        P("group", None, "dp"),
        P("group", None, "dp"),
        P("dp", "group"),
        P("dp", "group"),
        P("dp", "group"),
        P("group", "dp"),
        P("group", "dp"),
        P("group", "dp"),
        P("group", "dp", None),
        P("group", None, "dp", None),
        P("group", "dp", None),
    )
    return jax.shard_map(
        functools.partial(body, (mesh.shape["dp"], mesh.shape["group"])), mesh=mesh, in_specs=in_specs, out_specs=out_specs, check_vma=False)
```

```python
import functools

import jax
import jax.numpy as jnp
from jax import lax
from jax.experimental import pallas as pl
from jax.experimental.pallas import tpu as pltpu
from jax.sharding import PartitionSpec as P

D = 768
HEADS = 12
HEAD = 64
TAPS = 128
CLIP = 128
SPAN = 10
NEWTON = 3
STEP = 10


HIGH = lax.Precision.HIGHEST
beta_one = 0.9
beta_two = 0.98
adam_eps = 1e-08
rate_matrix = 0.02
rate_vector = 0.5
rate_shampoo = 0.2
decay_weight = 0.01
stat_decay = 0.95
max_norm = 0.01
inv_temp = 10.0
STRIDE = 4


def for_sending(array):

    def short(part):
        return part.astype(jnp.bfloat16) if part.dtype == jnp.float32 else part

    return jax.tree.map(short, array)


def spread_2(array, axis, root):
    mine = lax.axis_index(axis) == root
    return lax.psum(jnp.where(mine, array, jnp.zeros_like(array)), axis)


def to_low(values):
    return values.astype(jnp.bfloat16)


def frame_mask(starts):
    frames = jnp.arange(CLIP, dtype=jnp.int32)[:, None]
    inside = (frames >= starts[None, :]) & (frames < starts[None, :] + SPAN)
    return jnp.any(inside, axis=1).astype(jnp.float32)


def inverse_root(matrix):
    size = matrix.shape[0]
    identity = jnp.eye(size, dtype=jnp.float32)
    damped = matrix + 0.0001 * (jnp.trace(matrix) / size) * identity
    magnitude = jnp.sqrt(jnp.sum(damped * damped))
    current = damped / magnitude
    result = identity * magnitude ** (-0.25)
    for sweep in range(NEWTON):
        factor = (5.0 * identity - current) * 0.25
        result = jnp.dot(result, factor, precision=HIGH)
        square = jnp.dot(factor, factor, precision=HIGH)
        current = jnp.dot(jnp.dot(square, square, precision=HIGH), current, precision=HIGH)
    return result


def adamw(weight, grad, first, second, rate, decay):
    first = beta_one * first + (1 - beta_one) * grad
    second = beta_two * second + (1 - beta_two) * grad * grad
    corrected = first / (1 - beta_one**STEP)
    scaled = jnp.sqrt(second / (1 - beta_two**STEP)) + adam_eps
    return (first, second, weight - rate * (corrected / scaled + decay * weight))


def reduce_grads(parts):
    proj_part, kernel_part, head_part, center_part, block_part = parts
    grouped = (
        lax.psum_scatter(proj_part, "group", scatter_dimension=1, tiled=True),
        lax.psum_scatter(kernel_part, "group", scatter_dimension=0, tiled=True),
        lax.psum_scatter(head_part, "group", scatter_dimension=1, tiled=True),
        lax.psum_scatter(center_part, "group", scatter_dimension=0, tiled=True),
        lax.psum_scatter(block_part, "group", scatter_dimension=0, tiled=True),
    )
    proj_part, kernel_part, head_part, center_part, block_part = grouped
    return (
        lax.psum_scatter(proj_part, "dp", scatter_dimension=0, tiled=True),
        lax.psum_scatter(kernel_part, "dp", scatter_dimension=2, tiled=True),
        lax.psum_scatter(head_part, "dp", scatter_dimension=0, tiled=True),
        lax.psum_scatter(center_part, "dp", scatter_dimension=1, tiled=True),
        lax.psum_scatter(block_part, "dp", scatter_dimension=1, tiled=True),
    )


def gather_plain(projection, conv_weight, head, clusters, blocks):
    gathered = (
        lax.all_gather(to_low(projection), "dp", axis=0, tiled=True),
        lax.all_gather(to_low(conv_weight), "dp", axis=2, tiled=True),
        lax.all_gather(to_low(head), "dp", axis=0, tiled=True),
        lax.all_gather(to_low(clusters), "dp", axis=1, tiled=True),
        lax.all_gather(to_low(blocks), "dp", axis=1, tiled=True),
    )
    proj_part, kernel_part, head_part, center_part, block_part = gathered
    return (
        lax.all_gather(proj_part, "group", axis=1, tiled=True),
        lax.all_gather(kernel_part, "group", axis=0, tiled=True),
        lax.all_gather(head_part, "group", axis=1, tiled=True),
        lax.all_gather(center_part, "group", axis=0, tiled=True),
        lax.all_gather(block_part, "group", axis=0, tiled=True),
    )


def shampoo_plain(block_rows, statistics):
    full_blocks = lax.all_gather(block_rows.astype(jnp.bfloat16), "dp", axis=1, tiled=True).astype(
        block_rows.dtype
    )
    rows = block_rows.shape[1]
    here = lax.axis_index("dp")
    first_row = here * rows
    column_slice = lax.dynamic_slice_in_dim(full_blocks, first_row, rows, 2)
    left_rows = stat_decay * statistics[:, 0] + (1 - stat_decay) * jnp.einsum(
        "brk,bck->brc", block_rows, full_blocks, precision=HIGH
    )
    right_rows = stat_decay * statistics[:, 1] + (1 - stat_decay) * jnp.einsum(
        "bkr,bkc->brc", column_slice, full_blocks, precision=HIGH
    )
    group_blocks = block_rows.shape[0]
    dp_size = lax.axis_size("dp")
    owners = [
        (2 * member + side) * dp_size // (2 * group_blocks)
        for member in range(group_blocks)
        for side in range(2)
    ]
    left_full, right_full = (
        lax.all_gather(left_rows.astype(jnp.bfloat16), "dp", axis=1, tiled=True).astype(
            left_rows.dtype
        ),
        lax.all_gather(right_rows.astype(jnp.bfloat16), "dp", axis=1, tiled=True).astype(
            right_rows.dtype
        ),
    )
    sources = [
        left_full[member] if side == 0 else right_full[member]
        for member in range(group_blocks)
        for side in range(2)
    ]
    roots = []
    for index in range(2 * group_blocks):
        owner = owners[index]
        root = lax.cond(here == owner, inverse_root, jnp.zeros_like, sources[index])
        root = spread_2(for_sending(root), "dp", owner).astype(root.dtype)
        roots.append(root)
    stacked = jnp.stack(roots).reshape(group_blocks, 2, D, D)
    left_root_rows = lax.dynamic_slice_in_dim(stacked[:, 0], first_row, rows, 1)
    update_rows = jnp.einsum(
        "brk,bkc->brc",
        jnp.einsum("brk,bkc->brc", left_root_rows, full_blocks, precision=HIGH),
        stacked[:, 1],
        precision=HIGH,
    )
    return jnp.stack([left_rows, right_rows], 1), update_rows


MESH = pl.DeviceIdType.MESH
HBM = pl.BlockSpec(memory_space=pltpu.HBM)
VMEM = pl.BlockSpec(memory_space=pltpu.VMEM)
VMEM_LIMIT = 60 * 1024 * 1024


class Place:
    def __init__(self, dp_size, group_size):
        self.dp_size, self.group_size = dp_size, group_size
        self.lines = dp_size // 2
        self.dp, self.group = lax.axis_index("dp"), lax.axis_index("group")
        self.z, self.y = self.dp // 2, self.dp % 2
        self.x, self.core = self.group // 2, self.group % 2

    def at(self, z, flip_y=0, flip_x=0, flip_core=0):
        y = self.y + flip_y * (1 - 2 * self.y)
        x = self.x + flip_x * (1 - 2 * self.x)
        core = self.core + flip_core * (1 - 2 * self.core)
        return (z * 2 + y, x * 2 + core)

    def near(self, z, p, q):
        return self.at(z, p * (1 - self.core) + q * self.core, q * (1 - self.core) + p * self.core)

    def across(self, z, p, q):
        return self.at(z, p * self.core + q * (1 - self.core), q * self.core + p * (1 - self.core), 1)


def greet(place):
    barrier = pltpu.get_barrier_semaphore()
    first = place.x * 2
    for other in range(place.dp_size):
        for core in range(2):

            @pl.when((place.dp != other) | (place.core != core))
            def _():
                pl.semaphore_signal(
                    barrier, inc=1, device_id=(other, first + core), device_id_type=MESH
                )

    for core in range(2):
        pl.semaphore_signal(
            barrier,
            inc=1,
            device_id=(place.dp, (1 - place.x) * 2 + core),
            device_id_type=MESH,
        )
    pl.semaphore_wait(barrier, 2 * place.dp_size - 1 + 2)


def guarded(condition, action):
    if condition is None:
        action()
    else:
        pl.when(condition)(action)


def both(one, two):
    if one is None:
        return two
    if two is None:
        return one
    return one & two


def piece_at(kind, ref, dp, group, shape):
    if kind == "blocks":
        start = pl.multiple_of(dp * shape[1], shape[1])
        return ref.at[pl.ds(group * shape[0], shape[0]), pl.ds(start, shape[1])]
    if kind == "conv":
        return ref.at[group, pl.ds(dp * shape[0], shape[0])]
    return ref.at[dp, group]


KINDS = ("conv", "small", "blocks")


def make_shards(refs, mask, conv, small, blocks_low, stats_low):
    starts, projection, weight, head_t, clusters_t, blocks, statistics = refs
    for clip in range(starts.shape[0]):
        frame = lax.broadcasted_iota(jnp.int32, (CLIP, starts.shape[1]), 0)
        begins = starts[clip : clip + 1, :]
        inside = ((frame >= begins) & (frame < begins + SPAN)).astype(jnp.float32)
        mask[clip * CLIP : (clip + 1) * CLIP, :] = jnp.max(inside, 1, keepdims=True)
    note = jnp.sum(mask[...], 0, keepdims=True)
    runs, steps, c, channels = weight.shape
    for offset in range(steps):
        turned = weight[:, offset].reshape(runs * c, channels).T.astype(jnp.bfloat16)
        for group in range(channels // c):
            conv[group, offset * c : (offset + 1) * c, :] = turned[group * c : (group + 1) * c]
    low = jnp.bfloat16

    def padded(values):
        spare = jnp.zeros((values.shape[0], 128 - values.shape[1]), jnp.float32)
        return jnp.concatenate([values, spare], 1)

    small[0:64, :] = projection[:, 0:128].astype(low)
    small[64:128, :] = padded(projection[:, 128:]).astype(low)
    small[128:224, :] = padded(head_t[...].T).astype(low)
    lane = lax.broadcasted_iota(jnp.int32, (32, 128), 1)
    small[224:256, :] = jnp.where(lane < CLUSTER_ROWS, padded(clusters_t[...]), note).astype(low)
    blocks_low[...] = blocks[...].astype(low)
    stats_low[...] = statistics[...].astype(low)


def gather_kernel(sizes, shapes, taps, *refs):
    place = Place(*sizes)
    count = len(KINDS)
    refs = list(refs)

    def pull(number):
        taken = refs[:number]
        del refs[:number]
        return taken

    raw, (features, feature_norm, vectors) = pull(7), pull(3)
    outs, (stats_out,), results, (mask,) = pull(count), pull(1), pull(7), pull(1)
    ins, (stats_in, small_here), scratch = pull(count), pull(2), pull(5)
    (send_sem, recv_sem, own_sem, stat_send, stat_recv, stat_own, small_sem) = pull(7)
    z, last = place.z, place.lines - 1
    me = (place.dp, place.group)
    make_shards(raw, mask, *ins, stats_in)
    greet(place)
    sent = []
    slots = [0] * count
    conv, tiny = KINDS.index("conv"), KINDS.index("small")
    enter, project, convolve, leave = front_compute(
        taps,
        (features, mask, feature_norm, vectors, small_here, outs[conv]),
        results,
        scratch,
    )

    def view(k, source):
        return piece_at(KINDS[k], outs[k], source[0], source[1], shapes[k])

    def identity(source):
        return source[0] * place.group_size + source[1]

    def copy_of(k, source, target, slot, own=False):
        spot = view(k, source)
        return pltpu.make_async_remote_copy(
            src_ref=ins[k] if own else spot,
            dst_ref=spot,
            send_sem=send_sem.at[k, slot],
            recv_sem=recv_sem.at[k, identity(source)],
            device_id=target,
            device_id_type=MESH,
        )

    def send(k, source, target, condition=None, own=False):
        slot = slots[k]
        slots[k] += 1
        guarded(condition, lambda: copy_of(k, source, target, slot, own).start())
        sent.append((k, source, target, slot, condition, own))

    def arrive(k, source, condition=None):
        guarded(condition, lambda: copy_of(k, source, me, 0).wait_recv())

    links = {
        "left": (place.at(z - 1), z > 0),
        "right": (place.at(z + 1), z < last),
        "p": (place.near(z, 1, 0), None),
        "q": (place.near(z, 0, 1), None),
        "core": (place.at(z, 0, 0, 1), None),
    }

    def forward(k, source, ways, condition=None, own=False):
        for way in ways:
            target, open_way = links[way]
            send(k, source, target, both(condition, open_way), own)

    def spots(offset):
        if offset == 0:
            return [(z, None, ("left", "right"))]
        return [
            (z - offset, z >= offset, ("right",)),
            (z + offset, z + offset <= last, ("left",)),
        ]

    def take(k, source, condition, ways):
        arrive(k, source, condition)
        forward(k, source, ways, condition)

    def step_z_first(k, step):
        if step == 0:
            forward(k, me, ("left", "right", "q", "p", "core"), own=True)
            return
        if step < place.lines:
            for spot, there, ways in spots(step):
                take(k, place.near(spot, 0, 0), there, ways + ("q", "p", "core"))
        if 0 <= step - 1 < place.lines:
            for spot, there, _ in spots(step - 1):
                take(k, place.near(spot, 1, 0), there, ("q", "core"))
                take(k, place.near(spot, 0, 1), there, ("core",))
        if 0 <= step - 2 < place.lines:
            for spot, there, _ in spots(step - 2):
                take(k, place.near(spot, 1, 1), there, ("core",))

    def step_z_second(k, step):
        if step == 0:
            forward(k, me, ("q", "left", "right", "p", "core"), own=True)
            return
        if step == 1:
            take(k, place.near(z, 0, 1), None, ("left", "right", "p", "core"))
        if step < place.lines:
            for spot, there, ways in spots(step):
                take(k, place.near(spot, 0, 0), there, ways + ("p", "core"))
        if 1 <= step - 1 < place.lines:
            for spot, there, ways in spots(step - 1):
                take(k, place.near(spot, 0, 1), there, ways + ("p", "core"))
        if 0 <= step - 1 < place.lines:
            for spot, there, _ in spots(step - 1):
                take(k, place.near(spot, 1, 0), there, ("core",))
        if 0 <= step - 2 < place.lines:
            for spot, there, _ in spots(step - 2):
                take(k, place.near(spot, 1, 1), there, ("core",))

    members = shapes[KINDS.index("blocks")][0]
    rows = shapes[KINDS.index("blocks")][1]

    owners = Owners(place, members)

    def stat_copy(member, side):
        owner = owners.of(member)
        start = pl.multiple_of(place.dp * rows, rows)
        return owner, pltpu.make_async_remote_copy(
            src_ref=stats_in.at[member, side],
            dst_ref=stats_out.at[pl.ds(start, rows)],
            send_sem=stat_send.at[member, side],
            recv_sem=stat_recv.at[place.dp],
            device_id=(owner, place.x * 2 + side),
            device_id_type=MESH,
        )

    def stat_local(member, side):
        start = pl.multiple_of(place.dp * rows, rows)
        return pltpu.make_async_copy(
            stats_in.at[member, side], stats_out.at[pl.ds(start, rows)], stat_own
        )

    def each_stat(remote, local):
        for member in range(members):
            for side in range(2):
                owner = owners.of(member)
                mine = (place.dp == owner) & (place.core == side)
                pl.when(jnp.logical_not(mine))(lambda m=member, s=side: remote(m, s))
                pl.when(mine)(lambda m=member, s=side: local(m, s))

    own_copies = [
        pltpu.make_async_copy(ins[k], view(k, me), own_sem.at[k]) for k in range(count)
    ]
    def from_core(k):
        for spot in range(place.lines):
            for p in range(2):
                for q in range(2):
                    arrive(k, place.across(spot, p, q))

    def read_small():
        copy = pltpu.make_async_copy(outs[tiny], small_here, small_sem)
        copy.start()
        copy.wait()

    def compute(part):
        groups = outs[conv].shape[1]
        if part == 0:
            read_small()
            project()
        elif part < 4:
            convolve(groups * (part - 1) // 3, groups * part // 3)
        else:
            leave()

    for name, kind, step in GATHER_PLAN:
        if name == "step":
            k = KINDS.index(kind)
            (step_z_second if kind == "blocks" else step_z_first)(k, step)
            if step == 0:
                own_copies[k].start()
        elif name == "stats":
            each_stat(
                lambda m, s: stat_copy(m, s)[1].start(), lambda m, s: stat_local(m, s).start()
            )
        elif name == "core":
            from_core(KINDS.index(kind))
            own_copies[KINDS.index(kind)].wait()
        elif name == "enter":
            enter()
        else:
            compute(step)
    from_core(KINDS.index("blocks"))
    own_copies[KINDS.index("blocks")].wait()
    each_stat(lambda m, s: stat_copy(m, s)[1].wait_send(), lambda m, s: stat_local(m, s).wait())

    @pl.when(owners.here)
    def _():
        for other in range(place.dp_size):

            @pl.when((place.dp != other) | (place.group != owners.group))
            def _():
                pltpu.make_async_remote_copy(
                    src_ref=stats_in.at[0, 0],
                    dst_ref=stats_out.at[pl.ds(other * rows, rows)],
                    send_sem=stat_send.at[0, 0],
                    recv_sem=stat_recv.at[other],
                    device_id=me,
                    device_id_type=MESH,
                ).wait_recv()

    for k, source, target, slot, condition, own in sent:
        guarded(
            condition,
            lambda k=k, source=source, target=target, slot=slot, own=own: copy_of(
                k, source, target, slot, own
            ).wait_send(),
        )


def full_shapes(sizes, shapes):
    dp_size, group_size = sizes
    conv, small, blocks = shapes
    return [
        (group_size, dp_size * conv[0]) + conv[1:],
        (dp_size, group_size) + small,
        (group_size * blocks[0], dp_size * blocks[1], blocks[2]),
    ]


def gather_weights(sizes, shapes, taps, raw, features, feature_norm, vectors):
    low, out = jnp.bfloat16, jax.ShapeDtypeStruct
    full = full_shapes(sizes, shapes)
    frames, width = features.shape
    count, devices = len(shapes), sizes[0] * sizes[1]
    members = shapes[-1][0]
    dma = pltpu.SemaphoreType.DMA
    return pl.pallas_call(
        functools.partial(gather_kernel, sizes, shapes, taps),
        out_shape=[out(shape, low) for shape in full]
        + [out((D, D), low)]
        + front_shapes(frames, width)
        + [out((frames, 1), jnp.float32)],
        in_specs=[VMEM] * (len(raw) + 3),
        out_specs=[HBM] * (count + 1) + [VMEM] * 8,
        scratch_shapes=[pltpu.VMEM(shape, low) for shape in shapes]
        + [pltpu.VMEM(raw[-1].shape, low), pltpu.VMEM(full[1], low)]
        + front_scratch(full[0], frames)
        + [
            dma((count, 3 * devices)),
            dma((count, devices)),
            dma((count,)),
            dma((members, 2)),
            dma((sizes[0],)),
            dma,
            dma,
        ],
        name="gather_front",
        compiler_params=pltpu.CompilerParams(
            collective_id=0, has_side_effects=True, vmem_limit_bytes=VMEM_LIMIT
        ),
    )(*raw, features, feature_norm, vectors)


def shift_right(values, by):
    if by == 0:
        return values
    parts = []
    for first in range(0, values.shape[1], CLIP):
        part = values[:, first : first + CLIP]
        lane = lax.broadcasted_iota(jnp.int32, part.shape, 1)
        turned = pltpu.roll(part, by % CLIP, 1)
        inside = lane >= by if by > 0 else lane < CLIP + by
        parts.append(jnp.where(inside, turned, 0.0))
    return jnp.concatenate(parts, 1)


def place_windows(hidden, windows, taps):
    channels = hidden.shape[0]
    runs, half = taps // STRIDE, taps // STRIDE // 2
    for run in range(runs):
        by = STRIDE * (half - 1 - run) if run < half else -STRIDE * (run - half)
        windows[run * channels : (run + 1) * channels, :] = shift_right(hidden, by).astype(
            jnp.bfloat16
        )


def conv_group(hidden, weight_at, windows, taps, shape):
    channels = hidden.shape[0]
    chunks, _, _, chunk = shape
    place_windows(hidden, windows, taps)
    total = None
    for side in range(2):
        part = None
        for index in range(side * chunks // 2, (side + 1) * chunks // 2):
            term = dot(weight_at(index), windows[index * chunk : (index + 1) * chunk, :])
            part = term if part is None else part + term
        for offset in range(STRIDE):
            by = STRIDE - offset if side == 0 else -offset
            moved = shift_right(part[offset * channels : (offset + 1) * channels], by)
            total = moved if total is None else total + moved
    return total


def conv_group_back(hidden, grad, weight_at, put, windows, moved, taps, shape):
    channels = hidden.shape[0]
    chunks, _, _, chunk = shape
    half, runs = taps // STRIDE // 2, chunk // channels
    place_windows(hidden, windows, taps)
    total = None
    for side in range(2):
        for offset in range(STRIDE):
            by = offset - STRIDE if side == 0 else offset
            moved[offset * channels : (offset + 1) * channels, :] = shift_right(grad, by).astype(
                jnp.bfloat16
            )
        for index in range(side * chunks // 2, (side + 1) * chunks // 2):
            put(
                index,
                dot_nt(moved[...], windows[index * chunk : (index + 1) * chunk, :]).astype(
                    jnp.bfloat16
                ),
            )
            turned = dot_tn(weight_at(index), moved[...])
            for step in range(runs):
                run = index * runs + step
                by = -STRIDE * (half - 1 - run) if run < half else STRIDE * (run - half)
                part = shift_right(turned[step * channels : (step + 1) * channels], by)
                total = part if total is None else total + part
    return total


def over_rows(total, tile, action):
    def step(index, _):
        action(pl.ds(pl.multiple_of(index * tile, tile), tile))
        return 0

    lax.fori_loop(0, total // tile, step, 0, unroll=2)


def dot(one, two):
    return jnp.dot(one, two, preferred_element_type=jnp.float32)


def dot_nt(one, two):
    return lax.dot_general(one, two, (((1,), (1,)), ((), ())), preferred_element_type=jnp.float32)


def dot_tn(one, two):
    return lax.dot_general(one, two, (((0,), (0,)), ((), ())), preferred_element_type=jnp.float32)


def norm_parts(values):
    average = jnp.mean(values, -1, keepdims=True)
    centred = values - average
    inverse = lax.rsqrt(jnp.mean(centred * centred, -1, keepdims=True) + 1e-05)
    return centred * inverse, inverse


def norm_back(upstream, unit, inverse, gain):
    scaled = upstream * gain
    along = jnp.mean(scaled * unit, -1, keepdims=True)
    return inverse * (scaled - jnp.mean(scaled, -1, keepdims=True) - unit * along)


def gelu_pair(values):
    below = 0.5 + 0.5 * lax.erf(values * 0.7071067811865476)
    density = jnp.exp(values * values * -0.5) * 0.3989422804014327
    return values * below, below + values * density


def add_row(ref, row, values):
    ref[row : row + 1, :] += jnp.sum(values, 0, keepdims=True)


def front_compute(taps, refs, outs, scratch):
    features, mask, feature_norm, vectors, small, kernel = refs
    feature_unit, normed, hidden_t, encoded, encoder_unit, encoder_inverse, slope = outs
    held, windows, hidden, out_t, load_sem = scratch
    frames = features.shape[0]
    groups = kernel.shape[1]
    channels = hidden_t.shape[0] // groups

    def load(group):
        return pltpu.make_async_copy(kernel.at[:, group], held.at[:, group], load_sem.at[group])

    def enter():
        def one(at):
            unit, _ = norm_parts(features[at, :].astype(jnp.float32))
            feature_unit[at, :] = unit
            scaled = unit * feature_norm[0:1, :] + feature_norm[1:2, :]
            normed[at, :] = scaled.astype(jnp.bfloat16)

        over_rows(frames, 32, one)

    def project():
        for group in range(groups):
            load(group).start()
        normed_t = normed[...].T
        parts, columns = small.shape[0], small.shape[1]
        third = D // columns
        for group in range(columns):
            for first, size in ((0, 128), (128, third - 128)):
                row = first // 2
                part = small[:, group, row : row + 64, :].reshape(parts * 64, 128)
                at = group * third + first
                out_t[at : at + size, :] = dot_tn(part, normed_t)[:size]
        hidden[...] = jnp.where(mask[...] > 0, vectors[0:1, :], out_t[...].T)
        hidden_t[...] = hidden[...].T.astype(jnp.bfloat16)

    def one_group(group, _):
        load(group).wait()
        at = pl.ds(pl.multiple_of(group * channels, channels), channels)
        out_t[at, :] = conv_group(
            hidden_t[at, :].astype(jnp.float32),
            lambda index: held[index, group],
            windows,
            taps,
            kernel.shape,
        )
        return 0

    def convolve(first, last):
        lax.fori_loop(first, last, one_group, 0)

    def leave():
        slope[...] = out_t[...].T

        def one(at):
            active, derivative = gelu_pair(slope[at, :])
            slope[at, :] = derivative
            unit, inverse = norm_parts(hidden[at, :] + active)
            encoder_unit[at, :] = unit
            encoder_inverse[at, :] = inverse
            encoded[at, :] = unit * vectors[1:2, :] + vectors[2:3, :]

        over_rows(frames, 32, one)

    return enter, project, convolve, leave


def front_kernel(taps, *refs):
    enter, project, convolve, leave = front_compute(taps, refs[:6], refs[6:13], refs[13:])
    enter()
    project()
    convolve(0, refs[5].shape[1])
    leave()


def front_shapes(frames, width):
    out, full, low = jax.ShapeDtypeStruct, jnp.float32, jnp.bfloat16
    return [
        out((frames, width), full),
        out((frames, width), low),
        out((D, frames), low),
        out((frames, D), full),
        out((frames, D), full),
        out((frames, 1), full),
        out((frames, D), full),
    ]


def front_scratch(kernel_shape, frames):
    chunks, groups, rows, chunk = kernel_shape
    return [
        pltpu.VMEM(kernel_shape, jnp.bfloat16),
        pltpu.VMEM((chunks * chunk, frames), jnp.bfloat16),
        pltpu.VMEM((frames, D), jnp.float32),
        pltpu.VMEM((D, frames), jnp.float32),
        pltpu.SemaphoreType.DMA((groups,)),
    ]


def front(features, mask, feature_norm, vectors, small, kernel, taps):
    frames, width = features.shape
    return pl.pallas_call(
        functools.partial(front_kernel, taps),
        out_shape=front_shapes(frames, width),
        in_specs=[VMEM] * 5 + [HBM],
        out_specs=[VMEM] * 7,
        scratch_shapes=front_scratch(kernel.shape, frames),
        name="front",
        compiler_params=pltpu.CompilerParams(vmem_limit_bytes=VMEM_LIMIT),
    )(features, mask, feature_norm, vectors, small, kernel)


def trunk_kernel(*refs):
    (
        encoded, mask, labels, vectors, small, blocks,
        encoded_grad, block_grad, head_grad, center_grad_t, rows_out, counted,
        head, table, centers, held, made, low, triple, attention, mixed, unit_one, inverse_one, middle, middle_low,
        active, slope, unit_two, inverse_two, work, work_low, flow_low, triple_grad, turned,
        load_sem, save_sem,
    ) = refs
    frames = encoded.shape[0]
    count = blocks.shape[0]
    ups = (count - 4) // 2
    tile = 32
    pairs = D // 128

    def load(block):
        return pltpu.make_async_copy(blocks.at[block], held.at[block], load_sem.at[block])

    def save(block):
        return pltpu.make_async_copy(made.at[block], block_grad.at[block], save_sem.at[block])

    for block in range(count):
        load(block).start()
    rows_out[...] = jnp.zeros_like(rows_out)
    parts, columns = small.shape[0], small.shape[1]
    notes = small[:, :, 224:240, :].astype(jnp.float32)
    first = lax.broadcasted_iota(jnp.int32, notes.shape, 2) == 0
    first &= lax.broadcasted_iota(jnp.int32, notes.shape, 3) == CLUSTER_ROWS
    notes = jnp.sum(jnp.where(first, notes, 0.0), (0, 1))
    masked = jnp.sum(jnp.sum(notes, 1, keepdims=True), 0, keepdims=True)
    counted[...] = jnp.broadcast_to(masked, counted.shape)

    def to_inputs(at):
        low[at, :] = encoded[at, :].astype(jnp.bfloat16)

    over_rows(frames, tile, to_inputs)

    def first_three(block, _):
        load(block).wait()
        triple[block] = dot(low[...], held[block]).astype(jnp.bfloat16)
        return 0

    lax.fori_loop(0, 3, first_three, 0)
    lane = lax.broadcasted_iota(jnp.int32, (CLIP, 128), 1)
    even = lane < HEAD

    def apart(values):
        zero = jnp.zeros_like(values)
        return jnp.concatenate([jnp.where(even, values, zero), jnp.where(even, zero, values)], 0)

    def beside(values):
        return jnp.concatenate([values[:CLIP], values[CLIP:]], 1)

    def spot(index):
        at = pl.ds(pl.multiple_of(index // pairs * CLIP, CLIP), CLIP)
        return at, pl.ds(pl.multiple_of(index % pairs * 128, 128), 128)

    def attend(index, _):
        at, lanes = spot(index)
        query, keys, values = triple[0, at, lanes], triple[1, at, lanes], triple[2, at, lanes]
        scores = dot_nt(apart(query), keys) * HEAD ** (-0.5)
        raised = jnp.exp(scores - jnp.max(scores, -1, keepdims=True))
        full = raised / jnp.sum(raised, -1, keepdims=True)
        attention[index] = full
        mixed[at, lanes] = dot(beside(full.astype(jnp.bfloat16)), apart(values)).astype(jnp.bfloat16)
        return 0

    lax.fori_loop(0, frames // CLIP * pairs, attend, 0, unroll=pairs)
    load(3).wait()
    work[...] = dot(mixed[...], held[3])

    def first_norm(at):
        unit, inverse = norm_parts(encoded[at, :] + work[at, :])
        unit_one[at, :] = unit
        inverse_one[at, :] = inverse
        value = unit * vectors[3:4, :] + vectors[4:5, :]
        middle[at, :] = value
        middle_low[at, :] = value.astype(jnp.bfloat16)

    over_rows(frames, tile, first_norm)

    def expand(step, _):
        load(4 + step).wait()
        slope[step] = dot(middle_low[...], held[4 + step])

        def bend(at):
            value, derivative = gelu_pair(slope[step, at, :])
            active[step, at, :] = value.astype(jnp.bfloat16)
            slope[step, at, :] = derivative

        over_rows(frames, tile, bend)
        return 0

    lax.fori_loop(0, ups, expand, 0)

    def contract(step, _):
        load(4 + ups + step).wait()
        middle[...] += dot(active[step], held[4 + ups + step])
        return 0

    lax.fori_loop(0, ups, contract, 0)

    def second_norm(at):
        unit, inverse = norm_parts(middle[at, :])
        unit_two[at, :] = unit
        inverse_two[at, :] = inverse
        flow_low[at, :] = (unit * vectors[5:6, :] + vectors[6:7, :]).astype(jnp.bfloat16)

    over_rows(frames, tile, second_norm)
    table[...] = jnp.zeros_like(table)
    for group in range(columns):
        across = slice(group * 128, group * 128 + 128)
        head[:, across] = small[:, group, 128:224, :].reshape(parts * 96, 128)
        for part in range(parts):
            row = part // 2 * 128 + part % 2 * 32
            table[row : row + 32, across] = small[part, group, 224:256, :].astype(jnp.float32)
    real = lax.broadcasted_iota(jnp.int32, (1, table.shape[1]), 1) % 128 < CLUSTER_ROWS
    table[...] = jnp.where(real, table[...], 0.0)
    size = lax.rsqrt(jnp.sum(table[...] * table[...], 0, keepdims=True) + 1e-06)
    centers[...] = (table[...] * size).astype(jnp.bfloat16)
    embedded = dot(flow_low[...], head[...])
    length = lax.rsqrt(jnp.sum(embedded * embedded, -1, keepdims=True) + 1e-06)
    unit_low = (embedded * length).astype(jnp.bfloat16)
    logits = jnp.where(real, dot(unit_low, centers[...]) * inv_temp, -1e30)
    top = jnp.max(logits, -1, keepdims=True)
    raised = jnp.exp(logits - top)
    amount = jnp.sum(raised, -1, keepdims=True)
    choose = labels[...] == lax.broadcasted_iota(jnp.int32, logits.shape, 1)
    target = jnp.sum(jnp.where(choose, logits, 0.0), -1, keepdims=True)
    losses = mask[...] * (jnp.log(amount) + top - target)
    rows_out[7:8, :] = jnp.broadcast_to(jnp.sum(losses, 0, keepdims=True), (1, D))
    logit_grad = (
        (raised / amount - choose.astype(jnp.float32)) * (mask[...] * (1.0 / masked))
    ).astype(jnp.bfloat16)
    unit_grad = dot_nt(logit_grad, centers[...]) * inv_temp
    spread = dot_tn(unit_low, logit_grad) * inv_temp
    shared = jnp.sum(spread * table[...], 0, keepdims=True)
    spread = size * spread - table[...] * (size * size * size * shared)
    for group in range(columns):
        center_grad_t[group * 64 : group * 64 + 64, :] = spread[group * 128 : group * 128 + 64, :]
    along = jnp.sum(unit_grad * embedded, -1, keepdims=True)
    embedded_grad = (
        length * unit_grad - embedded * (length * length * length * along)
    ).astype(jnp.bfloat16)
    work[...] = dot_nt(embedded_grad, head[...])
    head_grad[...] = dot_tn(flow_low[...], embedded_grad).astype(jnp.bfloat16)

    def second_back(at):
        upstream = work[at, :]
        add_row(rows_out, 5, upstream * unit_two[at, :])
        add_row(rows_out, 6, upstream)
        value = norm_back(upstream, unit_two[at, :], inverse_two[at, :], vectors[5:6, :])
        middle[at, :] = value
        flow_low[at, :] = value.astype(jnp.bfloat16)

    over_rows(frames, tile, second_back)
    turned[...] = middle_low[...].T

    def feed_back(step, _):
        work[...] = dot_nt(flow_low[...], held[4 + ups + step])
        made[4 + ups + step] = dot_tn(active[step], flow_low[...]).astype(jnp.bfloat16)
        save(4 + ups + step).start()

        def bend(at):
            work_low[at, :] = (work[at, :] * slope[step, at, :]).astype(jnp.bfloat16)

        over_rows(frames, tile, bend)
        made[4 + step] = dot(turned[...], work_low[...]).astype(jnp.bfloat16)
        save(4 + step).start()
        middle[...] += dot_nt(work_low[...], held[4 + step])
        return 0

    lax.fori_loop(0, ups, feed_back, 0)

    def first_back(at):
        upstream = middle[at, :]
        add_row(rows_out, 3, upstream * unit_one[at, :])
        add_row(rows_out, 4, upstream)
        value = norm_back(upstream, unit_one[at, :], inverse_one[at, :], vectors[3:4, :])
        middle[at, :] = value
        flow_low[at, :] = value.astype(jnp.bfloat16)

    over_rows(frames, tile, first_back)
    made[3] = dot_tn(mixed[...], flow_low[...]).astype(jnp.bfloat16)
    save(3).start()
    work_low[...] = dot_nt(flow_low[...], held[3]).astype(jnp.bfloat16)

    def attend_back(index, _):
        at, lanes = spot(index)
        query, keys, values = triple[0, at, lanes], triple[1, at, lanes], triple[2, at, lanes]
        upstream = apart(work_low[at, lanes])
        full = attention[index]
        full_grad = dot_nt(upstream, values)
        triple_grad[2, at, lanes] = dot_tn(full.astype(jnp.bfloat16), upstream).astype(jnp.bfloat16)
        along = jnp.sum(full * full_grad, -1, keepdims=True)
        score_grad = (full * (full_grad - along)).astype(jnp.bfloat16)
        triple_grad[0, at, lanes] = (
            dot(beside(score_grad), apart(keys)) * HEAD ** (-0.5)
        ).astype(jnp.bfloat16)
        triple_grad[1, at, lanes] = (
            dot_tn(score_grad, apart(query)) * HEAD ** (-0.5)
        ).astype(jnp.bfloat16)
        return 0

    lax.fori_loop(0, frames // CLIP * pairs, attend_back, 0, unroll=pairs)
    turned[...] = low[...].T

    def last_three(block, _):
        made[block] = dot(turned[...], triple_grad[block]).astype(jnp.bfloat16)
        save(block).start()
        middle[...] += dot_nt(triple_grad[block], held[block])
        return 0

    lax.fori_loop(0, 3, last_three, 0)
    encoded_grad[...] = middle[...]
    for block in range(count):
        save(block).wait()


def trunk(encoded, mask, labels, vectors, small, blocks):
    frames, count = encoded.shape[0], blocks.shape[0]
    ups, columns = (count - 4) // 2, small.shape[1] * 128
    full, low = jnp.float32, jnp.bfloat16
    out = jax.ShapeDtypeStruct
    wide, wide_low = pltpu.VMEM((frames, D), full), pltpu.VMEM((frames, D), low)
    column = pltpu.VMEM((frames, 1), full)
    return pl.pallas_call(
        trunk_kernel,
        out_shape=[
            out((frames, D), full),
            out(blocks.shape, low),
            out((D, columns), low),
            out((columns // 2, columns), full),
            out((8, D), full),
            out((8, 128), full),
        ],
        in_specs=[VMEM] * 5 + [HBM],
        out_specs=[VMEM, HBM] + [VMEM] * 4,
        scratch_shapes=[
            pltpu.VMEM((D, columns), low),
            pltpu.VMEM((columns, columns), full),
            pltpu.VMEM((columns, columns), low),
            pltpu.VMEM(blocks.shape, low),
            pltpu.VMEM(blocks.shape, low),
            wide_low,
            pltpu.VMEM((3, frames, D), low),
            pltpu.VMEM((frames // CLIP * D // 128, 2 * CLIP, CLIP), full),
            wide_low,
            wide,
            column,
            wide,
            wide_low,
            pltpu.VMEM((ups, frames, D), low),
            pltpu.VMEM((ups, frames, D), full),
            wide,
            column,
            wide,
            wide_low,
            wide_low,
            pltpu.VMEM((3, frames, D), low),
            pltpu.VMEM((D, frames), low),
            pltpu.SemaphoreType.DMA((count,)),
            pltpu.SemaphoreType.DMA((count,)),
        ],
        name="trunk",
        compiler_params=pltpu.CompilerParams(vmem_limit_bytes=VMEM_LIMIT),
    )(encoded, mask, labels, vectors, small, blocks)


LOSS_ROW = 7


class Owners:
    def __init__(self, place, members):
        self.place, self.members = place, members
        self.first = (place.dp_size - 2 * members) // 2
        index = place.dp - self.first
        self.here = (index >= 0) & (index < 2 * members)
        self.group = place.x * 2 + index // members
        self.member = index % members

    def of(self, member):
        return self.first + self.place.core * self.members + member

    def to_rows(self, other, remote_action, local_action):
        place = self.place
        away = (place.dp != other) | (place.group != self.group)
        pl.when(away)(functools.partial(remote_action, other))
        pl.when(jnp.logical_not(away))(local_action)


class Reducer:
    def __init__(self, place, shapes, local, refs, sems):
        self.place, self.shapes, self.local = place, shapes, local
        self.z, self.lines, self.last = place.z, place.lines, place.lines - 1
        self.blocks = KINDS.index("blocks")
        self.rest = [k for k in range(len(KINDS)) if k != self.blocks]
        self.crossed, self.first_in, self.second_in, self.line_in = refs[:4]
        self.held, self.source = refs[4:]
        (
            self.load_sem, self.cross_send, self.cross_recv, self.first_send, self.first_recv,
            self.second_send, self.second_recv, self.left_send, self.left_recv, self.right_send,
            self.right_recv,
        ) = sems
        self.p_mate, self.q_mate = place.near(self.z, 1, 0), place.near(self.z, 0, 1)
        self.c_mate = place.at(self.z, 0, 0, 1)
        self.left, self.right = place.at(self.z - 1), place.at(self.z + 1)

    def remote(self, source, target, send, recv, device):
        return pltpu.make_async_remote_copy(
            src_ref=source,
            dst_ref=target,
            send_sem=send,
            recv_sem=recv,
            device_id=device,
            device_id_type=MESH,
        )

    def load_of(self, p, q, spot):
        k = self.blocks
        dp, group = self.place.near(spot, p, q)
        return pltpu.make_async_copy(
            piece_at("blocks", self.source[k], dp, group, self.shapes[k]),
            self.held.at[p, spot],
            self.load_sem.at[p, q, spot],
        )

    def cross_of(self, k, p, q, spot):
        dp, group = self.place.across(spot, p, q)
        return self.remote(
            piece_at(KINDS[k], self.source[k], dp, group, self.shapes[k]),
            self.crossed[k].at[p, q, spot],
            self.cross_send.at[k, p, q, spot],
            self.cross_recv.at[k, p, q, spot],
            self.c_mate,
        )

    def own(self, k, p, q, spot):
        if k == self.blocks:
            self.load_of(p, q, spot).wait()
            return f32(self.held, (p, spot))
        dp, group = self.place.near(spot, p, q)
        return piece_at(KINDS[k], self.source[k], dp, group, self.shapes[k])[...].astype(jnp.float32)

    def met(self, k, p, q, spot):
        own = self.own(k, p, q, spot)
        self.cross_of(k, p, q, spot).wait_recv()
        return own + f32(self.crossed[k], (p, q, spot))

    def turn(self, index):
        odd = index % 2
        return (1 - odd) * (self.last - index // 2) + odd * (index // 2)

    def first_out(self, k, p, spot):
        return self.remote(
            self.crossed[k].at[p, 1, spot],
            self.first_in[k].at[p, spot],
            self.first_send.at[k, p, spot],
            self.first_recv.at[k, p, spot],
            self.q_mate,
        )

    def stage_one(self, k, index):
        p, spot = 1 - index // self.lines, self.turn(index % self.lines)
        self.crossed[k][p, 1, spot] = self.met(k, p, 1, spot).astype(jnp.bfloat16)
        self.first_out(k, p, spot).start()
        if k == self.blocks:
            self.load_of(p, 0, spot).start()

    def joined(self, k, p, spot):
        total = self.met(k, p, 0, spot)
        self.first_out(k, p, spot).wait_recv()
        return total + f32(self.first_in[k], (p, spot))

    def second_out(self, k, spot):
        return self.remote(
            self.crossed[k].at[1, 0, spot],
            self.second_in[k].at[spot],
            self.second_send.at[k, spot],
            self.second_recv.at[k, spot],
            self.p_mate,
        )

    def stage_two(self, k, index):
        spot = self.turn(index)
        self.crossed[k][1, 0, spot] = self.joined(k, 1, spot).astype(jnp.bfloat16)
        self.second_out(k, spot).start()

    def line_total(self, k, spot):
        total = self.joined(k, 0, spot)
        self.second_out(k, spot).wait_recv()
        return total + f32(self.second_in[k], (spot,))

    def line_out(self, k, spot, way):
        if way == "right":
            send, recv, device, slot = self.right_send, self.left_recv, self.right, spot
        else:
            send, recv, device = self.left_send, self.right_recv, self.left
            ends = (self.last - (self.z - 1 - spot)) // self.last
            slot = spot + ends * (self.lines - spot)
        return self.remote(
            self.crossed[k].at[0, 0, spot],
            self.line_in[k].at[slot],
            send.at[k, spot],
            recv.at[k, spot],
            device,
        )

    def came_in(self, k, spot, way):
        recv = self.left_recv if way == "right" else self.right_recv
        send = self.right_send if way == "right" else self.left_send
        return self.remote(
            self.crossed[k].at[0, 0, spot],
            self.line_in[k].at[spot],
            send.at[k, spot],
            recv.at[k, spot],
            self.c_mate,
        )

    def pass_on(self, k, spot, way, inner):
        z = self.z
        if way == "right":
            here = (z < spot) & ((z > 0) if inner else (z == 0))
        else:
            here = (z > spot) & ((z < self.last) if inner else (z == self.last))

        @pl.when(here)
        def _():
            total = self.line_total(k, spot)
            if inner:
                self.came_in(k, spot, way).wait_recv()
                total = total + f32(self.line_in[k], (spot,))
            self.crossed[k][0, 0, spot] = total.astype(jnp.bfloat16)
            self.line_out(k, spot, way).start()

    def line_step(self, k, step, inner):
        self.pass_on(k, self.last - step, "right", inner)
        self.pass_on(k, step, "left", inner)

    def line_end(self, k, out):
        z = self.z
        out[...] = self.line_total(k, z)

        @pl.when(z > 0)
        def _():
            self.came_in(k, z, "right").wait_recv()
            out[...] += f32(self.line_in[k], (z,))

        @pl.when(z < self.last)
        def _():
            self.came_in(k, z, "left").wait_recv()
            out[...] += f32(self.line_in[k], (self.lines,))

    def drain(self):
        for k in range(len(KINDS)):

            def one(spot, _, k=k):
                for p in range(2):
                    for q in range(2):
                        self.cross_of(k, p, q, spot).wait_send()
                    self.first_out(k, p, spot).wait_send()
                self.second_out(k, spot).wait_send()

                @pl.when(self.z < spot)
                def _():
                    self.line_out(k, spot, "right").wait_send()

                @pl.when(self.z > spot)
                def _():
                    self.line_out(k, spot, "left").wait_send()

                return 0

            lax.fori_loop(0, self.lines, one, 0)


def f32(ref, at):
    return ref[at].astype(jnp.float32)


def back_compute(taps, refs, made, small_made, rows, scratch, hook):
    (
        encoded_grad, mask, vectors, small, feature_unit, normed, hidden_t,
        encoder_unit, encoder_inverse, slope, trunk_rows, head_grad, center_grad_t, kernel,
    ) = refs
    slots, windows, moved, grad, grad_t, through, through_t, load_sem = scratch
    frames, width = feature_unit.shape
    groups = kernel.shape[1]
    channels = hidden_t.shape[0] // groups

    def load(group):
        slot = group % 2
        return pltpu.make_async_copy(kernel.at[:, group], slots.at[slot], load_sem.at[slot])

    def begin():
        load(0).start()
        rows[...] = jnp.zeros_like(rows)
        rows[0:8, :] = trunk_rows[...]
        over_rows(frames, 32, enter)
        grad_t[...] = through[...].T.astype(jnp.bfloat16)

    def enter(at):
        upstream = encoded_grad[at, :]
        add_row(rows, 1, upstream * encoder_unit[at, :])
        add_row(rows, 2, upstream)
        value = norm_back(upstream, encoder_unit[at, :], encoder_inverse[at, :], vectors[1:2, :])
        grad[at, :] = value
        through[at, :] = value * slope[at, :]

    def one_group(group, _):
        pl.when(group + 1 < groups)(lambda: load(group + 1).start())
        load(group).wait()
        at = pl.ds(pl.multiple_of(group * channels, channels), channels)

        def put(index, value):
            made[index, group] = value

        through_t[at, :] = conv_group_back(
            hidden_t[at, :].astype(jnp.float32),
            grad_t[at, :].astype(jnp.float32),
            lambda index: slots[group % 2, index],
            put,
            windows,
            moved,
            taps,
            kernel.shape,
        )
        hook(group)
        return 0

    def convolve(first, last):
        lax.fori_loop(first, last, one_group, 0)

    def leave(at):
        total = grad[at, :] + through[at, :]
        inside = mask[at, :] > 0
        add_row(rows, 0, jnp.where(inside, total, 0.0))
        grad[at, :] = jnp.where(inside, 0.0, total)

    def finish():
        through[...] = through_t[...].T
        over_rows(frames, 32, leave)
        grad_t[...] = grad[...].T.astype(jnp.bfloat16)
        normed_t = normed[...].T
        parts, columns = small.shape[0], small.shape[1]
        third = D // columns
        total = None
        for group in range(columns):
            one = grad_t[group * third : group * third + 128, :]
            two = grad_t[group * third + 128 : (group + 1) * third, :]
            lane = third - 128
            wide = dot_nt(normed_t, one).astype(jnp.bfloat16)
            thin = dot_nt(normed_t, two).astype(jnp.bfloat16)
            small_made[:, group, 0:64, :] = wide.reshape(parts, 64, 128)
            small_made[:, group, 64:128, :] = jnp.concatenate(
                [thin, jnp.zeros((thin.shape[0], 128 - lane), jnp.bfloat16)], 1
            ).reshape(parts, 64, 128)
            small_made[:, group, 128:224, :] = head_grad[:, group * 128 : group * 128 + 128].reshape(
                parts, 96, 128
            )
            small_made[:, group, 224:256, :] = (
                center_grad_t[:, group * 128 : group * 128 + 128]
                .astype(jnp.bfloat16)
                .reshape(parts, 32, 128)
            )
            first = small[:, group, 0:64, :].reshape(parts * 64, 128)
            second = small[:, group, 64:128, :].reshape(parts * 64, 128)[:, :lane]
            term = dot(first, one) + dot(second, two)
            total = term if total is None else total + term
        normed_grad = total.T
        rows[8:9, 0:width] = jnp.sum(normed_grad * feature_unit[...], 0, keepdims=True)
        rows[9:10, 0:width] = jnp.sum(normed_grad, 0, keepdims=True)

    return begin, convolve, finish


def back_scratch(kernel_shape, frames):
    chunks, groups, rows, chunk = kernel_shape
    full, low = jnp.float32, jnp.bfloat16
    return [
        pltpu.VMEM((2, chunks, rows, chunk), low),
        pltpu.VMEM((chunks * chunk, frames), low),
        pltpu.VMEM((rows, frames), low),
        pltpu.VMEM((frames, D), full),
        pltpu.VMEM((D, frames), low),
        pltpu.VMEM((frames, D), full),
        pltpu.VMEM((D, frames), full),
        pltpu.SemaphoreType.DMA((2,)),
    ]


BACK_INPUTS = 14


def back_kernel(taps, *refs):
    made, small_made, rows = refs[BACK_INPUTS : BACK_INPUTS + 3]
    begin, convolve, finish = back_compute(
        taps, refs[:BACK_INPUTS], made, small_made, rows, refs[BACK_INPUTS + 3 :], lambda group: None
    )
    begin()
    convolve(0, made.shape[1])
    finish()


def back(taps, operands):
    kernel, small, frames = operands[-1], operands[3], operands[0].shape[0]
    return pl.pallas_call(
        functools.partial(back_kernel, taps),
        out_shape=[
            jax.ShapeDtypeStruct(kernel.shape, jnp.bfloat16),
            jax.ShapeDtypeStruct(small.shape, jnp.bfloat16),
            jax.ShapeDtypeStruct((16, D), jnp.float32),
        ],
        in_specs=[VMEM] * (BACK_INPUTS - 1) + [HBM],
        out_specs=[VMEM] * 3,
        scratch_shapes=back_scratch(kernel.shape, frames),
        name="back",
        compiler_params=pltpu.CompilerParams(vmem_limit_bytes=48 * 1024 * 1024),
    )(*operands)


def back_reduce_kernel(sizes, shapes, taps, *refs):
    place = Place(*sizes)
    refs = list(refs)

    def pull(number):
        taken = refs[:number]
        del refs[:number]
        return taken

    count = len(KINDS)
    inputs, (block_grad,) = pull(BACK_INPUTS), pull(1)
    outs, (small_out, square_out, whole_box) = pull(count), pull(3)
    made, small_made, rows, scratch = *pull(3), pull(8)
    crossed, first_in, second_in, line_in = (pull(count) for _ in range(4))
    (held, group_box, dp_box, rows_low) = pull(4)
    sems = pull(11)
    (group_send, group_recv, dp_send, dp_recv, row_send, row_recv, pair_send, pair_recv) = pull(8)
    me = (place.dp, place.group)
    source = {"conv": made, "small": small_made, "blocks": block_grad}
    run = Reducer(
        place,
        shapes,
        None,
        (crossed, first_in, second_in, line_in, held, [source[kind] for kind in KINDS]),
        sems,
    )
    lines, b = run.lines, run.blocks
    conv, tiny = KINDS.index("conv"), KINDS.index("small")
    greet(place)

    def cross_all(k):
        for q in (1, 0):
            for p in (1, 0):

                def begin_one(index, _, p=p, q=q):
                    run.cross_of(k, p, q, run.turn(index)).start()
                    if k == b and q == 1:
                        run.load_of(p, q, run.turn(index)).start()
                    return 0

                lax.fori_loop(0, lines, begin_one, 0)

    def hook(group):
        pairs = shapes[conv][0]

        @pl.when(group % pairs == pairs - 1)
        def _():
            dp = group // pairs
            spot, flip_y = dp // 2, (dp % 2 + place.y) % 2
            for x in range(2):
                flip_x = (x + place.x) % 2
                p = flip_y * place.core + flip_x * (1 - place.core)
                q = flip_x * place.core + flip_y * (1 - place.core)
                run.cross_of(conv, p, q, spot).start()

    begin, convolve, finish = back_compute(taps, inputs, made, small_made, rows, scratch, hook)

    def remote(source, target, send, recv, device):
        return run.remote(source, target, send, recv, device)

    def each_other(size, mine, action):
        for other in range(size):
            pl.when(mine != other)(functools.partial(action, other))

    def group_copy(other):
        return remote(
            rows,
            group_box.at[place.group],
            group_send.at[other],
            group_recv.at[place.group],
            (place.dp, other),
        )

    def dp_copy(other):
        return remote(
            dp_box.at[place.dp], dp_box.at[place.dp], dp_send.at[other], dp_recv.at[place.dp], (other, place.group)
        )

    def group_wait(other):
        group_copy(other).wait_send()
        remote(rows, group_box.at[other], group_send.at[other], group_recv.at[other], me).wait_recv()

    def dp_wait(other):
        dp_copy(other).wait_send()
        remote(dp_box.at[other], dp_box.at[other], dp_send.at[other], dp_recv.at[other], me).wait_recv()

    def rows_to_group():
        group_box[place.group] = rows[...]
        each_other(place.group_size, place.group, lambda other: group_copy(other).start())

    def rows_to_all():
        each_other(place.group_size, place.group, group_wait)
        total = group_box[0]
        for other in range(1, place.group_size):
            total = total + group_box[other]
        dp_box[place.dp] = total
        each_other(place.dp_size, place.dp, lambda other: dp_copy(other).start())

    def some(first, last, action):
        def one(index, _):
            action(index)
            return 0

        lax.fori_loop(first, last, one, 0)

    members, depth = shapes[b][0], shapes[b][1]
    owners = Owners(place, members)
    my_rows = pl.ds(pl.multiple_of(place.dp * depth, depth), depth)
    owner_here = owners.here & (owners.group == place.group)
    owner_there = owners.here & (owners.group != place.group)

    def row_copy(member):
        return remote(
            rows_low.at[member],
            whole_box.at[my_rows],
            row_send.at[member],
            row_recv.at[place.dp],
            (owners.of(member), place.group),
        )

    def pair_copy(other):
        spot = pl.ds(pl.multiple_of(other * depth, depth), depth)
        return remote(
            whole_box.at[spot], whole_box.at[spot], pair_send.at[other], pair_recv.at[other], run.c_mate
        )

    def send_rows():
        rows_low[...] = outs[b][...].astype(jnp.bfloat16)
        for member in range(members):

            @pl.when(place.dp != owners.of(member))
            def _(member=member):
                row_copy(member).start()

            @pl.when(place.dp == owners.of(member))
            def _(member=member):
                whole_box[my_rows] = rows_low[member]
                pair_copy(place.dp).start()

    def take_rows():
        @pl.when(owner_here)
        def _():
            for other in range(place.dp_size):

                @pl.when(place.dp != other)
                def _(other=other):
                    spot = pl.ds(other * depth, depth)
                    remote(
                        rows_low.at[0], whole_box.at[spot], row_send.at[0], row_recv.at[other], me
                    ).wait_recv()
                    pair_copy(other).start()

        @pl.when(owner_there)
        def _():
            for other in range(place.dp_size):
                pair_copy(other).wait_recv()

    cross_all(b)
    begin()
    actions = {
        "one": lambda index, k: run.stage_one(k, index),
        "two": lambda index, k: run.stage_two(k, index),
        "edge": lambda index, k: run.line_step(k, index, False),
        "inner": lambda index, k: run.line_step(k, index, True),
        "end": lambda index, k: run.line_end(k, outs[k]),
    }

    def leave():
        finish()
        cross_all(tiny)
        rows_to_group()

    plain = {"leave": leave, "rows": send_rows, "take": take_rows}
    for name, kind, first, last in PLAN:
        if name == "groups":
            convolve(first, last)
        elif name in plain:
            plain[name]()
        else:
            action = functools.partial(lambda index, k, name: actions[name](index, k), k=KINDS.index(kind), name=name)
            if last - first == 1:
                action(first)
            else:
                some(first, last, action)
        if name == "rows":
            rows_to_all()
    square = jnp.sum(outs[b][...] * outs[b][...])
    for k in run.rest:
        square = square + jnp.sum(outs[k][...] * outs[k][...])
    each_other(place.dp_size, place.dp, dp_wait)
    total = dp_box[0]
    for other in range(1, place.dp_size):
        total = total + dp_box[other]
    small_out[...] = total
    skipped = lax.broadcasted_iota(jnp.int32, total.shape, 0) != LOSS_ROW
    square = square + jnp.sum(jnp.where(skipped, total * total, 0.0)) * (
        1.0 / (place.dp_size * place.group_size)
    )
    square_out[...] = jnp.full(square_out.shape, square, jnp.float32)
    for member in range(members):
        @pl.when(place.dp != owners.of(member))
        def _(member=member):
            row_copy(member).wait_send()

    @pl.when(owner_here)
    def _():
        for other in range(place.dp_size):
            pair_copy(other).wait_send()

    run.drain()


def back_reduce(sizes, shapes, taps, operands, block_grad):
    dp_size, group_size = sizes
    lines, count = dp_size // 2, len(KINDS)
    kernel, small, frames = operands[-1], operands[3], operands[0].shape[0]
    low, full = jnp.bfloat16, jnp.float32

    def boxes(lead):
        return [
            pltpu.VMEM(tuple(lead(kind)) + tuple(shape), low) for kind, shape in zip(KINDS, shapes)
        ]

    dma = pltpu.SemaphoreType.DMA
    scratch = (
        [pltpu.VMEM(kernel.shape, low), pltpu.VMEM(small.shape, low), pltpu.VMEM((16, D), full)]
        + back_scratch(kernel.shape, frames)
        + boxes(lambda kind: (2, 2, lines))
        + boxes(lambda kind: (2, lines))
        + boxes(lambda kind: (lines,))
        + boxes(lambda kind: (lines + 1,))
        + [
            pltpu.VMEM((2, lines) + tuple(shapes[-1]), low),
            pltpu.VMEM((group_size, 16, D), full),
            pltpu.VMEM((dp_size, 16, D), full),
            pltpu.VMEM(shapes[-1], low),
        ]
        + [dma((2, 2, lines))]
        + [dma((count, 2, 2, lines))] * 2
        + [dma((count, 2, lines))] * 2
        + [dma((count, lines))] * 6
        + [dma((group_size,))] * 2
        + [dma((dp_size,))] * 2
        + [dma((shapes[-1][0],)), dma((dp_size,))]
        + [dma((dp_size,))] * 2
    )
    return pl.pallas_call(
        functools.partial(back_reduce_kernel, sizes, shapes, taps),
        out_shape=[jax.ShapeDtypeStruct(shape, full) for shape in shapes]
        + [
            jax.ShapeDtypeStruct((16, D), full),
            jax.ShapeDtypeStruct((8, 128), full),
            jax.ShapeDtypeStruct((D, D), low),
        ],
        in_specs=[VMEM] * (BACK_INPUTS - 1) + [HBM, HBM],
        out_specs=[VMEM] * (count + 3),
        scratch_shapes=scratch,
        name="back_reduce",
        compiler_params=pltpu.CompilerParams(
            collective_id=1, has_side_effects=True, vmem_limit_bytes=VMEM_LIMIT
        ),
    )(*operands, block_grad)


PLAN = (
    ("one", "blocks", 0, 1),
    ("groups", "", 0, 3),
    ("one", "blocks", 4, 5),
    ("two", "blocks", 0, 1),
    ("groups", "", 3, 6),
    ("one", "blocks", 1, 2),
    ("groups", "", 6, 9),
    ("one", "blocks", 5, 6),
    ("two", "blocks", 1, 2),
    ("one", "blocks", 3, 4),
    ("groups", "", 9, 16),
    ("one", "blocks", 2, 3),
    ("leave", "", 0, 1),
    ("edge", "blocks", 0, 1),
    ("one", "blocks", 6, 7),
    ("one", "small", 1, 2),
    ("inner", "blocks", 2, 3),
    ("one", "blocks", 7, 8),
    ("one", "conv", 3, 4),
    ("two", "blocks", 2, 4),
    ("one", "conv", 0, 1),
    ("one", "small", 0, 1),
    ("one", "small", 5, 6),
    ("one", "small", 4, 5),
    ("one", "small", 2, 3),
    ("two", "small", 1, 2),
    ("edge", "blocks", 1, 2),
    ("inner", "blocks", 0, 1),
    ("one", "small", 3, 4),
    ("inner", "blocks", 1, 2),
    ("one", "conv", 5, 6),
    ("inner", "conv", 2, 3),
    ("one", "conv", 2, 3),
    ("edge", "blocks", 2, 3),
    ("two", "small", 0, 1),
    ("edge", "small", 0, 1),
    ("one", "conv", 1, 2),
    ("one", "conv", 4, 5),
    ("two", "small", 3, 4),
    ("end", "blocks", 0, 1),
    ("two", "conv", 0, 1),
    ("one", "small", 7, 8),
    ("inner", "small", 0, 1),
    ("two", "small", 2, 3),
    ("one", "conv", 7, 8),
    ("rows", "", 0, 1),
    ("inner", "small", 2, 3),
    ("one", "small", 6, 7),
    ("two", "conv", 1, 4),
    ("edge", "small", 1, 2),
    ("edge", "conv", 0, 1),
    ("inner", "small", 1, 2),
    ("one", "conv", 6, 7),
    ("edge", "conv", 1, 2),
    ("edge", "small", 2, 3),
    ("inner", "conv", 0, 1),
    ("edge", "conv", 2, 3),
    ("inner", "conv", 1, 2),
    ("take", "", 0, 1),
    ("end", "small", 0, 1),
    ("end", "conv", 0, 1),
)


GATHER_PLAN = (
    ("step", "small", 0),
    ("step", "blocks", 0),
    ("step", "conv", 0),
    ("enter", "", 0),
    ("step", "small", 1),
    ("step", "conv", 1),
    ("step", "blocks", 1),
    ("step", "small", 2),
    ("step", "conv", 2),
    ("step", "blocks", 2),
    ("step", "small", 3),
    ("step", "conv", 3),
    ("stats", "", 0),
    ("step", "small", 4),
    ("step", "conv", 4),
    ("step", "conv", 5),
    ("step", "small", 5),
    ("step", "blocks", 3),
    ("core", "conv", 0),
    ("core", "small", 0),
    ("compute", "", 0),
    ("compute", "", 1),
    ("compute", "", 2),
    ("compute", "", 3),
    ("step", "blocks", 4),
    ("compute", "", 4),
    ("step", "blocks", 5),
    ("step", "blocks", 6),
    ("step", "conv", 6),
    ("step", "small", 6),
)


def roots_kernel(sizes, members, *refs):
    (
        whole, stat, square_in, sides_out, update_out, square_out,
        gram, big, m0, m0b, m1, m1b, s1, s1b, s2b, s3, s3b, root, mixed,
        group_box, dp_box, group_send, group_recv, dp_send, dp_recv,
        side_send, side_recv, side_own, mixed_send, mixed_recv, update_send, update_recv, update_own,
    ) = refs
    place = Place(*sizes)
    owners = Owners(place, members)
    dp_size, rows = place.dp_size, D // place.dp_size
    me, c_mate = (place.dp, place.group), place.at(place.z, 0, 0, 1)
    owner = owners.here
    tile = 256
    greet(place)

    def remote(source, target, send, recv, device):
        return pltpu.make_async_remote_copy(
            src_ref=source,
            dst_ref=target,
            send_sem=send,
            recv_sem=recv,
            device_id=device,
            device_id_type=MESH,
        )

    def each_other(size, mine, action):
        for other in range(size):
            pl.when(mine != other)(functools.partial(action, other))

    def group_copy(other, slot):
        return remote(
            group_box.at[slot], group_box.at[slot], group_send.at[other], group_recv.at[slot], (place.dp, other)
        )

    def dp_copy(other, slot):
        return remote(dp_box.at[slot], dp_box.at[slot], dp_send.at[other], dp_recv.at[slot], (other, place.group))

    group_box[place.group] = square_in[...]
    each_other(place.group_size, place.group, lambda other: group_copy(other, place.group).start())

    def product_rows(one, two, then):
        def step(index, _):
            at = pl.ds(pl.multiple_of(index * tile, tile), tile)
            then(at, jnp.dot(one[at, :], two[...], preferred_element_type=jnp.float32))
            return 0

        lax.fori_loop(0, D // tile, step, 0)

    half = D // 2

    @pl.when(owner)
    def _():
        for index in range(2):
            at = slice(index * half, (index + 1) * half)

            @pl.when(place.core == 0)
            def _(at=at):
                gram[at, :] = dot_nt(whole[at, :], whole[...]).astype(jnp.bfloat16)

            @pl.when(place.core == 1)
            def _(at=at):
                gram[at, :] = dot_tn(whole[:, at], whole[...]).astype(jnp.bfloat16)

    def side_copy(other):
        spot = pl.ds(pl.multiple_of(other * rows, rows), rows)
        return remote(
            gram.at[spot],
            sides_out.at[owners.member, place.core],
            side_send.at[other],
            side_recv.at[owners.member, place.core],
            (other, owners.group),
        )

    def side_local():
        spot = pl.ds(pl.multiple_of(place.dp * rows, rows), rows)
        return pltpu.make_async_copy(gram.at[spot], sides_out.at[owners.member, place.core], side_own)

    def group_wait(other):
        group_copy(other, place.group).wait_send()
        group_copy(other, other).wait_recv()

    each_other(place.group_size, place.group, group_wait)
    total = group_box[0]
    for other in range(1, place.group_size):
        total = total + group_box[other]
    dp_box[place.dp] = total
    each_other(dp_size, place.dp, lambda other: dp_copy(other, place.dp).start())

    @pl.when(owner)
    def _():
        for other in range(dp_size):
            owners.to_rows(other, lambda other: side_copy(other).start(), lambda: side_local().start())

    def dp_wait(other):
        dp_copy(other, place.dp).wait_send()
        dp_copy(other, other).wait_recv()

    each_other(dp_size, place.dp, dp_wait)
    total = dp_box[0]
    for other in range(1, dp_size):
        total = total + dp_box[other]
    square_out[...] = total

    @pl.when(owner)
    def _():
        factor = jnp.minimum(1.0, max_norm / (jnp.sqrt(total[0:1, 0:1]) + 1e-06))
        square_factor = factor * factor
        spread_f = (1 - stat_decay) * square_factor

        def diagonal(at_start, shape):
            row = lax.broadcasted_iota(jnp.int32, shape, 0) + at_start
            return row == lax.broadcasted_iota(jnp.int32, shape, 1)

        def each_tile(action, carry):
            def step(index, carry):
                start = pl.multiple_of(index * tile, tile)
                return action(pl.ds(start, tile), start, carry)

            return lax.fori_loop(0, D // tile, step, carry)

        def renew(at, start, trace):
            value = stat_decay * stat[at, :].astype(jnp.float32) + spread_f * gram[at, :].astype(
                jnp.float32
            )
            big[at, :] = value
            on = jnp.where(diagonal(start, value.shape), value, 0.0)
            return trace + jnp.sum(jnp.sum(on, 1, keepdims=True), 0, keepdims=True)

        trace = each_tile(renew, jnp.zeros((1, 1), jnp.float32))
        damping = 0.0001 * (trace / D)

        def damp(at, start, total):
            value = big[at, :]
            value = value + jnp.where(diagonal(start, value.shape), damping, 0.0)
            big[at, :] = value
            return total + jnp.sum(jnp.sum(value * value, 1, keepdims=True), 0, keepdims=True)

        magnitude = jnp.sqrt(each_tile(damp, jnp.zeros((1, 1), jnp.float32)))

        def scale(at, start, carry):
            value = big[at, :] / magnitude
            m0[at, :] = value
            m0b[at, :] = value.astype(jnp.bfloat16)
            return carry

        each_tile(scale, 0)
        a = 1.5625

        def square_of(source):
            def then(at, value):
                value = value * 0.0625 - 0.625 * source[at, :]
                s1[at, :] = value
                s1b[at, :] = value.astype(jnp.bfloat16)

            return then

        def fourth(at, value):
            s2b[at, :] = (value + (2 * a) * s1[at, :]).astype(jnp.bfloat16)

        product_rows(m0b, m0b, square_of(m0))
        product_rows(s1b, s1b, fourth)

        def next_one(at, value):
            value = value + (a * a) * m0[at, :]
            m1[at, :] = value
            m1b[at, :] = value.astype(jnp.bfloat16)

        product_rows(s2b, m0b, next_one)

        def joined(at, value):
            value = value * 0.0625 - 0.3125 * (m0[at, :] + m1[at, :])
            s3[at, :] = value
            s3b[at, :] = value.astype(jnp.bfloat16)

        product_rows(m0b, m1b, joined)
        product_rows(m1b, m1b, square_of(m1))
        product_rows(s1b, s1b, fourth)

        def next_two(at, value):
            value = value + (a * a) * m1[at, :]
            m0[at, :] = value
            m0b[at, :] = value.astype(jnp.bfloat16)

        product_rows(s2b, m1b, next_two)
        outer = lax.rsqrt(jnp.sqrt(magnitude))

        def final(at, value):
            value = 1.25 * s3[at, :] - (0.25 * a) * m0[at, :] - 0.25 * value
            start = at.start
            value = value + jnp.where(diagonal(start, value.shape), 1.25 * a, 0.0)
            root[at, :] = (value * outer).astype(jnp.bfloat16)

        product_rows(s3b, m0b, final)

    per_part = dp_size // 2

    def mixed_copy(part):
        at = pl.ds(part * half, half)
        return remote(mixed.at[at], mixed.at[at], mixed_send.at[part], mixed_recv.at[part], c_mate)

    def update_copy(other):
        spot = pl.ds(pl.multiple_of(other * rows, rows), rows)
        return remote(
            m1b.at[spot],
            update_out.at[owners.member],
            update_send.at[other],
            update_recv.at[owners.member],
            (other, owners.group),
        )

    def update_local():
        spot = pl.ds(pl.multiple_of(place.dp * rows, rows), rows)
        return pltpu.make_async_copy(m1b.at[spot], update_out.at[owners.member], update_own)

    @pl.when(owner & (place.core == 0))
    def _():
        for part in range(2):
            at = slice(part * half, (part + 1) * half)
            mixed[at, :] = dot(root[at, :], whole[...]).astype(jnp.bfloat16)
            mixed_copy(part).start()
        for part in range(2):
            mixed_copy(part).wait_send()

    @pl.when(owner & (place.core == 1))
    def _():
        for part in range(2):
            mixed_copy(part).wait_recv()
            at = slice(part * half, (part + 1) * half)
            m1b[at, :] = dot(mixed[at, :], root[...]).astype(jnp.bfloat16)
            for other in range(part * per_part, (part + 1) * per_part):
                owners.to_rows(
                    other, lambda other: update_copy(other).start(), lambda: update_local().start()
                )
        for other in range(dp_size):
            owners.to_rows(
                other, lambda other: update_copy(other).wait_send(), lambda: update_local().wait()
            )

    @pl.when(owner)
    def _():
        for other in range(dp_size):
            owners.to_rows(
                other, lambda other: side_copy(other).wait_send(), lambda: side_local().wait()
            )

    for member in range(members):
        for side in range(2):

            @pl.when((place.dp != owners.of(member)) | (place.core != side))
            def _(member=member, side=side):
                remote(
                    gram.at[pl.ds(0, rows)],
                    sides_out.at[member, side],
                    side_send.at[0],
                    side_recv.at[member, side],
                    me,
                ).wait_recv()

        @pl.when((place.dp != owners.of(member)) | (place.core != 1))
        def _(member=member):
            remote(
                m1b.at[pl.ds(0, rows)],
                update_out.at[member],
                update_send.at[0],
                update_recv.at[member],
                me,
            ).wait_recv()


def shampoo_roots(sizes, members, whole, stat, square):
    dp_size, group_size = sizes
    rows = D // dp_size
    low, full = jnp.bfloat16, jnp.float32
    dma = pltpu.SemaphoreType.DMA
    half, word = pltpu.VMEM((D, D), low), pltpu.VMEM((D, D), full)
    return pl.pallas_call(
        functools.partial(roots_kernel, sizes, members),
        out_shape=[
            jax.ShapeDtypeStruct((members, 2, rows, D), low),
            jax.ShapeDtypeStruct((members, rows, D), low),
            jax.ShapeDtypeStruct((8, 128), full),
        ],
        in_specs=[VMEM] * 3,
        out_specs=[VMEM] * 3,
        scratch_shapes=[half, word, word, half, word, half, word, half, half, word, half, half, half]
        + [pltpu.VMEM((group_size, 8, 128), full), pltpu.VMEM((dp_size, 8, 128), full)]
        + [dma((group_size,))] * 2
        + [dma((dp_size,))] * 2
        + [dma((dp_size,)), dma((members, 2)), dma]
        + [dma((2,)), dma((2,))]
        + [dma((dp_size,)), dma((members,)), dma],
        name="shampoo_roots",
        compiler_params=pltpu.CompilerParams(
            collective_id=2, has_side_effects=True, vmem_limit_bytes=VMEM_LIMIT
        ),
    )(whole, stat, square)


def finish_kernel(rates, *refs):
    square, rows, block_sum, small, kernel, sides, update = refs[:7]
    weights, blocks, statistics = refs[7:25], refs[25], refs[26]
    norm_out, outs = refs[27], refs[28:46]
    block_out, stat_out, blocks_out = refs[46:]
    norm = jnp.sqrt(square[0:1, 0:1])
    norm_out[...] = norm
    factor = jnp.minimum(1.0, max_norm / (norm + 1e-06))

    def renew(index, at, grad):
        rate, decay = rates[index]
        ins, out = weights[3 * index : 3 * index + 3], outs[3 * index : 3 * index + 3]
        result = adamw(ins[0][at], grad * factor, ins[1][at], ins[2][at], rate, decay)
        for ref, value in zip(out, result):
            ref[at] = value

    width = weights[0].shape[1]
    vector_rows = weights[6].shape[0]
    renew(0, ..., rows[LOSS_ROW + 1 : LOSS_ROW + 3, :width])
    renew(1, (slice(None), slice(0, 128)), small[0:64, :])
    renew(1, (slice(None), slice(128, 192)), small[64:128, 0:64])
    renew(2, ..., rows[0:vector_rows, :])
    runs, steps, c, channels = weights[9].shape
    for offset in range(steps):
        parts = [kernel[group, offset * c : (offset + 1) * c, :] for group in range(channels // c)]
        renew(
            3,
            (slice(None), offset),
            jnp.concatenate(parts, 0).T.reshape(runs, c, channels),
        )
    renew(4, ..., small[128:224, :].T[0:64])
    renew(5, ..., small[224:256, 0:CLUSTER_ROWS])
    for member in range(blocks.shape[0]):
        block_out[member] = block_sum[member] * factor
        step = update[member].astype(jnp.float32) * factor + decay_weight * blocks[member]
        blocks_out[member] = blocks[member] - rate_shampoo * step
        for side in range(2):
            spread = (1 - stat_decay) * factor * factor
            stat_out[member, side] = stat_decay * statistics[member, side] + spread * sides[
                member, side
            ].astype(jnp.float32)


def finish(sums, weights, blocks, statistics):
    full = jnp.float32
    rates = [(rate_vector, 0.0), (rate_matrix, decay_weight), (rate_vector, 0.0)]
    rates += [(rate_matrix, decay_weight)] * 3
    operands = [*sums, *weights, blocks, statistics]
    shapes = [(1, 1)] + [weight.shape for weight in weights]
    shapes += [blocks.shape, statistics.shape, blocks.shape]
    return pl.pallas_call(
        functools.partial(finish_kernel, rates),
        out_shape=[jax.ShapeDtypeStruct(shape, full) for shape in shapes],
        in_specs=[VMEM] * len(operands),
        out_specs=[VMEM] * len(shapes),
        name="finish",
        compiler_params=pltpu.CompilerParams(vmem_limit_bytes=VMEM_LIMIT),
    )(*operands)


def conv_to_shard(weight):
    taps, c, channels = weight.shape
    split = weight.reshape(taps // STRIDE, STRIDE, c, channels // c, c)
    return split.transpose(3, 1, 4, 0, 2).reshape(channels // c, STRIDE * c, taps // STRIDE * c)


def conv_from_shard(shard):
    groups, rows, columns = shard.shape
    c = rows // STRIDE
    split = shard.reshape(groups, STRIDE, c, columns // c, c)
    return split.transpose(3, 1, 4, 0, 2).reshape(columns // c * STRIDE, c, groups * c)


def pack_small(projection, head, clusters, note):
    lead, kind = projection.shape[:-2], projection.dtype
    notes = jnp.broadcast_to(note, lead + (32, 2)).astype(kind)
    return jnp.concatenate(
        [
            projection[..., :128],
            jnp.concatenate([projection[..., 128:], jnp.zeros(lead + (64, 64), kind)], -1),
            jnp.concatenate([head, jnp.zeros(lead + (96, 64), kind)], -1),
            jnp.concatenate([jnp.swapaxes(clusters, -1, -2), notes], -1),
        ],
        -2,
    )


def unpack_small(packed):
    projection = jnp.concatenate([packed[..., :64, :], packed[..., 64:128, :64]], -1)
    head = packed[..., 128:224, :64]
    clusters = jnp.swapaxes(packed[..., 224:, :CLUSTER_ROWS], -1, -2)
    return projection, head, clusters


def pack_whole(projection, head, clusters, note):
    def cut(values, down, across):
        rows, columns = values.shape
        return values.reshape(down, rows // down, across, columns // across).transpose(0, 2, 1, 3)

    return pack_small(
        cut(projection, 8, 4), cut(head, 8, 4), cut(clusters, 4, 8).transpose(1, 0, 2, 3), note
    )


def unpack_whole(packed):
    def join(values):
        down, across, rows, columns = values.shape
        return values.transpose(0, 2, 1, 3).reshape(down * rows, across * columns)

    projection, head, clusters = unpack_small(packed)
    return join(projection), join(head), join(clusters.transpose(1, 0, 2, 3))


def parts_of_rows(rows, vector_rows, width):
    return rows[:vector_rows], rows[vector_rows + 1 : vector_rows + 3, :width], rows[vector_rows, 0]


CLUSTER_ROWS = 126
SMALL = ((64, 192), (96, 64), (CLUSTER_ROWS, 32))


def body(
    sizes,
    features,
    span_starts,
    labels,
    feature_norm,
    feature_first,
    feature_second,
    projection,
    projection_first,
    projection_second,
    vectors,
    vector_first,
    vector_second,
    conv_weight,
    conv_first,
    conv_second,
    head,
    head_first,
    head_second,
    clusters,
    cluster_first,
    cluster_second,
    blocks,
    statistics,
):
    dp_size, group_size = sizes
    members, rows = blocks.shape[0], blocks.shape[1]
    masks = jax.vmap(jax.vmap(frame_mask))(span_starts)
    local_count = jnp.sum(masks)
    fast = (
        rows % 16 == 0
        and dp_size % 2 == 0
        and group_size == 4
        and dp_size >= 2 * members
        and (projection.shape, head.shape, clusters.shape) == SMALL
        and conv_weight.shape[2] % conv_weight.shape[1] == 0
        and masks.size <= 256
    )
    frames, vector_rows, width = masks.size, vectors.shape[0], feature_norm.shape[1]
    flat = features.reshape(frames, -1)

    def runs(values):
        return values.reshape((-1, STRIDE) + values.shape[1:])

    if fast:
        taps, c, channels = conv_weight.shape
        taps *= group_size
        shapes = [
            (channels // c, STRIDE * c, taps // group_size // STRIDE * c),
            (256, 128),
            blocks.shape,
        ]
        raw = (
            span_starts.reshape(-1, span_starts.shape[-1]),
            projection, runs(conv_weight), head.T, clusters.T, blocks, statistics,
        )
        kernel_w, small_w, blocks_w, stat_whole, *saved, mask = gather_weights(
            sizes, shapes, taps, raw, flat, feature_norm, vectors
        )
    else:
        proj_w, kernel_full, head_w, clusters_w, blocks_w = gather_plain(
            projection, conv_weight, head, clusters, blocks
        )
        whole = conv_to_shard(kernel_full)
        kernel_w = whole.reshape(whole.shape[:2] + (4, -1)).transpose(2, 0, 1, 3)
        count = lax.psum(local_count, ("dp", "group"))
        high = jnp.floor(count / 256.0) * 256.0
        notes = jnp.concatenate([jnp.stack([high, count - high]), jnp.zeros(30, jnp.float32)])
        small_w = pack_whole(proj_w, head_w, clusters_w, notes.reshape(8, 4, 1, 1))
        taps = kernel_w.shape[0] * kernel_w.shape[3] // (D // kernel_w.shape[1]) * STRIDE
        mask = masks.reshape(frames, 1)
        saved = front(flat, mask, feature_norm, vectors, small_w, kernel_w, taps)
    feature_unit, normed, hidden_t, encoded, encoder_unit, encoder_inverse, slope = saved
    targets = labels.reshape(frames, 1)
    encoded_grad, block_part, head_part, center_part, trunk_rows, counted = trunk(
        encoded, mask, targets + targets // CLUSTER_ROWS * 2, vectors, small_w, blocks_w
    )
    masked_count = counted[0, 0]
    operands = (
        encoded_grad, mask, vectors, small_w, feature_unit, normed, hidden_t,
        encoder_unit, encoder_inverse, slope, trunk_rows, head_part, center_part, kernel_w,
    )
    if fast:
        kernel_sum, small_sum, block_sum, extra, square, whole = back_reduce(
            sizes, shapes, taps, operands, block_part
        )
        sides, update_rows, square = shampoo_roots(sizes, members, whole, stat_whole, square)

        done = finish(
            (square, extra, block_sum, small_sum, kernel_sum, sides, update_rows),
            (
                feature_norm, feature_first, feature_second,
                projection, projection_first, projection_second,
                vectors, vector_first, vector_second,
                runs(conv_weight), runs(conv_first), runs(conv_second),
                head.T, head_first.T, head_second.T,
                clusters.T, cluster_first.T, cluster_second.T,
            ),
            blocks,
            statistics,
        )
        outs = []
        for index in range(0, 18, 3):
            parts = done[1 + index : 4 + index]
            if index == 9:
                parts = [part.reshape(conv_weight.shape) for part in parts]
            if index >= 12:
                parts = [part.T for part in parts]
            outs += parts
        return (extra[LOSS_ROW, 0], masked_count, done[0][0, 0], *outs, *done[19:])
    kernel_part, small_part, row_part = back(taps, operands)
    proj_part, head_part, center_part = unpack_whole(small_part)
    kernel_plain = conv_from_shard(
        kernel_part.transpose(1, 2, 0, 3).reshape(kernel_part.shape[1:3] + (-1,))
    )
    large_total = reduce_grads(
        tuple(
            part.astype(jnp.float32)
            for part in (proj_part, kernel_plain, head_part, center_part, block_part)
        )
    )
    vector_grad, feature_grad, loss_sum = parts_of_rows(
        lax.psum(row_part, ("dp", "group")), vector_rows, width
    )
    local_squares = sum((jnp.sum(part * part) for part in large_total))
    norm_square = (
        lax.psum(local_squares, ("dp", "group"))
        + jnp.sum(feature_grad * feature_grad)
        + jnp.sum(vector_grad * vector_grad)
    )
    grad_norm = jnp.sqrt(norm_square)
    factor = jnp.minimum(1.0, max_norm / (grad_norm + 1e-06))
    proj_grad, kernel_grad, head_grad, cluster_grad, block_rows = [
        part * factor for part in large_total
    ]
    feature_out = adamw(
        feature_norm, feature_grad * factor, feature_first, feature_second, rate_vector, 0.0
    )
    projection_out = adamw(
        projection, proj_grad, projection_first, projection_second, rate_matrix, decay_weight
    )
    vector_out = adamw(vectors, vector_grad * factor, vector_first, vector_second, rate_vector, 0.0)
    conv_out = adamw(conv_weight, kernel_grad, conv_first, conv_second, rate_matrix, decay_weight)
    head_out = adamw(head, head_grad, head_first, head_second, rate_matrix, decay_weight)
    cluster_out = adamw(
        clusters, cluster_grad, cluster_first, cluster_second, rate_matrix, decay_weight
    )
    statistics_new, update_rows = shampoo_plain(block_rows, statistics)
    blocks_new = blocks - rate_shampoo * (update_rows + decay_weight * blocks)
    return (
        loss_sum,
        masked_count,
        grad_norm,
        *feature_out,
        *projection_out,
        *vector_out,
        *conv_out,
        *head_out,
        *cluster_out,
        block_rows,
        statistics_new,
        blocks_new,
    )


def solution(mesh):
    in_specs = (
        P(None, ("dp", "group"), None, None),
        P(None, ("dp", "group"), None),
        P(None, ("dp", "group"), None),
        P(),
        P(),
        P(),
        P("dp", "group"),
        P("dp", "group"),
        P("dp", "group"),
        P(),
        P(),
        P(),
        P("group", None, "dp"),
        P("group", None, "dp"),
        P("group", None, "dp"),
        P("dp", "group"),
        P("dp", "group"),
        P("dp", "group"),
        P("group", "dp"),
        P("group", "dp"),
        P("group", "dp"),
        P("group", "dp", None),
        P("group", None, "dp", None),
    )
    out_specs = (
        P(),
        P(),
        P(),
        P(),
        P(),
        P(),
        P("dp", "group"),
        P("dp", "group"),
        P("dp", "group"),
        P(),
        P(),
        P(),
        P("group", None, "dp"),
        P("group", None, "dp"),
        P("group", None, "dp"),
        P("dp", "group"),
        P("dp", "group"),
        P("dp", "group"),
        P("group", "dp"),
        P("group", "dp"),
        P("group", "dp"),
        P("group", "dp", None),
        P("group", None, "dp", None),
        P("group", "dp", None),
    )
    return jax.shard_map(
        functools.partial(body, (mesh.shape["dp"], mesh.shape["group"])), mesh=mesh, in_specs=in_specs, out_specs=out_specs, check_vma=False)
```

```python
import functools

import jax
import jax.numpy as jnp
from jax import lax
from jax.experimental import pallas as pl
from jax.experimental.pallas import tpu as pltpu
from jax.sharding import PartitionSpec as P

D = 768
HEADS = 12
HEAD = 64
TAPS = 128
CLIP = 128
SPAN = 10
NEWTON = 3
STEP = 10


HIGH = lax.Precision.HIGHEST
beta_one = 0.9
beta_two = 0.98
adam_eps = 1e-08
rate_matrix = 0.02
rate_vector = 0.5
rate_shampoo = 0.2
decay_weight = 0.01
stat_decay = 0.95
max_norm = 0.01
inv_temp = 10.0
STRIDE = 4


def for_sending(array):

    def short(part):
        return part.astype(jnp.bfloat16) if part.dtype == jnp.float32 else part

    return jax.tree.map(short, array)


def spread_2(array, axis, root):
    mine = lax.axis_index(axis) == root
    return lax.psum(jnp.where(mine, array, jnp.zeros_like(array)), axis)


def to_low(values):
    return values.astype(jnp.bfloat16)


def frame_mask(starts):
    frames = jnp.arange(CLIP, dtype=jnp.int32)[:, None]
    inside = (frames >= starts[None, :]) & (frames < starts[None, :] + SPAN)
    return jnp.any(inside, axis=1).astype(jnp.float32)


def inverse_root(matrix):
    size = matrix.shape[0]
    identity = jnp.eye(size, dtype=jnp.float32)
    damped = matrix + 0.0001 * (jnp.trace(matrix) / size) * identity
    magnitude = jnp.sqrt(jnp.sum(damped * damped))
    current = damped / magnitude
    result = identity * magnitude ** (-0.25)
    for sweep in range(NEWTON):
        factor = (5.0 * identity - current) * 0.25
        result = jnp.dot(result, factor, precision=HIGH)
        square = jnp.dot(factor, factor, precision=HIGH)
        current = jnp.dot(jnp.dot(square, square, precision=HIGH), current, precision=HIGH)
    return result


def adamw(weight, grad, first, second, rate, decay):
    first = beta_one * first + (1 - beta_one) * grad
    second = beta_two * second + (1 - beta_two) * grad * grad
    corrected = first / (1 - beta_one**STEP)
    scaled = jnp.sqrt(second / (1 - beta_two**STEP)) + adam_eps
    return (first, second, weight - rate * (corrected / scaled + decay * weight))


def reduce_grads(parts):
    proj_part, kernel_part, head_part, center_part, block_part = parts
    grouped = (
        lax.psum_scatter(proj_part, "group", scatter_dimension=1, tiled=True),
        lax.psum_scatter(kernel_part, "group", scatter_dimension=0, tiled=True),
        lax.psum_scatter(head_part, "group", scatter_dimension=1, tiled=True),
        lax.psum_scatter(center_part, "group", scatter_dimension=0, tiled=True),
        lax.psum_scatter(block_part, "group", scatter_dimension=0, tiled=True),
    )
    proj_part, kernel_part, head_part, center_part, block_part = grouped
    return (
        lax.psum_scatter(proj_part, "dp", scatter_dimension=0, tiled=True),
        lax.psum_scatter(kernel_part, "dp", scatter_dimension=2, tiled=True),
        lax.psum_scatter(head_part, "dp", scatter_dimension=0, tiled=True),
        lax.psum_scatter(center_part, "dp", scatter_dimension=1, tiled=True),
        lax.psum_scatter(block_part, "dp", scatter_dimension=1, tiled=True),
    )


def gather_plain(projection, conv_weight, head, clusters, blocks):
    gathered = (
        lax.all_gather(to_low(projection), "dp", axis=0, tiled=True),
        lax.all_gather(to_low(conv_weight), "dp", axis=2, tiled=True),
        lax.all_gather(to_low(head), "dp", axis=0, tiled=True),
        lax.all_gather(to_low(clusters), "dp", axis=1, tiled=True),
        lax.all_gather(to_low(blocks), "dp", axis=1, tiled=True),
    )
    proj_part, kernel_part, head_part, center_part, block_part = gathered
    return (
        lax.all_gather(proj_part, "group", axis=1, tiled=True),
        lax.all_gather(kernel_part, "group", axis=0, tiled=True),
        lax.all_gather(head_part, "group", axis=1, tiled=True),
        lax.all_gather(center_part, "group", axis=0, tiled=True),
        lax.all_gather(block_part, "group", axis=0, tiled=True),
    )


def shampoo_plain(block_rows, statistics):
    full_blocks = lax.all_gather(block_rows.astype(jnp.bfloat16), "dp", axis=1, tiled=True).astype(
        block_rows.dtype
    )
    rows = block_rows.shape[1]
    here = lax.axis_index("dp")
    first_row = here * rows
    column_slice = lax.dynamic_slice_in_dim(full_blocks, first_row, rows, 2)
    left_rows = stat_decay * statistics[:, 0] + (1 - stat_decay) * jnp.einsum(
        "brk,bck->brc", block_rows, full_blocks, precision=HIGH
    )
    right_rows = stat_decay * statistics[:, 1] + (1 - stat_decay) * jnp.einsum(
        "bkr,bkc->brc", column_slice, full_blocks, precision=HIGH
    )
    group_blocks = block_rows.shape[0]
    dp_size = lax.axis_size("dp")
    owners = [
        (2 * member + side) * dp_size // (2 * group_blocks)
        for member in range(group_blocks)
        for side in range(2)
    ]
    left_full, right_full = (
        lax.all_gather(left_rows.astype(jnp.bfloat16), "dp", axis=1, tiled=True).astype(
            left_rows.dtype
        ),
        lax.all_gather(right_rows.astype(jnp.bfloat16), "dp", axis=1, tiled=True).astype(
            right_rows.dtype
        ),
    )
    sources = [
        left_full[member] if side == 0 else right_full[member]
        for member in range(group_blocks)
        for side in range(2)
    ]
    roots = []
    for index in range(2 * group_blocks):
        owner = owners[index]
        root = lax.cond(here == owner, inverse_root, jnp.zeros_like, sources[index])
        root = spread_2(for_sending(root), "dp", owner).astype(root.dtype)
        roots.append(root)
    stacked = jnp.stack(roots).reshape(group_blocks, 2, D, D)
    left_root_rows = lax.dynamic_slice_in_dim(stacked[:, 0], first_row, rows, 1)
    update_rows = jnp.einsum(
        "brk,bkc->brc",
        jnp.einsum("brk,bkc->brc", left_root_rows, full_blocks, precision=HIGH),
        stacked[:, 1],
        precision=HIGH,
    )
    return jnp.stack([left_rows, right_rows], 1), update_rows


MESH = pl.DeviceIdType.MESH
HBM = pl.BlockSpec(memory_space=pltpu.HBM)
VMEM = pl.BlockSpec(memory_space=pltpu.VMEM)
VMEM_LIMIT = 60 * 1024 * 1024


class Place:
    def __init__(self, dp_size, group_size):
        self.dp_size, self.group_size = dp_size, group_size
        self.lines = dp_size // 2
        self.dp, self.group = lax.axis_index("dp"), lax.axis_index("group")
        self.z, self.y = self.dp // 2, self.dp % 2
        self.x, self.core = self.group // 2, self.group % 2

    def at(self, z, flip_y=0, flip_x=0, flip_core=0):
        y = self.y + flip_y * (1 - 2 * self.y)
        x = self.x + flip_x * (1 - 2 * self.x)
        core = self.core + flip_core * (1 - 2 * self.core)
        return (z * 2 + y, x * 2 + core)

    def near(self, z, p, q):
        return self.at(z, p * (1 - self.core) + q * self.core, q * (1 - self.core) + p * self.core)

    def across(self, z, p, q):
        return self.at(z, p * self.core + q * (1 - self.core), q * self.core + p * (1 - self.core), 1)


def greet(place):
    barrier = pltpu.get_barrier_semaphore()
    first = place.x * 2
    for other in range(place.dp_size):
        for core in range(2):

            @pl.when((place.dp != other) | (place.core != core))
            def _():
                pl.semaphore_signal(
                    barrier, inc=1, device_id=(other, first + core), device_id_type=MESH
                )

    for core in range(2):
        pl.semaphore_signal(
            barrier,
            inc=1,
            device_id=(place.dp, (1 - place.x) * 2 + core),
            device_id_type=MESH,
        )
    pl.semaphore_wait(barrier, 2 * place.dp_size - 1 + 2)


def guarded(condition, action):
    if condition is None:
        action()
    else:
        pl.when(condition)(action)


def both(one, two):
    if one is None:
        return two
    if two is None:
        return one
    return one & two


def piece_at(kind, ref, dp, group, shape):
    if kind == "blocks":
        start = pl.multiple_of(dp * shape[1], shape[1])
        return ref.at[pl.ds(group * shape[0], shape[0]), pl.ds(start, shape[1])]
    if kind == "conv":
        return ref.at[group, pl.ds(dp * shape[0], shape[0])]
    return ref.at[dp, group]


KINDS = ("conv", "small", "blocks")


def make_shards(refs, mask, conv, small, blocks_low, stats_low):
    starts, projection, weight, head_t, clusters_t, blocks, statistics = refs
    for clip in range(starts.shape[0]):
        frame = lax.broadcasted_iota(jnp.int32, (CLIP, starts.shape[1]), 0)
        begins = starts[clip : clip + 1, :]
        inside = ((frame >= begins) & (frame < begins + SPAN)).astype(jnp.float32)
        mask[clip * CLIP : (clip + 1) * CLIP, :] = jnp.max(inside, 1, keepdims=True)
    note = jnp.sum(mask[...], 0, keepdims=True)
    runs, steps, c, channels = weight.shape
    for offset in range(steps):
        turned = weight[:, offset].reshape(runs * c, channels).T.astype(jnp.bfloat16)
        for group in range(channels // c):
            conv[group, offset * c : (offset + 1) * c, :] = turned[group * c : (group + 1) * c]
    low = jnp.bfloat16

    def padded(values):
        spare = jnp.zeros((values.shape[0], 128 - values.shape[1]), jnp.float32)
        return jnp.concatenate([values, spare], 1)

    small[0:64, :] = projection[:, 0:128].astype(low)
    small[64:128, :] = padded(projection[:, 128:]).astype(low)
    small[128:224, :] = padded(head_t[...].T).astype(low)
    lane = lax.broadcasted_iota(jnp.int32, (32, 128), 1)
    small[224:256, :] = jnp.where(lane < CLUSTER_ROWS, padded(clusters_t[...]), note).astype(low)
    blocks_low[...] = blocks[...].astype(low)
    stats_low[...] = statistics[...].astype(low)


def gather_kernel(sizes, shapes, taps, *refs):
    place = Place(*sizes)
    count = len(KINDS)
    refs = list(refs)

    def pull(number):
        taken = refs[:number]
        del refs[:number]
        return taken

    raw, (features, feature_norm, vectors) = pull(7), pull(3)
    outs, results, (mask, stats_low) = pull(count), pull(7), pull(2)
    ins, (small_here,), scratch = pull(count), pull(1), pull(5)
    (send_sem, recv_sem, own_sem, small_sem) = pull(4)
    z, last = place.z, place.lines - 1
    me = (place.dp, place.group)
    make_shards(raw, mask, *ins, stats_low)
    greet(place)
    sent = []
    slots = [0] * count
    conv, tiny = KINDS.index("conv"), KINDS.index("small")
    enter, project, convolve, leave = front_compute(
        taps,
        (features, mask, feature_norm, vectors, small_here, outs[conv]),
        results,
        scratch,
    )

    def view(k, source):
        return piece_at(KINDS[k], outs[k], source[0], source[1], shapes[k])

    def identity(source):
        return source[0] * place.group_size + source[1]

    def copy_of(k, source, target, slot, own=False):
        spot = view(k, source)
        return pltpu.make_async_remote_copy(
            src_ref=ins[k] if own else spot,
            dst_ref=spot,
            send_sem=send_sem.at[k, slot],
            recv_sem=recv_sem.at[k, identity(source)],
            device_id=target,
            device_id_type=MESH,
        )

    def send(k, source, target, condition=None, own=False):
        slot = slots[k]
        slots[k] += 1
        guarded(condition, lambda: copy_of(k, source, target, slot, own).start())
        sent.append((k, source, target, slot, condition, own))

    def arrive(k, source, condition=None):
        guarded(condition, lambda: copy_of(k, source, me, 0).wait_recv())

    links = {
        "left": (place.at(z - 1), z > 0),
        "right": (place.at(z + 1), z < last),
        "p": (place.near(z, 1, 0), None),
        "q": (place.near(z, 0, 1), None),
        "core": (place.at(z, 0, 0, 1), None),
    }

    def forward(k, source, ways, condition=None, own=False):
        for way in ways:
            target, open_way = links[way]
            send(k, source, target, both(condition, open_way), own)

    def spots(offset):
        if offset == 0:
            return [(z, None, ("left", "right"))]
        return [
            (z - offset, z >= offset, ("right",)),
            (z + offset, z + offset <= last, ("left",)),
        ]

    def take(k, source, condition, ways):
        arrive(k, source, condition)
        forward(k, source, ways, condition)

    def step_z_first(k, step):
        if step == 0:
            forward(k, me, ("left", "right", "q", "p", "core"), own=True)
            return
        if step < place.lines:
            for spot, there, ways in spots(step):
                take(k, place.near(spot, 0, 0), there, ways + ("q", "p", "core"))
        if 0 <= step - 1 < place.lines:
            for spot, there, _ in spots(step - 1):
                take(k, place.near(spot, 1, 0), there, ("q", "core"))
                take(k, place.near(spot, 0, 1), there, ("core",))
        if 0 <= step - 2 < place.lines:
            for spot, there, _ in spots(step - 2):
                take(k, place.near(spot, 1, 1), there, ("core",))

    def step_z_second(k, step):
        if step == 0:
            forward(k, me, ("q", "left", "right", "p", "core"), own=True)
            return
        if step == 1:
            take(k, place.near(z, 0, 1), None, ("left", "right", "p", "core"))
        if step < place.lines:
            for spot, there, ways in spots(step):
                take(k, place.near(spot, 0, 0), there, ways + ("p", "core"))
        if 1 <= step - 1 < place.lines:
            for spot, there, ways in spots(step - 1):
                take(k, place.near(spot, 0, 1), there, ways + ("p", "core"))
        if 0 <= step - 1 < place.lines:
            for spot, there, _ in spots(step - 1):
                take(k, place.near(spot, 1, 0), there, ("core",))
        if 0 <= step - 2 < place.lines:
            for spot, there, _ in spots(step - 2):
                take(k, place.near(spot, 1, 1), there, ("core",))

    own_copies = [
        pltpu.make_async_copy(ins[k], view(k, me), own_sem.at[k]) for k in range(count)
    ]
    def from_core(k):
        for spot in range(place.lines):
            for p in range(2):
                for q in range(2):
                    arrive(k, place.across(spot, p, q))

    def read_small():
        copy = pltpu.make_async_copy(outs[tiny], small_here, small_sem)
        copy.start()
        copy.wait()

    def compute(part):
        groups = outs[conv].shape[1]
        if part == 0:
            read_small()
            project()
        elif part < 4:
            convolve(groups * (part - 1) // 3, groups * part // 3)
        else:
            leave()

    for name, kind, step in GATHER_PLAN:
        if name == "step":
            k = KINDS.index(kind)
            (step_z_second if kind == "blocks" else step_z_first)(k, step)
            if step == 0:
                own_copies[k].start()
        elif name == "core":
            from_core(KINDS.index(kind))
            own_copies[KINDS.index(kind)].wait()
        elif name == "enter":
            enter()
        else:
            compute(step)
    from_core(KINDS.index("blocks"))
    own_copies[KINDS.index("blocks")].wait()
    for k, source, target, slot, condition, own in sent:
        guarded(
            condition,
            lambda k=k, source=source, target=target, slot=slot, own=own: copy_of(
                k, source, target, slot, own
            ).wait_send(),
        )


def full_shapes(sizes, shapes):
    dp_size, group_size = sizes
    conv, small, blocks = shapes
    return [
        (group_size, dp_size * conv[0]) + conv[1:],
        (dp_size, group_size) + small,
        (group_size * blocks[0], dp_size * blocks[1], blocks[2]),
    ]


def gather_weights(sizes, shapes, taps, raw, features, feature_norm, vectors):
    low, out = jnp.bfloat16, jax.ShapeDtypeStruct
    full = full_shapes(sizes, shapes)
    frames, width = features.shape
    count, devices = len(shapes), sizes[0] * sizes[1]
    dma = pltpu.SemaphoreType.DMA
    return pl.pallas_call(
        functools.partial(gather_kernel, sizes, shapes, taps),
        out_shape=[out(shape, low) for shape in full]
        + front_shapes(frames, width)
        + [out((frames, 1), jnp.float32), out(raw[-1].shape, low)],
        in_specs=[VMEM] * (len(raw) + 3),
        out_specs=[HBM] * count + [VMEM] * 9,
        scratch_shapes=[pltpu.VMEM(shape, low) for shape in shapes]
        + [pltpu.VMEM(full[1], low)]
        + front_scratch(full[0], frames)
        + [
            dma((count, 3 * devices)),
            dma((count, devices)),
            dma((count,)),
            dma,
        ],
        name="gather_front",
        compiler_params=pltpu.CompilerParams(
            collective_id=0, has_side_effects=True, vmem_limit_bytes=VMEM_LIMIT
        ),
    )(*raw, features, feature_norm, vectors)


class StatRows:
    def __init__(self, sizes, stats_in, stats_out, sems):
        self.place = Place(*sizes)
        self.members, _, self.rows, _ = stats_in.shape
        self.owners = Owners(self.place, self.members)
        self.stats_in, self.stats_out = stats_in, stats_out
        self.send_sem, self.recv_sem, self.own_sem = sems

    def spot(self, other):
        return pl.ds(pl.multiple_of(other * self.rows, self.rows), self.rows)

    def away(self, member, side):
        place = self.place
        return pltpu.make_async_remote_copy(
            src_ref=self.stats_in.at[member, side],
            dst_ref=self.stats_out.at[self.spot(place.dp)],
            send_sem=self.send_sem.at[member, side],
            recv_sem=self.recv_sem.at[place.dp],
            device_id=(self.owners.of(member), place.x * 2 + side),
            device_id_type=MESH,
        )

    def here(self, member, side):
        return pltpu.make_async_copy(
            self.stats_in.at[member, side], self.stats_out.at[self.spot(self.place.dp)], self.own_sem
        )

    def each(self, away, here):
        place = self.place
        for member in range(self.members):
            for side in range(2):
                mine = (place.dp == self.owners.of(member)) & (place.core == side)
                pl.when(jnp.logical_not(mine))(functools.partial(away, member, side))
                pl.when(mine)(functools.partial(here, member, side))

    def start(self):
        self.each(lambda m, s: self.away(m, s).start(), lambda m, s: self.here(m, s).start())

    def finish(self):
        place = self.place
        self.each(lambda m, s: self.away(m, s).wait_send(), lambda m, s: self.here(m, s).wait())

        @pl.when(self.owners.here)
        def _():
            for other in range(place.dp_size):

                @pl.when((place.dp != other) | (place.group != self.owners.group))
                def _(other=other):
                    pltpu.make_async_remote_copy(
                        src_ref=self.stats_in.at[0, 0],
                        dst_ref=self.stats_out.at[self.spot(other)],
                        send_sem=self.send_sem.at[0, 0],
                        recv_sem=self.recv_sem.at[other],
                        device_id=(place.dp, place.group),
                        device_id_type=MESH,
                    ).wait_recv()


def shift_right(values, by):
    if by == 0:
        return values
    parts = []
    for first in range(0, values.shape[1], CLIP):
        part = values[:, first : first + CLIP]
        lane = lax.broadcasted_iota(jnp.int32, part.shape, 1)
        turned = pltpu.roll(part, by % CLIP, 1)
        inside = lane >= by if by > 0 else lane < CLIP + by
        parts.append(jnp.where(inside, turned, 0.0))
    return jnp.concatenate(parts, 1)


def place_windows(hidden, windows, taps):
    channels = hidden.shape[0]
    runs, half = taps // STRIDE, taps // STRIDE // 2
    for run in range(runs):
        by = STRIDE * (half - 1 - run) if run < half else -STRIDE * (run - half)
        windows[run * channels : (run + 1) * channels, :] = shift_right(hidden, by).astype(
            jnp.bfloat16
        )


def conv_group(hidden, weight_at, windows, taps, shape):
    channels = hidden.shape[0]
    chunks, _, _, chunk = shape
    place_windows(hidden, windows, taps)
    total = None
    for side in range(2):
        part = None
        for index in range(side * chunks // 2, (side + 1) * chunks // 2):
            term = dot(weight_at(index), windows[index * chunk : (index + 1) * chunk, :])
            part = term if part is None else part + term
        for offset in range(STRIDE):
            by = STRIDE - offset if side == 0 else -offset
            moved = shift_right(part[offset * channels : (offset + 1) * channels], by)
            total = moved if total is None else total + moved
    return total


def conv_group_back(hidden, grad, weight_at, put, windows, moved, taps, shape):
    channels = hidden.shape[0]
    chunks, _, _, chunk = shape
    half, runs = taps // STRIDE // 2, chunk // channels
    place_windows(hidden, windows, taps)
    total = None
    for side in range(2):
        for offset in range(STRIDE):
            by = offset - STRIDE if side == 0 else offset
            moved[offset * channels : (offset + 1) * channels, :] = shift_right(grad, by).astype(
                jnp.bfloat16
            )
        for index in range(side * chunks // 2, (side + 1) * chunks // 2):
            put(
                index,
                dot_nt(moved[...], windows[index * chunk : (index + 1) * chunk, :]).astype(
                    jnp.bfloat16
                ),
            )
            turned = dot_tn(weight_at(index), moved[...])
            for step in range(runs):
                run = index * runs + step
                by = -STRIDE * (half - 1 - run) if run < half else STRIDE * (run - half)
                part = shift_right(turned[step * channels : (step + 1) * channels], by)
                total = part if total is None else total + part
    return total


def over_rows(total, tile, action):
    def step(index, _):
        action(pl.ds(pl.multiple_of(index * tile, tile), tile))
        return 0

    lax.fori_loop(0, total // tile, step, 0, unroll=2)


def dot(one, two):
    return jnp.dot(one, two, preferred_element_type=jnp.float32)


def dot_nt(one, two):
    return lax.dot_general(one, two, (((1,), (1,)), ((), ())), preferred_element_type=jnp.float32)


def dot_tn(one, two):
    return lax.dot_general(one, two, (((0,), (0,)), ((), ())), preferred_element_type=jnp.float32)


def norm_parts(values):
    average = jnp.mean(values, -1, keepdims=True)
    centred = values - average
    inverse = lax.rsqrt(jnp.mean(centred * centred, -1, keepdims=True) + 1e-05)
    return centred * inverse, inverse


def norm_back(upstream, unit, inverse, gain):
    scaled = upstream * gain
    along = jnp.mean(scaled * unit, -1, keepdims=True)
    return inverse * (scaled - jnp.mean(scaled, -1, keepdims=True) - unit * along)


def gelu_pair(values):
    below = 0.5 + 0.5 * lax.erf(values * 0.7071067811865476)
    density = jnp.exp(values * values * -0.5) * 0.3989422804014327
    return values * below, below + values * density


def add_row(ref, row, values):
    ref[row : row + 1, :] += jnp.sum(values, 0, keepdims=True)


def front_compute(taps, refs, outs, scratch):
    features, mask, feature_norm, vectors, small, kernel = refs
    feature_unit, normed, hidden_t, encoded, encoder_unit, encoder_inverse, slope = outs
    held, windows, hidden, out_t, load_sem = scratch
    frames = features.shape[0]
    groups = kernel.shape[1]
    channels = hidden_t.shape[0] // groups

    def load(group):
        return pltpu.make_async_copy(kernel.at[:, group], held.at[:, group], load_sem.at[group])

    def enter():
        def one(at):
            unit, _ = norm_parts(features[at, :].astype(jnp.float32))
            feature_unit[at, :] = unit
            scaled = unit * feature_norm[0:1, :] + feature_norm[1:2, :]
            normed[at, :] = scaled.astype(jnp.bfloat16)

        over_rows(frames, 32, one)

    def project():
        for group in range(groups):
            load(group).start()
        normed_t = normed[...].T
        parts, columns = small.shape[0], small.shape[1]
        third = D // columns
        for group in range(columns):
            for first, size in ((0, 128), (128, third - 128)):
                row = first // 2
                part = small[:, group, row : row + 64, :].reshape(parts * 64, 128)
                at = group * third + first
                out_t[at : at + size, :] = dot_tn(part, normed_t)[:size]
        hidden[...] = jnp.where(mask[...] > 0, vectors[0:1, :], out_t[...].T)
        hidden_t[...] = hidden[...].T.astype(jnp.bfloat16)

    def one_group(group, _):
        load(group).wait()
        at = pl.ds(pl.multiple_of(group * channels, channels), channels)
        out_t[at, :] = conv_group(
            hidden_t[at, :].astype(jnp.float32),
            lambda index: held[index, group],
            windows,
            taps,
            kernel.shape,
        )
        return 0

    def convolve(first, last):
        lax.fori_loop(first, last, one_group, 0)

    def leave():
        slope[...] = out_t[...].T

        def one(at):
            active, derivative = gelu_pair(slope[at, :])
            slope[at, :] = derivative
            unit, inverse = norm_parts(hidden[at, :] + active)
            encoder_unit[at, :] = unit
            encoder_inverse[at, :] = inverse
            encoded[at, :] = unit * vectors[1:2, :] + vectors[2:3, :]

        over_rows(frames, 32, one)

    return enter, project, convolve, leave


def front_kernel(taps, *refs):
    enter, project, convolve, leave = front_compute(taps, refs[:6], refs[6:13], refs[13:])
    enter()
    project()
    convolve(0, refs[5].shape[1])
    leave()


def front_shapes(frames, width):
    out, full, low = jax.ShapeDtypeStruct, jnp.float32, jnp.bfloat16
    return [
        out((frames, width), full),
        out((frames, width), low),
        out((D, frames), low),
        out((frames, D), full),
        out((frames, D), full),
        out((frames, 1), full),
        out((frames, D), full),
    ]


def front_scratch(kernel_shape, frames):
    chunks, groups, rows, chunk = kernel_shape
    return [
        pltpu.VMEM(kernel_shape, jnp.bfloat16),
        pltpu.VMEM((chunks * chunk, frames), jnp.bfloat16),
        pltpu.VMEM((frames, D), jnp.float32),
        pltpu.VMEM((D, frames), jnp.float32),
        pltpu.SemaphoreType.DMA((groups,)),
    ]


def front(features, mask, feature_norm, vectors, small, kernel, taps):
    frames, width = features.shape
    return pl.pallas_call(
        functools.partial(front_kernel, taps),
        out_shape=front_shapes(frames, width),
        in_specs=[VMEM] * 5 + [HBM],
        out_specs=[VMEM] * 7,
        scratch_shapes=front_scratch(kernel.shape, frames),
        name="front",
        compiler_params=pltpu.CompilerParams(vmem_limit_bytes=VMEM_LIMIT),
    )(features, mask, feature_norm, vectors, small, kernel)


def trunk_kernel(sizes, *refs):
    refs = list(refs)
    rows_moved = None
    if sizes is not None:
        stats_in, stats_out = refs.pop(6), refs.pop(12)
        rows_moved = StatRows(sizes, stats_in, stats_out, refs[-3:])
        refs = refs[:-3]
    (
        encoded, mask, labels, vectors, small, blocks,
        encoded_grad, block_grad, head_grad, center_grad_t, rows_out, counted,
        head, table, centers, held, made, low, triple, attention, mixed, unit_one, inverse_one, middle, middle_low,
        active, slope, unit_two, inverse_two, work, work_low, flow_low, triple_grad, turned,
        load_sem, save_sem,
    ) = refs
    frames = encoded.shape[0]
    count = blocks.shape[0]
    ups = (count - 4) // 2
    tile = 32
    pairs = D // 128

    def load(block):
        return pltpu.make_async_copy(blocks.at[block], held.at[block], load_sem.at[block])

    def save(block):
        return pltpu.make_async_copy(made.at[block], block_grad.at[block], save_sem.at[block])

    for block in range(count):
        load(block).start()
    if rows_moved is not None:
        greet(rows_moved.place)
        rows_moved.start()
    rows_out[...] = jnp.zeros_like(rows_out)
    parts, columns = small.shape[0], small.shape[1]
    notes = small[:, :, 224:240, :].astype(jnp.float32)
    first = lax.broadcasted_iota(jnp.int32, notes.shape, 2) == 0
    first &= lax.broadcasted_iota(jnp.int32, notes.shape, 3) == CLUSTER_ROWS
    notes = jnp.sum(jnp.where(first, notes, 0.0), (0, 1))
    masked = jnp.sum(jnp.sum(notes, 1, keepdims=True), 0, keepdims=True)
    counted[...] = masked

    def to_inputs(at):
        low[at, :] = encoded[at, :].astype(jnp.bfloat16)

    over_rows(frames, tile, to_inputs)

    def first_three(block, _):
        load(block).wait()
        triple[block] = dot(low[...], held[block]).astype(jnp.bfloat16)
        return 0

    lax.fori_loop(0, 3, first_three, 0)
    lane = lax.broadcasted_iota(jnp.int32, (CLIP, 128), 1)
    even = lane < HEAD

    def apart(values):
        zero = jnp.zeros_like(values)
        return jnp.concatenate([jnp.where(even, values, zero), jnp.where(even, zero, values)], 0)

    def beside(values):
        return jnp.concatenate([values[:CLIP], values[CLIP:]], 1)

    def spot(index):
        at = pl.ds(pl.multiple_of(index // pairs * CLIP, CLIP), CLIP)
        return at, pl.ds(pl.multiple_of(index % pairs * 128, 128), 128)

    def attend(index, _):
        at, lanes = spot(index)
        query, keys, values = triple[0, at, lanes], triple[1, at, lanes], triple[2, at, lanes]
        scores = dot_nt(apart(query), keys) * HEAD ** (-0.5)
        raised = jnp.exp(scores - jnp.max(scores, -1, keepdims=True))
        full = raised / jnp.sum(raised, -1, keepdims=True)
        attention[index] = full
        mixed[at, lanes] = dot(beside(full.astype(jnp.bfloat16)), apart(values)).astype(jnp.bfloat16)
        return 0

    lax.fori_loop(0, frames // CLIP * pairs, attend, 0, unroll=pairs)
    load(3).wait()
    work[...] = dot(mixed[...], held[3])

    def first_norm(at):
        unit, inverse = norm_parts(encoded[at, :] + work[at, :])
        unit_one[at, :] = unit
        inverse_one[at, :] = inverse
        value = unit * vectors[3:4, :] + vectors[4:5, :]
        middle[at, :] = value
        middle_low[at, :] = value.astype(jnp.bfloat16)

    over_rows(frames, tile, first_norm)

    def expand(step, _):
        load(4 + step).wait()
        slope[step] = dot(middle_low[...], held[4 + step])

        def bend(at):
            value, derivative = gelu_pair(slope[step, at, :])
            active[step, at, :] = value.astype(jnp.bfloat16)
            slope[step, at, :] = derivative

        over_rows(frames, tile, bend)
        return 0

    lax.fori_loop(0, ups, expand, 0)

    def contract(step, _):
        load(4 + ups + step).wait()
        middle[...] += dot(active[step], held[4 + ups + step])
        return 0

    lax.fori_loop(0, ups, contract, 0)

    def second_norm(at):
        unit, inverse = norm_parts(middle[at, :])
        unit_two[at, :] = unit
        inverse_two[at, :] = inverse
        flow_low[at, :] = (unit * vectors[5:6, :] + vectors[6:7, :]).astype(jnp.bfloat16)

    over_rows(frames, tile, second_norm)
    table[...] = jnp.zeros_like(table)
    for group in range(columns):
        across = slice(group * 128, group * 128 + 128)
        head[:, across] = small[:, group, 128:224, :].reshape(parts * 96, 128)
        for part in range(parts):
            row = part // 2 * 128 + part % 2 * 32
            table[row : row + 32, across] = small[part, group, 224:256, :].astype(jnp.float32)
    real = lax.broadcasted_iota(jnp.int32, (1, table.shape[1]), 1) % 128 < CLUSTER_ROWS
    table[...] = jnp.where(real, table[...], 0.0)
    size = lax.rsqrt(jnp.sum(table[...] * table[...], 0, keepdims=True) + 1e-06)
    centers[...] = (table[...] * size).astype(jnp.bfloat16)
    embedded = dot(flow_low[...], head[...])
    length = lax.rsqrt(jnp.sum(embedded * embedded, -1, keepdims=True) + 1e-06)
    unit_low = (embedded * length).astype(jnp.bfloat16)
    logits = jnp.where(real, dot(unit_low, centers[...]) * inv_temp, -1e30)
    top = jnp.max(logits, -1, keepdims=True)
    raised = jnp.exp(logits - top)
    amount = jnp.sum(raised, -1, keepdims=True)
    columns_of = labels[...]
    for group in range(1, columns):
        columns_of = columns_of + jnp.where(labels[...] >= group * CLUSTER_ROWS, 128 - CLUSTER_ROWS, 0)
    choose = columns_of == lax.broadcasted_iota(jnp.int32, logits.shape, 1)
    target = jnp.sum(jnp.where(choose, logits, 0.0), -1, keepdims=True)
    losses = mask[...] * (jnp.log(amount) + top - target)
    rows_out[7:8, :] = jnp.broadcast_to(jnp.sum(losses, 0, keepdims=True), (1, D))
    logit_grad = (
        (raised / amount - choose.astype(jnp.float32)) * (mask[...] * (1.0 / masked))
    ).astype(jnp.bfloat16)
    unit_grad = dot_nt(logit_grad, centers[...]) * inv_temp
    spread = dot_tn(unit_low, logit_grad) * inv_temp
    shared = jnp.sum(spread * table[...], 0, keepdims=True)
    spread = size * spread - table[...] * (size * size * size * shared)
    for group in range(columns):
        center_grad_t[group * 64 : group * 64 + 64, :] = spread[group * 128 : group * 128 + 64, :]
    along = jnp.sum(unit_grad * embedded, -1, keepdims=True)
    embedded_grad = (
        length * unit_grad - embedded * (length * length * length * along)
    ).astype(jnp.bfloat16)
    work[...] = dot_nt(embedded_grad, head[...])
    head_grad[...] = dot_tn(flow_low[...], embedded_grad).astype(jnp.bfloat16)

    def second_back(at):
        upstream = work[at, :]
        add_row(rows_out, 5, upstream * unit_two[at, :])
        add_row(rows_out, 6, upstream)
        value = norm_back(upstream, unit_two[at, :], inverse_two[at, :], vectors[5:6, :])
        middle[at, :] = value
        flow_low[at, :] = value.astype(jnp.bfloat16)

    over_rows(frames, tile, second_back)
    turned[...] = middle_low[...].T

    def feed_back(step, _):
        work[...] = dot_nt(flow_low[...], held[4 + ups + step])
        made[4 + ups + step] = dot_tn(active[step], flow_low[...]).astype(jnp.bfloat16)
        save(4 + ups + step).start()

        def bend(at):
            work_low[at, :] = (work[at, :] * slope[step, at, :]).astype(jnp.bfloat16)

        over_rows(frames, tile, bend)
        made[4 + step] = dot(turned[...], work_low[...]).astype(jnp.bfloat16)
        save(4 + step).start()
        middle[...] += dot_nt(work_low[...], held[4 + step])
        return 0

    lax.fori_loop(0, ups, feed_back, 0)

    def first_back(at):
        upstream = middle[at, :]
        add_row(rows_out, 3, upstream * unit_one[at, :])
        add_row(rows_out, 4, upstream)
        value = norm_back(upstream, unit_one[at, :], inverse_one[at, :], vectors[3:4, :])
        middle[at, :] = value
        flow_low[at, :] = value.astype(jnp.bfloat16)

    over_rows(frames, tile, first_back)
    made[3] = dot_tn(mixed[...], flow_low[...]).astype(jnp.bfloat16)
    save(3).start()
    work_low[...] = dot_nt(flow_low[...], held[3]).astype(jnp.bfloat16)

    def attend_back(index, _):
        at, lanes = spot(index)
        query, keys, values = triple[0, at, lanes], triple[1, at, lanes], triple[2, at, lanes]
        upstream = apart(work_low[at, lanes])
        full = attention[index]
        full_grad = dot_nt(upstream, values)
        triple_grad[2, at, lanes] = dot_tn(full.astype(jnp.bfloat16), upstream).astype(jnp.bfloat16)
        along = jnp.sum(full * full_grad, -1, keepdims=True)
        score_grad = (full * (full_grad - along)).astype(jnp.bfloat16)
        triple_grad[0, at, lanes] = (
            dot(beside(score_grad), apart(keys)) * HEAD ** (-0.5)
        ).astype(jnp.bfloat16)
        triple_grad[1, at, lanes] = (
            dot_tn(score_grad, apart(query)) * HEAD ** (-0.5)
        ).astype(jnp.bfloat16)
        return 0

    lax.fori_loop(0, frames // CLIP * pairs, attend_back, 0, unroll=pairs)
    turned[...] = low[...].T

    def last_three(block, _):
        made[block] = dot(turned[...], triple_grad[block]).astype(jnp.bfloat16)
        save(block).start()
        middle[...] += dot_nt(triple_grad[block], held[block])
        return 0

    lax.fori_loop(0, 3, last_three, 0)
    encoded_grad[...] = middle[...]
    if rows_moved is not None:
        rows_moved.finish()
    for block in range(count):
        save(block).wait()


def trunk(encoded, mask, labels, vectors, small, blocks, sizes=None, stats_low=None):
    frames, count = encoded.shape[0], blocks.shape[0]
    ups, columns = (count - 4) // 2, small.shape[1] * 128
    full, low = jnp.float32, jnp.bfloat16
    out = jax.ShapeDtypeStruct
    wide, wide_low = pltpu.VMEM((frames, D), full), pltpu.VMEM((frames, D), low)
    column = pltpu.VMEM((frames, 1), full)
    more_in, more_out, sems, settings = [], [], [], {}
    if sizes is not None:
        dma = pltpu.SemaphoreType.DMA
        more_in, more_out = [stats_low], [out((D, D), low)]
        sems = [dma((stats_low.shape[0], 2)), dma((sizes[0],)), dma]
        settings = {"collective_id": 3, "has_side_effects": True}
    return pl.pallas_call(
        functools.partial(trunk_kernel, sizes),
        out_shape=[
            out((frames, D), full),
            out(blocks.shape, low),
            out((D, columns), low),
            out((columns // 2, columns), full),
            out((8, D), full),
            out((1, 1), full),
        ]
        + more_out,
        in_specs=[VMEM] * 5 + [HBM] * (1 + len(more_in)),
        out_specs=[VMEM, HBM] + [VMEM] * 4 + [HBM] * len(more_out),
        scratch_shapes=[
            pltpu.VMEM((D, columns), low),
            pltpu.VMEM((columns, columns), full),
            pltpu.VMEM((columns, columns), low),
            pltpu.VMEM(blocks.shape, low),
            pltpu.VMEM(blocks.shape, low),
            wide_low,
            pltpu.VMEM((3, frames, D), low),
            pltpu.VMEM((frames // CLIP * D // 128, 2 * CLIP, CLIP), full),
            wide_low,
            wide,
            column,
            wide,
            wide_low,
            pltpu.VMEM((ups, frames, D), low),
            pltpu.VMEM((ups, frames, D), full),
            wide,
            column,
            wide,
            wide_low,
            wide_low,
            pltpu.VMEM((3, frames, D), low),
            pltpu.VMEM((D, frames), low),
            pltpu.SemaphoreType.DMA((count,)),
            pltpu.SemaphoreType.DMA((count,)),
        ]
        + sems,
        name="trunk",
        compiler_params=pltpu.CompilerParams(vmem_limit_bytes=VMEM_LIMIT, **settings),
    )(encoded, mask, labels, vectors, small, blocks, *more_in)


LOSS_ROW = 7


class Owners:
    def __init__(self, place, members):
        self.place, self.members = place, members
        self.first = (place.dp_size - 2 * members) // 2
        index = place.dp - self.first
        self.here = (index >= 0) & (index < 2 * members)
        self.group = place.x * 2 + index // members
        self.member = index % members

    def of(self, member):
        return self.first + self.place.core * self.members + member

    def to_rows(self, other, remote_action, local_action):
        place = self.place
        away = (place.dp != other) | (place.group != self.group)
        pl.when(away)(functools.partial(remote_action, other))
        pl.when(jnp.logical_not(away))(local_action)


class Reducer:
    def __init__(self, place, shapes, local, refs, sems):
        self.place, self.shapes, self.local = place, shapes, local
        self.z, self.lines, self.last = place.z, place.lines, place.lines - 1
        self.blocks = KINDS.index("blocks")
        self.rest = [k for k in range(len(KINDS)) if k != self.blocks]
        self.crossed, self.first_in, self.second_in, self.line_in = refs[:4]
        self.held, self.source = refs[4:]
        (
            self.load_sem, self.cross_send, self.cross_recv, self.first_send, self.first_recv,
            self.second_send, self.second_recv, self.left_send, self.left_recv, self.right_send,
            self.right_recv,
        ) = sems
        self.p_mate, self.q_mate = place.near(self.z, 1, 0), place.near(self.z, 0, 1)
        self.c_mate = place.at(self.z, 0, 0, 1)
        self.left, self.right = place.at(self.z - 1), place.at(self.z + 1)

    def remote(self, source, target, send, recv, device):
        return pltpu.make_async_remote_copy(
            src_ref=source,
            dst_ref=target,
            send_sem=send,
            recv_sem=recv,
            device_id=device,
            device_id_type=MESH,
        )

    def load_of(self, p, q, spot):
        k = self.blocks
        dp, group = self.place.near(spot, p, q)
        return pltpu.make_async_copy(
            piece_at("blocks", self.source[k], dp, group, self.shapes[k]),
            self.held.at[p, spot],
            self.load_sem.at[p, q, spot],
        )

    def cross_of(self, k, p, q, spot):
        dp, group = self.place.across(spot, p, q)
        return self.remote(
            piece_at(KINDS[k], self.source[k], dp, group, self.shapes[k]),
            self.crossed[k].at[p, q, spot],
            self.cross_send.at[k, p, q, spot],
            self.cross_recv.at[k, p, q, spot],
            self.c_mate,
        )

    def own(self, k, p, q, spot):
        if k == self.blocks:
            self.load_of(p, q, spot).wait()
            return f32(self.held, (p, spot))
        dp, group = self.place.near(spot, p, q)
        return piece_at(KINDS[k], self.source[k], dp, group, self.shapes[k])[...].astype(jnp.float32)

    def met(self, k, p, q, spot):
        own = self.own(k, p, q, spot)
        self.cross_of(k, p, q, spot).wait_recv()
        return own + f32(self.crossed[k], (p, q, spot))

    def turn(self, index):
        odd = index % 2
        return (1 - odd) * (self.last - index // 2) + odd * (index // 2)

    def first_out(self, k, p, spot):
        return self.remote(
            self.crossed[k].at[p, 1, spot],
            self.first_in[k].at[p, spot],
            self.first_send.at[k, p, spot],
            self.first_recv.at[k, p, spot],
            self.q_mate,
        )

    def stage_one(self, k, index):
        p, spot = 1 - index // self.lines, self.turn(index % self.lines)
        self.crossed[k][p, 1, spot] = self.met(k, p, 1, spot).astype(jnp.bfloat16)
        self.first_out(k, p, spot).start()
        if k == self.blocks:
            self.load_of(p, 0, spot).start()

    def joined(self, k, p, spot):
        total = self.met(k, p, 0, spot)
        self.first_out(k, p, spot).wait_recv()
        return total + f32(self.first_in[k], (p, spot))

    def second_out(self, k, spot):
        return self.remote(
            self.crossed[k].at[1, 0, spot],
            self.second_in[k].at[spot],
            self.second_send.at[k, spot],
            self.second_recv.at[k, spot],
            self.p_mate,
        )

    def stage_two(self, k, index):
        spot = self.turn(index)
        self.crossed[k][1, 0, spot] = self.joined(k, 1, spot).astype(jnp.bfloat16)
        self.second_out(k, spot).start()

    def line_total(self, k, spot):
        total = self.joined(k, 0, spot)
        self.second_out(k, spot).wait_recv()
        return total + f32(self.second_in[k], (spot,))

    def line_out(self, k, spot, way):
        if way == "right":
            send, recv, device, slot = self.right_send, self.left_recv, self.right, spot
        else:
            send, recv, device = self.left_send, self.right_recv, self.left
            ends = (self.last - (self.z - 1 - spot)) // self.last
            slot = spot + ends * (self.lines - spot)
        return self.remote(
            self.crossed[k].at[0, 0, spot],
            self.line_in[k].at[slot],
            send.at[k, spot],
            recv.at[k, spot],
            device,
        )

    def came_in(self, k, spot, way):
        recv = self.left_recv if way == "right" else self.right_recv
        send = self.right_send if way == "right" else self.left_send
        return self.remote(
            self.crossed[k].at[0, 0, spot],
            self.line_in[k].at[spot],
            send.at[k, spot],
            recv.at[k, spot],
            self.c_mate,
        )

    def pass_on(self, k, spot, way, inner):
        z = self.z
        if way == "right":
            here = (z < spot) & ((z > 0) if inner else (z == 0))
        else:
            here = (z > spot) & ((z < self.last) if inner else (z == self.last))

        @pl.when(here)
        def _():
            total = self.line_total(k, spot)
            if inner:
                self.came_in(k, spot, way).wait_recv()
                total = total + f32(self.line_in[k], (spot,))
            self.crossed[k][0, 0, spot] = total.astype(jnp.bfloat16)
            self.line_out(k, spot, way).start()

    def line_step(self, k, step, inner):
        self.pass_on(k, self.last - step, "right", inner)
        self.pass_on(k, step, "left", inner)

    def line_end(self, k, out):
        z = self.z
        out[...] = self.line_total(k, z)

        @pl.when(z > 0)
        def _():
            self.came_in(k, z, "right").wait_recv()
            out[...] += f32(self.line_in[k], (z,))

        @pl.when(z < self.last)
        def _():
            self.came_in(k, z, "left").wait_recv()
            out[...] += f32(self.line_in[k], (self.lines,))

    def drain(self):
        for k in range(len(KINDS)):

            def one(spot, _, k=k):
                for p in range(2):
                    for q in range(2):
                        self.cross_of(k, p, q, spot).wait_send()
                    self.first_out(k, p, spot).wait_send()
                self.second_out(k, spot).wait_send()

                @pl.when(self.z < spot)
                def _():
                    self.line_out(k, spot, "right").wait_send()

                @pl.when(self.z > spot)
                def _():
                    self.line_out(k, spot, "left").wait_send()

                return 0

            lax.fori_loop(0, self.lines, one, 0)


def f32(ref, at):
    return ref[at].astype(jnp.float32)


def back_compute(taps, refs, made, small_made, rows, scratch, hook):
    (
        encoded_grad, mask, vectors, small, feature_unit, normed, hidden_t,
        encoder_unit, encoder_inverse, slope, trunk_rows, head_grad, center_grad_t, kernel,
    ) = refs
    slots, windows, moved, grad, grad_t, through, through_t, load_sem = scratch
    frames, width = feature_unit.shape
    groups = kernel.shape[1]
    channels = hidden_t.shape[0] // groups

    def load(group):
        slot = group % 2
        return pltpu.make_async_copy(kernel.at[:, group], slots.at[slot], load_sem.at[slot])

    def begin():
        load(0).start()
        rows[...] = jnp.zeros_like(rows)
        rows[0:8, :] = trunk_rows[...]
        over_rows(frames, 32, enter)
        grad_t[...] = through[...].T.astype(jnp.bfloat16)

    def enter(at):
        upstream = encoded_grad[at, :]
        add_row(rows, 1, upstream * encoder_unit[at, :])
        add_row(rows, 2, upstream)
        value = norm_back(upstream, encoder_unit[at, :], encoder_inverse[at, :], vectors[1:2, :])
        grad[at, :] = value
        through[at, :] = value * slope[at, :]

    def one_group(group, _):
        pl.when(group + 1 < groups)(lambda: load(group + 1).start())
        load(group).wait()
        at = pl.ds(pl.multiple_of(group * channels, channels), channels)

        def put(index, value):
            made[index, group] = value

        through_t[at, :] = conv_group_back(
            hidden_t[at, :].astype(jnp.float32),
            grad_t[at, :].astype(jnp.float32),
            lambda index: slots[group % 2, index],
            put,
            windows,
            moved,
            taps,
            kernel.shape,
        )
        hook(group)
        return 0

    def convolve(first, last):
        lax.fori_loop(first, last, one_group, 0)

    def leave(at):
        total = grad[at, :] + through[at, :]
        inside = mask[at, :] > 0
        add_row(rows, 0, jnp.where(inside, total, 0.0))
        grad[at, :] = jnp.where(inside, 0.0, total)

    def finish():
        through[...] = through_t[...].T
        over_rows(frames, 32, leave)
        grad_t[...] = grad[...].T.astype(jnp.bfloat16)
        normed_t = normed[...].T
        parts, columns = small.shape[0], small.shape[1]
        third = D // columns
        total = None
        for group in range(columns):
            one = grad_t[group * third : group * third + 128, :]
            two = grad_t[group * third + 128 : (group + 1) * third, :]
            lane = third - 128
            wide = dot_nt(normed_t, one).astype(jnp.bfloat16)
            thin = dot_nt(normed_t, two).astype(jnp.bfloat16)
            small_made[:, group, 0:64, :] = wide.reshape(parts, 64, 128)
            small_made[:, group, 64:128, :] = jnp.concatenate(
                [thin, jnp.zeros((thin.shape[0], 128 - lane), jnp.bfloat16)], 1
            ).reshape(parts, 64, 128)
            small_made[:, group, 128:224, :] = head_grad[:, group * 128 : group * 128 + 128].reshape(
                parts, 96, 128
            )
            small_made[:, group, 224:256, :] = (
                center_grad_t[:, group * 128 : group * 128 + 128]
                .astype(jnp.bfloat16)
                .reshape(parts, 32, 128)
            )
            first = small[:, group, 0:64, :].reshape(parts * 64, 128)
            second = small[:, group, 64:128, :].reshape(parts * 64, 128)[:, :lane]
            term = dot(first, one) + dot(second, two)
            total = term if total is None else total + term
        normed_grad = total.T
        rows[8:9, 0:width] = jnp.sum(normed_grad * feature_unit[...], 0, keepdims=True)
        rows[9:10, 0:width] = jnp.sum(normed_grad, 0, keepdims=True)

    return begin, convolve, finish


def back_scratch(kernel_shape, frames):
    chunks, groups, rows, chunk = kernel_shape
    full, low = jnp.float32, jnp.bfloat16
    return [
        pltpu.VMEM((2, chunks, rows, chunk), low),
        pltpu.VMEM((chunks * chunk, frames), low),
        pltpu.VMEM((rows, frames), low),
        pltpu.VMEM((frames, D), full),
        pltpu.VMEM((D, frames), low),
        pltpu.VMEM((frames, D), full),
        pltpu.VMEM((D, frames), full),
        pltpu.SemaphoreType.DMA((2,)),
    ]


BACK_INPUTS = 14


def back_kernel(taps, *refs):
    made, small_made, rows = refs[BACK_INPUTS : BACK_INPUTS + 3]
    begin, convolve, finish = back_compute(
        taps, refs[:BACK_INPUTS], made, small_made, rows, refs[BACK_INPUTS + 3 :], lambda group: None
    )
    begin()
    convolve(0, made.shape[1])
    finish()


def back(taps, operands):
    kernel, small, frames = operands[-1], operands[3], operands[0].shape[0]
    return pl.pallas_call(
        functools.partial(back_kernel, taps),
        out_shape=[
            jax.ShapeDtypeStruct(kernel.shape, jnp.bfloat16),
            jax.ShapeDtypeStruct(small.shape, jnp.bfloat16),
            jax.ShapeDtypeStruct((16, D), jnp.float32),
        ],
        in_specs=[VMEM] * (BACK_INPUTS - 1) + [HBM],
        out_specs=[VMEM] * 3,
        scratch_shapes=back_scratch(kernel.shape, frames),
        name="back",
        compiler_params=pltpu.CompilerParams(vmem_limit_bytes=48 * 1024 * 1024),
    )(*operands)


def back_reduce_kernel(sizes, shapes, taps, *refs):
    place = Place(*sizes)
    refs = list(refs)

    def pull(number):
        taken = refs[:number]
        del refs[:number]
        return taken

    count = len(KINDS)
    inputs, (block_grad,) = pull(BACK_INPUTS), pull(1)
    outs, (small_out, square_out, whole_box) = pull(count), pull(3)
    made, small_made, rows, scratch = *pull(3), pull(8)
    crossed, first_in, second_in, line_in = (pull(count) for _ in range(4))
    (held, group_box, dp_box, rows_low) = pull(4)
    sems = pull(11)
    (group_send, group_recv, dp_send, dp_recv, row_send, row_recv, pair_send, pair_recv) = pull(8)
    me = (place.dp, place.group)
    source = {"conv": made, "small": small_made, "blocks": block_grad}
    run = Reducer(
        place,
        shapes,
        None,
        (crossed, first_in, second_in, line_in, held, [source[kind] for kind in KINDS]),
        sems,
    )
    lines, b = run.lines, run.blocks
    conv, tiny = KINDS.index("conv"), KINDS.index("small")
    greet(place)

    def cross_all(k):
        for q in (1, 0):
            for p in (1, 0):

                def begin_one(index, _, p=p, q=q):
                    run.cross_of(k, p, q, run.turn(index)).start()
                    if k == b and q == 1:
                        run.load_of(p, q, run.turn(index)).start()
                    return 0

                lax.fori_loop(0, lines, begin_one, 0)

    def hook(group):
        pairs = shapes[conv][0]

        @pl.when(group % pairs == pairs - 1)
        def _():
            dp = group // pairs
            spot, flip_y = dp // 2, (dp % 2 + place.y) % 2
            for x in range(2):
                flip_x = (x + place.x) % 2
                p = flip_y * place.core + flip_x * (1 - place.core)
                q = flip_x * place.core + flip_y * (1 - place.core)
                run.cross_of(conv, p, q, spot).start()

    begin, convolve, finish = back_compute(taps, inputs, made, small_made, rows, scratch, hook)

    def remote(source, target, send, recv, device):
        return run.remote(source, target, send, recv, device)

    def each_other(size, mine, action):
        for other in range(size):
            pl.when(mine != other)(functools.partial(action, other))

    def group_copy(other):
        return remote(
            rows,
            group_box.at[place.group],
            group_send.at[other],
            group_recv.at[place.group],
            (place.dp, other),
        )

    def dp_copy(other):
        return remote(
            dp_box.at[place.dp], dp_box.at[place.dp], dp_send.at[other], dp_recv.at[place.dp], (other, place.group)
        )

    def group_wait(other):
        group_copy(other).wait_send()
        remote(rows, group_box.at[other], group_send.at[other], group_recv.at[other], me).wait_recv()

    def dp_wait(other):
        dp_copy(other).wait_send()
        remote(dp_box.at[other], dp_box.at[other], dp_send.at[other], dp_recv.at[other], me).wait_recv()

    def rows_to_group():
        group_box[place.group] = rows[...]
        each_other(place.group_size, place.group, lambda other: group_copy(other).start())

    def rows_to_all():
        each_other(place.group_size, place.group, group_wait)
        total = group_box[0]
        for other in range(1, place.group_size):
            total = total + group_box[other]
        dp_box[place.dp] = total
        each_other(place.dp_size, place.dp, lambda other: dp_copy(other).start())

    def some(first, last, action):
        def one(index, _):
            action(index)
            return 0

        lax.fori_loop(first, last, one, 0)

    members, depth = shapes[b][0], shapes[b][1]
    owners = Owners(place, members)
    my_rows = pl.ds(pl.multiple_of(place.dp * depth, depth), depth)
    owner_here = owners.here & (owners.group == place.group)
    owner_there = owners.here & (owners.group != place.group)

    def row_copy(member):
        return remote(
            rows_low.at[member],
            whole_box.at[my_rows],
            row_send.at[member],
            row_recv.at[place.dp],
            (owners.of(member), place.group),
        )

    def pair_copy(other):
        spot = pl.ds(pl.multiple_of(other * depth, depth), depth)
        return remote(
            whole_box.at[spot], whole_box.at[spot], pair_send.at[other], pair_recv.at[other], run.c_mate
        )

    def send_rows():
        rows_low[...] = outs[b][...].astype(jnp.bfloat16)
        for member in range(members):

            @pl.when(place.dp != owners.of(member))
            def _(member=member):
                row_copy(member).start()

            @pl.when(place.dp == owners.of(member))
            def _(member=member):
                whole_box[my_rows] = rows_low[member]
                pair_copy(place.dp).start()

    def take_rows():
        @pl.when(owner_here)
        def _():
            for other in range(place.dp_size):

                @pl.when(place.dp != other)
                def _(other=other):
                    spot = pl.ds(other * depth, depth)
                    remote(
                        rows_low.at[0], whole_box.at[spot], row_send.at[0], row_recv.at[other], me
                    ).wait_recv()
                    pair_copy(other).start()

        @pl.when(owner_there)
        def _():
            for other in range(place.dp_size):
                pair_copy(other).wait_recv()

    cross_all(b)
    begin()
    actions = {
        "one": lambda index, k: run.stage_one(k, index),
        "two": lambda index, k: run.stage_two(k, index),
        "edge": lambda index, k: run.line_step(k, index, False),
        "inner": lambda index, k: run.line_step(k, index, True),
        "end": lambda index, k: run.line_end(k, outs[k]),
    }

    def leave():
        finish()
        cross_all(tiny)
        rows_to_group()

    plain = {"leave": leave, "rows": send_rows, "take": take_rows}
    for name, kind, first, last in PLAN:
        if name == "groups":
            convolve(first, last)
        elif name in plain:
            plain[name]()
        else:
            action = functools.partial(lambda index, k, name: actions[name](index, k), k=KINDS.index(kind), name=name)
            if last - first == 1:
                action(first)
            else:
                some(first, last, action)
        if name == "rows":
            rows_to_all()
    square = jnp.sum(outs[b][...] * outs[b][...])
    for k in run.rest:
        square = square + jnp.sum(outs[k][...] * outs[k][...])
    each_other(place.dp_size, place.dp, dp_wait)
    total = dp_box[0]
    for other in range(1, place.dp_size):
        total = total + dp_box[other]
    small_out[...] = total
    skipped = lax.broadcasted_iota(jnp.int32, total.shape, 0) != LOSS_ROW
    square = square + jnp.sum(jnp.where(skipped, total * total, 0.0)) * (
        1.0 / (place.dp_size * place.group_size)
    )
    square_out[...] = jnp.full(square_out.shape, square, jnp.float32)
    for member in range(members):
        @pl.when(place.dp != owners.of(member))
        def _(member=member):
            row_copy(member).wait_send()

    @pl.when(owner_here)
    def _():
        for other in range(place.dp_size):
            pair_copy(other).wait_send()

    run.drain()


def back_reduce(sizes, shapes, taps, operands, block_grad):
    dp_size, group_size = sizes
    lines, count = dp_size // 2, len(KINDS)
    kernel, small, frames = operands[-1], operands[3], operands[0].shape[0]
    low, full = jnp.bfloat16, jnp.float32

    def boxes(lead):
        return [
            pltpu.VMEM(tuple(lead(kind)) + tuple(shape), low) for kind, shape in zip(KINDS, shapes)
        ]

    dma = pltpu.SemaphoreType.DMA
    scratch = (
        [pltpu.VMEM(kernel.shape, low), pltpu.VMEM(small.shape, low), pltpu.VMEM((16, D), full)]
        + back_scratch(kernel.shape, frames)
        + boxes(lambda kind: (2, 2, lines))
        + boxes(lambda kind: (2, lines))
        + boxes(lambda kind: (lines,))
        + boxes(lambda kind: (lines + 1,))
        + [
            pltpu.VMEM((2, lines) + tuple(shapes[-1]), low),
            pltpu.VMEM((group_size, 16, D), full),
            pltpu.VMEM((dp_size, 16, D), full),
            pltpu.VMEM(shapes[-1], low),
        ]
        + [dma((2, 2, lines))]
        + [dma((count, 2, 2, lines))] * 2
        + [dma((count, 2, lines))] * 2
        + [dma((count, lines))] * 6
        + [dma((group_size,))] * 2
        + [dma((dp_size,))] * 2
        + [dma((shapes[-1][0],)), dma((dp_size,))]
        + [dma((dp_size,))] * 2
    )
    return pl.pallas_call(
        functools.partial(back_reduce_kernel, sizes, shapes, taps),
        out_shape=[jax.ShapeDtypeStruct(shape, full) for shape in shapes]
        + [
            jax.ShapeDtypeStruct((16, D), full),
            jax.ShapeDtypeStruct((8, 128), full),
            jax.ShapeDtypeStruct((D, D), low),
        ],
        in_specs=[VMEM] * (BACK_INPUTS - 1) + [HBM, HBM],
        out_specs=[VMEM] * (count + 3),
        scratch_shapes=scratch,
        name="back_reduce",
        compiler_params=pltpu.CompilerParams(
            collective_id=1, has_side_effects=True, vmem_limit_bytes=VMEM_LIMIT
        ),
    )(*operands, block_grad)


PLAN = (
    ("one", "blocks", 0, 1),
    ("groups", "", 0, 3),
    ("one", "blocks", 4, 5),
    ("two", "blocks", 0, 1),
    ("groups", "", 3, 6),
    ("one", "blocks", 1, 2),
    ("groups", "", 6, 9),
    ("one", "blocks", 5, 6),
    ("two", "blocks", 1, 2),
    ("one", "blocks", 3, 4),
    ("groups", "", 9, 16),
    ("one", "blocks", 2, 3),
    ("leave", "", 0, 1),
    ("edge", "blocks", 0, 1),
    ("one", "blocks", 6, 7),
    ("one", "small", 1, 2),
    ("inner", "blocks", 2, 3),
    ("one", "blocks", 7, 8),
    ("one", "conv", 3, 4),
    ("two", "blocks", 2, 4),
    ("one", "conv", 0, 1),
    ("one", "small", 0, 1),
    ("one", "small", 5, 6),
    ("one", "small", 4, 5),
    ("one", "small", 2, 3),
    ("two", "small", 1, 2),
    ("edge", "blocks", 1, 2),
    ("inner", "blocks", 0, 1),
    ("one", "small", 3, 4),
    ("inner", "blocks", 1, 2),
    ("one", "conv", 5, 6),
    ("inner", "conv", 2, 3),
    ("one", "conv", 2, 3),
    ("edge", "blocks", 2, 3),
    ("two", "small", 0, 1),
    ("edge", "small", 0, 1),
    ("one", "conv", 1, 2),
    ("one", "conv", 4, 5),
    ("two", "small", 3, 4),
    ("end", "blocks", 0, 1),
    ("two", "conv", 0, 1),
    ("one", "small", 7, 8),
    ("inner", "small", 0, 1),
    ("two", "small", 2, 3),
    ("one", "conv", 7, 8),
    ("rows", "", 0, 1),
    ("inner", "small", 2, 3),
    ("one", "small", 6, 7),
    ("two", "conv", 1, 4),
    ("edge", "small", 1, 2),
    ("edge", "conv", 0, 1),
    ("inner", "small", 1, 2),
    ("one", "conv", 6, 7),
    ("edge", "conv", 1, 2),
    ("edge", "small", 2, 3),
    ("inner", "conv", 0, 1),
    ("edge", "conv", 2, 3),
    ("inner", "conv", 1, 2),
    ("take", "", 0, 1),
    ("end", "small", 0, 1),
    ("end", "conv", 0, 1),
)


GATHER_PLAN = (
    ("step", "small", 0),
    ("step", "conv", 0),
    ("step", "blocks", 0),
    ("enter", "", 0),
    ("step", "small", 1),
    ("step", "conv", 1),
    ("step", "blocks", 1),
    ("step", "conv", 2),
    ("step", "small", 2),
    ("step", "blocks", 2),
    ("step", "conv", 3),
    ("step", "small", 3),
    ("step", "conv", 4),
    ("step", "small", 4),
    ("step", "conv", 5),
    ("step", "small", 5),
    ("step", "small", 6),
    ("core", "conv", 0),
    ("core", "small", 0),
    ("compute", "", 0),
    ("step", "blocks", 3),
    ("compute", "", 1),
    ("compute", "", 2),
    ("compute", "", 3),
    ("step", "blocks", 4),
    ("step", "conv", 6),
    ("compute", "", 4),
    ("step", "blocks", 5),
    ("step", "blocks", 6),
)


def roots_kernel(sizes, members, *refs):
    (
        whole, stat, square_in, sides_out, update_out, square_out,
        gram, big, m0, m0b, m1, m1b, s1, s1b, s2b, s3, s3b, root, mixed,
        group_box, dp_box, group_send, group_recv, dp_send, dp_recv,
        side_send, side_recv, side_own, mixed_send, mixed_recv, update_send, update_recv, update_own,
    ) = refs
    place = Place(*sizes)
    owners = Owners(place, members)
    dp_size, rows = place.dp_size, D // place.dp_size
    me, c_mate = (place.dp, place.group), place.at(place.z, 0, 0, 1)
    owner = owners.here
    tile = 256
    greet(place)

    def remote(source, target, send, recv, device):
        return pltpu.make_async_remote_copy(
            src_ref=source,
            dst_ref=target,
            send_sem=send,
            recv_sem=recv,
            device_id=device,
            device_id_type=MESH,
        )

    def each_other(size, mine, action):
        for other in range(size):
            pl.when(mine != other)(functools.partial(action, other))

    def group_copy(other, slot):
        return remote(
            group_box.at[slot], group_box.at[slot], group_send.at[other], group_recv.at[slot], (place.dp, other)
        )

    def dp_copy(other, slot):
        return remote(dp_box.at[slot], dp_box.at[slot], dp_send.at[other], dp_recv.at[slot], (other, place.group))

    group_box[place.group] = square_in[...]
    each_other(place.group_size, place.group, lambda other: group_copy(other, place.group).start())

    def product_rows(one, two, then):
        def step(index, _):
            at = pl.ds(pl.multiple_of(index * tile, tile), tile)
            then(at, jnp.dot(one[at, :], two[...], preferred_element_type=jnp.float32))
            return 0

        lax.fori_loop(0, D // tile, step, 0)

    half = D // 2

    @pl.when(owner)
    def _():
        for index in range(2):
            at = slice(index * half, (index + 1) * half)

            @pl.when(place.core == 0)
            def _(at=at):
                gram[at, :] = dot_nt(whole[at, :], whole[...]).astype(jnp.bfloat16)

            @pl.when(place.core == 1)
            def _(at=at):
                gram[at, :] = dot_tn(whole[:, at], whole[...]).astype(jnp.bfloat16)

    def side_copy(other):
        spot = pl.ds(pl.multiple_of(other * rows, rows), rows)
        return remote(
            gram.at[spot],
            sides_out.at[owners.member, place.core],
            side_send.at[other],
            side_recv.at[owners.member, place.core],
            (other, owners.group),
        )

    def side_local():
        spot = pl.ds(pl.multiple_of(place.dp * rows, rows), rows)
        return pltpu.make_async_copy(gram.at[spot], sides_out.at[owners.member, place.core], side_own)

    def group_wait(other):
        group_copy(other, place.group).wait_send()
        group_copy(other, other).wait_recv()

    each_other(place.group_size, place.group, group_wait)
    total = group_box[0]
    for other in range(1, place.group_size):
        total = total + group_box[other]
    dp_box[place.dp] = total
    each_other(dp_size, place.dp, lambda other: dp_copy(other, place.dp).start())

    @pl.when(owner)
    def _():
        for other in range(dp_size):
            owners.to_rows(other, lambda other: side_copy(other).start(), lambda: side_local().start())

    def dp_wait(other):
        dp_copy(other, place.dp).wait_send()
        dp_copy(other, other).wait_recv()

    each_other(dp_size, place.dp, dp_wait)
    total = dp_box[0]
    for other in range(1, dp_size):
        total = total + dp_box[other]
    square_out[...] = total

    @pl.when(owner)
    def _():
        factor = jnp.minimum(1.0, max_norm / (jnp.sqrt(total[0:1, 0:1]) + 1e-06))
        square_factor = factor * factor
        spread_f = (1 - stat_decay) * square_factor

        def diagonal(at_start, shape):
            row = lax.broadcasted_iota(jnp.int32, shape, 0) + at_start
            return row == lax.broadcasted_iota(jnp.int32, shape, 1)

        def each_tile(action, carry):
            def step(index, carry):
                start = pl.multiple_of(index * tile, tile)
                return action(pl.ds(start, tile), start, carry)

            return lax.fori_loop(0, D // tile, step, carry)

        def renew(at, start, trace):
            value = stat_decay * stat[at, :].astype(jnp.float32) + spread_f * gram[at, :].astype(
                jnp.float32
            )
            big[at, :] = value
            on = jnp.where(diagonal(start, value.shape), value, 0.0)
            return trace + jnp.sum(jnp.sum(on, 1, keepdims=True), 0, keepdims=True)

        trace = each_tile(renew, jnp.zeros((1, 1), jnp.float32))
        damping = 0.0001 * (trace / D)

        def damp(at, start, total):
            value = big[at, :]
            value = value + jnp.where(diagonal(start, value.shape), damping, 0.0)
            big[at, :] = value
            return total + jnp.sum(jnp.sum(value * value, 1, keepdims=True), 0, keepdims=True)

        magnitude = jnp.sqrt(each_tile(damp, jnp.zeros((1, 1), jnp.float32)))

        def scale(at, start, carry):
            value = big[at, :] / magnitude
            m0[at, :] = value
            m0b[at, :] = value.astype(jnp.bfloat16)
            return carry

        each_tile(scale, 0)
        a = 1.5625

        def square_of(source):
            def then(at, value):
                value = value * 0.0625 - 0.625 * source[at, :]
                s1[at, :] = value
                s1b[at, :] = value.astype(jnp.bfloat16)

            return then

        def fourth(at, value):
            s2b[at, :] = (value + (2 * a) * s1[at, :]).astype(jnp.bfloat16)

        product_rows(m0b, m0b, square_of(m0))
        product_rows(s1b, s1b, fourth)

        def next_one(at, value):
            value = value + (a * a) * m0[at, :]
            m1[at, :] = value
            m1b[at, :] = value.astype(jnp.bfloat16)

        product_rows(s2b, m0b, next_one)

        def joined(at, value):
            value = value * 0.0625 - 0.3125 * (m0[at, :] + m1[at, :])
            s3[at, :] = value
            s3b[at, :] = value.astype(jnp.bfloat16)

        product_rows(m0b, m1b, joined)
        product_rows(m1b, m1b, square_of(m1))
        product_rows(s1b, s1b, fourth)

        def next_two(at, value):
            value = value + (a * a) * m1[at, :]
            m0[at, :] = value
            m0b[at, :] = value.astype(jnp.bfloat16)

        product_rows(s2b, m1b, next_two)
        outer = lax.rsqrt(jnp.sqrt(magnitude))

        def final(at, value):
            value = 1.25 * s3[at, :] - (0.25 * a) * m0[at, :] - 0.25 * value
            start = at.start
            value = value + jnp.where(diagonal(start, value.shape), 1.25 * a, 0.0)
            root[at, :] = (value * outer).astype(jnp.bfloat16)

        product_rows(s3b, m0b, final)

    per_part = dp_size // 2

    def mixed_copy(part):
        at = pl.ds(part * half, half)
        return remote(mixed.at[at], mixed.at[at], mixed_send.at[part], mixed_recv.at[part], c_mate)

    def update_copy(other):
        spot = pl.ds(pl.multiple_of(other * rows, rows), rows)
        return remote(
            m1b.at[spot],
            update_out.at[owners.member],
            update_send.at[other],
            update_recv.at[owners.member],
            (other, owners.group),
        )

    def update_local():
        spot = pl.ds(pl.multiple_of(place.dp * rows, rows), rows)
        return pltpu.make_async_copy(m1b.at[spot], update_out.at[owners.member], update_own)

    @pl.when(owner & (place.core == 0))
    def _():
        for part in range(2):
            at = slice(part * half, (part + 1) * half)
            mixed[at, :] = dot(root[at, :], whole[...]).astype(jnp.bfloat16)
            mixed_copy(part).start()
        for part in range(2):
            mixed_copy(part).wait_send()

    @pl.when(owner & (place.core == 1))
    def _():
        for part in range(2):
            mixed_copy(part).wait_recv()
            at = slice(part * half, (part + 1) * half)
            m1b[at, :] = dot(mixed[at, :], root[...]).astype(jnp.bfloat16)
            for other in range(part * per_part, (part + 1) * per_part):
                owners.to_rows(
                    other, lambda other: update_copy(other).start(), lambda: update_local().start()
                )
        for other in range(dp_size):
            owners.to_rows(
                other, lambda other: update_copy(other).wait_send(), lambda: update_local().wait()
            )

    @pl.when(owner)
    def _():
        for other in range(dp_size):
            owners.to_rows(
                other, lambda other: side_copy(other).wait_send(), lambda: side_local().wait()
            )

    for member in range(members):
        for side in range(2):

            @pl.when((place.dp != owners.of(member)) | (place.core != side))
            def _(member=member, side=side):
                remote(
                    gram.at[pl.ds(0, rows)],
                    sides_out.at[member, side],
                    side_send.at[0],
                    side_recv.at[member, side],
                    me,
                ).wait_recv()

        @pl.when((place.dp != owners.of(member)) | (place.core != 1))
        def _(member=member):
            remote(
                m1b.at[pl.ds(0, rows)],
                update_out.at[member],
                update_send.at[0],
                update_recv.at[member],
                me,
            ).wait_recv()


def shampoo_roots(sizes, members, whole, stat, square):
    dp_size, group_size = sizes
    rows = D // dp_size
    low, full = jnp.bfloat16, jnp.float32
    dma = pltpu.SemaphoreType.DMA
    half, word = pltpu.VMEM((D, D), low), pltpu.VMEM((D, D), full)
    return pl.pallas_call(
        functools.partial(roots_kernel, sizes, members),
        out_shape=[
            jax.ShapeDtypeStruct((members, 2, rows, D), low),
            jax.ShapeDtypeStruct((members, rows, D), low),
            jax.ShapeDtypeStruct((8, 128), full),
        ],
        in_specs=[VMEM] * 3,
        out_specs=[VMEM] * 3,
        scratch_shapes=[half, word, word, half, word, half, word, half, half, word, half, half, half]
        + [pltpu.VMEM((group_size, 8, 128), full), pltpu.VMEM((dp_size, 8, 128), full)]
        + [dma((group_size,))] * 2
        + [dma((dp_size,))] * 2
        + [dma((dp_size,)), dma((members, 2)), dma]
        + [dma((2,)), dma((2,))]
        + [dma((dp_size,)), dma((members,)), dma],
        name="shampoo_roots",
        compiler_params=pltpu.CompilerParams(
            collective_id=2, has_side_effects=True, vmem_limit_bytes=VMEM_LIMIT
        ),
    )(whole, stat, square)


def finish_kernel(rates, *refs):
    square, rows, block_sum, small, kernel, sides, update = refs[:7]
    weights, blocks, statistics = refs[7:25], refs[25], refs[26]
    norm_out, outs = refs[27], refs[28:46]
    block_out, stat_out, blocks_out, loss_out = refs[46:]
    loss_out[...] = rows[LOSS_ROW : LOSS_ROW + 1, 0:1]
    norm = jnp.sqrt(square[0:1, 0:1])
    norm_out[...] = norm
    factor = jnp.minimum(1.0, max_norm / (norm + 1e-06))

    def renew(index, at, grad):
        rate, decay = rates[index]
        ins, out = weights[3 * index : 3 * index + 3], outs[3 * index : 3 * index + 3]
        result = adamw(ins[0][at], grad * factor, ins[1][at], ins[2][at], rate, decay)
        for ref, value in zip(out, result):
            ref[at] = value

    width = weights[0].shape[1]
    vector_rows = weights[6].shape[0]
    renew(0, ..., rows[LOSS_ROW + 1 : LOSS_ROW + 3, :width])
    renew(1, (slice(None), slice(0, 128)), small[0:64, :])
    renew(1, (slice(None), slice(128, 192)), small[64:128, 0:64])
    renew(2, ..., rows[0:vector_rows, :])
    runs, steps, c, channels = weights[9].shape
    for offset in range(steps):
        parts = [kernel[group, offset * c : (offset + 1) * c, :] for group in range(channels // c)]
        renew(
            3,
            (slice(None), offset),
            jnp.concatenate(parts, 0).T.reshape(runs, c, channels),
        )
    renew(4, ..., small[128:224, :].T[0:64])
    renew(5, ..., small[224:256, 0:CLUSTER_ROWS])
    for member in range(blocks.shape[0]):
        block_out[member] = block_sum[member] * factor
        step = update[member].astype(jnp.float32) * factor + decay_weight * blocks[member]
        blocks_out[member] = blocks[member] - rate_shampoo * step
        for side in range(2):
            spread = (1 - stat_decay) * factor * factor
            stat_out[member, side] = stat_decay * statistics[member, side] + spread * sides[
                member, side
            ].astype(jnp.float32)


def finish(sums, weights, blocks, statistics):
    full = jnp.float32
    rates = [(rate_vector, 0.0), (rate_matrix, decay_weight), (rate_vector, 0.0)]
    rates += [(rate_matrix, decay_weight)] * 3
    operands = [*sums, *weights, blocks, statistics]
    shapes = [(1, 1)] + [weight.shape for weight in weights]
    shapes += [blocks.shape, statistics.shape, blocks.shape, (1, 1)]
    return pl.pallas_call(
        functools.partial(finish_kernel, rates),
        out_shape=[jax.ShapeDtypeStruct(shape, full) for shape in shapes],
        in_specs=[VMEM] * len(operands),
        out_specs=[VMEM] * len(shapes),
        name="finish",
        compiler_params=pltpu.CompilerParams(vmem_limit_bytes=VMEM_LIMIT),
    )(*operands)


def conv_to_shard(weight):
    taps, c, channels = weight.shape
    split = weight.reshape(taps // STRIDE, STRIDE, c, channels // c, c)
    return split.transpose(3, 1, 4, 0, 2).reshape(channels // c, STRIDE * c, taps // STRIDE * c)


def conv_from_shard(shard):
    groups, rows, columns = shard.shape
    c = rows // STRIDE
    split = shard.reshape(groups, STRIDE, c, columns // c, c)
    return split.transpose(3, 1, 4, 0, 2).reshape(columns // c * STRIDE, c, groups * c)


def pack_small(projection, head, clusters, note):
    lead, kind = projection.shape[:-2], projection.dtype
    notes = jnp.broadcast_to(note, lead + (32, 2)).astype(kind)
    return jnp.concatenate(
        [
            projection[..., :128],
            jnp.concatenate([projection[..., 128:], jnp.zeros(lead + (64, 64), kind)], -1),
            jnp.concatenate([head, jnp.zeros(lead + (96, 64), kind)], -1),
            jnp.concatenate([jnp.swapaxes(clusters, -1, -2), notes], -1),
        ],
        -2,
    )


def unpack_small(packed):
    projection = jnp.concatenate([packed[..., :64, :], packed[..., 64:128, :64]], -1)
    head = packed[..., 128:224, :64]
    clusters = jnp.swapaxes(packed[..., 224:, :CLUSTER_ROWS], -1, -2)
    return projection, head, clusters


def pack_whole(projection, head, clusters, note):
    def cut(values, down, across):
        rows, columns = values.shape
        return values.reshape(down, rows // down, across, columns // across).transpose(0, 2, 1, 3)

    return pack_small(
        cut(projection, 8, 4), cut(head, 8, 4), cut(clusters, 4, 8).transpose(1, 0, 2, 3), note
    )


def unpack_whole(packed):
    def join(values):
        down, across, rows, columns = values.shape
        return values.transpose(0, 2, 1, 3).reshape(down * rows, across * columns)

    projection, head, clusters = unpack_small(packed)
    return join(projection), join(head), join(clusters.transpose(1, 0, 2, 3))


def parts_of_rows(rows, vector_rows, width):
    return rows[:vector_rows], rows[vector_rows + 1 : vector_rows + 3, :width], rows[vector_rows, 0]


CLUSTER_ROWS = 126
SMALL = ((64, 192), (96, 64), (CLUSTER_ROWS, 32))


def body(
    sizes,
    features,
    span_starts,
    labels,
    feature_norm,
    feature_first,
    feature_second,
    projection,
    projection_first,
    projection_second,
    vectors,
    vector_first,
    vector_second,
    conv_weight,
    conv_first,
    conv_second,
    head,
    head_first,
    head_second,
    clusters,
    cluster_first,
    cluster_second,
    blocks,
    statistics,
):
    dp_size, group_size = sizes
    members, rows = blocks.shape[0], blocks.shape[1]
    masks = jax.vmap(jax.vmap(frame_mask))(span_starts)
    local_count = jnp.sum(masks)
    fast = (
        rows % 16 == 0
        and dp_size % 2 == 0
        and group_size == 4
        and dp_size >= 2 * members
        and (projection.shape, head.shape, clusters.shape) == SMALL
        and conv_weight.shape[2] % conv_weight.shape[1] == 0
        and masks.size <= 256
    )
    frames, vector_rows, width = masks.size, vectors.shape[0], feature_norm.shape[1]
    flat = features.reshape(frames, -1)

    def runs(values):
        return values.reshape((-1, STRIDE) + values.shape[1:])

    if fast:
        taps, c, channels = conv_weight.shape
        taps *= group_size
        shapes = [
            (channels // c, STRIDE * c, taps // group_size // STRIDE * c),
            (256, 128),
            blocks.shape,
        ]
        raw = (
            span_starts.reshape(-1, span_starts.shape[-1]),
            projection, runs(conv_weight), head.T, clusters.T, blocks, statistics,
        )
        kernel_w, small_w, blocks_w, *saved, mask, stats_low = gather_weights(
            sizes, shapes, taps, raw, flat, feature_norm, vectors
        )
    else:
        proj_w, kernel_full, head_w, clusters_w, blocks_w = gather_plain(
            projection, conv_weight, head, clusters, blocks
        )
        whole = conv_to_shard(kernel_full)
        kernel_w = whole.reshape(whole.shape[:2] + (4, -1)).transpose(2, 0, 1, 3)
        count = lax.psum(local_count, ("dp", "group"))
        high = jnp.floor(count / 256.0) * 256.0
        notes = jnp.concatenate([jnp.stack([high, count - high]), jnp.zeros(30, jnp.float32)])
        small_w = pack_whole(proj_w, head_w, clusters_w, notes.reshape(8, 4, 1, 1))
        taps = kernel_w.shape[0] * kernel_w.shape[3] // (D // kernel_w.shape[1]) * STRIDE
        mask = masks.reshape(frames, 1)
        saved = front(flat, mask, feature_norm, vectors, small_w, kernel_w, taps)
    feature_unit, normed, hidden_t, encoded, encoder_unit, encoder_inverse, slope = saved
    extra_parts = (sizes, stats_low) if fast else ()
    encoded_grad, block_part, head_part, center_part, trunk_rows, counted, *stat_whole = trunk(
        encoded, mask, labels.reshape(frames, 1), vectors, small_w, blocks_w, *extra_parts
    )
    masked_count = counted[0, 0]
    operands = (
        encoded_grad, mask, vectors, small_w, feature_unit, normed, hidden_t,
        encoder_unit, encoder_inverse, slope, trunk_rows, head_part, center_part, kernel_w,
    )
    if fast:
        kernel_sum, small_sum, block_sum, extra, square, whole = back_reduce(
            sizes, shapes, taps, operands, block_part
        )
        sides, update_rows, square = shampoo_roots(sizes, members, whole, *stat_whole, square)

        done = finish(
            (square, extra, block_sum, small_sum, kernel_sum, sides, update_rows),
            (
                feature_norm, feature_first, feature_second,
                projection, projection_first, projection_second,
                vectors, vector_first, vector_second,
                runs(conv_weight), runs(conv_first), runs(conv_second),
                head.T, head_first.T, head_second.T,
                clusters.T, cluster_first.T, cluster_second.T,
            ),
            blocks,
            statistics,
        )
        outs = []
        for index in range(0, 18, 3):
            parts = done[1 + index : 4 + index]
            if index == 9:
                parts = [part.reshape(conv_weight.shape) for part in parts]
            if index >= 12:
                parts = [part.T for part in parts]
            outs += parts
        return (done[-1][0, 0], masked_count, done[0][0, 0], *outs, *done[19:22])
    kernel_part, small_part, row_part = back(taps, operands)
    proj_part, head_part, center_part = unpack_whole(small_part)
    kernel_plain = conv_from_shard(
        kernel_part.transpose(1, 2, 0, 3).reshape(kernel_part.shape[1:3] + (-1,))
    )
    large_total = reduce_grads(
        tuple(
            part.astype(jnp.float32)
            for part in (proj_part, kernel_plain, head_part, center_part, block_part)
        )
    )
    vector_grad, feature_grad, loss_sum = parts_of_rows(
        lax.psum(row_part, ("dp", "group")), vector_rows, width
    )
    local_squares = sum((jnp.sum(part * part) for part in large_total))
    norm_square = (
        lax.psum(local_squares, ("dp", "group"))
        + jnp.sum(feature_grad * feature_grad)
        + jnp.sum(vector_grad * vector_grad)
    )
    grad_norm = jnp.sqrt(norm_square)
    factor = jnp.minimum(1.0, max_norm / (grad_norm + 1e-06))
    proj_grad, kernel_grad, head_grad, cluster_grad, block_rows = [
        part * factor for part in large_total
    ]
    feature_out = adamw(
        feature_norm, feature_grad * factor, feature_first, feature_second, rate_vector, 0.0
    )
    projection_out = adamw(
        projection, proj_grad, projection_first, projection_second, rate_matrix, decay_weight
    )
    vector_out = adamw(vectors, vector_grad * factor, vector_first, vector_second, rate_vector, 0.0)
    conv_out = adamw(conv_weight, kernel_grad, conv_first, conv_second, rate_matrix, decay_weight)
    head_out = adamw(head, head_grad, head_first, head_second, rate_matrix, decay_weight)
    cluster_out = adamw(
        clusters, cluster_grad, cluster_first, cluster_second, rate_matrix, decay_weight
    )
    statistics_new, update_rows = shampoo_plain(block_rows, statistics)
    blocks_new = blocks - rate_shampoo * (update_rows + decay_weight * blocks)
    return (
        loss_sum,
        masked_count,
        grad_norm,
        *feature_out,
        *projection_out,
        *vector_out,
        *conv_out,
        *head_out,
        *cluster_out,
        block_rows,
        statistics_new,
        blocks_new,
    )


def solution(mesh):
    in_specs = (
        P(None, ("dp", "group"), None, None),
        P(None, ("dp", "group"), None),
        P(None, ("dp", "group"), None),
        P(),
        P(),
        P(),
        P("dp", "group"),
        P("dp", "group"),
        P("dp", "group"),
        P(),
        P(),
        P(),
        P("group", None, "dp"),
        P("group", None, "dp"),
        P("group", None, "dp"),
        P("dp", "group"),
        P("dp", "group"),
        P("dp", "group"),
        P("group", "dp"),
        P("group", "dp"),
        P("group", "dp"),
        P("group", "dp", None),
        P("group", None, "dp", None),
    )
    out_specs = (
        P(),
        P(),
        P(),
        P(),
        P(),
        P(),
        P("dp", "group"),
        P("dp", "group"),
        P("dp", "group"),
        P(),
        P(),
        P(),
        P("group", None, "dp"),
        P("group", None, "dp"),
        P("group", None, "dp"),
        P("dp", "group"),
        P("dp", "group"),
        P("dp", "group"),
        P("group", "dp"),
        P("group", "dp"),
        P("group", "dp"),
        P("group", "dp", None),
        P("group", None, "dp", None),
        P("group", "dp", None),
    )
    return jax.shard_map(
        functools.partial(body, (mesh.shape["dp"], mesh.shape["group"])), mesh=mesh, in_specs=in_specs, out_specs=out_specs, check_vma=False)
```

```python
import functools

import jax
import jax.numpy as jnp
from jax import lax
from jax.experimental import pallas as pl
from jax.experimental.pallas import tpu as pltpu
from jax.sharding import PartitionSpec as P

D = 768
HEADS = 12
HEAD = 64
TAPS = 128
CLIP = 128
SPAN = 10
NEWTON = 3
STEP = 10


HIGH = lax.Precision.HIGHEST
beta_one = 0.9
beta_two = 0.98
adam_eps = 1e-08
rate_matrix = 0.02
rate_vector = 0.5
rate_shampoo = 0.2
decay_weight = 0.01
stat_decay = 0.95
max_norm = 0.01
inv_temp = 10.0
STRIDE = 4


def for_sending(array):

    def short(part):
        return part.astype(jnp.bfloat16) if part.dtype == jnp.float32 else part

    return jax.tree.map(short, array)


def spread_2(array, axis, root):
    mine = lax.axis_index(axis) == root
    return lax.psum(jnp.where(mine, array, jnp.zeros_like(array)), axis)


def to_low(values):
    return values.astype(jnp.bfloat16)


def frame_mask(starts):
    frames = jnp.arange(CLIP, dtype=jnp.int32)[:, None]
    inside = (frames >= starts[None, :]) & (frames < starts[None, :] + SPAN)
    return jnp.any(inside, axis=1).astype(jnp.float32)


def inverse_root(matrix):
    size = matrix.shape[0]
    identity = jnp.eye(size, dtype=jnp.float32)
    damped = matrix + 0.0001 * (jnp.trace(matrix) / size) * identity
    magnitude = jnp.sqrt(jnp.sum(damped * damped))
    current = damped / magnitude
    result = identity * magnitude ** (-0.25)
    for sweep in range(NEWTON):
        factor = (5.0 * identity - current) * 0.25
        result = jnp.dot(result, factor, precision=HIGH)
        square = jnp.dot(factor, factor, precision=HIGH)
        current = jnp.dot(jnp.dot(square, square, precision=HIGH), current, precision=HIGH)
    return result


def adamw(weight, grad, first, second, rate, decay):
    first = beta_one * first + (1 - beta_one) * grad
    second = beta_two * second + (1 - beta_two) * grad * grad
    corrected = first / (1 - beta_one**STEP)
    scaled = jnp.sqrt(second / (1 - beta_two**STEP)) + adam_eps
    return (first, second, weight - rate * (corrected / scaled + decay * weight))


def reduce_grads(parts):
    proj_part, kernel_part, head_part, center_part, block_part = parts
    grouped = (
        lax.psum_scatter(proj_part, "group", scatter_dimension=1, tiled=True),
        lax.psum_scatter(kernel_part, "group", scatter_dimension=0, tiled=True),
        lax.psum_scatter(head_part, "group", scatter_dimension=1, tiled=True),
        lax.psum_scatter(center_part, "group", scatter_dimension=0, tiled=True),
        lax.psum_scatter(block_part, "group", scatter_dimension=0, tiled=True),
    )
    proj_part, kernel_part, head_part, center_part, block_part = grouped
    return (
        lax.psum_scatter(proj_part, "dp", scatter_dimension=0, tiled=True),
        lax.psum_scatter(kernel_part, "dp", scatter_dimension=2, tiled=True),
        lax.psum_scatter(head_part, "dp", scatter_dimension=0, tiled=True),
        lax.psum_scatter(center_part, "dp", scatter_dimension=1, tiled=True),
        lax.psum_scatter(block_part, "dp", scatter_dimension=1, tiled=True),
    )


def gather_plain(projection, conv_weight, head, clusters, blocks):
    gathered = (
        lax.all_gather(to_low(projection), "dp", axis=0, tiled=True),
        lax.all_gather(to_low(conv_weight), "dp", axis=2, tiled=True),
        lax.all_gather(to_low(head), "dp", axis=0, tiled=True),
        lax.all_gather(to_low(clusters), "dp", axis=1, tiled=True),
        lax.all_gather(to_low(blocks), "dp", axis=1, tiled=True),
    )
    proj_part, kernel_part, head_part, center_part, block_part = gathered
    return (
        lax.all_gather(proj_part, "group", axis=1, tiled=True),
        lax.all_gather(kernel_part, "group", axis=0, tiled=True),
        lax.all_gather(head_part, "group", axis=1, tiled=True),
        lax.all_gather(center_part, "group", axis=0, tiled=True),
        lax.all_gather(block_part, "group", axis=0, tiled=True),
    )


def shampoo_plain(block_rows, statistics):
    full_blocks = lax.all_gather(block_rows.astype(jnp.bfloat16), "dp", axis=1, tiled=True).astype(
        block_rows.dtype
    )
    rows = block_rows.shape[1]
    here = lax.axis_index("dp")
    first_row = here * rows
    column_slice = lax.dynamic_slice_in_dim(full_blocks, first_row, rows, 2)
    left_rows = stat_decay * statistics[:, 0] + (1 - stat_decay) * jnp.einsum(
        "brk,bck->brc", block_rows, full_blocks, precision=HIGH
    )
    right_rows = stat_decay * statistics[:, 1] + (1 - stat_decay) * jnp.einsum(
        "bkr,bkc->brc", column_slice, full_blocks, precision=HIGH
    )
    group_blocks = block_rows.shape[0]
    dp_size = lax.axis_size("dp")
    owners = [
        (2 * member + side) * dp_size // (2 * group_blocks)
        for member in range(group_blocks)
        for side in range(2)
    ]
    left_full, right_full = (
        lax.all_gather(left_rows.astype(jnp.bfloat16), "dp", axis=1, tiled=True).astype(
            left_rows.dtype
        ),
        lax.all_gather(right_rows.astype(jnp.bfloat16), "dp", axis=1, tiled=True).astype(
            right_rows.dtype
        ),
    )
    sources = [
        left_full[member] if side == 0 else right_full[member]
        for member in range(group_blocks)
        for side in range(2)
    ]
    roots = []
    for index in range(2 * group_blocks):
        owner = owners[index]
        root = lax.cond(here == owner, inverse_root, jnp.zeros_like, sources[index])
        root = spread_2(for_sending(root), "dp", owner).astype(root.dtype)
        roots.append(root)
    stacked = jnp.stack(roots).reshape(group_blocks, 2, D, D)
    left_root_rows = lax.dynamic_slice_in_dim(stacked[:, 0], first_row, rows, 1)
    update_rows = jnp.einsum(
        "brk,bkc->brc",
        jnp.einsum("brk,bkc->brc", left_root_rows, full_blocks, precision=HIGH),
        stacked[:, 1],
        precision=HIGH,
    )
    return jnp.stack([left_rows, right_rows], 1), update_rows


MESH = pl.DeviceIdType.MESH
HBM = pl.BlockSpec(memory_space=pltpu.HBM)
VMEM = pl.BlockSpec(memory_space=pltpu.VMEM)
VMEM_LIMIT = 60 * 1024 * 1024


class Place:
    def __init__(self, dp_size, group_size):
        self.dp_size, self.group_size = dp_size, group_size
        self.lines = dp_size // 2
        self.dp, self.group = lax.axis_index("dp"), lax.axis_index("group")
        self.z, self.y = self.dp // 2, self.dp % 2
        self.x, self.core = self.group // 2, self.group % 2

    def at(self, z, flip_y=0, flip_x=0, flip_core=0):
        y = self.y + flip_y * (1 - 2 * self.y)
        x = self.x + flip_x * (1 - 2 * self.x)
        core = self.core + flip_core * (1 - 2 * self.core)
        return (z * 2 + y, x * 2 + core)

    def near(self, z, p, q):
        return self.at(z, p * (1 - self.core) + q * self.core, q * (1 - self.core) + p * self.core)

    def across(self, z, p, q):
        return self.at(z, p * self.core + q * (1 - self.core), q * self.core + p * (1 - self.core), 1)


def greet(place):
    barrier = pltpu.get_barrier_semaphore()
    first = place.x * 2
    for other in range(place.dp_size):
        for core in range(2):

            @pl.when((place.dp != other) | (place.core != core))
            def _():
                pl.semaphore_signal(
                    barrier, inc=1, device_id=(other, first + core), device_id_type=MESH
                )

    for core in range(2):
        pl.semaphore_signal(
            barrier,
            inc=1,
            device_id=(place.dp, (1 - place.x) * 2 + core),
            device_id_type=MESH,
        )
    pl.semaphore_wait(barrier, 2 * place.dp_size - 1 + 2)


def guarded(condition, action):
    if condition is None:
        action()
    else:
        pl.when(condition)(action)


def both(one, two):
    if one is None:
        return two
    if two is None:
        return one
    return one & two


def piece_at(kind, ref, dp, group, shape):
    if kind == "blocks":
        start = pl.multiple_of(dp * shape[1], shape[1])
        return ref.at[pl.ds(group * shape[0], shape[0]), pl.ds(start, shape[1])]
    if kind == "conv":
        return ref.at[group, pl.ds(dp * shape[0], shape[0])]
    return ref.at[dp, group]


KINDS = ("conv", "small", "blocks")


def make_shards(refs, mask, conv, small):
    starts, projection, weight, head_t, clusters_t = refs
    for clip in range(starts.shape[0]):
        frame = lax.broadcasted_iota(jnp.int32, (CLIP, starts.shape[1]), 0)
        begins = starts[clip : clip + 1, :]
        inside = ((frame >= begins) & (frame < begins + SPAN)).astype(jnp.float32)
        mask[clip * CLIP : (clip + 1) * CLIP, :] = jnp.max(inside, 1, keepdims=True)
    note = jnp.sum(mask[...], 0, keepdims=True)
    runs, steps, c, channels = weight.shape
    for offset in range(steps):
        turned = weight[:, offset].reshape(runs * c, channels).T.astype(jnp.bfloat16)
        for group in range(channels // c):
            conv[group, offset * c : (offset + 1) * c, :] = turned[group * c : (group + 1) * c]
    low = jnp.bfloat16

    def padded(values):
        spare = jnp.zeros((values.shape[0], 128 - values.shape[1]), jnp.float32)
        return jnp.concatenate([values, spare], 1)

    small[0:64, :] = projection[:, 0:128].astype(low)
    small[64:128, :] = padded(projection[:, 128:]).astype(low)
    small[128:224, :] = padded(head_t[...].T).astype(low)
    lane = lax.broadcasted_iota(jnp.int32, (32, 128), 1)
    small[224:256, :] = jnp.where(lane < CLUSTER_ROWS, padded(clusters_t[...]), note).astype(low)


def gather_kernel(sizes, shapes, taps, *refs):
    place = Place(*sizes)
    count = len(KINDS)
    refs = list(refs)

    def pull(number):
        taken = refs[:number]
        del refs[:number]
        return taken

    raw, (features, feature_norm, vectors) = pull(7), pull(3)
    outs, results, (mask, stats_low) = pull(count), pull(7), pull(2)
    ins, (small_here,), scratch = pull(count), pull(1), pull(5)
    (send_sem, recv_sem, own_sem, small_sem) = pull(4)
    z, last = place.z, place.lines - 1
    me = (place.dp, place.group)
    make_shards(raw[:5], mask, *ins[:2])
    greet(place)
    sent = []
    slots = [0] * count
    conv, tiny = KINDS.index("conv"), KINDS.index("small")
    enter, project, convolve, leave = front_compute(
        taps,
        (features, mask, feature_norm, vectors, small_here, outs[conv]),
        results,
        scratch,
    )

    def view(k, source):
        return piece_at(KINDS[k], outs[k], source[0], source[1], shapes[k])

    def identity(source):
        return source[0] * place.group_size + source[1]

    def copy_of(k, source, target, slot, own=False):
        spot = view(k, source)
        return pltpu.make_async_remote_copy(
            src_ref=ins[k] if own else spot,
            dst_ref=spot,
            send_sem=send_sem.at[k, slot],
            recv_sem=recv_sem.at[k, identity(source)],
            device_id=target,
            device_id_type=MESH,
        )

    def send(k, source, target, condition=None, own=False):
        slot = slots[k]
        slots[k] += 1
        guarded(condition, lambda: copy_of(k, source, target, slot, own).start())
        sent.append((k, source, target, slot, condition, own))

    def arrive(k, source, condition=None):
        guarded(condition, lambda: copy_of(k, source, me, 0).wait_recv())

    links = {
        "left": (place.at(z - 1), z > 0),
        "right": (place.at(z + 1), z < last),
        "p": (place.near(z, 1, 0), None),
        "q": (place.near(z, 0, 1), None),
        "core": (place.at(z, 0, 0, 1), None),
    }

    def forward(k, source, ways, condition=None, own=False):
        for way in ways:
            target, open_way = links[way]
            send(k, source, target, both(condition, open_way), own)

    def spots(offset):
        if offset == 0:
            return [(z, None, ("left", "right"))]
        return [
            (z - offset, z >= offset, ("right",)),
            (z + offset, z + offset <= last, ("left",)),
        ]

    def take(k, source, condition, ways):
        arrive(k, source, condition)
        forward(k, source, ways, condition)

    def step_z_first(k, step):
        if step == 0:
            forward(k, me, ("left", "right", "q", "p", "core"), own=True)
            return
        if step < place.lines:
            for spot, there, ways in spots(step):
                take(k, place.near(spot, 0, 0), there, ways + ("q", "p", "core"))
        if 0 <= step - 1 < place.lines:
            for spot, there, _ in spots(step - 1):
                take(k, place.near(spot, 1, 0), there, ("q", "core"))
                take(k, place.near(spot, 0, 1), there, ("core",))
        if 0 <= step - 2 < place.lines:
            for spot, there, _ in spots(step - 2):
                take(k, place.near(spot, 1, 1), there, ("core",))

    def step_z_second(k, step):
        if step == 0:
            forward(k, me, ("q", "left", "right", "p", "core"), own=True)
            return
        if step == 1:
            take(k, place.near(z, 0, 1), None, ("left", "right", "p", "core"))
        if step < place.lines:
            for spot, there, ways in spots(step):
                take(k, place.near(spot, 0, 0), there, ways + ("p", "core"))
        if 1 <= step - 1 < place.lines:
            for spot, there, ways in spots(step - 1):
                take(k, place.near(spot, 0, 1), there, ways + ("p", "core"))
        if 0 <= step - 1 < place.lines:
            for spot, there, _ in spots(step - 1):
                take(k, place.near(spot, 1, 0), there, ("core",))
        if 0 <= step - 2 < place.lines:
            for spot, there, _ in spots(step - 2):
                take(k, place.near(spot, 1, 1), there, ("core",))

    own_copies = [
        pltpu.make_async_copy(ins[k], view(k, me), own_sem.at[k]) for k in range(count)
    ]
    def from_core(k):
        for spot in range(place.lines):
            for p in range(2):
                for q in range(2):
                    arrive(k, place.across(spot, p, q))

    def read_small():
        copy = pltpu.make_async_copy(outs[tiny], small_here, small_sem)
        copy.start()
        copy.wait()

    def compute(part):
        groups = outs[conv].shape[1]
        if part == 0:
            read_small()
            project()
        elif part < 4:
            convolve(groups * (part - 1) // 3, groups * part // 3)
        else:
            leave()

    for name, kind, step in GATHER_PLAN:
        if name == "step":
            k = KINDS.index(kind)
            if step == 0 and kind == "blocks":
                ins[k][...] = raw[5][...].astype(jnp.bfloat16)
            (step_z_second if kind == "blocks" else step_z_first)(k, step)
            if step == 0:
                own_copies[k].start()
        elif name == "core":
            from_core(KINDS.index(kind))
            own_copies[KINDS.index(kind)].wait()
        elif name == "enter":
            enter()
            stats_low[...] = raw[6][...].astype(jnp.bfloat16)
        else:
            compute(step)
    from_core(KINDS.index("blocks"))
    own_copies[KINDS.index("blocks")].wait()
    for k, source, target, slot, condition, own in sent:
        guarded(
            condition,
            lambda k=k, source=source, target=target, slot=slot, own=own: copy_of(
                k, source, target, slot, own
            ).wait_send(),
        )


def full_shapes(sizes, shapes):
    dp_size, group_size = sizes
    conv, small, blocks = shapes
    return [
        (group_size, dp_size * conv[0]) + conv[1:],
        (dp_size, group_size) + small,
        (group_size * blocks[0], dp_size * blocks[1], blocks[2]),
    ]


def gather_weights(sizes, shapes, taps, raw, features, feature_norm, vectors):
    low, out = jnp.bfloat16, jax.ShapeDtypeStruct
    full = full_shapes(sizes, shapes)
    frames, width = features.shape
    count, devices = len(shapes), sizes[0] * sizes[1]
    dma = pltpu.SemaphoreType.DMA
    return pl.pallas_call(
        functools.partial(gather_kernel, sizes, shapes, taps),
        out_shape=[out(shape, low) for shape in full]
        + front_shapes(frames, width)
        + [out((frames, 1), jnp.float32), out(raw[-1].shape, low)],
        in_specs=[VMEM] * (len(raw) + 3),
        out_specs=[HBM] * count + [VMEM] * 9,
        scratch_shapes=[pltpu.VMEM(shape, low) for shape in shapes]
        + [pltpu.VMEM(full[1], low)]
        + front_scratch(full[0], frames)
        + [
            dma((count, 3 * devices)),
            dma((count, devices)),
            dma((count,)),
            dma,
        ],
        name="gather_front",
        compiler_params=pltpu.CompilerParams(
            collective_id=0, has_side_effects=True, vmem_limit_bytes=VMEM_LIMIT
        ),
    )(*raw, features, feature_norm, vectors)


class StatRows:
    def __init__(self, sizes, stats_in, stats_out, sems):
        self.place = Place(*sizes)
        self.members, _, self.rows, _ = stats_in.shape
        self.owners = Owners(self.place, self.members)
        self.stats_in, self.stats_out = stats_in, stats_out
        self.send_sem, self.recv_sem, self.own_sem = sems

    def spot(self, other):
        return pl.ds(pl.multiple_of(other * self.rows, self.rows), self.rows)

    def away(self, member, side):
        place = self.place
        return pltpu.make_async_remote_copy(
            src_ref=self.stats_in.at[member, side],
            dst_ref=self.stats_out.at[self.spot(place.dp)],
            send_sem=self.send_sem.at[member, side],
            recv_sem=self.recv_sem.at[place.dp],
            device_id=(self.owners.of(member), place.x * 2 + side),
            device_id_type=MESH,
        )

    def here(self, member, side):
        return pltpu.make_async_copy(
            self.stats_in.at[member, side], self.stats_out.at[self.spot(self.place.dp)], self.own_sem
        )

    def each(self, away, here):
        place = self.place
        for member in range(self.members):
            for side in range(2):
                mine = (place.dp == self.owners.of(member)) & (place.core == side)
                pl.when(jnp.logical_not(mine))(functools.partial(away, member, side))
                pl.when(mine)(functools.partial(here, member, side))

    def start(self):
        self.each(lambda m, s: self.away(m, s).start(), lambda m, s: self.here(m, s).start())

    def finish(self):
        place = self.place
        self.each(lambda m, s: self.away(m, s).wait_send(), lambda m, s: self.here(m, s).wait())

        @pl.when(self.owners.here)
        def _():
            for other in range(place.dp_size):

                @pl.when((place.dp != other) | (place.group != self.owners.group))
                def _(other=other):
                    pltpu.make_async_remote_copy(
                        src_ref=self.stats_in.at[0, 0],
                        dst_ref=self.stats_out.at[self.spot(other)],
                        send_sem=self.send_sem.at[0, 0],
                        recv_sem=self.recv_sem.at[other],
                        device_id=(place.dp, place.group),
                        device_id_type=MESH,
                    ).wait_recv()


def shift_right(values, by):
    if by == 0:
        return values
    parts = []
    for first in range(0, values.shape[1], CLIP):
        part = values[:, first : first + CLIP]
        lane = lax.broadcasted_iota(jnp.int32, part.shape, 1)
        turned = pltpu.roll(part, by % CLIP, 1)
        inside = lane >= by if by > 0 else lane < CLIP + by
        parts.append(jnp.where(inside, turned, 0.0))
    return jnp.concatenate(parts, 1)


def place_windows(hidden, windows, taps):
    channels = hidden.shape[0]
    runs, half = taps // STRIDE, taps // STRIDE // 2
    for run in range(runs):
        by = STRIDE * (half - 1 - run) if run < half else -STRIDE * (run - half)
        windows[run * channels : (run + 1) * channels, :] = shift_right(hidden, by).astype(
            jnp.bfloat16
        )


def conv_group(hidden, weight_at, windows, taps, shape):
    channels = hidden.shape[0]
    chunks, _, _, chunk = shape
    place_windows(hidden, windows, taps)
    total = None
    for side in range(2):
        part = None
        for index in range(side * chunks // 2, (side + 1) * chunks // 2):
            term = dot(weight_at(index), windows[index * chunk : (index + 1) * chunk, :])
            part = term if part is None else part + term
        for offset in range(STRIDE):
            by = STRIDE - offset if side == 0 else -offset
            moved = shift_right(part[offset * channels : (offset + 1) * channels], by)
            total = moved if total is None else total + moved
    return total


def conv_group_back(hidden, grad, weight_at, put, windows, moved, taps, shape):
    channels = hidden.shape[0]
    chunks, _, _, chunk = shape
    half, runs = taps // STRIDE // 2, chunk // channels
    place_windows(hidden, windows, taps)
    total = None
    for side in range(2):
        for offset in range(STRIDE):
            by = offset - STRIDE if side == 0 else offset
            moved[offset * channels : (offset + 1) * channels, :] = shift_right(grad, by).astype(
                jnp.bfloat16
            )
        for index in range(side * chunks // 2, (side + 1) * chunks // 2):
            put(
                index,
                dot_nt(moved[...], windows[index * chunk : (index + 1) * chunk, :]).astype(
                    jnp.bfloat16
                ),
            )
            turned = dot_tn(weight_at(index), moved[...])
            for step in range(runs):
                run = index * runs + step
                by = -STRIDE * (half - 1 - run) if run < half else STRIDE * (run - half)
                part = shift_right(turned[step * channels : (step + 1) * channels], by)
                total = part if total is None else total + part
    return total


def over_rows(total, tile, action):
    def step(index, _):
        action(pl.ds(pl.multiple_of(index * tile, tile), tile))
        return 0

    lax.fori_loop(0, total // tile, step, 0, unroll=4)


def dot(one, two):
    return jnp.dot(one, two, preferred_element_type=jnp.float32)


def dot_nt(one, two):
    return lax.dot_general(one, two, (((1,), (1,)), ((), ())), preferred_element_type=jnp.float32)


def dot_tn(one, two):
    return lax.dot_general(one, two, (((0,), (0,)), ((), ())), preferred_element_type=jnp.float32)


def norm_parts(values):
    average = jnp.mean(values, -1, keepdims=True)
    centred = values - average
    inverse = lax.rsqrt(jnp.mean(centred * centred, -1, keepdims=True) + 1e-05)
    return centred * inverse, inverse


def norm_back(upstream, unit, inverse, gain):
    scaled = upstream * gain
    along = jnp.mean(scaled * unit, -1, keepdims=True)
    return inverse * (scaled - jnp.mean(scaled, -1, keepdims=True) - unit * along)


def gelu_pair(values):
    below = 0.5 + 0.5 * lax.erf(values * 0.7071067811865476)
    density = jnp.exp(values * values * -0.5) * 0.3989422804014327
    return values * below, below + values * density


def add_row(ref, row, values):
    ref[row : row + 1, :] += jnp.sum(values, 0, keepdims=True)


def front_compute(taps, refs, outs, scratch):
    features, mask, feature_norm, vectors, small, kernel = refs
    feature_unit, normed, hidden_t, encoded, encoder_unit, encoder_inverse, slope = outs
    held, windows, hidden, out_t, load_sem = scratch
    frames = features.shape[0]
    groups = kernel.shape[1]
    channels = hidden_t.shape[0] // groups

    def load(group):
        return pltpu.make_async_copy(kernel.at[:, group], held.at[:, group], load_sem.at[group])

    def enter():
        def one(at):
            unit, _ = norm_parts(features[at, :].astype(jnp.float32))
            feature_unit[at, :] = unit
            scaled = unit * feature_norm[0:1, :] + feature_norm[1:2, :]
            normed[at, :] = scaled.astype(jnp.bfloat16)

        over_rows(frames, 32, one)

    def project():
        for group in range(groups):
            load(group).start()
        normed_t = normed[...].T
        parts, columns = small.shape[0], small.shape[1]
        third = D // columns
        for group in range(columns):
            for first, size in ((0, 128), (128, third - 128)):
                row = first // 2
                part = small[:, group, row : row + 64, :].reshape(parts * 64, 128)
                at = group * third + first
                out_t[at : at + size, :] = dot_tn(part, normed_t)[:size]
        hidden[...] = jnp.where(mask[...] > 0, vectors[0:1, :], out_t[...].T)
        hidden_t[...] = hidden[...].T.astype(jnp.bfloat16)

    def one_group(group, _):
        load(group).wait()
        at = pl.ds(pl.multiple_of(group * channels, channels), channels)
        out_t[at, :] = conv_group(
            hidden_t[at, :].astype(jnp.float32),
            lambda index: held[index, group],
            windows,
            taps,
            kernel.shape,
        )
        return 0

    def convolve(first, last):
        lax.fori_loop(first, last, one_group, 0)

    def leave():
        slope[...] = out_t[...].T

        def one(at):
            active, derivative = gelu_pair(slope[at, :])
            slope[at, :] = derivative
            unit, inverse = norm_parts(hidden[at, :] + active)
            encoder_unit[at, :] = unit
            encoder_inverse[at, :] = inverse
            encoded[at, :] = unit * vectors[1:2, :] + vectors[2:3, :]

        over_rows(frames, 32, one)

    return enter, project, convolve, leave


def front_kernel(taps, *refs):
    enter, project, convolve, leave = front_compute(taps, refs[:6], refs[6:13], refs[13:])
    enter()
    project()
    convolve(0, refs[5].shape[1])
    leave()


def front_shapes(frames, width):
    out, full, low = jax.ShapeDtypeStruct, jnp.float32, jnp.bfloat16
    return [
        out((frames, width), full),
        out((frames, width), low),
        out((D, frames), low),
        out((frames, D), full),
        out((frames, D), full),
        out((frames, 1), full),
        out((frames, D), full),
    ]


def front_scratch(kernel_shape, frames):
    chunks, groups, rows, chunk = kernel_shape
    return [
        pltpu.VMEM(kernel_shape, jnp.bfloat16),
        pltpu.VMEM((chunks * chunk, frames), jnp.bfloat16),
        pltpu.VMEM((frames, D), jnp.float32),
        pltpu.VMEM((D, frames), jnp.float32),
        pltpu.SemaphoreType.DMA((groups,)),
    ]


def front(features, mask, feature_norm, vectors, small, kernel, taps):
    frames, width = features.shape
    return pl.pallas_call(
        functools.partial(front_kernel, taps),
        out_shape=front_shapes(frames, width),
        in_specs=[VMEM] * 5 + [HBM],
        out_specs=[VMEM] * 7,
        scratch_shapes=front_scratch(kernel.shape, frames),
        name="front",
        compiler_params=pltpu.CompilerParams(vmem_limit_bytes=VMEM_LIMIT),
    )(features, mask, feature_norm, vectors, small, kernel)


def trunk_kernel(sizes, *refs):
    refs = list(refs)
    rows_moved = None
    if sizes is not None:
        stats_in, stats_out = refs.pop(6), refs.pop(12)
        rows_moved = StatRows(sizes, stats_in, stats_out, refs[-3:])
        refs = refs[:-3]
    (
        encoded, mask, labels, vectors, small, blocks,
        encoded_grad, block_grad, head_grad, center_grad_t, rows_out, counted,
        head, table, centers, held, made, low, triple, attention, mixed, unit_one, inverse_one, middle, middle_low,
        active, slope, unit_two, inverse_two, work, work_low, flow_low, triple_grad, turned,
        load_sem, save_sem,
    ) = refs
    frames = encoded.shape[0]
    count = blocks.shape[0]
    ups = (count - 4) // 2
    tile = 32
    pairs = D // 128

    def load(block):
        return pltpu.make_async_copy(blocks.at[block], held.at[block], load_sem.at[block])

    def save(block):
        return pltpu.make_async_copy(made.at[block], block_grad.at[block], save_sem.at[block])

    for block in range(count):
        load(block).start()
    if rows_moved is not None:
        greet(rows_moved.place)
        rows_moved.start()
    rows_out[...] = jnp.zeros_like(rows_out)
    parts, columns = small.shape[0], small.shape[1]
    notes = small[:, :, 224:240, :].astype(jnp.float32)
    first = lax.broadcasted_iota(jnp.int32, notes.shape, 2) == 0
    first &= lax.broadcasted_iota(jnp.int32, notes.shape, 3) == CLUSTER_ROWS
    notes = jnp.sum(jnp.where(first, notes, 0.0), (0, 1))
    masked = jnp.sum(jnp.sum(notes, 1, keepdims=True), 0, keepdims=True)
    counted[...] = masked

    def to_inputs(at):
        low[at, :] = encoded[at, :].astype(jnp.bfloat16)

    over_rows(frames, tile, to_inputs)

    def first_three(block, _):
        load(block).wait()
        triple[block] = dot(low[...], held[block]).astype(jnp.bfloat16)
        return 0

    lax.fori_loop(0, 3, first_three, 0)
    lane = lax.broadcasted_iota(jnp.int32, (CLIP, 128), 1)
    even = lane < HEAD

    def apart(values):
        zero = jnp.zeros_like(values)
        return jnp.concatenate([jnp.where(even, values, zero), jnp.where(even, zero, values)], 0)

    def beside(values):
        return jnp.concatenate([values[:CLIP], values[CLIP:]], 1)

    def spot(index):
        at = pl.ds(pl.multiple_of(index // pairs * CLIP, CLIP), CLIP)
        return at, pl.ds(pl.multiple_of(index % pairs * 128, 128), 128)

    def attend(index, _):
        at, lanes = spot(index)
        query, keys, values = triple[0, at, lanes], triple[1, at, lanes], triple[2, at, lanes]
        scores = dot_nt(apart(query), keys) * HEAD ** (-0.5)
        raised = jnp.exp(scores - jnp.max(scores, -1, keepdims=True))
        full = raised / jnp.sum(raised, -1, keepdims=True)
        attention[index] = full
        mixed[at, lanes] = dot(beside(full.astype(jnp.bfloat16)), apart(values)).astype(jnp.bfloat16)
        return 0

    lax.fori_loop(0, frames // CLIP * pairs, attend, 0, unroll=pairs)
    load(3).wait()
    work[...] = dot(mixed[...], held[3])

    def first_norm(at):
        unit, inverse = norm_parts(encoded[at, :] + work[at, :])
        unit_one[at, :] = unit
        inverse_one[at, :] = inverse
        value = unit * vectors[3:4, :] + vectors[4:5, :]
        middle[at, :] = value
        middle_low[at, :] = value.astype(jnp.bfloat16)

    over_rows(frames, tile, first_norm)

    def expand(step, _):
        load(4 + step).wait()
        slope[step] = dot(middle_low[...], held[4 + step])

        def bend(at):
            value, derivative = gelu_pair(slope[step, at, :])
            active[step, at, :] = value.astype(jnp.bfloat16)
            slope[step, at, :] = derivative

        over_rows(frames, tile, bend)
        return 0

    lax.fori_loop(0, ups, expand, 0)

    def contract(step, _):
        load(4 + ups + step).wait()
        middle[...] += dot(active[step], held[4 + ups + step])
        return 0

    lax.fori_loop(0, ups, contract, 0)

    def second_norm(at):
        unit, inverse = norm_parts(middle[at, :])
        unit_two[at, :] = unit
        inverse_two[at, :] = inverse
        flow_low[at, :] = (unit * vectors[5:6, :] + vectors[6:7, :]).astype(jnp.bfloat16)

    over_rows(frames, tile, second_norm)
    table[...] = jnp.zeros_like(table)
    for group in range(columns):
        across = slice(group * 128, group * 128 + 128)
        head[:, across] = small[:, group, 128:224, :].reshape(parts * 96, 128)
        for part in range(parts):
            row = part // 2 * 128 + part % 2 * 32
            table[row : row + 32, across] = small[part, group, 224:256, :].astype(jnp.float32)
    real = lax.broadcasted_iota(jnp.int32, (1, table.shape[1]), 1) % 128 < CLUSTER_ROWS
    table[...] = jnp.where(real, table[...], 0.0)
    size = lax.rsqrt(jnp.sum(table[...] * table[...], 0, keepdims=True) + 1e-06)
    centers[...] = (table[...] * size).astype(jnp.bfloat16)
    embedded = dot(flow_low[...], head[...])
    length = lax.rsqrt(jnp.sum(embedded * embedded, -1, keepdims=True) + 1e-06)
    unit_low = (embedded * length).astype(jnp.bfloat16)
    logits = jnp.where(real, dot(unit_low, centers[...]) * inv_temp, -1e30)
    top = jnp.max(logits, -1, keepdims=True)
    raised = jnp.exp(logits - top)
    amount = jnp.sum(raised, -1, keepdims=True)
    columns_of = labels[...]
    for group in range(1, columns):
        columns_of = columns_of + jnp.where(labels[...] >= group * CLUSTER_ROWS, 128 - CLUSTER_ROWS, 0)
    choose = columns_of == lax.broadcasted_iota(jnp.int32, logits.shape, 1)
    target = jnp.sum(jnp.where(choose, logits, 0.0), -1, keepdims=True)
    losses = mask[...] * (jnp.log(amount) + top - target)
    rows_out[7:8, :] = jnp.broadcast_to(jnp.sum(losses, 0, keepdims=True), (1, D))
    logit_grad = (
        (raised / amount - choose.astype(jnp.float32)) * (mask[...] * (1.0 / masked))
    ).astype(jnp.bfloat16)
    unit_grad = dot_nt(logit_grad, centers[...]) * inv_temp
    spread = dot_tn(unit_low, logit_grad) * inv_temp
    shared = jnp.sum(spread * table[...], 0, keepdims=True)
    spread = size * spread - table[...] * (size * size * size * shared)
    for group in range(columns):
        center_grad_t[group * 64 : group * 64 + 64, :] = spread[group * 128 : group * 128 + 64, :]
    along = jnp.sum(unit_grad * embedded, -1, keepdims=True)
    embedded_grad = (
        length * unit_grad - embedded * (length * length * length * along)
    ).astype(jnp.bfloat16)
    work[...] = dot_nt(embedded_grad, head[...])
    head_grad[...] = dot_tn(flow_low[...], embedded_grad).astype(jnp.bfloat16)

    def second_back(at):
        upstream = work[at, :]
        add_row(rows_out, 5, upstream * unit_two[at, :])
        add_row(rows_out, 6, upstream)
        value = norm_back(upstream, unit_two[at, :], inverse_two[at, :], vectors[5:6, :])
        middle[at, :] = value
        flow_low[at, :] = value.astype(jnp.bfloat16)

    over_rows(frames, tile, second_back)
    turned[...] = middle_low[...].T

    def feed_back(step, _):
        work[...] = dot_nt(flow_low[...], held[4 + ups + step])
        made[4 + ups + step] = dot_tn(active[step], flow_low[...]).astype(jnp.bfloat16)
        save(4 + ups + step).start()

        def bend(at):
            work_low[at, :] = (work[at, :] * slope[step, at, :]).astype(jnp.bfloat16)

        over_rows(frames, tile, bend)
        made[4 + step] = dot(turned[...], work_low[...]).astype(jnp.bfloat16)
        save(4 + step).start()
        middle[...] += dot_nt(work_low[...], held[4 + step])
        return 0

    lax.fori_loop(0, ups, feed_back, 0)

    def first_back(at):
        upstream = middle[at, :]
        add_row(rows_out, 3, upstream * unit_one[at, :])
        add_row(rows_out, 4, upstream)
        value = norm_back(upstream, unit_one[at, :], inverse_one[at, :], vectors[3:4, :])
        middle[at, :] = value
        flow_low[at, :] = value.astype(jnp.bfloat16)

    over_rows(frames, tile, first_back)
    made[3] = dot_tn(mixed[...], flow_low[...]).astype(jnp.bfloat16)
    save(3).start()
    work_low[...] = dot_nt(flow_low[...], held[3]).astype(jnp.bfloat16)

    def attend_back(index, _):
        at, lanes = spot(index)
        query, keys, values = triple[0, at, lanes], triple[1, at, lanes], triple[2, at, lanes]
        upstream = apart(work_low[at, lanes])
        full = attention[index]
        full_grad = dot_nt(upstream, values)
        triple_grad[2, at, lanes] = dot_tn(full.astype(jnp.bfloat16), upstream).astype(jnp.bfloat16)
        along = jnp.sum(full * full_grad, -1, keepdims=True)
        score_grad = (full * (full_grad - along)).astype(jnp.bfloat16)
        triple_grad[0, at, lanes] = (
            dot(beside(score_grad), apart(keys)) * HEAD ** (-0.5)
        ).astype(jnp.bfloat16)
        triple_grad[1, at, lanes] = (
            dot_tn(score_grad, apart(query)) * HEAD ** (-0.5)
        ).astype(jnp.bfloat16)
        return 0

    lax.fori_loop(0, frames // CLIP * pairs, attend_back, 0, unroll=pairs)
    turned[...] = low[...].T

    def last_three(block, _):
        made[block] = dot(turned[...], triple_grad[block]).astype(jnp.bfloat16)
        save(block).start()
        middle[...] += dot_nt(triple_grad[block], held[block])
        return 0

    lax.fori_loop(0, 3, last_three, 0)
    encoded_grad[...] = middle[...]
    if rows_moved is not None:
        rows_moved.finish()
    for block in range(count):
        save(block).wait()


def trunk(encoded, mask, labels, vectors, small, blocks, sizes=None, stats_low=None):
    frames, count = encoded.shape[0], blocks.shape[0]
    ups, columns = (count - 4) // 2, small.shape[1] * 128
    full, low = jnp.float32, jnp.bfloat16
    out = jax.ShapeDtypeStruct
    wide, wide_low = pltpu.VMEM((frames, D), full), pltpu.VMEM((frames, D), low)
    column = pltpu.VMEM((frames, 1), full)
    more_in, more_out, sems, settings = [], [], [], {}
    if sizes is not None:
        dma = pltpu.SemaphoreType.DMA
        more_in, more_out = [stats_low], [out((D, D), low)]
        sems = [dma((stats_low.shape[0], 2)), dma((sizes[0],)), dma]
        settings = {"collective_id": 3, "has_side_effects": True}
    return pl.pallas_call(
        functools.partial(trunk_kernel, sizes),
        out_shape=[
            out((frames, D), full),
            out(blocks.shape, low),
            out((D, columns), low),
            out((columns // 2, columns), full),
            out((8, D), full),
            out((1, 1), full),
        ]
        + more_out,
        in_specs=[VMEM] * 5 + [HBM] * (1 + len(more_in)),
        out_specs=[VMEM, HBM] + [VMEM] * 4 + [HBM] * len(more_out),
        scratch_shapes=[
            pltpu.VMEM((D, columns), low),
            pltpu.VMEM((columns, columns), full),
            pltpu.VMEM((columns, columns), low),
            pltpu.VMEM(blocks.shape, low),
            pltpu.VMEM(blocks.shape, low),
            wide_low,
            pltpu.VMEM((3, frames, D), low),
            pltpu.VMEM((frames // CLIP * D // 128, 2 * CLIP, CLIP), full),
            wide_low,
            wide,
            column,
            wide,
            wide_low,
            pltpu.VMEM((ups, frames, D), low),
            pltpu.VMEM((ups, frames, D), full),
            wide,
            column,
            wide,
            wide_low,
            wide_low,
            pltpu.VMEM((3, frames, D), low),
            pltpu.VMEM((D, frames), low),
            pltpu.SemaphoreType.DMA((count,)),
            pltpu.SemaphoreType.DMA((count,)),
        ]
        + sems,
        name="trunk",
        compiler_params=pltpu.CompilerParams(vmem_limit_bytes=VMEM_LIMIT, **settings),
    )(encoded, mask, labels, vectors, small, blocks, *more_in)


LOSS_ROW = 7


class Owners:
    def __init__(self, place, members):
        self.place, self.members = place, members
        self.first = (place.dp_size - 2 * members) // 2
        index = place.dp - self.first
        self.here = (index >= 0) & (index < 2 * members)
        self.group = place.x * 2 + index // members
        self.member = index % members

    def of(self, member):
        return self.first + self.place.core * self.members + member

    def to_rows(self, other, remote_action, local_action):
        place = self.place
        away = (place.dp != other) | (place.group != self.group)
        pl.when(away)(functools.partial(remote_action, other))
        pl.when(jnp.logical_not(away))(local_action)


class Reducer:
    def __init__(self, place, shapes, local, refs, sems):
        self.place, self.shapes, self.local = place, shapes, local
        self.z, self.lines, self.last = place.z, place.lines, place.lines - 1
        self.blocks = KINDS.index("blocks")
        self.rest = [k for k in range(len(KINDS)) if k != self.blocks]
        self.crossed, self.first_in, self.second_in, self.line_in = refs[:4]
        self.held, self.source = refs[4:]
        (
            self.load_sem, self.cross_send, self.cross_recv, self.first_send, self.first_recv,
            self.second_send, self.second_recv, self.left_send, self.left_recv, self.right_send,
            self.right_recv,
        ) = sems
        self.p_mate, self.q_mate = place.near(self.z, 1, 0), place.near(self.z, 0, 1)
        self.c_mate = place.at(self.z, 0, 0, 1)
        self.left, self.right = place.at(self.z - 1), place.at(self.z + 1)

    def remote(self, source, target, send, recv, device):
        return pltpu.make_async_remote_copy(
            src_ref=source,
            dst_ref=target,
            send_sem=send,
            recv_sem=recv,
            device_id=device,
            device_id_type=MESH,
        )

    def load_of(self, p, q, spot):
        k = self.blocks
        dp, group = self.place.near(spot, p, q)
        return pltpu.make_async_copy(
            piece_at("blocks", self.source[k], dp, group, self.shapes[k]),
            self.held.at[p, spot],
            self.load_sem.at[p, q, spot],
        )

    def cross_of(self, k, p, q, spot):
        dp, group = self.place.across(spot, p, q)
        return self.remote(
            piece_at(KINDS[k], self.source[k], dp, group, self.shapes[k]),
            self.crossed[k].at[p, q, spot],
            self.cross_send.at[k, p, q, spot],
            self.cross_recv.at[k, p, q, spot],
            self.c_mate,
        )

    def own(self, k, p, q, spot):
        if k == self.blocks:
            self.load_of(p, q, spot).wait()
            return f32(self.held, (p, spot))
        dp, group = self.place.near(spot, p, q)
        return piece_at(KINDS[k], self.source[k], dp, group, self.shapes[k])[...].astype(jnp.float32)

    def met(self, k, p, q, spot):
        own = self.own(k, p, q, spot)
        self.cross_of(k, p, q, spot).wait_recv()
        return own + f32(self.crossed[k], (p, q, spot))

    def turn(self, index):
        odd = index % 2
        return (1 - odd) * (self.last - index // 2) + odd * (index // 2)

    def first_out(self, k, p, spot):
        return self.remote(
            self.crossed[k].at[p, 1, spot],
            self.first_in[k].at[p, spot],
            self.first_send.at[k, p, spot],
            self.first_recv.at[k, p, spot],
            self.q_mate,
        )

    def stage_one(self, k, index):
        p, spot = 1 - index // self.lines, self.turn(index % self.lines)
        self.crossed[k][p, 1, spot] = self.met(k, p, 1, spot).astype(jnp.bfloat16)
        self.first_out(k, p, spot).start()
        if k == self.blocks:
            self.load_of(p, 0, spot).start()

    def joined(self, k, p, spot):
        total = self.met(k, p, 0, spot)
        self.first_out(k, p, spot).wait_recv()
        return total + f32(self.first_in[k], (p, spot))

    def second_out(self, k, spot):
        return self.remote(
            self.crossed[k].at[1, 0, spot],
            self.second_in[k].at[spot],
            self.second_send.at[k, spot],
            self.second_recv.at[k, spot],
            self.p_mate,
        )

    def stage_two(self, k, index):
        spot = self.turn(index)
        self.crossed[k][1, 0, spot] = self.joined(k, 1, spot).astype(jnp.bfloat16)
        self.second_out(k, spot).start()

    def line_total(self, k, spot):
        total = self.joined(k, 0, spot)
        self.second_out(k, spot).wait_recv()
        return total + f32(self.second_in[k], (spot,))

    def line_out(self, k, spot, way):
        if way == "right":
            send, recv, device, slot = self.right_send, self.left_recv, self.right, spot
        else:
            send, recv, device = self.left_send, self.right_recv, self.left
            ends = (self.last - (self.z - 1 - spot)) // self.last
            slot = spot + ends * (self.lines - spot)
        return self.remote(
            self.crossed[k].at[0, 0, spot],
            self.line_in[k].at[slot],
            send.at[k, spot],
            recv.at[k, spot],
            device,
        )

    def came_in(self, k, spot, way):
        recv = self.left_recv if way == "right" else self.right_recv
        send = self.right_send if way == "right" else self.left_send
        return self.remote(
            self.crossed[k].at[0, 0, spot],
            self.line_in[k].at[spot],
            send.at[k, spot],
            recv.at[k, spot],
            self.c_mate,
        )

    def pass_on(self, k, spot, way, inner):
        z = self.z
        if way == "right":
            here = (z < spot) & ((z > 0) if inner else (z == 0))
        else:
            here = (z > spot) & ((z < self.last) if inner else (z == self.last))

        @pl.when(here)
        def _():
            total = self.line_total(k, spot)
            if inner:
                self.came_in(k, spot, way).wait_recv()
                total = total + f32(self.line_in[k], (spot,))
            self.crossed[k][0, 0, spot] = total.astype(jnp.bfloat16)
            self.line_out(k, spot, way).start()

    def line_step(self, k, step, inner):
        self.pass_on(k, self.last - step, "right", inner)
        self.pass_on(k, step, "left", inner)

    def line_end(self, k, out):
        z = self.z
        out[...] = self.line_total(k, z)

        @pl.when(z > 0)
        def _():
            self.came_in(k, z, "right").wait_recv()
            out[...] += f32(self.line_in[k], (z,))

        @pl.when(z < self.last)
        def _():
            self.came_in(k, z, "left").wait_recv()
            out[...] += f32(self.line_in[k], (self.lines,))

    def drain(self):
        for k in range(len(KINDS)):

            def one(spot, _, k=k):
                for p in range(2):
                    for q in range(2):
                        self.cross_of(k, p, q, spot).wait_send()
                    self.first_out(k, p, spot).wait_send()
                self.second_out(k, spot).wait_send()

                @pl.when(self.z < spot)
                def _():
                    self.line_out(k, spot, "right").wait_send()

                @pl.when(self.z > spot)
                def _():
                    self.line_out(k, spot, "left").wait_send()

                return 0

            lax.fori_loop(0, self.lines, one, 0)


def f32(ref, at):
    return ref[at].astype(jnp.float32)


def back_compute(taps, refs, made, small_made, rows, scratch, hook):
    (
        encoded_grad, mask, vectors, small, feature_unit, normed, hidden_t,
        encoder_unit, encoder_inverse, slope, trunk_rows, head_grad, center_grad_t, kernel,
    ) = refs
    slots, windows, moved, grad, grad_t, through, through_t, load_sem = scratch
    frames, width = feature_unit.shape
    groups = kernel.shape[1]
    channels = hidden_t.shape[0] // groups

    def load(group):
        slot = group % 2
        return pltpu.make_async_copy(kernel.at[:, group], slots.at[slot], load_sem.at[slot])

    def begin():
        load(0).start()
        rows[...] = jnp.zeros_like(rows)
        rows[0:8, :] = trunk_rows[...]
        over_rows(frames, 32, enter)
        grad_t[...] = through[...].T.astype(jnp.bfloat16)

    def enter(at):
        upstream = encoded_grad[at, :]
        add_row(rows, 1, upstream * encoder_unit[at, :])
        add_row(rows, 2, upstream)
        value = norm_back(upstream, encoder_unit[at, :], encoder_inverse[at, :], vectors[1:2, :])
        grad[at, :] = value
        through[at, :] = value * slope[at, :]

    def one_group(group, _):
        pl.when(group + 1 < groups)(lambda: load(group + 1).start())
        load(group).wait()
        at = pl.ds(pl.multiple_of(group * channels, channels), channels)

        def put(index, value):
            made[index, group] = value

        through_t[at, :] = conv_group_back(
            hidden_t[at, :].astype(jnp.float32),
            grad_t[at, :].astype(jnp.float32),
            lambda index: slots[group % 2, index],
            put,
            windows,
            moved,
            taps,
            kernel.shape,
        )
        hook(group)
        return 0

    def convolve(first, last):
        lax.fori_loop(first, last, one_group, 0)

    def leave(at):
        total = grad[at, :] + through[at, :]
        inside = mask[at, :] > 0
        add_row(rows, 0, jnp.where(inside, total, 0.0))
        grad[at, :] = jnp.where(inside, 0.0, total)

    def finish():
        through[...] = through_t[...].T
        over_rows(frames, 32, leave)
        grad_t[...] = grad[...].T.astype(jnp.bfloat16)
        normed_t = normed[...].T
        parts, columns = small.shape[0], small.shape[1]
        third = D // columns
        total = None
        for group in range(columns):
            one = grad_t[group * third : group * third + 128, :]
            two = grad_t[group * third + 128 : (group + 1) * third, :]
            lane = third - 128
            wide = dot_nt(normed_t, one).astype(jnp.bfloat16)
            thin = dot_nt(normed_t, two).astype(jnp.bfloat16)
            small_made[:, group, 0:64, :] = wide.reshape(parts, 64, 128)
            small_made[:, group, 64:128, :] = jnp.concatenate(
                [thin, jnp.zeros((thin.shape[0], 128 - lane), jnp.bfloat16)], 1
            ).reshape(parts, 64, 128)
            small_made[:, group, 128:224, :] = head_grad[:, group * 128 : group * 128 + 128].reshape(
                parts, 96, 128
            )
            small_made[:, group, 224:256, :] = (
                center_grad_t[:, group * 128 : group * 128 + 128]
                .astype(jnp.bfloat16)
                .reshape(parts, 32, 128)
            )
            first = small[:, group, 0:64, :].reshape(parts * 64, 128)
            second = small[:, group, 64:128, :].reshape(parts * 64, 128)[:, :lane]
            term = dot(first, one) + dot(second, two)
            total = term if total is None else total + term
        normed_grad = total.T
        rows[8:9, 0:width] = jnp.sum(normed_grad * feature_unit[...], 0, keepdims=True)
        rows[9:10, 0:width] = jnp.sum(normed_grad, 0, keepdims=True)

    return begin, convolve, finish


def back_scratch(kernel_shape, frames):
    chunks, groups, rows, chunk = kernel_shape
    full, low = jnp.float32, jnp.bfloat16
    return [
        pltpu.VMEM((2, chunks, rows, chunk), low),
        pltpu.VMEM((chunks * chunk, frames), low),
        pltpu.VMEM((rows, frames), low),
        pltpu.VMEM((frames, D), full),
        pltpu.VMEM((D, frames), low),
        pltpu.VMEM((frames, D), full),
        pltpu.VMEM((D, frames), full),
        pltpu.SemaphoreType.DMA((2,)),
    ]


BACK_INPUTS = 14


def back_kernel(taps, *refs):
    made, small_made, rows = refs[BACK_INPUTS : BACK_INPUTS + 3]
    begin, convolve, finish = back_compute(
        taps, refs[:BACK_INPUTS], made, small_made, rows, refs[BACK_INPUTS + 3 :], lambda group: None
    )
    begin()
    convolve(0, made.shape[1])
    finish()


def back(taps, operands):
    kernel, small, frames = operands[-1], operands[3], operands[0].shape[0]
    return pl.pallas_call(
        functools.partial(back_kernel, taps),
        out_shape=[
            jax.ShapeDtypeStruct(kernel.shape, jnp.bfloat16),
            jax.ShapeDtypeStruct(small.shape, jnp.bfloat16),
            jax.ShapeDtypeStruct((16, D), jnp.float32),
        ],
        in_specs=[VMEM] * (BACK_INPUTS - 1) + [HBM],
        out_specs=[VMEM] * 3,
        scratch_shapes=back_scratch(kernel.shape, frames),
        name="back",
        compiler_params=pltpu.CompilerParams(vmem_limit_bytes=48 * 1024 * 1024),
    )(*operands)


def back_reduce_kernel(sizes, shapes, taps, *refs):
    place = Place(*sizes)
    refs = list(refs)

    def pull(number):
        taken = refs[:number]
        del refs[:number]
        return taken

    count = len(KINDS)
    inputs, (block_grad,) = pull(BACK_INPUTS), pull(1)
    outs, (small_out, square_out, whole_box) = pull(count), pull(3)
    made, small_made, rows, scratch = *pull(3), pull(8)
    crossed, first_in, second_in, line_in = (pull(count) for _ in range(4))
    (held, group_box, dp_box, rows_low) = pull(4)
    sems = pull(11)
    (group_send, group_recv, dp_send, dp_recv, row_send, row_recv, pair_send, pair_recv) = pull(8)
    me = (place.dp, place.group)
    source = {"conv": made, "small": small_made, "blocks": block_grad}
    run = Reducer(
        place,
        shapes,
        None,
        (crossed, first_in, second_in, line_in, held, [source[kind] for kind in KINDS]),
        sems,
    )
    lines, b = run.lines, run.blocks
    conv, tiny = KINDS.index("conv"), KINDS.index("small")
    greet(place)

    def cross_all(k):
        for q in (1, 0):
            for p in (1, 0):

                def begin_one(index, _, p=p, q=q):
                    run.cross_of(k, p, q, run.turn(index)).start()
                    if k == b and q == 1:
                        run.load_of(p, q, run.turn(index)).start()
                    return 0

                lax.fori_loop(0, lines, begin_one, 0)

    def hook(group):
        pairs = shapes[conv][0]

        @pl.when(group % pairs == pairs - 1)
        def _():
            dp = group // pairs
            spot, flip_y = dp // 2, (dp % 2 + place.y) % 2
            for x in range(2):
                flip_x = (x + place.x) % 2
                p = flip_y * place.core + flip_x * (1 - place.core)
                q = flip_x * place.core + flip_y * (1 - place.core)
                run.cross_of(conv, p, q, spot).start()

    begin, convolve, finish = back_compute(taps, inputs, made, small_made, rows, scratch, hook)

    def remote(source, target, send, recv, device):
        return run.remote(source, target, send, recv, device)

    def each_other(size, mine, action):
        for other in range(size):
            pl.when(mine != other)(functools.partial(action, other))

    def group_copy(other):
        return remote(
            rows,
            group_box.at[place.group],
            group_send.at[other],
            group_recv.at[place.group],
            (place.dp, other),
        )

    def dp_copy(other):
        return remote(
            dp_box.at[place.dp], dp_box.at[place.dp], dp_send.at[other], dp_recv.at[place.dp], (other, place.group)
        )

    def group_wait(other):
        group_copy(other).wait_send()
        remote(rows, group_box.at[other], group_send.at[other], group_recv.at[other], me).wait_recv()

    def dp_wait(other):
        dp_copy(other).wait_send()
        remote(dp_box.at[other], dp_box.at[other], dp_send.at[other], dp_recv.at[other], me).wait_recv()

    def rows_to_group():
        group_box[place.group] = rows[...]
        each_other(place.group_size, place.group, lambda other: group_copy(other).start())

    def rows_to_all():
        each_other(place.group_size, place.group, group_wait)
        total = group_box[0]
        for other in range(1, place.group_size):
            total = total + group_box[other]
        dp_box[place.dp] = total
        each_other(place.dp_size, place.dp, lambda other: dp_copy(other).start())

    def some(first, last, action):
        def one(index, _):
            action(index)
            return 0

        lax.fori_loop(first, last, one, 0)

    members, depth = shapes[b][0], shapes[b][1]
    owners = Owners(place, members)
    my_rows = pl.ds(pl.multiple_of(place.dp * depth, depth), depth)
    owner_here = owners.here & (owners.group == place.group)
    owner_there = owners.here & (owners.group != place.group)

    def row_copy(member):
        return remote(
            rows_low.at[member],
            whole_box.at[my_rows],
            row_send.at[member],
            row_recv.at[place.dp],
            (owners.of(member), place.group),
        )

    def pair_copy(other):
        spot = pl.ds(pl.multiple_of(other * depth, depth), depth)
        return remote(
            whole_box.at[spot], whole_box.at[spot], pair_send.at[other], pair_recv.at[other], run.c_mate
        )

    def send_rows():
        rows_low[...] = outs[b][...].astype(jnp.bfloat16)
        for member in range(members):

            @pl.when(place.dp != owners.of(member))
            def _(member=member):
                row_copy(member).start()

            @pl.when(place.dp == owners.of(member))
            def _(member=member):
                whole_box[my_rows] = rows_low[member]
                pair_copy(place.dp).start()

    def take_rows():
        @pl.when(owner_here)
        def _():
            for other in range(place.dp_size):

                @pl.when(place.dp != other)
                def _(other=other):
                    spot = pl.ds(other * depth, depth)
                    remote(
                        rows_low.at[0], whole_box.at[spot], row_send.at[0], row_recv.at[other], me
                    ).wait_recv()
                    pair_copy(other).start()

        @pl.when(owner_there)
        def _():
            for other in range(place.dp_size):
                pair_copy(other).wait_recv()

    cross_all(b)
    begin()
    actions = {
        "one": lambda index, k: run.stage_one(k, index),
        "two": lambda index, k: run.stage_two(k, index),
        "edge": lambda index, k: run.line_step(k, index, False),
        "inner": lambda index, k: run.line_step(k, index, True),
        "end": lambda index, k: run.line_end(k, outs[k]),
    }

    def leave():
        finish()
        cross_all(tiny)
        rows_to_group()

    plain = {"leave": leave, "rows": send_rows, "take": take_rows}
    for name, kind, first, last in PLAN:
        if name == "groups":
            convolve(first, last)
        elif name in plain:
            plain[name]()
        else:
            action = functools.partial(lambda index, k, name: actions[name](index, k), k=KINDS.index(kind), name=name)
            if last - first == 1:
                action(first)
            else:
                some(first, last, action)
        if name == "rows":
            rows_to_all()
    square = jnp.sum(outs[b][...] * outs[b][...])
    for k in run.rest:
        square = square + jnp.sum(outs[k][...] * outs[k][...])
    each_other(place.dp_size, place.dp, dp_wait)
    total = dp_box[0]
    for other in range(1, place.dp_size):
        total = total + dp_box[other]
    small_out[...] = total
    skipped = lax.broadcasted_iota(jnp.int32, total.shape, 0) != LOSS_ROW
    square = square + jnp.sum(jnp.where(skipped, total * total, 0.0)) * (
        1.0 / (place.dp_size * place.group_size)
    )
    square_out[...] = jnp.full(square_out.shape, square, jnp.float32)
    for member in range(members):
        @pl.when(place.dp != owners.of(member))
        def _(member=member):
            row_copy(member).wait_send()

    @pl.when(owner_here)
    def _():
        for other in range(place.dp_size):
            pair_copy(other).wait_send()

    run.drain()


def back_reduce(sizes, shapes, taps, operands, block_grad):
    dp_size, group_size = sizes
    lines, count = dp_size // 2, len(KINDS)
    kernel, small, frames = operands[-1], operands[3], operands[0].shape[0]
    low, full = jnp.bfloat16, jnp.float32

    def boxes(lead):
        return [
            pltpu.VMEM(tuple(lead(kind)) + tuple(shape), low) for kind, shape in zip(KINDS, shapes)
        ]

    dma = pltpu.SemaphoreType.DMA
    scratch = (
        [pltpu.VMEM(kernel.shape, low), pltpu.VMEM(small.shape, low), pltpu.VMEM((16, D), full)]
        + back_scratch(kernel.shape, frames)
        + boxes(lambda kind: (2, 2, lines))
        + boxes(lambda kind: (2, lines))
        + boxes(lambda kind: (lines,))
        + boxes(lambda kind: (lines + 1,))
        + [
            pltpu.VMEM((2, lines) + tuple(shapes[-1]), low),
            pltpu.VMEM((group_size, 16, D), full),
            pltpu.VMEM((dp_size, 16, D), full),
            pltpu.VMEM(shapes[-1], low),
        ]
        + [dma((2, 2, lines))]
        + [dma((count, 2, 2, lines))] * 2
        + [dma((count, 2, lines))] * 2
        + [dma((count, lines))] * 6
        + [dma((group_size,))] * 2
        + [dma((dp_size,))] * 2
        + [dma((shapes[-1][0],)), dma((dp_size,))]
        + [dma((dp_size,))] * 2
    )
    return pl.pallas_call(
        functools.partial(back_reduce_kernel, sizes, shapes, taps),
        out_shape=[jax.ShapeDtypeStruct(shape, full) for shape in shapes]
        + [
            jax.ShapeDtypeStruct((16, D), full),
            jax.ShapeDtypeStruct((8, 128), full),
            jax.ShapeDtypeStruct((D, D), low),
        ],
        in_specs=[VMEM] * (BACK_INPUTS - 1) + [HBM, HBM],
        out_specs=[VMEM] * (count + 3),
        scratch_shapes=scratch,
        name="back_reduce",
        compiler_params=pltpu.CompilerParams(
            collective_id=1, has_side_effects=True, vmem_limit_bytes=VMEM_LIMIT
        ),
    )(*operands, block_grad)


PLAN = (
    ("one", "blocks", 0, 1),
    ("groups", "", 0, 3),
    ("one", "blocks", 4, 5),
    ("two", "blocks", 0, 1),
    ("groups", "", 3, 6),
    ("one", "blocks", 1, 2),
    ("groups", "", 6, 9),
    ("one", "blocks", 5, 6),
    ("two", "blocks", 1, 2),
    ("one", "blocks", 3, 4),
    ("groups", "", 9, 16),
    ("one", "blocks", 2, 3),
    ("leave", "", 0, 1),
    ("edge", "blocks", 0, 1),
    ("one", "blocks", 6, 7),
    ("one", "small", 1, 2),
    ("inner", "blocks", 2, 3),
    ("one", "blocks", 7, 8),
    ("one", "conv", 3, 4),
    ("two", "blocks", 2, 4),
    ("one", "conv", 0, 1),
    ("one", "small", 0, 1),
    ("one", "small", 5, 6),
    ("one", "small", 4, 5),
    ("one", "small", 2, 3),
    ("two", "small", 1, 2),
    ("edge", "blocks", 1, 2),
    ("inner", "blocks", 0, 1),
    ("one", "small", 3, 4),
    ("inner", "blocks", 1, 2),
    ("one", "conv", 5, 6),
    ("inner", "conv", 2, 3),
    ("one", "conv", 2, 3),
    ("edge", "blocks", 2, 3),
    ("two", "small", 0, 1),
    ("edge", "small", 0, 1),
    ("one", "conv", 1, 2),
    ("one", "conv", 4, 5),
    ("two", "small", 3, 4),
    ("end", "blocks", 0, 1),
    ("two", "conv", 0, 1),
    ("one", "small", 7, 8),
    ("inner", "small", 0, 1),
    ("two", "small", 2, 3),
    ("one", "conv", 7, 8),
    ("rows", "", 0, 1),
    ("inner", "small", 2, 3),
    ("one", "small", 6, 7),
    ("two", "conv", 1, 4),
    ("edge", "small", 1, 2),
    ("edge", "conv", 0, 1),
    ("inner", "small", 1, 2),
    ("one", "conv", 6, 7),
    ("edge", "conv", 1, 2),
    ("edge", "small", 2, 3),
    ("inner", "conv", 0, 1),
    ("edge", "conv", 2, 3),
    ("inner", "conv", 1, 2),
    ("take", "", 0, 1),
    ("end", "small", 0, 1),
    ("end", "conv", 0, 1),
)


GATHER_PLAN = (
    ("step", "small", 0),
    ("step", "conv", 0),
    ("step", "blocks", 0),
    ("enter", "", 0),
    ("step", "small", 1),
    ("step", "conv", 1),
    ("step", "blocks", 1),
    ("step", "conv", 2),
    ("step", "small", 2),
    ("step", "blocks", 2),
    ("step", "conv", 3),
    ("step", "small", 3),
    ("step", "conv", 4),
    ("step", "small", 4),
    ("step", "conv", 5),
    ("step", "small", 5),
    ("step", "small", 6),
    ("core", "conv", 0),
    ("core", "small", 0),
    ("compute", "", 0),
    ("step", "blocks", 3),
    ("compute", "", 1),
    ("compute", "", 2),
    ("compute", "", 3),
    ("step", "blocks", 4),
    ("step", "conv", 6),
    ("compute", "", 4),
    ("step", "blocks", 5),
    ("step", "blocks", 6),
)


def roots_kernel(sizes, members, *refs):
    (
        whole, stat, square_in, sides_out, update_out, square_out,
        gram, big, m0, m0b, m1, m1b, s1, s1b, s2b, s3, s3b, root, mixed,
        group_box, dp_box, group_send, group_recv, dp_send, dp_recv,
        side_send, side_recv, side_own, mixed_send, mixed_recv, update_send, update_recv, update_own,
    ) = refs
    place = Place(*sizes)
    owners = Owners(place, members)
    dp_size, rows = place.dp_size, D // place.dp_size
    me, c_mate = (place.dp, place.group), place.at(place.z, 0, 0, 1)
    owner = owners.here
    tile = 256
    greet(place)

    def remote(source, target, send, recv, device):
        return pltpu.make_async_remote_copy(
            src_ref=source,
            dst_ref=target,
            send_sem=send,
            recv_sem=recv,
            device_id=device,
            device_id_type=MESH,
        )

    def each_other(size, mine, action):
        for other in range(size):
            pl.when(mine != other)(functools.partial(action, other))

    def group_copy(other, slot):
        return remote(
            group_box.at[slot], group_box.at[slot], group_send.at[other], group_recv.at[slot], (place.dp, other)
        )

    def dp_copy(other, slot):
        return remote(dp_box.at[slot], dp_box.at[slot], dp_send.at[other], dp_recv.at[slot], (other, place.group))

    group_box[place.group] = square_in[...]
    each_other(place.group_size, place.group, lambda other: group_copy(other, place.group).start())

    def product_rows(one, two, then):
        def step(index, _):
            at = pl.ds(pl.multiple_of(index * tile, tile), tile)
            then(at, jnp.dot(one[at, :], two[...], preferred_element_type=jnp.float32))
            return 0

        lax.fori_loop(0, D // tile, step, 0, unroll=True)

    half = D // 2

    @pl.when(owner)
    def _():
        for index in range(2):
            at = slice(index * half, (index + 1) * half)

            @pl.when(place.core == 0)
            def _(at=at):
                gram[at, :] = dot_nt(whole[at, :], whole[...]).astype(jnp.bfloat16)

            @pl.when(place.core == 1)
            def _(at=at):
                gram[at, :] = dot_tn(whole[:, at], whole[...]).astype(jnp.bfloat16)

    def side_copy(other):
        spot = pl.ds(pl.multiple_of(other * rows, rows), rows)
        return remote(
            gram.at[spot],
            sides_out.at[owners.member, place.core],
            side_send.at[other],
            side_recv.at[owners.member, place.core],
            (other, owners.group),
        )

    def side_local():
        spot = pl.ds(pl.multiple_of(place.dp * rows, rows), rows)
        return pltpu.make_async_copy(gram.at[spot], sides_out.at[owners.member, place.core], side_own)

    def group_wait(other):
        group_copy(other, place.group).wait_send()
        group_copy(other, other).wait_recv()

    each_other(place.group_size, place.group, group_wait)
    total = group_box[0]
    for other in range(1, place.group_size):
        total = total + group_box[other]
    dp_box[place.dp] = total
    each_other(dp_size, place.dp, lambda other: dp_copy(other, place.dp).start())

    @pl.when(owner)
    def _():
        for other in range(dp_size):
            owners.to_rows(other, lambda other: side_copy(other).start(), lambda: side_local().start())

    def dp_wait(other):
        dp_copy(other, place.dp).wait_send()
        dp_copy(other, other).wait_recv()

    each_other(dp_size, place.dp, dp_wait)
    total = dp_box[0]
    for other in range(1, dp_size):
        total = total + dp_box[other]
    square_out[...] = total

    @pl.when(owner)
    def _():
        factor = jnp.minimum(1.0, max_norm / (jnp.sqrt(total[0:1, 0:1]) + 1e-06))
        square_factor = factor * factor
        spread_f = (1 - stat_decay) * square_factor

        def diagonal(at_start, shape):
            row = lax.broadcasted_iota(jnp.int32, shape, 0) + at_start
            return row == lax.broadcasted_iota(jnp.int32, shape, 1)

        def each_tile(action, carry):
            def step(index, carry):
                start = pl.multiple_of(index * tile, tile)
                return action(pl.ds(start, tile), start, carry)

            return lax.fori_loop(0, D // tile, step, carry, unroll=True)

        def renew(at, start, trace):
            value = stat_decay * stat[at, :].astype(jnp.float32) + spread_f * gram[at, :].astype(
                jnp.float32
            )
            big[at, :] = value
            on = jnp.where(diagonal(start, value.shape), value, 0.0)
            return trace + jnp.sum(jnp.sum(on, 1, keepdims=True), 0, keepdims=True)

        trace = each_tile(renew, jnp.zeros((1, 1), jnp.float32))
        damping = 0.0001 * (trace / D)

        def damp(at, start, total):
            value = big[at, :]
            value = value + jnp.where(diagonal(start, value.shape), damping, 0.0)
            big[at, :] = value
            return total + jnp.sum(jnp.sum(value * value, 1, keepdims=True), 0, keepdims=True)

        magnitude = jnp.sqrt(each_tile(damp, jnp.zeros((1, 1), jnp.float32)))

        def scale(at, start, carry):
            value = big[at, :] / magnitude
            m0[at, :] = value
            m0b[at, :] = value.astype(jnp.bfloat16)
            return carry

        each_tile(scale, 0)
        a = 1.5625

        def square_of(source):
            def then(at, value):
                value = value * 0.0625 - 0.625 * source[at, :]
                s1[at, :] = value
                s1b[at, :] = value.astype(jnp.bfloat16)

            return then

        def fourth(at, value):
            s2b[at, :] = (value + (2 * a) * s1[at, :]).astype(jnp.bfloat16)

        product_rows(m0b, m0b, square_of(m0))
        product_rows(s1b, s1b, fourth)

        def next_one(at, value):
            value = value + (a * a) * m0[at, :]
            m1[at, :] = value
            m1b[at, :] = value.astype(jnp.bfloat16)

        product_rows(s2b, m0b, next_one)

        def joined(at, value):
            value = value * 0.0625 - 0.3125 * (m0[at, :] + m1[at, :])
            s3[at, :] = value
            s3b[at, :] = value.astype(jnp.bfloat16)

        product_rows(m0b, m1b, joined)
        product_rows(m1b, m1b, square_of(m1))
        product_rows(s1b, s1b, fourth)

        def next_two(at, value):
            value = value + (a * a) * m1[at, :]
            m0[at, :] = value
            m0b[at, :] = value.astype(jnp.bfloat16)

        product_rows(s2b, m1b, next_two)
        outer = lax.rsqrt(jnp.sqrt(magnitude))

        def final(at, value):
            value = 1.25 * s3[at, :] - (0.25 * a) * m0[at, :] - 0.25 * value
            start = at.start
            value = value + jnp.where(diagonal(start, value.shape), 1.25 * a, 0.0)
            root[at, :] = (value * outer).astype(jnp.bfloat16)

        product_rows(s3b, m0b, final)

    per_part = dp_size // 2

    def mixed_copy(part):
        at = pl.ds(part * half, half)
        return remote(mixed.at[at], mixed.at[at], mixed_send.at[part], mixed_recv.at[part], c_mate)

    def update_copy(other):
        spot = pl.ds(pl.multiple_of(other * rows, rows), rows)
        return remote(
            m1b.at[spot],
            update_out.at[owners.member],
            update_send.at[other],
            update_recv.at[owners.member],
            (other, owners.group),
        )

    def update_local():
        spot = pl.ds(pl.multiple_of(place.dp * rows, rows), rows)
        return pltpu.make_async_copy(m1b.at[spot], update_out.at[owners.member], update_own)

    @pl.when(owner & (place.core == 0))
    def _():
        for part in range(2):
            at = slice(part * half, (part + 1) * half)
            mixed[at, :] = dot(root[at, :], whole[...]).astype(jnp.bfloat16)
            mixed_copy(part).start()
        for part in range(2):
            mixed_copy(part).wait_send()

    @pl.when(owner & (place.core == 1))
    def _():
        for part in range(2):
            mixed_copy(part).wait_recv()
            at = slice(part * half, (part + 1) * half)
            m1b[at, :] = dot(mixed[at, :], root[...]).astype(jnp.bfloat16)
            for other in range(part * per_part, (part + 1) * per_part):
                owners.to_rows(
                    other, lambda other: update_copy(other).start(), lambda: update_local().start()
                )
        for other in range(dp_size):
            owners.to_rows(
                other, lambda other: update_copy(other).wait_send(), lambda: update_local().wait()
            )

    @pl.when(owner)
    def _():
        for other in range(dp_size):
            owners.to_rows(
                other, lambda other: side_copy(other).wait_send(), lambda: side_local().wait()
            )

    for member in range(members):
        for side in range(2):

            @pl.when((place.dp != owners.of(member)) | (place.core != side))
            def _(member=member, side=side):
                remote(
                    gram.at[pl.ds(0, rows)],
                    sides_out.at[member, side],
                    side_send.at[0],
                    side_recv.at[member, side],
                    me,
                ).wait_recv()

        @pl.when((place.dp != owners.of(member)) | (place.core != 1))
        def _(member=member):
            remote(
                m1b.at[pl.ds(0, rows)],
                update_out.at[member],
                update_send.at[0],
                update_recv.at[member],
                me,
            ).wait_recv()


def shampoo_roots(sizes, members, whole, stat, square):
    dp_size, group_size = sizes
    rows = D // dp_size
    low, full = jnp.bfloat16, jnp.float32
    dma = pltpu.SemaphoreType.DMA
    half, word = pltpu.VMEM((D, D), low), pltpu.VMEM((D, D), full)
    return pl.pallas_call(
        functools.partial(roots_kernel, sizes, members),
        out_shape=[
            jax.ShapeDtypeStruct((members, 2, rows, D), low),
            jax.ShapeDtypeStruct((members, rows, D), low),
            jax.ShapeDtypeStruct((8, 128), full),
        ],
        in_specs=[VMEM] * 3,
        out_specs=[VMEM] * 3,
        scratch_shapes=[half, word, word, half, word, half, word, half, half, word, half, half, half]
        + [pltpu.VMEM((group_size, 8, 128), full), pltpu.VMEM((dp_size, 8, 128), full)]
        + [dma((group_size,))] * 2
        + [dma((dp_size,))] * 2
        + [dma((dp_size,)), dma((members, 2)), dma]
        + [dma((2,)), dma((2,))]
        + [dma((dp_size,)), dma((members,)), dma],
        name="shampoo_roots",
        compiler_params=pltpu.CompilerParams(
            collective_id=2, has_side_effects=True, vmem_limit_bytes=VMEM_LIMIT
        ),
    )(whole, stat, square)


def finish_kernel(rates, *refs):
    square, rows, block_sum, small, kernel, sides, update = refs[:7]
    weights, blocks, statistics = refs[7:25], refs[25], refs[26]
    norm_out, outs = refs[27], refs[28:46]
    block_out, stat_out, blocks_out, loss_out = refs[46:]
    loss_out[...] = rows[LOSS_ROW : LOSS_ROW + 1, 0:1]
    norm = jnp.sqrt(square[0:1, 0:1])
    norm_out[...] = norm
    factor = jnp.minimum(1.0, max_norm / (norm + 1e-06))

    def renew(index, at, grad):
        rate, decay = rates[index]
        ins, out = weights[3 * index : 3 * index + 3], outs[3 * index : 3 * index + 3]
        result = adamw(ins[0][at], grad * factor, ins[1][at], ins[2][at], rate, decay)
        for ref, value in zip(out, result):
            ref[at] = value

    width = weights[0].shape[1]
    vector_rows = weights[6].shape[0]
    renew(0, ..., rows[LOSS_ROW + 1 : LOSS_ROW + 3, :width])
    renew(1, (slice(None), slice(0, 128)), small[0:64, :])
    renew(1, (slice(None), slice(128, 192)), small[64:128, 0:64])
    renew(2, ..., rows[0:vector_rows, :])
    runs, steps, c, channels = weights[9].shape
    for offset in range(steps):
        parts = [kernel[group, offset * c : (offset + 1) * c, :] for group in range(channels // c)]
        renew(
            3,
            (slice(None), offset),
            jnp.concatenate(parts, 0).T.reshape(runs, c, channels),
        )
    renew(4, ..., small[128:224, :].T[0:64])
    renew(5, ..., small[224:256, 0:CLUSTER_ROWS])
    for member in range(blocks.shape[0]):
        block_out[member] = block_sum[member] * factor
        step = update[member].astype(jnp.float32) * factor + decay_weight * blocks[member]
        blocks_out[member] = blocks[member] - rate_shampoo * step
        for side in range(2):
            spread = (1 - stat_decay) * factor * factor
            stat_out[member, side] = stat_decay * statistics[member, side] + spread * sides[
                member, side
            ].astype(jnp.float32)


def finish(sums, weights, blocks, statistics):
    full = jnp.float32
    rates = [(rate_vector, 0.0), (rate_matrix, decay_weight), (rate_vector, 0.0)]
    rates += [(rate_matrix, decay_weight)] * 3
    operands = [*sums, *weights, blocks, statistics]
    shapes = [(1, 1)] + [weight.shape for weight in weights]
    shapes += [blocks.shape, statistics.shape, blocks.shape, (1, 1)]
    return pl.pallas_call(
        functools.partial(finish_kernel, rates),
        out_shape=[jax.ShapeDtypeStruct(shape, full) for shape in shapes],
        in_specs=[VMEM] * len(operands),
        out_specs=[VMEM] * len(shapes),
        name="finish",
        compiler_params=pltpu.CompilerParams(vmem_limit_bytes=VMEM_LIMIT),
    )(*operands)


def conv_to_shard(weight):
    taps, c, channels = weight.shape
    split = weight.reshape(taps // STRIDE, STRIDE, c, channels // c, c)
    return split.transpose(3, 1, 4, 0, 2).reshape(channels // c, STRIDE * c, taps // STRIDE * c)


def conv_from_shard(shard):
    groups, rows, columns = shard.shape
    c = rows // STRIDE
    split = shard.reshape(groups, STRIDE, c, columns // c, c)
    return split.transpose(3, 1, 4, 0, 2).reshape(columns // c * STRIDE, c, groups * c)


def pack_small(projection, head, clusters, note):
    lead, kind = projection.shape[:-2], projection.dtype
    notes = jnp.broadcast_to(note, lead + (32, 2)).astype(kind)
    return jnp.concatenate(
        [
            projection[..., :128],
            jnp.concatenate([projection[..., 128:], jnp.zeros(lead + (64, 64), kind)], -1),
            jnp.concatenate([head, jnp.zeros(lead + (96, 64), kind)], -1),
            jnp.concatenate([jnp.swapaxes(clusters, -1, -2), notes], -1),
        ],
        -2,
    )


def unpack_small(packed):
    projection = jnp.concatenate([packed[..., :64, :], packed[..., 64:128, :64]], -1)
    head = packed[..., 128:224, :64]
    clusters = jnp.swapaxes(packed[..., 224:, :CLUSTER_ROWS], -1, -2)
    return projection, head, clusters


def pack_whole(projection, head, clusters, note):
    def cut(values, down, across):
        rows, columns = values.shape
        return values.reshape(down, rows // down, across, columns // across).transpose(0, 2, 1, 3)

    return pack_small(
        cut(projection, 8, 4), cut(head, 8, 4), cut(clusters, 4, 8).transpose(1, 0, 2, 3), note
    )


def unpack_whole(packed):
    def join(values):
        down, across, rows, columns = values.shape
        return values.transpose(0, 2, 1, 3).reshape(down * rows, across * columns)

    projection, head, clusters = unpack_small(packed)
    return join(projection), join(head), join(clusters.transpose(1, 0, 2, 3))


def parts_of_rows(rows, vector_rows, width):
    return rows[:vector_rows], rows[vector_rows + 1 : vector_rows + 3, :width], rows[vector_rows, 0]


CLUSTER_ROWS = 126
SMALL = ((64, 192), (96, 64), (CLUSTER_ROWS, 32))


def body(
    sizes,
    features,
    span_starts,
    labels,
    feature_norm,
    feature_first,
    feature_second,
    projection,
    projection_first,
    projection_second,
    vectors,
    vector_first,
    vector_second,
    conv_weight,
    conv_first,
    conv_second,
    head,
    head_first,
    head_second,
    clusters,
    cluster_first,
    cluster_second,
    blocks,
    statistics,
):
    dp_size, group_size = sizes
    members, rows = blocks.shape[0], blocks.shape[1]
    masks = jax.vmap(jax.vmap(frame_mask))(span_starts)
    local_count = jnp.sum(masks)
    fast = (
        rows % 16 == 0
        and dp_size % 2 == 0
        and group_size == 4
        and dp_size >= 2 * members
        and (projection.shape, head.shape, clusters.shape) == SMALL
        and conv_weight.shape[2] % conv_weight.shape[1] == 0
        and masks.size <= 256
    )
    frames, vector_rows, width = masks.size, vectors.shape[0], feature_norm.shape[1]
    flat = features.reshape(frames, -1)

    def runs(values):
        return values.reshape((-1, STRIDE) + values.shape[1:])

    if fast:
        taps, c, channels = conv_weight.shape
        taps *= group_size
        shapes = [
            (channels // c, STRIDE * c, taps // group_size // STRIDE * c),
            (256, 128),
            blocks.shape,
        ]
        raw = (
            span_starts.reshape(-1, span_starts.shape[-1]),
            projection, runs(conv_weight), head.T, clusters.T, blocks, statistics,
        )
        kernel_w, small_w, blocks_w, *saved, mask, stats_low = gather_weights(
            sizes, shapes, taps, raw, flat, feature_norm, vectors
        )
    else:
        proj_w, kernel_full, head_w, clusters_w, blocks_w = gather_plain(
            projection, conv_weight, head, clusters, blocks
        )
        whole = conv_to_shard(kernel_full)
        kernel_w = whole.reshape(whole.shape[:2] + (4, -1)).transpose(2, 0, 1, 3)
        count = lax.psum(local_count, ("dp", "group"))
        high = jnp.floor(count / 256.0) * 256.0
        notes = jnp.concatenate([jnp.stack([high, count - high]), jnp.zeros(30, jnp.float32)])
        small_w = pack_whole(proj_w, head_w, clusters_w, notes.reshape(8, 4, 1, 1))
        taps = kernel_w.shape[0] * kernel_w.shape[3] // (D // kernel_w.shape[1]) * STRIDE
        mask = masks.reshape(frames, 1)
        saved = front(flat, mask, feature_norm, vectors, small_w, kernel_w, taps)
    feature_unit, normed, hidden_t, encoded, encoder_unit, encoder_inverse, slope = saved
    extra_parts = (sizes, stats_low) if fast else ()
    encoded_grad, block_part, head_part, center_part, trunk_rows, counted, *stat_whole = trunk(
        encoded, mask, labels.reshape(frames, 1), vectors, small_w, blocks_w, *extra_parts
    )
    masked_count = counted[0, 0]
    operands = (
        encoded_grad, mask, vectors, small_w, feature_unit, normed, hidden_t,
        encoder_unit, encoder_inverse, slope, trunk_rows, head_part, center_part, kernel_w,
    )
    if fast:
        kernel_sum, small_sum, block_sum, extra, square, whole = back_reduce(
            sizes, shapes, taps, operands, block_part
        )
        sides, update_rows, square = shampoo_roots(sizes, members, whole, *stat_whole, square)

        done = finish(
            (square, extra, block_sum, small_sum, kernel_sum, sides, update_rows),
            (
                feature_norm, feature_first, feature_second,
                projection, projection_first, projection_second,
                vectors, vector_first, vector_second,
                runs(conv_weight), runs(conv_first), runs(conv_second),
                head.T, head_first.T, head_second.T,
                clusters.T, cluster_first.T, cluster_second.T,
            ),
            blocks,
            statistics,
        )
        outs = []
        for index in range(0, 18, 3):
            parts = done[1 + index : 4 + index]
            if index == 9:
                parts = [part.reshape(conv_weight.shape) for part in parts]
            if index >= 12:
                parts = [part.T for part in parts]
            outs += parts
        return (done[-1][0, 0], masked_count, done[0][0, 0], *outs, *done[19:22])
    kernel_part, small_part, row_part = back(taps, operands)
    proj_part, head_part, center_part = unpack_whole(small_part)
    kernel_plain = conv_from_shard(
        kernel_part.transpose(1, 2, 0, 3).reshape(kernel_part.shape[1:3] + (-1,))
    )
    large_total = reduce_grads(
        tuple(
            part.astype(jnp.float32)
            for part in (proj_part, kernel_plain, head_part, center_part, block_part)
        )
    )
    vector_grad, feature_grad, loss_sum = parts_of_rows(
        lax.psum(row_part, ("dp", "group")), vector_rows, width
    )
    local_squares = sum((jnp.sum(part * part) for part in large_total))
    norm_square = (
        lax.psum(local_squares, ("dp", "group"))
        + jnp.sum(feature_grad * feature_grad)
        + jnp.sum(vector_grad * vector_grad)
    )
    grad_norm = jnp.sqrt(norm_square)
    factor = jnp.minimum(1.0, max_norm / (grad_norm + 1e-06))
    proj_grad, kernel_grad, head_grad, cluster_grad, block_rows = [
        part * factor for part in large_total
    ]
    feature_out = adamw(
        feature_norm, feature_grad * factor, feature_first, feature_second, rate_vector, 0.0
    )
    projection_out = adamw(
        projection, proj_grad, projection_first, projection_second, rate_matrix, decay_weight
    )
    vector_out = adamw(vectors, vector_grad * factor, vector_first, vector_second, rate_vector, 0.0)
    conv_out = adamw(conv_weight, kernel_grad, conv_first, conv_second, rate_matrix, decay_weight)
    head_out = adamw(head, head_grad, head_first, head_second, rate_matrix, decay_weight)
    cluster_out = adamw(
        clusters, cluster_grad, cluster_first, cluster_second, rate_matrix, decay_weight
    )
    statistics_new, update_rows = shampoo_plain(block_rows, statistics)
    blocks_new = blocks - rate_shampoo * (update_rows + decay_weight * blocks)
    return (
        loss_sum,
        masked_count,
        grad_norm,
        *feature_out,
        *projection_out,
        *vector_out,
        *conv_out,
        *head_out,
        *cluster_out,
        block_rows,
        statistics_new,
        blocks_new,
    )


def solution(mesh):
    in_specs = (
        P(None, ("dp", "group"), None, None),
        P(None, ("dp", "group"), None),
        P(None, ("dp", "group"), None),
        P(),
        P(),
        P(),
        P("dp", "group"),
        P("dp", "group"),
        P("dp", "group"),
        P(),
        P(),
        P(),
        P("group", None, "dp"),
        P("group", None, "dp"),
        P("group", None, "dp"),
        P("dp", "group"),
        P("dp", "group"),
        P("dp", "group"),
        P("group", "dp"),
        P("group", "dp"),
        P("group", "dp"),
        P("group", "dp", None),
        P("group", None, "dp", None),
    )
    out_specs = (
        P(),
        P(),
        P(),
        P(),
        P(),
        P(),
        P("dp", "group"),
        P("dp", "group"),
        P("dp", "group"),
        P(),
        P(),
        P(),
        P("group", None, "dp"),
        P("group", None, "dp"),
        P("group", None, "dp"),
        P("dp", "group"),
        P("dp", "group"),
        P("dp", "group"),
        P("group", "dp"),
        P("group", "dp"),
        P("group", "dp"),
        P("group", "dp", None),
        P("group", None, "dp", None),
        P("group", "dp", None),
    )
    return jax.shard_map(
        functools.partial(body, (mesh.shape["dp"], mesh.shape["group"])), mesh=mesh, in_specs=in_specs, out_specs=out_specs, check_vma=False)
```
